32 devices in a mesh: rows: 2 (over x), samples: 4 (over y, core), chan: 4 (over z).
Axes of the slice: x: 2, y: 2, z: 4, core: 2. Of those that a mesh axis runs over, the one named last changes fastest.
Arguments:
- feature: bfloat16 [4, 256, 16, 512], P('samples', 'chan', 'rows'), may hold values from -6 to 6
- out_grad: bfloat16 [4, 256, 16, 512], P('samples', 'chan', 'rows'), may hold values from -6 to 6
- bank: float32 [4, 9, 256, 256], P(None, None, 'chan', 'rows'), may hold values from -0.125 to 0.125
- select: int32 [4, 4], P('samples'), may hold values from 1 to 8
- latent: float32 [4, 512], P('samples'), may hold values from -6 to 6
- affine_w: float32 [512, 256], P(None, 'rows'), may hold values from -0.25 to 0.25
- affine_b: float32 [256], P('rows'), may hold values from 0.5 to 1.5
Outputs:
- feature_grad: bfloat16 [4, 256, 16, 512], P('samples', 'chan', 'rows')
- bank_grad: float32 [4, 9, 256, 256], P(None, None, 'chan', 'rows')
- affine_w_grad: float32 [512, 256], P(None, 'rows')
- affine_b_grad: float32 [256], P('rows')
The draws below stay inside these ranges and needn't reach their ends.
All inputs are finite; a program needn't handle non-finite values.
Results may differ from the reference program's by a relative error of at most 0.0049.
Values may be sent and summed in bfloat16 or wider, within the bound.
No kernel may reach another device: no remote copies, remote signals or barrier semaphores. Data moves between devices by JAX's collectives and lax.ppermute only.
A program may use at most 128 MiB of HBM per device.

```python
import jax
import jax.numpy as jnp
from jax import lax

C = 256
NB = 4
Z = 512
WIDTH = 512
HEIGHT = 16
SAMPLES = 4


def set_ends(array, own_key, low, largest):
    place = [jax.random.randint(jax.random.fold_in(own_key, axis), (), 0, length) for axis, length in enumerate(array.shape)]
    longest = array.shape.index(max(array.shape))
    next_to = place[:longest] + [(place[longest] + 1) % array.shape[longest]] + place[longest + 1:]
    return array.at[tuple(place)].set(low).at[tuple(next_to)].set(largest)


def block_scale(rng, dims, split, low, top_value):
    factor_of, own = 1.0, jax.random.fold_in(rng, 6)
    for position, blocks in split:
        draws = jnp.exp(jax.random.uniform(jax.random.fold_in(own, position), (blocks,), jnp.float32, low / len(split), top_value / len(split)))
        factor_of = factor_of * jnp.repeat(draws, dims[position] // blocks).reshape([-1 if axis == position else 1 for axis in range(len(dims))])
    return factor_of


def bell_draw(stream_key, dims, scale, most, pieces=(), held_as=jnp.bfloat16):
    result = jax.random.normal(stream_key, dims, jnp.float32) * scale
    if len(pieces) > 0:
        result = block_scale(stream_key, dims, pieces, -0.22, 0.18) * result
    return jnp.clip(result, min=-most, max=most).astype(held_as)


def setup_inputs(seed: int = 0) -> dict:
    streams_of = jax.random.split(jax.random.key(seed), 8)
    return {
        "feature": bell_draw(streams_of[0], (SAMPLES, C, HEIGHT, WIDTH), 1.0, 6.0, ((0, 4), (1, 4), (2, 2))),
        "out_grad": bell_draw(streams_of[1], (SAMPLES, C, HEIGHT, WIDTH), 1.0, 6.0, ((0, 4), (1, 4), (2, 2))),
        "bank": bell_draw(streams_of[2], (NB, 9, C, C), (9 * C) ** -0.5, 0.125, ((2, 4), (3, 2)), jnp.float32),
        "select": set_ends(jax.random.randint(streams_of[3], (SAMPLES, NB), 1, 9), jax.random.fold_in(streams_of[3], 1), 1, 8).astype(jnp.int32),
        "latent": bell_draw(streams_of[4], (SAMPLES, Z), 1.0, 6.0, ((0, 4),), jnp.float32),
        "affine_w": bell_draw(streams_of[5], (Z, C), Z ** -0.5, 0.25, ((1, 2),), jnp.float32),
        "affine_b": jnp.clip(0.5 + 1.0 * jax.random.uniform(streams_of[6], (C,), jnp.float32) ** block_scale(streams_of[6], (C,), ((0, 2),), -0.2, 0.2), 0.5, 1.5),
    }


EPS = 1e-08

def reference(feature, out_grad, bank, select, latent, affine_w, affine_b):
    chans = feature.shape[1]
    height = feature.shape[2]
    width = feature.shape[3]

    def one_sample(items):
        feat, cotan, weights, style_in = items
        kernel = jnp.einsum('k,ktoc->toc', weights.astype(jnp.float32), bank, precision=lax.Precision.HIGHEST)
        style = jnp.dot(style_in, affine_w, precision=lax.Precision.HIGHEST) + affine_b
        plain = kernel * style[None, None, :]
        scale = lax.rsqrt(lax.optimization_barrier(jnp.sum(plain * plain, axis=(0, 2))) + EPS)
        modulated = (plain * scale[None, :, None]).astype(jnp.bfloat16)
        feat_pad = jnp.pad(feat, ((0, 0), (1, 1), (1, 1)))
        cotan_pad = jnp.pad(cotan, ((0, 0), (1, 1), (1, 1)))
        cotan_flat = cotan.reshape(chans, height * width)
        input_total = jnp.zeros((chans, height * width), jnp.float32)
        grads = []
        for tap_index in range(9):
            row_off = tap_index // 3
            col_off = tap_index % 3
            feat_tap = feat_pad[:, row_off:row_off + height, col_off:col_off + width].reshape(chans, height * width)
            cotan_tap = cotan_pad[:, 2 - row_off:2 - row_off + height, 2 - col_off:2 - col_off + width].reshape(chans, height * width)
            grads.append(jnp.dot(cotan_flat, feat_tap.T, preferred_element_type=jnp.float32))
            input_total = input_total + jnp.dot(modulated[tap_index].T, cotan_tap, preferred_element_type=jnp.float32)
        mod_grad = jnp.stack(grads, 0)
        slope = lax.optimization_barrier(jnp.sum(mod_grad * plain, axis=(0, 2)))
        plain_grad = mod_grad * scale[None, :, None] - plain * (slope * scale ** 3)[None, :, None]
        kernel_grad = plain_grad * style[None, None, :]
        style_grad = lax.optimization_barrier(jnp.sum(plain_grad * kernel, axis=(0, 1)))
        return (input_total.reshape(chans, height, width).astype(jnp.bfloat16), kernel_grad, style_grad)
    feature_grad, kernel_grads, style_grads = lax.map(one_sample, (feature, out_grad, select, latent))
    bank_grad = jnp.einsum('bk,btoc->ktoc', select.astype(jnp.float32), kernel_grads, precision=lax.Precision.HIGHEST)
    affine_w_grad = jnp.dot(latent.T, style_grads, precision=lax.Precision.HIGHEST)
    affine_b_grad = lax.optimization_barrier(jnp.sum(style_grads, axis=0))
    return (feature_grad, bank_grad, affine_w_grad, affine_b_grad)
```

```python
import functools

import jax
import jax.numpy as jnp
from jax import lax
from jax.experimental import pallas as pl
from jax.experimental.pallas import tpu as pltpu
from jax.sharding import PartitionSpec as P

EPS = 1e-08
TAPS = 9
F32 = jnp.float32
BF16 = jnp.bfloat16
VMEM_LIMIT = 48 * 2**20


def params():
    return pltpu.CompilerParams(vmem_limit_bytes=VMEM_LIMIT)


def vspec(n):
    return [pl.BlockSpec(memory_space=pltpu.VMEM)] * n


def sspec(n):
    return [pl.BlockSpec(memory_space=pltpu.SMEM)] * n


def cost(flops, moved):
    return pl.CostEstimate(flops=flops, bytes_accessed=moved, transcendentals=0)


def column(table, index):
    lane = lax.broadcasted_iota(jnp.int32, table.shape, 1)
    return jnp.sum(jnp.where(lane == index, table, 0.0), axis=1, keepdims=True)


def beside(pieces):
    return pieces[0] if len(pieces) == 1 else jnp.concatenate(pieces, axis=1)


def mixed(bank_ref, sel, sample, tap):
    total = sel[sample, 0] * bank_ref[0, tap]
    for k in range(1, bank_ref.shape[0]):
        total = total + sel[sample, k] * bank_ref[k, tap]
    return total


class Routes:
    def __init__(self, rows, size):
        self.rows, self.size = rows, size
        self.blocks, self.fold = max(1, size // rows), max(1, rows // size)
        self.steps = max(rows, size)

    def user_code(self, row, chan):
        return lax.rem(chan, self.blocks) + self.blocks * row

    def owner_code(self, row, chan):
        return chan + self.size * lax.rem(row, self.fold)

    def pairs(self, step):
        out = []
        for row in range(self.rows):
            for chan in range(self.size):
                code = (chan % self.blocks + self.blocks * row + step) % self.steps
                owner_row = chan // self.blocks * self.fold + code // self.size
                out.append((owner_row * self.size + code % self.size, row * self.size + chan))
        return out


def energy_kernel(sel, bank, latent, affine_w, affine_b, style_out, energy_out):
    samples = latent.shape[0]
    style = (
        jnp.dot(latent[...], affine_w[...], precision=lax.Precision.HIGHEST, preferred_element_type=F32)
        + affine_b[...]
    )
    style_out[...] = style
    out_ch, in_ch = bank.shape[2], bank.shape[3]
    totals = [jnp.zeros((out_ch, in_ch), F32) for _ in range(samples)]
    for tap in range(TAPS):
        for b in range(samples):
            plain = mixed(bank, sel, b, tap) * style[b : b + 1]
            totals[b] = totals[b] + plain * plain
    lane = lax.broadcasted_iota(jnp.int32, (out_ch, 128), 1)
    table = jnp.zeros((out_ch, 128), F32)
    for b in range(samples):
        table = jnp.where(lane == b, jnp.sum(totals[b], axis=1, keepdims=True), table)
    energy_out[...] = table


def modulated_kernel(routes, width, place, sel, bank, style, energy, *outs):
    sample, blocks = place[0], routes.blocks
    scale = lax.rsqrt(column(energy[...], sample) + EPS)
    own_style = style[pl.ds(sample, 1), :]
    mods = [mixed(bank, sel, sample, tap) * own_style * scale for tap in range(TAPS)]
    messages = [
        beside([m[:, j * width : (j + 1) * width] for m in mods]).astype(BF16)
        for j in range(blocks)
    ]
    code = routes.owner_code(place[2], place[1])
    for m in range(routes.steps):
        pick = lax.rem(lax.rem(code - m + routes.steps, routes.steps), blocks)
        value = messages[0]
        for j in range(1, blocks):
            value = jnp.where(pick == j, messages[j], value)
        outs[m][...] = value


def shifted(x, by):
    width = x.shape[1]
    lane = lax.broadcasted_iota(jnp.int32, x.shape, 1)
    moved = pltpu.roll(x, by % width, 1)
    return jnp.where(lane == (0 if by == 1 else width - 1), 0.0, moved)


def kernel_grad_kernel(routes, height, width, *refs):
    size, fold = routes.size, routes.fold
    cotan_own, left, right = refs[0], refs[1:size], refs[size : 2 * size - 1]
    feat, feat_before, feat_after = refs[2 * size - 1 : 2 * size + 2]
    outs = refs[2 * size + 2 : 2 * size + 2 + routes.steps]
    wide, gathered, total = refs[2 * size + 2 + routes.steps :]
    ch = feat.shape[0]
    gathered[0:ch] = cotan_own[...]
    for d in range(1, size):
        gathered[d * ch : (d + 1) * ch] = left[d - 1][...] + right[size - d - 1][...]
    for row in range(height + 2):
        if row == 0:
            x = feat_before[...]
        elif row == height + 1:
            x = feat_after[...]
        else:
            x = feat[:, (row - 1) * width : row * width]
        wide[ch : 2 * ch, row * width : (row + 1) * width] = x
        x = x.astype(F32)
        wide[0:ch, row * width : (row + 1) * width] = shifted(x, 1).astype(BF16)
        wide[2 * ch : 3 * ch, row * width : (row + 1) * width] = shifted(x, -1).astype(BF16)
    total[...] = jnp.zeros(total.shape, F32)

    def body(row, _):
        g = gathered[:, pl.ds(pl.multiple_of(row * width, width), width)]
        for kh in range(3):
            x = wide[:, pl.ds(pl.multiple_of((row + kh) * width, width), width)]
            total[kh] += lax.dot_general(g, x, (((1,), (1,)), ((), ())), preferred_element_type=F32)
        return 0

    lax.fori_loop(0, height, body, 0)
    whole = jnp.concatenate([total[kh] for kh in range(3)], axis=1)
    part = ch // fold
    for k in range(fold):
        value = whole
        if fold > 1:
            starts = [tap * ch + k * part for tap in range(TAPS)]
            value = jnp.concatenate([whole[:, at : at + part] for at in starts], axis=1)
        for d in range(size):
            outs[k * size + d][...] = value[d * ch : (d + 1) * ch].astype(BF16)


def input_grad_kernel(routes, height, width, place, *refs):
    size, fold, steps = routes.size, routes.fold, routes.steps
    cotan_own, left, right = refs[0], refs[1:size], refs[size : 2 * size - 1]
    mods = refs[2 * size - 1 : 2 * size - 1 + steps]
    main, before, after, gathered, taps, taps_t, total = refs[2 * size - 1 + steps :]
    ch = cotan_own.shape[0]
    chan = place[1]
    gathered[0:ch] = cotan_own[...]
    for d in range(1, size):
        gathered[d * ch : (d + 1) * ch] = left[d - 1][...] + right[size - d - 1][...]
    code = routes.user_code(place[2], chan)
    for m in range(steps):
        owner = lax.rem(code + m, steps)
        slot = lax.rem(chan - lax.rem(owner, size) + size, size)
        taps[lax.div(owner, size) * size + slot] = mods[m][...].astype(F32)
    part = ch // fold
    every = taps[0:size].reshape(size * ch, TAPS * part)
    if fold > 1:
        pieces = [taps[k * size : (k + 1) * size].reshape(size * ch, TAPS * part) for k in range(fold)]
        every = jnp.concatenate(
            [p[:, tap * part : (tap + 1) * part] for tap in range(TAPS) for p in pieces], axis=1
        )
    taps_t[...] = every.T.astype(BF16)
    total[...] = jnp.zeros(total.shape, F32)

    def body(row, _):
        g = gathered[:, pl.ds(pl.multiple_of(row * width, width), width)]
        for kh in range(3):
            y = jnp.dot(taps_t[kh * 3 * ch : (kh + 1) * 3 * ch], g, preferred_element_type=F32)
            total[row + kh] += y
        return 0

    lax.fori_loop(0, height, body, 0)
    for row in range(height + 2):
        value = total[row, ch : 2 * ch]
        value = value + shifted(total[row, 0:ch], -1) + shifted(total[row, 2 * ch : 3 * ch], 1)
        if row == 0:
            before[...] = value
        elif row == height + 1:
            after[...] = value
        else:
            main[:, (row - 1) * width : row * width] = value


def collect_kernel(routes, place, sel, bank, style, *refs):
    rows, blocks, steps = routes.rows, routes.blocks, routes.steps
    parts = refs[:steps]
    out, slope_out, held = refs[steps:]
    sample = place[0]
    code = routes.owner_code(place[2], place[1])
    for m in range(steps):
        held[lax.rem(code - m + steps, steps)] = parts[m][...].astype(F32)
    sums = []
    for j in range(blocks):
        value = held[j]
        for r in range(1, rows):
            value = value + held[r * blocks + j]
        sums.append(value)
    width = sums[0].shape[1] // TAPS
    own_style = style[pl.ds(sample, 1), :]
    product = jnp.zeros(bank.shape[2:], F32)
    for tap in range(TAPS):
        whole = beside([s[:, tap * width : (tap + 1) * width] for s in sums]).astype(BF16)
        out[tap] = whole
        product = product + whole.astype(F32) * (mixed(bank, sel, sample, tap) * own_style)
    slope = jnp.sum(product, axis=1, keepdims=True)
    lane = lax.broadcasted_iota(jnp.int32, slope_out.shape, 1)
    slope_out[...] = jnp.where(lane == sample, slope, 0.0)


def bank_grad_kernel(samples, place, sel, bank, style, energy, slope, *refs):
    parts = refs[:samples]
    bank_grad, style_grad, held = refs[samples:]
    sample = place[0]
    for s in range(samples):
        held[lax.rem(sample - s + samples, samples)] = parts[s][...]
    styles = style[...]
    energies, slopes = energy[...], slope[...]
    scales, falls = [], []
    for b in range(samples):
        scale = lax.rsqrt(energies[:, b : b + 1] + EPS)
        scales.append(scale)
        falls.append(slopes[:, b : b + 1] * (scale * scale * scale))
    sums = [jnp.zeros(bank.shape[2:], F32) for _ in range(samples)]
    for tap in range(TAPS):
        totals = [None] * bank.shape[0]
        for b in range(samples):
            kern = mixed(bank, sel, b, tap)
            own_style = styles[b : b + 1]
            plain_grad = held[b, tap].astype(F32) * scales[b] - kern * own_style * falls[b]
            sums[b] = sums[b] + plain_grad * kern
            kernel_grad = plain_grad * own_style
            for k in range(bank.shape[0]):
                term = sel[b, k] * kernel_grad
                totals[k] = term if totals[k] is None else totals[k] + term
        for k in range(bank.shape[0]):
            bank_grad[k, tap] = totals[k]
    for b in range(samples):
        style_grad[b : b + 1] = jnp.sum(sums[b], axis=0, keepdims=True)


def on_device(feature, out_grad, bank, select, latent, affine_w, affine_b):
    rows, samples, size = (lax.axis_size(a) for a in ("rows", "samples", "chan"))
    row_at, sample_at, chan_at = (lax.axis_index(a) for a in ("rows", "samples", "chan"))
    _, ch, height, width = feature.shape
    pixels = height * width
    in_ch = bank.shape[3]
    routes = Routes(rows, size)
    place = jnp.stack([sample_at, chan_at, row_at]).astype(jnp.int32)

    cotan = out_grad[0].reshape(ch, pixels)
    left, right = [], []
    from_left = from_right = cotan
    for step in range(1, size):
        from_left = lax.ppermute(from_left, "chan", [(i, i + 1) for i in range(step - 1, size - 1)])
        from_right = lax.ppermute(from_right, "chan", [(i + 1, i) for i in range(size - step)])
        left.append(from_left)
        right.append(from_right)

    feat = feature[0].reshape(ch, pixels)
    up = [(i, i + 1) for i in range(rows - 1)]
    down = [(i + 1, i) for i in range(rows - 1)]
    feat_before = lax.ppermute(feat[:, pixels - width :], "rows", up)
    feat_after = lax.ppermute(feat[:, :width], "rows", down)

    small = jnp.concatenate([latent[0], select[0].astype(F32)])
    small = lax.all_gather(small, "samples", axis=0)
    latents, sel = small[:, : latent.shape[1]], small[:, latent.shape[1] :]
    out_ch = bank.shape[2]
    style, energy = pl.pallas_call(
        energy_kernel,
        out_shape=(
            jax.ShapeDtypeStruct((samples, in_ch), F32),
            jax.ShapeDtypeStruct((out_ch, 128), F32),
        ),
        in_specs=sspec(1) + vspec(4),
        out_specs=tuple(vspec(2)),
        compiler_params=params(),
        cost_estimate=cost(10**7, bank.size * 4),
        name="energy",
    )(sel, bank, latents, affine_w, affine_b[None])
    energy = lax.psum(energy, "rows")
    message = jax.ShapeDtypeStruct((ch, TAPS * min(ch, in_ch)), BF16)
    to_send = pl.pallas_call(
        functools.partial(modulated_kernel, routes, min(ch, in_ch)),
        out_shape=(message,) * routes.steps,
        in_specs=sspec(2) + vspec(3),
        out_specs=tuple(vspec(routes.steps)),
        compiler_params=params(),
        cost_estimate=cost(10**7, bank.size * 4),
        name="modulated",
    )(place, sel, bank, style, energy)
    mods = [lax.ppermute(to_send[m], ("rows", "chan"), routes.pairs(m)) for m in range(routes.steps)]

    parts = pl.pallas_call(
        functools.partial(kernel_grad_kernel, routes, height, width),
        out_shape=(message,) * routes.steps,
        in_specs=vspec(2 * size + 2),
        out_specs=tuple(vspec(routes.steps)),
        scratch_shapes=[
            pltpu.VMEM((3 * ch, (height + 2) * width), BF16),
            pltpu.VMEM((size * ch, pixels), BF16),
            pltpu.VMEM((3, size * ch, 3 * ch), F32),
        ],
        compiler_params=params(),
        cost_estimate=cost(2 * TAPS * ch * ch * size * pixels, (2 * size + 1) * ch * pixels * 2),
        name="kernel_grad",
    )(cotan, *left, *right, feat, feat_before, feat_after)

    code = routes.user_code(row_at, chan_at)
    received = []
    for m in range(routes.steps):
        owner = lax.rem(code + m, routes.steps)
        slot = lax.rem(chan_at - lax.rem(owner, size) + size, size) + lax.div(owner, size) * size
        value = parts[0]
        for d in range(1, routes.steps):
            value = jnp.where(slot == d, parts[d], value)
        pairs = [(user, owner_at) for owner_at, user in routes.pairs(m)]
        received.append(lax.ppermute(value, ("rows", "chan"), pairs))

    main, before, after = pl.pallas_call(
        functools.partial(input_grad_kernel, routes, height, width),
        out_shape=(
            jax.ShapeDtypeStruct((ch, pixels), F32),
            jax.ShapeDtypeStruct((ch, width), F32),
            jax.ShapeDtypeStruct((ch, width), F32),
        ),
        in_specs=sspec(1) + vspec(2 * size - 1 + routes.steps),
        out_specs=tuple(vspec(3)),
        scratch_shapes=[
            pltpu.VMEM((size * ch, pixels), BF16),
            pltpu.VMEM((routes.steps, *message.shape), F32),
            pltpu.VMEM((TAPS * ch, size * ch), BF16),
            pltpu.VMEM((height + 2, 3 * ch, width), F32),
        ],
        compiler_params=params(),
        cost_estimate=cost(2 * TAPS * ch * ch * size * pixels, (2 * size + 1) * ch * pixels * 2),
        name="input_grad",
    )(place, cotan, *left, *right, *mods)
    from_below = lax.ppermute(before, "rows", down)
    from_above = lax.ppermute(after, "rows", up)
    edge = jnp.concatenate(
        [from_above[:, None], jnp.zeros((ch, height - 2, width), F32), from_below[:, None]], axis=1
    )
    feature_grad = (main.reshape(ch, height, width) + edge).astype(BF16)[None]

    mod_grad, slope = pl.pallas_call(
        functools.partial(collect_kernel, routes),
        out_shape=(
            jax.ShapeDtypeStruct((TAPS, out_ch, in_ch), BF16),
            jax.ShapeDtypeStruct((out_ch, 128), F32),
        ),
        in_specs=sspec(2) + vspec(2 + routes.steps),
        out_specs=tuple(vspec(2)),
        scratch_shapes=[pltpu.VMEM((routes.steps, *message.shape), F32)],
        compiler_params=params(),
        cost_estimate=cost(10**7, bank.size * 4),
        name="collect",
    )(place, sel, bank, style, *received)
    others = [
        lax.ppermute(mod_grad, "samples", [(i, (i + s) % samples) for i in range(samples)])
        for s in range(1, samples)
    ]
    slope = lax.psum(slope, ("rows", "samples"))
    bank_grad, style_part = pl.pallas_call(
        functools.partial(bank_grad_kernel, samples),
        out_shape=(
            jax.ShapeDtypeStruct(bank.shape, F32),
            jax.ShapeDtypeStruct((samples, in_ch), F32),
        ),
        in_specs=sspec(2) + vspec(4 + samples),
        out_specs=tuple(vspec(2)),
        scratch_shapes=[pltpu.VMEM((samples, TAPS, out_ch, in_ch), BF16)],
        compiler_params=params(),
        cost_estimate=cost(4 * 10**7, bank.size * 8),
        name="bank_grad",
    )(place, sel, bank, style, energy, slope, mod_grad, *others)
    style_grad = lax.psum(style_part, "chan")
    affine_w_grad = jnp.sum(latents[:, :, None] * style_grad[:, None, :], axis=0)
    affine_b_grad = jnp.sum(style_grad, axis=0)
    return (feature_grad, bank_grad, affine_w_grad, affine_b_grad)


def solution(mesh):
    return jax.shard_map(
        on_device,
        mesh=mesh,
        in_specs=(
            P("samples", "chan", "rows", None),
            P("samples", "chan", "rows", None),
            P(None, None, "chan", "rows"),
            P("samples", None),
            P("samples", None),
            P(None, "rows"),
            P("rows"),
        ),
        out_specs=(
            P("samples", "chan", "rows", None),
            P(None, None, "chan", "rows"),
            P(None, "rows"),
            P("rows"),
        ),
        check_vma=False,
    )
```

```python
import functools

import jax
import jax.numpy as jnp
from jax import lax
from jax.experimental import pallas as pl
from jax.experimental.pallas import tpu as pltpu
from jax.sharding import PartitionSpec as P

EPS = 1e-08
TAPS = 9
F32 = jnp.float32
BF16 = jnp.bfloat16
VMEM_LIMIT = 48 * 2**20


def params():
    return pltpu.CompilerParams(vmem_limit_bytes=VMEM_LIMIT)


def vspec(n):
    return [pl.BlockSpec(memory_space=pltpu.VMEM)] * n


def sspec(n):
    return [pl.BlockSpec(memory_space=pltpu.SMEM)] * n


def cost(flops, moved):
    return pl.CostEstimate(flops=flops, bytes_accessed=moved, transcendentals=0)


def column(table, index):
    lane = lax.broadcasted_iota(jnp.int32, table.shape, 1)
    return jnp.sum(jnp.where(lane == index, table, 0.0), axis=1, keepdims=True)


def beside(pieces):
    return pieces[0] if len(pieces) == 1 else jnp.concatenate(pieces, axis=1)


def mixed(bank_ref, sel, sample, tap):
    total = sel[sample, 0] * bank_ref[0, tap]
    for k in range(1, bank_ref.shape[0]):
        total = total + sel[sample, k] * bank_ref[k, tap]
    return total


def energy_kernel(sel, bank, latent, affine_w, affine_b, style_out, energy_out):
    samples = latent.shape[0]
    style = (
        jnp.dot(latent[...], affine_w[...], precision=lax.Precision.HIGHEST, preferred_element_type=F32)
        + affine_b[...]
    )
    style_out[...] = style
    out_ch, in_ch = bank.shape[2], bank.shape[3]
    totals = [jnp.zeros((out_ch, in_ch), F32) for _ in range(samples)]
    for tap in range(TAPS):
        for b in range(samples):
            plain = mixed(bank, sel, b, tap) * style[b : b + 1]
            totals[b] = totals[b] + plain * plain
    lane = lax.broadcasted_iota(jnp.int32, (out_ch, 128), 1)
    table = jnp.zeros((out_ch, 128), F32)
    for b in range(samples):
        table = jnp.where(lane == b, jnp.sum(totals[b], axis=1, keepdims=True), table)
    energy_out[...] = table


def modulated_kernel(rows, place, sel, bank, style, *refs):
    energies, (mod_out, scale_out) = refs[:rows], refs[rows:]
    sample = place[0]
    energy = energies[0][...]
    for r in range(1, rows):
        energy = energy + energies[r][...]
    scales = lax.rsqrt(energy + EPS)
    scale_out[...] = scales
    scale = column(scales, sample)
    own_style = style[pl.ds(sample, 1), :]
    for tap in range(TAPS):
        mod_out[tap] = (mixed(bank, sel, sample, tap) * own_style * scale).astype(BF16)


def blocks_kernel(rows, size, place, *refs):
    parts, whole, outs = refs[:rows], refs[rows], refs[rows + 1 : rows + 1 + size]
    by_row, by_chan = refs[rows + 1 + size :]
    row_at, chan_at = place[2], place[1]
    for r in range(rows):
        by_row[lax.rem(row_at - r + rows, rows)] = parts[r][...]
    ch = whole.shape[2] // size
    taps = []
    for tap in range(TAPS):
        value = beside([by_row[r, tap].astype(F32) for r in range(rows)])
        whole[tap] = value.astype(BF16)
        taps.append(value)
    for z in range(size):
        by_chan[z] = beside([value[:, z * ch : (z + 1) * ch] for value in taps]).astype(BF16)
    for d in range(size):
        outs[d][...] = by_chan[lax.rem(chan_at + d, size)]


def shifted(x, by):
    width = x.shape[1]
    lane = lax.broadcasted_iota(jnp.int32, x.shape, 1)
    moved = pltpu.roll(x, by % width, 1)
    return jnp.where(lane == (0 if by == 1 else width - 1), 0.0, moved)


def tap_products(g_ref, wide, total, height, width):
    total[...] = jnp.zeros(total.shape, F32)

    def body(row, _):
        g = g_ref[:, pl.ds(pl.multiple_of(row * width, width), width)]
        for kh in range(3):
            x = wide[:, pl.ds(pl.multiple_of((row + kh) * width, width), width)]
            total[kh] += lax.dot_general(g, x, (((1,), (1,)), ((), ())), preferred_element_type=F32)
        return 0

    lax.fori_loop(0, height, body, 0)
    return jnp.concatenate([total[kh] for kh in range(3)], axis=1)


def near_grad_kernel(size, height, width, *refs):
    cotan_own, left, right = refs[0], refs[1 : size - 1], refs[size - 1 : 2 * size - 3]
    feat, feat_before, feat_after, out, wide, gathered, total = refs[2 * size - 3 :]
    ch = feat.shape[0]
    gathered[0:ch] = cotan_own[...]
    for d in range(1, size):
        found = []
        if d < size - 1:
            found.append(left[d - 1][...])
        if size - d < size - 1:
            found.append(right[size - d - 1][...])
        gathered[d * ch : (d + 1) * ch] = found[0] if len(found) == 1 else found[0] + found[1]
    for row in range(height + 2):
        if row == 0:
            x = feat_before[...]
        elif row == height + 1:
            x = feat_after[...]
        else:
            x = feat[:, (row - 1) * width : row * width]
        wide[ch : 2 * ch, row * width : (row + 1) * width] = x
        x = x.astype(F32)
        wide[0:ch, row * width : (row + 1) * width] = shifted(x, 1).astype(BF16)
        wide[2 * ch : 3 * ch, row * width : (row + 1) * width] = shifted(x, -1).astype(BF16)
    out[...] = tap_products(gathered, wide, total, height, width).astype(BF16)


def far_grad_kernel(rows, size, height, width, left, right, wide, *refs):
    nears, far_out, outs = refs[:rows], refs[rows], refs[rows + 1 : rows + 1 + size]
    cotan, total = refs[rows + 1 + size :]
    cotan[...] = left[...] + right[...]
    far_out[...] = tap_products(cotan, wide, total, height, width).astype(BF16)
    ch = cotan.shape[0]
    for d in range(size):
        value = nears[0][d * ch : (d + 1) * ch].astype(F32)
        for r in range(1, rows):
            value = value + nears[r][d * ch : (d + 1) * ch].astype(F32)
        outs[d][...] = value.astype(BF16)


def sum_kernel(*refs):
    value = refs[0][...].astype(F32)
    for ref in refs[1:-1]:
        value = value + ref[...].astype(F32)
    refs[-1][...] = value.astype(BF16)


def input_grad_kernel(size, height, width, *refs):
    cotan_own, left, right = refs[0], refs[1:size], refs[size : 2 * size - 1]
    mods = refs[2 * size - 1 : 3 * size - 1]
    main, before, after, gathered, taps_t, total = refs[3 * size - 1 :]
    ch = cotan_own.shape[0]
    gathered[0:ch] = cotan_own[...]
    for d in range(1, size):
        gathered[d * ch : (d + 1) * ch] = left[d - 1][...] + right[size - d - 1][...]
    every = jnp.concatenate([mod[...].astype(F32) for mod in mods], axis=0)
    taps_t[...] = every.T.astype(BF16)
    total[...] = jnp.zeros(total.shape, F32)

    def body(row, _):
        g = gathered[:, pl.ds(pl.multiple_of(row * width, width), width)]
        for kh in range(3):
            y = jnp.dot(taps_t[kh * 3 * ch : (kh + 1) * 3 * ch], g, preferred_element_type=F32)
            total[row + kh] += y
        return 0

    lax.fori_loop(0, height, body, 0)
    for row in range(height + 2):
        value = total[row, ch : 2 * ch]
        value = value + shifted(total[row, 0:ch], -1) + shifted(total[row, 2 * ch : 3 * ch], 1)
        if row == 0:
            before[...] = value
        elif row == height + 1:
            after[...] = value
        else:
            main[:, (row - 1) * width : row * width] = value


def split3(x):
    high = x.astype(BF16).astype(F32)
    mid = (x - high).astype(BF16).astype(F32)
    return high, mid, x - high - mid


def collect_kernel(rows, size, place, scales, whole_mod, far, *refs):
    nears, out, by_chan, by_row = refs[:size], refs[size], refs[size + 1], refs[size + 2]
    sample, chan_at, row_at = place[0], place[1], place[2]
    for d in range(size):
        by_chan[lax.rem(chan_at + d, size)] = nears[d][...].astype(F32)
    by_chan[jnp.where(chan_at == 0, size - 1, 0)] += far[...].astype(F32)
    ch = whole_mod.shape[2] // size
    in_ch = out.shape[2]
    product = jnp.zeros(whole_mod.shape[1:], F32)
    for tap in range(TAPS):
        value = beside([by_chan[z, :, tap * ch : (tap + 1) * ch] for z in range(size)])
        product = product + value * whole_mod[tap].astype(F32)
        for r in range(rows):
            by_row[r, tap] = value[:, r * in_ch : (r + 1) * in_ch].astype(BF16)
    out[0:TAPS] = by_row[row_at]
    scale = column(scales[...], sample)
    fall = jnp.sum(product, axis=1, keepdims=True) * (scale * scale)
    lane = lax.broadcasted_iota(jnp.int32, out.shape[1:], 1)
    last = jnp.zeros(out.shape[1:], F32)
    for at, piece in enumerate(split3(fall)):
        last = jnp.where(lane == at, piece, last)
    out[TAPS] = last.astype(BF16)


def bank_grad_kernel(samples, place, sel, bank, style, scales, *refs):
    parts = refs[:samples]
    bank_grad, style_grad, held = refs[samples:]
    sample = place[0]
    for s in range(samples):
        held[lax.rem(sample - s + samples, samples)] = parts[s][...]
    styles, every_scale = style[...], scales[...]
    falls = []
    for b in range(samples):
        last = held[b, TAPS].astype(F32)
        falls.append(last[:, 0:1] + last[:, 1:2] + last[:, 2:3])
    sums = [jnp.zeros(bank.shape[2:], F32) for _ in range(samples)]
    for tap in range(TAPS):
        totals = [None] * bank.shape[0]
        for b in range(samples):
            kern = mixed(bank, sel, b, tap)
            own_style = styles[b : b + 1]
            plain_grad = held[b, tap].astype(F32) * every_scale[:, b : b + 1] - kern * own_style * falls[b]
            sums[b] = sums[b] + plain_grad * kern
            kernel_grad = plain_grad * own_style
            for k in range(bank.shape[0]):
                term = sel[b, k] * kernel_grad
                totals[k] = term if totals[k] is None else totals[k] + term
        for k in range(bank.shape[0]):
            bank_grad[k, tap] = totals[k]
    for b in range(samples):
        style_grad[b : b + 1] = jnp.sum(sums[b], axis=0, keepdims=True)


def affine_kernel(size, place, latent_t, *refs):
    parts, w_grad, b_grad, held = refs[:size], refs[size], refs[size + 1], refs[size + 2]
    for d in range(size):
        held[lax.rem(place[1] - d + size, size)] = parts[d][...]
    style_grad = held[0]
    for z in range(1, size):
        style_grad = style_grad + held[z]
    columns = latent_t[...]
    samples = style_grad.shape[0]
    total, bias = None, None
    for b in range(samples):
        row = style_grad[b : b + 1]
        term = columns[:, b : b + 1] * row
        total = term if total is None else total + term
        bias = row if bias is None else bias + row
    w_grad[...] = total
    b_grad[...] = bias


def call(kernel, name, outs, *operands, scalars=0, scratch=(), flops=10**6):
    outs = tuple(jax.ShapeDtypeStruct(*o) for o in outs)
    moved = sum(o.size * o.dtype.itemsize for o in (*outs, *operands))
    return pl.pallas_call(
        kernel,
        out_shape=outs,
        in_specs=sspec(scalars) + vspec(len(operands) - scalars),
        out_specs=tuple(vspec(len(outs))),
        scratch_shapes=[pltpu.VMEM(*s) for s in scratch],
        compiler_params=params(),
        cost_estimate=cost(flops, moved),
        name=name,
    )(*operands)


def exchange(x, axis):
    size = lax.axis_size(axis)
    return [x] + [
        lax.ppermute(x, axis, [(i, (i + s) % size) for i in range(size)]) for s in range(1, size)
    ]


def from_sides(first, last, axis):
    size, at = lax.axis_size(axis), lax.axis_index(axis)
    if size == 2:
        got = lax.ppermute(jnp.where(at == 0, last, first), axis, [(0, 1), (1, 0)])
        nothing = jnp.zeros_like(got)
        return jnp.where(at == 1, got, nothing), jnp.where(at == 0, got, nothing)
    up = [(i, i + 1) for i in range(size - 1)]
    down = [(i + 1, i) for i in range(size - 1)]
    return lax.ppermute(last, axis, up), lax.ppermute(first, axis, down)


def on_device(feature, out_grad, bank, select, latent, affine_w, affine_b):
    rows, samples, size = (lax.axis_size(a) for a in ("rows", "samples", "chan"))
    row_at, sample_at, chan_at = (lax.axis_index(a) for a in ("rows", "samples", "chan"))
    _, ch, height, width = feature.shape
    out_ch, in_ch = bank.shape[2:]
    pixels, all_ch = height * width, ch * size
    place = jnp.stack([sample_at, chan_at, row_at]).astype(jnp.int32)
    flops = 2 * TAPS * ch * ch * size * pixels

    cotan = out_grad[0].reshape(ch, pixels)
    left, right = [], []

    def step(number, from_left, from_right):
        left.append(
            lax.ppermute(from_left, "chan", [(i, i + 1) for i in range(number - 1, size - 1)])
        )
        right.append(
            lax.ppermute(from_right, "chan", [(i + 1, i) for i in range(size - number)])
        )

    step(1, cotan, cotan)

    feat = feature[0].reshape(ch, pixels)
    feat_before, feat_after = from_sides(feat[:, :width], feat[:, pixels - width :], "rows")
    small = jnp.concatenate([latent[0], select[0].astype(F32)])[None]
    small = exchange(small, "samples")
    at = jnp.remainder(sample_at - jnp.arange(samples), samples)
    small = jnp.zeros((samples, small[0].shape[1]), F32).at[at].set(jnp.concatenate(small, axis=0))
    latents, sel = small[:, : latent.shape[1]], small[:, latent.shape[1] :]
    style, energy = call(
        energy_kernel,
        "energy",
        [((samples, in_ch), F32), ((out_ch, 128), F32)],
        sel,
        bank,
        latents,
        affine_w,
        affine_b[None],
        scalars=1,
    )
    energies = exchange(energy, "rows")
    left[0], right[0], energies, feat_before, feat_after = lax.optimization_barrier(
        (left[0], right[0], energies, feat_before, feat_after)
    )

    step(2, left[0], right[0])
    mod_own, scales = call(
        functools.partial(modulated_kernel, rows),
        "modulated",
        [((TAPS, out_ch, in_ch), BF16), ((out_ch, 128), F32)],
        place,
        sel,
        bank,
        style,
        *energies,
        scalars=2,
    )
    message = ((ch, TAPS * ch), BF16)
    whole_mod, *to_send = call(
        functools.partial(blocks_kernel, rows, size),
        "mod_blocks",
        [((TAPS, out_ch, all_ch), BF16)] + [message] * size,
        place,
        *exchange(mod_own, "rows"),
        scalars=1,
        scratch=[((rows, TAPS, out_ch, in_ch), BF16), ((size, *message[0]), BF16)],
    )
    left[1], right[1], to_send = lax.optimization_barrier((left[1], right[1], to_send))
    mods = [to_send[0]] + [
        lax.ppermute(to_send[d], "chan", [(i, (i + d) % size) for i in range(size)])
        for d in range(1, size)
    ]

    for number in range(3, size):
        step(number, left[number - 2], right[number - 2])
    near, wide = call(
        functools.partial(near_grad_kernel, size, height, width),
        "near_grad",
        [((all_ch, TAPS * ch), BF16), ((3 * ch, (height + 2) * width), BF16)],
        cotan,
        *left[: size - 2],
        *right[: size - 2],
        feat,
        feat_before,
        feat_after,
        scratch=[((all_ch, pixels), BF16), ((3, all_ch, 3 * ch), F32)],
        flops=flops,
    )
    nears = exchange(near, "rows")
    left[-1], right[-1], nears, mods = lax.optimization_barrier((left[-1], right[-1], nears, mods))
    far, *near_sums = call(
        functools.partial(far_grad_kernel, rows, size, height, width),
        "far_grad",
        [message] * (1 + size),
        left[-1],
        right[-1],
        wide,
        *nears,
        scratch=[((ch, pixels), BF16), ((3, ch, 3 * ch), F32)],
        flops=flops // size,
    )
    fars = exchange(far, "rows")
    got = [near_sums[0]]
    for d in range(1, size):
        pairs = [(i, i - d) for i in range(d, size) if d < size - 1]
        pairs += [(i, i - d + size) for i in range(d) if size - d < size - 1]
        got.append(lax.ppermute(near_sums[d], "chan", pairs))
    (far_sum,) = call(sum_kernel, "far_sum", [message], *fars)
    far_got = lax.ppermute(far_sum, "chan", [(0, size - 1), (size - 1, 0)])

    (own,) = call(
        functools.partial(collect_kernel, rows, size),
        "collect",
        [((TAPS + 1, out_ch, in_ch), BF16)],
        place,
        scales,
        whole_mod,
        far_got,
        *got,
        scalars=1,
        scratch=[((size, *message[0]), F32), ((rows, TAPS, out_ch, in_ch), BF16)],
    )
    every = exchange(own, "samples")

    own, mods = lax.optimization_barrier((own, mods))
    main, before, after = call(
        functools.partial(input_grad_kernel, size, height, width),
        "input_grad",
        [((ch, pixels), F32), ((ch, width), F32), ((ch, width), F32)],
        cotan,
        *left,
        *right,
        *mods,
        scratch=[
            ((all_ch, pixels), BF16),
            ((TAPS * ch, all_ch), BF16),
            ((height + 2, 3 * ch, width), F32),
        ],
        flops=flops,
    )
    every, main, before, after = lax.optimization_barrier((every, main, before, after))
    from_above, from_below = from_sides(before, after, "rows")
    edge = jnp.concatenate(
        [from_above[:, None], jnp.zeros((ch, height - 2, width), F32), from_below[:, None]], axis=1
    )
    feature_grad = (main.reshape(ch, height, width) + edge).astype(BF16)[None]

    bank_grad, style_part = call(
        functools.partial(bank_grad_kernel, samples),
        "bank_grad",
        [(bank.shape, F32), ((samples, in_ch), F32)],
        place,
        sel,
        bank,
        style,
        scales,
        *every,
        scalars=2,
        scratch=[((samples, TAPS + 1, out_ch, in_ch), BF16)],
    )
    affine_w_grad, affine_b_grad = call(
        functools.partial(affine_kernel, size),
        "affine",
        [(affine_w.shape, F32), ((1, in_ch), F32)],
        place,
        latents.T,
        *exchange(style_part, "chan"),
        scalars=1,
        scratch=[((size, samples, in_ch), F32)],
    )
    return (feature_grad, bank_grad, affine_w_grad, affine_b_grad[0])


def solution(mesh):
    return jax.shard_map(
        on_device,
        mesh=mesh,
        in_specs=(
            P("samples", "chan", "rows", None),
            P("samples", "chan", "rows", None),
            P(None, None, "chan", "rows"),
            P("samples", None),
            P("samples", None),
            P(None, "rows"),
            P("rows"),
        ),
        out_specs=(
            P("samples", "chan", "rows", None),
            P(None, None, "chan", "rows"),
            P(None, "rows"),
            P("rows"),
        ),
        check_vma=False,
    )
```

```python
import functools

import jax
import jax.numpy as jnp
from jax import lax
from jax.experimental import pallas as pl
from jax.experimental.pallas import tpu as pltpu
from jax.sharding import PartitionSpec as P

EPS = 1e-08
TAPS = 9
F32 = jnp.float32
BF16 = jnp.bfloat16
VMEM_LIMIT = 48 * 2**20


def params():
    return pltpu.CompilerParams(vmem_limit_bytes=VMEM_LIMIT)


def vspec(n):
    return [pl.BlockSpec(memory_space=pltpu.VMEM)] * n


def sspec(n):
    return [pl.BlockSpec(memory_space=pltpu.SMEM)] * n


def cost(flops, moved):
    return pl.CostEstimate(flops=flops, bytes_accessed=moved, transcendentals=0)


def beside(pieces):
    return pieces[0] if len(pieces) == 1 else jnp.concatenate(pieces, axis=1)


def mixed(bank_ref, sel, sample, tap):
    total = sel[sample, 0] * bank_ref[0, tap]
    for k in range(1, bank_ref.shape[0]):
        total = total + sel[sample, k] * bank_ref[k, tap]
    return total


def energy_kernel(sel, bank, latent, affine_w, affine_b, style_out, energy_out):
    style = (
        jnp.dot(latent[...], affine_w[...], precision=lax.Precision.HIGHEST, preferred_element_type=F32)
        + affine_b[...]
    )
    style_out[...] = style
    total = jnp.zeros(bank.shape[2:], F32)
    for tap in range(TAPS):
        plain = mixed(bank, sel, 0, tap) * style
        total = total + plain * plain
    energy_out[...] = jnp.broadcast_to(jnp.sum(total, axis=1, keepdims=True), energy_out.shape)


def modulated_kernel(sel, bank, style, *refs):
    energies, (mod_out, scale_out, row_out) = refs[:-3], refs[-3:]
    energy = energies[0][...]
    for other in energies[1:]:
        energy = energy + other[...]
    scales = lax.rsqrt(energy + EPS)
    scale_out[...] = scales
    row_out[...] = scales.T[0:1]
    scale = scales[:, 0:1]
    for tap in range(TAPS):
        mod_out[tap] = (mixed(bank, sel, 0, tap) * style[...] * scale).astype(BF16)


def blocks_kernel(rows, size, place, *refs):
    parts, whole, outs = refs[:rows], refs[rows], refs[rows + 1 : rows + 1 + size]
    by_row, by_chan = refs[rows + 1 + size :]
    row_at, chan_at, sign = place[2], place[1], place[3]
    for r in range(rows):
        by_row[lax.rem(row_at - r + rows, rows)] = parts[r][...]
    ch = whole.shape[2] // size
    taps = []
    for tap in range(TAPS):
        value = beside([by_row[r, tap].astype(F32) for r in range(rows)])
        whole[tap] = value.astype(BF16)
        taps.append(value)
    for z in range(size):
        by_chan[z] = beside([value[:, z * ch : (z + 1) * ch] for value in taps]).astype(BF16)
    for d in range(size):
        outs[d][...] = by_chan[lax.rem(chan_at + sign * d + size, size)]


def shifted(x, by):
    width = x.shape[1]
    lane = lax.broadcasted_iota(jnp.int32, x.shape, 1)
    moved = pltpu.roll(x, by % width, 1)
    return jnp.where(lane == (0 if by == 1 else width - 1), 0.0, moved)


def tap_products(g_ref, wide, total, height, width):
    total[...] = jnp.zeros(total.shape, F32)

    def body(row, _):
        g = g_ref[:, pl.ds(pl.multiple_of(row * width, width), width)]
        for kh in range(3):
            x = wide[:, pl.ds(pl.multiple_of((row + kh) * width, width), width)]
            total[kh] += lax.dot_general(g, x, (((1,), (1,)), ((), ())), preferred_element_type=F32)
        return 0

    lax.fori_loop(0, height, body, 0)
    return jnp.concatenate([total[kh] for kh in range(3)], axis=1)


def near_grad_kernel(size, height, width, *refs):
    cotan_own, first, second = refs[0], refs[1 : size - 1], refs[size - 1 : 2 * size - 3]
    feat, feat_before, feat_after, out, wide, gathered, total = refs[2 * size - 3 :]
    ch = feat.shape[0]
    gathered[0:ch] = cotan_own[...]
    for d in range(1, size):
        found = []
        if d < size - 1:
            found.append(first[d - 1][...])
        if size - d < size - 1:
            found.append(second[size - d - 1][...])
        gathered[d * ch : (d + 1) * ch] = found[0] if len(found) == 1 else found[0] + found[1]
    for row in range(height + 2):
        if row == 0:
            x = feat_before[...]
        elif row == height + 1:
            x = feat_after[...]
        else:
            x = feat[:, (row - 1) * width : row * width]
        wide[ch : 2 * ch, row * width : (row + 1) * width] = x
        x = x.astype(F32)
        wide[0:ch, row * width : (row + 1) * width] = shifted(x, 1).astype(BF16)
        wide[2 * ch : 3 * ch, row * width : (row + 1) * width] = shifted(x, -1).astype(BF16)
    out[...] = tap_products(gathered, wide, total, height, width).astype(BF16)


def far_grad_kernel(height, width, first, second, wide, out, cotan, total):
    cotan[...] = first[...] + second[...]
    out[...] = tap_products(cotan, wide, total, height, width).astype(BF16)


def near_sum_kernel(rows, size, *refs):
    nears, outs = refs[:rows], refs[rows:]
    ch = outs[0].shape[0]
    for d in range(size):
        value = nears[0][d * ch : (d + 1) * ch].astype(F32)
        for r in range(1, rows):
            value = value + nears[r][d * ch : (d + 1) * ch].astype(F32)
        outs[d][...] = value.astype(BF16)


def sum_kernel(*refs):
    value = refs[0][...].astype(F32)
    for ref in refs[1:-1]:
        value = value + ref[...].astype(F32)
    refs[-1][...] = value.astype(BF16)


def input_grad_kernel(size, height, width, *refs):
    cotan_own, first, second = refs[0], refs[1:size], refs[size : 2 * size - 1]
    mods = refs[2 * size - 1 : 3 * size - 1]
    main, before, after, gathered, taps_t, total = refs[3 * size - 1 :]
    ch = cotan_own.shape[0]
    gathered[0:ch] = cotan_own[...]
    for d in range(1, size):
        gathered[d * ch : (d + 1) * ch] = first[d - 1][...] + second[size - d - 1][...]
    every = jnp.concatenate([mod[...].astype(F32) for mod in mods], axis=0)
    taps_t[...] = every.T.astype(BF16)
    total[...] = jnp.zeros(total.shape, F32)

    def body(row, _):
        g = gathered[:, pl.ds(pl.multiple_of(row * width, width), width)]
        for kh in range(3):
            y = jnp.dot(taps_t[kh * 3 * ch : (kh + 1) * 3 * ch], g, preferred_element_type=F32)
            total[row + kh] += y
        return 0

    lax.fori_loop(0, height, body, 0)
    for row in range(height + 2):
        value = total[row, ch : 2 * ch]
        value = value + shifted(total[row, 0:ch], -1) + shifted(total[row, 2 * ch : 3 * ch], 1)
        if row == 0:
            before[...] = value
        elif row == height + 1:
            after[...] = value
        else:
            main[:, (row - 1) * width : row * width] = value


def split3(x):
    high = x.astype(BF16).astype(F32)
    mid = (x - high).astype(BF16).astype(F32)
    return high, mid, x - high - mid


def collect_kernel(rows, size, place, scale, whole_mod, far, *refs):
    nears, out, by_chan, by_row = refs[:size], refs[size], refs[size + 1], refs[size + 2]
    chan_at, row_at, sign = place[1], place[2], place[3]
    for d in range(size):
        by_chan[lax.rem(chan_at + sign * d + size, size)] = nears[d][...].astype(F32)
    by_chan[jnp.where(chan_at == 0, size - 1, 0)] += far[...].astype(F32)
    ch = whole_mod.shape[2] // size
    in_ch = out.shape[2]
    product = jnp.zeros(whole_mod.shape[1:], F32)
    for tap in range(TAPS):
        value = beside([by_chan[z, :, tap * ch : (tap + 1) * ch] for z in range(size)])
        product = product + value * whole_mod[tap].astype(F32)
        for r in range(rows):
            by_row[r, tap] = value[:, r * in_ch : (r + 1) * in_ch].astype(BF16)
    out[0:TAPS] = by_row[row_at]
    fall = jnp.sum(product, axis=1, keepdims=True) * (scale[:, 0:1] * scale[:, 0:1])
    lane = lax.broadcasted_iota(jnp.int32, out.shape[1:], 1)
    last = jnp.zeros(out.shape[1:], F32)
    for at, piece in enumerate(split3(fall)):
        last = jnp.where(lane == at, piece, last)
    out[TAPS] = last.astype(BF16)


def bank_grad_kernel(samples, place, sel, bank, style, scales, *refs):
    parts = refs[:samples]
    bank_grad, style_grad, held = refs[samples:]
    sample = place[0]
    for s in range(samples):
        held[lax.rem(sample - s + samples, samples)] = parts[s][...]
    styles, every_scale = style[...], scales[...]
    falls = []
    for b in range(samples):
        last = held[b, TAPS].astype(F32)
        falls.append(last[:, 0:1] + last[:, 1:2] + last[:, 2:3])
    sums = [jnp.zeros(bank.shape[2:], F32) for _ in range(samples)]
    for tap in range(TAPS):
        totals = [None] * bank.shape[0]
        for b in range(samples):
            kern = mixed(bank, sel, b, tap)
            own_style = styles[b : b + 1]
            plain_grad = held[b, tap].astype(F32) * every_scale[:, b : b + 1] - kern * own_style * falls[b]
            sums[b] = sums[b] + plain_grad * kern
            kernel_grad = plain_grad * own_style
            for k in range(bank.shape[0]):
                term = sel[b, k] * kernel_grad
                totals[k] = term if totals[k] is None else totals[k] + term
        for k in range(bank.shape[0]):
            bank_grad[k, tap] = totals[k]
    for b in range(samples):
        style_grad[b : b + 1] = jnp.sum(sums[b], axis=0, keepdims=True)


def affine_kernel(size, place, latent_t, *refs):
    parts, w_grad, b_grad, held = refs[:size], refs[size], refs[size + 1], refs[size + 2]
    for d in range(size):
        held[lax.rem(place[1] - d + size, size)] = parts[d][...]
    style_grad = held[0]
    for z in range(1, size):
        style_grad = style_grad + held[z]
    columns = latent_t[...]
    samples = style_grad.shape[0]
    total, bias = None, None
    for b in range(samples):
        row = style_grad[b : b + 1]
        term = columns[:, b : b + 1] * row
        total = term if total is None else total + term
        bias = row if bias is None else bias + row
    w_grad[...] = total
    b_grad[...] = bias


def call(kernel, name, outs, *operands, scalars=0, scratch=(), flops=10**6):
    outs = tuple(jax.ShapeDtypeStruct(*o) for o in outs)
    moved = sum(o.size * o.dtype.itemsize for o in (*outs, *operands))
    return pl.pallas_call(
        kernel,
        out_shape=outs,
        in_specs=sspec(scalars) + vspec(len(operands) - scalars),
        out_specs=tuple(vspec(len(outs))),
        scratch_shapes=[pltpu.VMEM(*s) for s in scratch],
        compiler_params=params(),
        cost_estimate=cost(flops, moved),
        name=name,
    )(*operands)


def exchange(x, axis):
    size = lax.axis_size(axis)
    return [x] + [
        lax.ppermute(x, axis, [(i, (i + s) % size) for i in range(size)]) for s in range(1, size)
    ]


def from_sides(first, last, axis):
    size, at = lax.axis_size(axis), lax.axis_index(axis)
    if size == 2:
        got = lax.ppermute(jnp.where(at == 0, last, first), axis, [(0, 1), (1, 0)])
        nothing = jnp.zeros_like(got)
        return jnp.where(at == 1, got, nothing), jnp.where(at == 0, got, nothing)
    up = [(i, i + 1) for i in range(size - 1)]
    down = [(i + 1, i) for i in range(size - 1)]
    return lax.ppermute(last, axis, up), lax.ppermute(first, axis, down)


def on_device(feature, out_grad, bank, select, latent, affine_w, affine_b):
    rows, samples, size = (lax.axis_size(a) for a in ("rows", "samples", "chan"))
    row_at, sample_at, chan_at = (lax.axis_index(a) for a in ("rows", "samples", "chan"))
    _, ch, height, width = feature.shape
    out_ch, in_ch = bank.shape[2:]
    pixels, all_ch = height * width, ch * size
    sign = 1 - 2 * jnp.remainder(sample_at, 2)
    place = jnp.stack([sample_at, chan_at, row_at, sign]).astype(jnp.int32)
    flops = 2 * TAPS * ch * ch * size * pixels

    def along(x, pairs):
        whole = []
        for b in range(samples):
            for i, j in pairs:
                if b % 2:
                    i, j = size - 1 - i, size - 1 - j
                whole.append((b * size + i, b * size + j))
        return lax.ppermute(x, ("samples", "chan"), whole)

    cotan = out_grad[0].reshape(ch, pixels)
    first, second = [], []

    def step(number, x, y):
        first.append(along(x, [(i, i + 1) for i in range(number - 1, size - 1)]))
        second.append(along(y, [(i + 1, i) for i in range(size - number)]))

    step(1, cotan, cotan)

    feat = feature[0].reshape(ch, pixels)
    feat_before, feat_after = from_sides(feat[:, :width], feat[:, pixels - width :], "rows")
    own_sel = select.astype(F32)
    style, energy = call(
        energy_kernel,
        "energy",
        [((1, in_ch), F32), ((out_ch, 128), F32)],
        own_sel,
        bank,
        latent,
        affine_w,
        affine_b[None],
        scalars=1,
    )
    mod_own, scale, scale_row = call(
        modulated_kernel,
        "modulated",
        [((TAPS, out_ch, in_ch), BF16), ((out_ch, 128), F32), ((1, out_ch), F32)],
        own_sel,
        bank,
        style,
        *exchange(energy, "rows"),
        scalars=1,
    )
    message = ((ch, TAPS * ch), BF16)
    whole_mod, *to_send = call(
        functools.partial(blocks_kernel, rows, size),
        "mod_blocks",
        [((TAPS, out_ch, all_ch), BF16)] + [message] * size,
        place,
        *exchange(mod_own, "rows"),
        scalars=1,
        scratch=[((rows, TAPS, out_ch, in_ch), BF16), ((size, *message[0]), BF16)],
    )
    first[0], second[0], to_send, feat_before, feat_after = lax.optimization_barrier(
        (first[0], second[0], to_send, feat_before, feat_after)
    )

    step(2, first[0], second[0])
    mods = [to_send[0]] + [
        along(to_send[d], [(i, (i + d) % size) for i in range(size)]) for d in range(1, size)
    ]
    small = jnp.concatenate([latent[0], own_sel[0], style[0], scale_row[0]])[None]
    smalls = exchange(small, "samples")
    first[1], second[1], mods, smalls = lax.optimization_barrier((first[1], second[1], mods, smalls))
    at = jnp.remainder(sample_at - jnp.arange(samples), samples)
    every = jnp.zeros((samples, small.shape[1]), F32).at[at].set(jnp.concatenate(smalls, axis=0))
    ends = [latent.shape[1], latent.shape[1] + select.shape[1]]
    latents, sel, styles, scales = jnp.split(every, ends + [ends[1] + in_ch], axis=1)
    tables = latents.T, sel, styles, scales.T

    for number in range(3, size):
        step(number, first[number - 2], second[number - 2])
    near, wide = call(
        functools.partial(near_grad_kernel, size, height, width),
        "near_grad",
        [((all_ch, TAPS * ch), BF16), ((3 * ch, (height + 2) * width), BF16)],
        cotan,
        *first[: size - 2],
        *second[: size - 2],
        feat,
        feat_before,
        feat_after,
        scratch=[((all_ch, pixels), BF16), ((3, all_ch, 3 * ch), F32)],
        flops=flops,
    )
    near_sums = call(
        functools.partial(near_sum_kernel, rows, size),
        "near_sum",
        [message] * size,
        *exchange(near, "rows"),
    )
    got = [near_sums[0]]
    for d in range(1, size):
        pairs = [(i, i - d) for i in range(d, size) if d < size - 1]
        pairs += [(i, i - d + size) for i in range(d) if size - d < size - 1]
        got.append(along(near_sums[d], pairs))
    first[-1], second[-1], near_sums, tables = lax.optimization_barrier(
        (first[-1], second[-1], near_sums, tables)
    )
    latents, sel, styles, scales = tables
    (far,) = call(
        functools.partial(far_grad_kernel, height, width),
        "far_grad",
        [message],
        first[-1],
        second[-1],
        wide,
        scratch=[((ch, pixels), BF16), ((3, ch, 3 * ch), F32)],
        flops=flops // size,
    )
    (far_sum,) = call(sum_kernel, "far_sum", [message], *exchange(far, "rows"))
    far_got = lax.ppermute(far_sum, "chan", [(0, size - 1), (size - 1, 0)])

    (own,) = call(
        functools.partial(collect_kernel, rows, size),
        "collect",
        [((TAPS + 1, out_ch, in_ch), BF16)],
        place,
        scale,
        whole_mod,
        far_got,
        *got,
        scalars=1,
        scratch=[((size, *message[0]), F32), ((rows, TAPS, out_ch, in_ch), BF16)],
    )
    every = exchange(own, "samples")

    own, mods = lax.optimization_barrier((own, mods))
    main, before, after = call(
        functools.partial(input_grad_kernel, size, height, width),
        "input_grad",
        [((ch, pixels), F32), ((ch, width), F32), ((ch, width), F32)],
        cotan,
        *first,
        *second,
        *mods,
        scratch=[
            ((all_ch, pixels), BF16),
            ((TAPS * ch, all_ch), BF16),
            ((height + 2, 3 * ch, width), F32),
        ],
        flops=flops,
    )
    every, main, before, after = lax.optimization_barrier((every, main, before, after))
    from_above, from_below = from_sides(before, after, "rows")
    edge = jnp.concatenate(
        [from_above[:, None], jnp.zeros((ch, height - 2, width), F32), from_below[:, None]], axis=1
    )
    feature_grad = (main.reshape(ch, height, width) + edge).astype(BF16)[None]

    bank_grad, style_part = call(
        functools.partial(bank_grad_kernel, samples),
        "bank_grad",
        [(bank.shape, F32), ((samples, in_ch), F32)],
        place,
        sel,
        bank,
        styles,
        scales,
        *every,
        scalars=2,
        scratch=[((samples, TAPS + 1, out_ch, in_ch), BF16)],
    )
    affine_w_grad, affine_b_grad = call(
        functools.partial(affine_kernel, size),
        "affine",
        [(affine_w.shape, F32), ((1, in_ch), F32)],
        place,
        latents,
        *exchange(style_part, "chan"),
        scalars=1,
        scratch=[((size, samples, in_ch), F32)],
    )
    return (feature_grad, bank_grad, affine_w_grad, affine_b_grad[0])


def solution(mesh):
    return jax.shard_map(
        on_device,
        mesh=mesh,
        in_specs=(
            P("samples", "chan", "rows", None),
            P("samples", "chan", "rows", None),
            P(None, None, "chan", "rows"),
            P("samples", None),
            P("samples", None),
            P(None, "rows"),
            P("rows"),
        ),
        out_specs=(
            P("samples", "chan", "rows", None),
            P(None, None, "chan", "rows"),
            P(None, "rows"),
            P("rows"),
        ),
        check_vma=False,
    )
```

```python
import functools

import jax
import jax.numpy as jnp
from jax import lax
from jax.experimental import pallas as pl
from jax.experimental.pallas import tpu as pltpu
from jax.sharding import PartitionSpec as P

EPS = 1e-08
TAPS = 9
F32 = jnp.float32
BF16 = jnp.bfloat16
VMEM_LIMIT = 16 * 2**20


def params():
    return pltpu.CompilerParams(vmem_limit_bytes=VMEM_LIMIT)


def vspec(n):
    return [pl.BlockSpec(memory_space=pltpu.VMEM)] * n


def sspec(n):
    return [pl.BlockSpec(memory_space=pltpu.SMEM)] * n


def cost(flops, moved):
    return pl.CostEstimate(flops=flops, bytes_accessed=moved, transcendentals=0)


def beside(pieces):
    return pieces[0] if len(pieces) == 1 else jnp.concatenate(pieces, axis=1)


def mixed(bank_ref, sel, sample, tap):
    total = sel[sample, 0] * bank_ref[0, tap]
    for k in range(1, bank_ref.shape[0]):
        total = total + sel[sample, k] * bank_ref[k, tap]
    return total


def energy_kernel(sel, bank, latent, affine_w, affine_b, style_out, energy_out):
    style = (
        jnp.dot(latent[...], affine_w[...], precision=lax.Precision.HIGHEST, preferred_element_type=F32)
        + affine_b[...]
    )
    style_out[...] = style
    total = jnp.zeros(bank.shape[2:], F32)
    for tap in range(TAPS):
        plain = mixed(bank, sel, 0, tap) * style
        total = total + plain * plain
    energy_out[...] = jnp.broadcast_to(jnp.sum(total, axis=1, keepdims=True), energy_out.shape)


def modulated_kernel(sel, bank, style, *refs):
    energies, (mod_out, scale_out, row_out) = refs[:-3], refs[-3:]
    energy = energies[0][...]
    for other in energies[1:]:
        energy = energy + other[...]
    scales = lax.rsqrt(energy + EPS)
    scale_out[...] = scales
    row_out[...] = scales.T[0:1]
    scale = scales[:, 0:1]
    for tap in range(TAPS):
        mod_out[tap] = (mixed(bank, sel, 0, tap) * style[...] * scale).astype(BF16)


def blocks_kernel(rows, size, shares, place, *refs):
    parts, whole, out, by_row, by_share = refs[:rows], *refs[rows:]
    row_at = place[2]
    for r in range(rows):
        by_row[lax.rem(row_at - r + rows, rows)] = parts[r][...]
    ch = whole.shape[2] // size
    share = out.shape[1]
    taps = []
    for tap in range(TAPS):
        value = beside([by_row[r, tap].astype(F32) for r in range(rows)])
        whole[tap] = value.astype(BF16)
        taps.append(value)
    for z in range(size):
        value = beside([value[:, z * ch : (z + 1) * ch] for value in taps]).astype(BF16)
        for k in range(shares):
            by_share[k, z] = value[k * share : (k + 1) * share]
    out[...] = by_share[row_at if shares > 1 else 0]


def shifted(x, by):
    width = x.shape[1]
    lane = lax.broadcasted_iota(jnp.int32, x.shape, 1)
    moved = pltpu.roll(x, by % width, 1)
    return jnp.where(lane == (0 if by == 1 else width - 1), 0.0, moved)


def tap_products(g_ref, wide, total, height, width):
    total[...] = jnp.zeros(total.shape, F32)

    def body(row, _):
        g = g_ref[:, pl.ds(pl.multiple_of(row * width, width), width)]
        for kh in range(3):
            x = wide[:, pl.ds(pl.multiple_of((row + kh) * width, width), width)]
            total[kh] += lax.dot_general(g, x, (((1,), (1,)), ((), ())), preferred_element_type=F32)
        return 0

    lax.fori_loop(0, height, body, 0)
    return jnp.concatenate([total[kh] for kh in range(3)], axis=1)


def near_grad_kernel(size, height, width, *refs):
    cotans, (feat, feat_before, feat_after) = refs[:3], refs[3:6]
    outs, (wide, gathered, total) = refs[6:9], refs[9:]
    ch = feat.shape[0]
    for at, cotan in enumerate(cotans):
        gathered[at * ch : (at + 1) * ch] = cotan[...]
    for row in range(height + 2):
        if row == 0:
            x = feat_before[...]
        elif row == height + 1:
            x = feat_after[...]
        else:
            x = feat[:, (row - 1) * width : row * width]
        wide[ch : 2 * ch, row * width : (row + 1) * width] = x
        x = x.astype(F32)
        wide[0:ch, row * width : (row + 1) * width] = shifted(x, 1).astype(BF16)
        wide[2 * ch : 3 * ch, row * width : (row + 1) * width] = shifted(x, -1).astype(BF16)
    whole = tap_products(gathered, wide, total, height, width).astype(BF16)
    for at, out in enumerate(outs):
        out[...] = whole[at * ch : (at + 1) * ch]


def far_grad_kernel(count, height, width, *refs):
    first, second, wide = refs[:count], refs[count : 2 * count], refs[2 * count]
    outs, (gathered, total) = refs[2 * count + 1 : 3 * count + 1], refs[3 * count + 1 :]
    ch = outs[0].shape[0]
    for at in range(count):
        gathered[at * ch : (at + 1) * ch] = first[at][...] + second[at][...]
    whole = tap_products(gathered, wide, total, height, width).astype(BF16)
    for at, out in enumerate(outs):
        out[...] = whole[at * ch : (at + 1) * ch]


def input_grad_kernel(rows, size, shares, height, width, place, *refs):
    cotan_own, first, second = refs[0], refs[1:size], refs[size : 2 * size - 1]
    mods = refs[2 * size - 1 : 2 * size - 1 + shares]
    main, before, after, gathered, taps, taps_t, total = refs[2 * size - 1 + shares :]
    ch = cotan_own.shape[0]
    gathered[0:ch] = cotan_own[...]
    for d in range(1, size):
        gathered[d * ch : (d + 1) * ch] = first[d - 1][...] + second[size - d - 1][...]
    for k in range(shares):
        share = lax.rem(place[2] - k + rows, rows) if shares > 1 else 0
        for d in range(size):
            taps[d, share] = mods[k][lax.rem(place[1] - place[3] * d + size, size)].astype(F32)
    taps_t[...] = taps[...].reshape(size * ch, taps.shape[3]).T.astype(BF16)
    total[...] = jnp.zeros(total.shape, F32)

    def body(row, _):
        g = gathered[:, pl.ds(pl.multiple_of(row * width, width), width)]
        for kh in range(3):
            y = jnp.dot(taps_t[kh * 3 * ch : (kh + 1) * 3 * ch], g, preferred_element_type=F32)
            total[row + kh] += y
        return 0

    lax.fori_loop(0, height, body, 0)
    for row in range(height + 2):
        value = total[row, ch : 2 * ch]
        value = value + shifted(total[row, 0:ch], -1) + shifted(total[row, 2 * ch : 3 * ch], 1)
        if row == 0:
            before[...] = value
        elif row == height + 1:
            after[...] = value
        else:
            main[:, (row - 1) * width : row * width] = value


def split3(x):
    high = x.astype(BF16).astype(F32)
    mid = (x - high).astype(BF16).astype(F32)
    return high, mid, x - high - mid


def put_fall(out, fall):
    lane = lax.broadcasted_iota(jnp.int32, out.shape[1:], 1)
    last = jnp.zeros(out.shape[1:], F32)
    for at, piece in enumerate(split3(fall)):
        last = jnp.where(lane == at, piece, last)
    out[TAPS] = last.astype(BF16)


def get_fall(last):
    last = last.astype(F32)
    return last[:, 0:1] + last[:, 1:2] + last[:, 2:3]


def collect_kernel(rows, size, place, scale, whole_mod, far, *refs):
    nears, outs = refs[:size], refs[size : size + rows]
    by_chan, by_row = refs[size + rows :]
    chan_at, row_at, sign = place[1], place[2], place[3]
    for d in range(size):
        by_chan[lax.rem(chan_at + sign * d + size, size)] = nears[d][...].astype(F32)
    by_chan[jnp.where(chan_at == 0, size - 1, 0)] += far[...].astype(F32)
    ch = whole_mod.shape[2] // size
    in_ch = outs[0].shape[2]
    product = jnp.zeros(whole_mod.shape[1:], F32)
    for tap in range(TAPS):
        value = beside([by_chan[z, :, tap * ch : (tap + 1) * ch] for z in range(size)])
        product = product + value * whole_mod[tap].astype(F32)
        for r in range(rows):
            by_row[r, tap] = value[:, r * in_ch : (r + 1) * in_ch].astype(BF16)
    fall = jnp.sum(product, axis=1, keepdims=True) * (scale[:, 0:1] * scale[:, 0:1])
    for r in range(rows):
        outs[r][0:TAPS] = by_row[lax.rem(row_at + r, rows)]
        put_fall(outs[r], fall)


def row_sum_kernel(*refs):
    parts, out = refs[:-1], refs[-1]
    fall = get_fall(parts[0][TAPS])
    for part in parts[1:]:
        fall = fall + get_fall(part[TAPS])
    for tap in range(TAPS):
        value = parts[0][tap].astype(F32)
        for part in parts[1:]:
            value = value + part[tap].astype(F32)
        out[tap] = value.astype(BF16)
    put_fall(out, fall)


def bank_grad_kernel(samples, place, sel, bank, style, scales, *refs):
    parts = refs[:samples]
    bank_grad, style_grad, held = refs[samples:]
    sample = place[0]
    for s in range(samples):
        held[lax.rem(sample - s + samples, samples)] = parts[s][...]
    styles, every_scale = style[...], scales[...]
    falls = []
    for b in range(samples):
        falls.append(get_fall(held[b, TAPS]))
    sums = [jnp.zeros(bank.shape[2:], F32) for _ in range(samples)]
    for tap in range(TAPS):
        totals = [None] * bank.shape[0]
        for b in range(samples):
            kern = mixed(bank, sel, b, tap)
            own_style = styles[b : b + 1]
            plain_grad = held[b, tap].astype(F32) * every_scale[:, b : b + 1] - kern * own_style * falls[b]
            sums[b] = sums[b] + plain_grad * kern
            kernel_grad = plain_grad * own_style
            for k in range(bank.shape[0]):
                term = sel[b, k] * kernel_grad
                totals[k] = term if totals[k] is None else totals[k] + term
        for k in range(bank.shape[0]):
            bank_grad[k, tap] = totals[k]
    for b in range(samples):
        style_grad[b : b + 1] = jnp.sum(sums[b], axis=0, keepdims=True)


def affine_kernel(size, place, latent_t, *refs):
    parts, w_grad, b_grad, held = refs[:size], refs[size], refs[size + 1], refs[size + 2]
    for d in range(size):
        held[lax.rem(place[1] - d + size, size)] = parts[d][...]
    style_grad = held[0]
    for z in range(1, size):
        style_grad = style_grad + held[z]
    columns = latent_t[...]
    samples = style_grad.shape[0]
    total, bias = None, None
    for b in range(samples):
        row = style_grad[b : b + 1]
        term = columns[:, b : b + 1] * row
        total = term if total is None else total + term
        bias = row if bias is None else bias + row
    w_grad[...] = total
    b_grad[...] = bias


def call(kernel, name, outs, *operands, scalars=0, scratch=(), flops=10**6):
    outs = tuple(jax.ShapeDtypeStruct(*o) for o in outs)
    moved = sum(o.size * o.dtype.itemsize for o in (*outs, *operands))
    return pl.pallas_call(
        kernel,
        out_shape=outs,
        in_specs=sspec(scalars) + vspec(len(operands) - scalars),
        out_specs=tuple(vspec(len(outs))),
        scratch_shapes=[pltpu.VMEM(*s) for s in scratch],
        compiler_params=params(),
        cost_estimate=cost(flops, moved),
        name=name,
    )(*operands)


def exchange(x, axis):
    size = lax.axis_size(axis)
    return [x] + [
        lax.ppermute(x, axis, [(i, (i + s) % size) for i in range(size)]) for s in range(1, size)
    ]


def from_sides(first, last, axis):
    size, at = lax.axis_size(axis), lax.axis_index(axis)
    if size == 2:
        got = lax.ppermute(jnp.where(at == 0, last, first), axis, [(0, 1), (1, 0)])
        nothing = jnp.zeros_like(got)
        return jnp.where(at == 1, got, nothing), jnp.where(at == 0, got, nothing)
    up = [(i, i + 1) for i in range(size - 1)]
    down = [(i + 1, i) for i in range(size - 1)]
    return lax.ppermute(last, axis, up), lax.ppermute(first, axis, down)


def on_device(feature, out_grad, bank, select, latent, affine_w, affine_b):
    rows, samples, size = (lax.axis_size(a) for a in ("rows", "samples", "chan"))
    row_at, sample_at, chan_at = (lax.axis_index(a) for a in ("rows", "samples", "chan"))
    _, ch, height, width = feature.shape
    out_ch, in_ch = bank.shape[2:]
    pixels, all_ch = height * width, ch * size
    sign = 1 - 2 * jnp.remainder(sample_at, 2)
    place = jnp.stack([sample_at, chan_at, row_at, sign]).astype(jnp.int32)
    flops = 2 * TAPS * ch * ch * size * pixels

    def along(x, pairs):
        whole = []
        for b in range(samples):
            for i, j in pairs:
                if b % 2:
                    i, j = size - 1 - i, size - 1 - j
                whole.append((b * size + i, b * size + j))
        return lax.ppermute(x, ("samples", "chan"), whole)

    cotan = out_grad[0].reshape(ch, pixels)
    first, second = [], []

    def step(number, x, y):
        first.append(along(x, [(i, i + 1) for i in range(number - 1, size - 1)]))
        second.append(along(y, [(i + 1, i) for i in range(size - number)]))

    step(1, cotan, cotan)

    feat = feature[0].reshape(ch, pixels)
    feat_before, feat_after = from_sides(feat[:, :width], feat[:, pixels - width :], "rows")
    own_sel = select.astype(F32)
    style, energy = call(
        energy_kernel,
        "energy",
        [((1, in_ch), F32), ((out_ch, 128), F32)],
        own_sel,
        bank,
        latent,
        affine_w,
        affine_b[None],
        scalars=1,
    )
    mod_own, scale, scale_row = call(
        modulated_kernel,
        "modulated",
        [((TAPS, out_ch, in_ch), BF16), ((out_ch, 128), F32), ((1, out_ch), F32)],
        own_sel,
        bank,
        style,
        *exchange(energy, "rows"),
        scalars=1,
    )
    message = ((ch, TAPS * ch), BF16)
    shares = rows if ch % (16 * rows) == 0 else 1
    share = (ch // shares, TAPS * ch)
    whole_mod, to_send = call(
        functools.partial(blocks_kernel, rows, size, shares),
        "mod_blocks",
        [((TAPS, out_ch, all_ch), BF16), ((size, *share), BF16)],
        place,
        *exchange(mod_own, "rows"),
        scalars=1,
        scratch=[((rows, TAPS, out_ch, in_ch), BF16), ((shares, size, *share), BF16)],
    )
    first[0], second[0], to_send, feat_before, feat_after = lax.optimization_barrier(
        (first[0], second[0], to_send, feat_before, feat_after)
    )

    step(2, first[0], second[0])
    *near, wide = call(
        functools.partial(near_grad_kernel, size, height, width),
        "near_grad",
        [message] * 3 + [((3 * ch, (height + 2) * width), BF16)],
        cotan,
        first[0],
        second[0],
        feat,
        feat_before,
        feat_after,
        scratch=[((3 * ch, pixels), BF16), ((3, 3 * ch, 3 * ch), F32)],
        flops=flops * 3 // size,
    )
    near, to_send = lax.optimization_barrier((near, to_send))
    got = [None] * size
    got[0] = near[0]
    got[1] = along(near[1], [(i, i - 1) for i in range(1, size)])
    got[size - 1] = along(near[2], [(i, i + 1) for i in range(size - 1)])
    mods = lax.all_to_all(to_send, "chan", 0, 0)
    small = jnp.concatenate([latent[0], own_sel[0], style[0], scale_row[0]])[None]
    smalls = exchange(small, "samples")
    first[1], second[1], mods, smalls, got[1], got[size - 1] = lax.optimization_barrier(
        (first[1], second[1], mods, smalls, got[1], got[size - 1])
    )
    at = jnp.remainder(sample_at - jnp.arange(samples), samples)
    every = jnp.zeros((samples, small.shape[1]), F32).at[at].set(jnp.concatenate(smalls, axis=0))
    ends = [latent.shape[1], latent.shape[1] + select.shape[1]]
    latents, sel, styles, scales = jnp.split(every, ends + [ends[1] + in_ch], axis=1)
    tables = latents.T, sel, styles, scales.T

    for number in range(3, size):
        step(number, first[number - 2], second[number - 2])
    mods = exchange(mods, "rows") if shares > 1 else [mods]

    def far_grad(slots, name):
        return call(
            functools.partial(far_grad_kernel, len(slots), height, width),
            name,
            [message] * len(slots),
            *[first[d - 1] for d in slots],
            *[second[size - d - 1] for d in slots],
            wide,
            scratch=[((len(slots) * ch, pixels), BF16), ((3, len(slots) * ch, 3 * ch), F32)],
            flops=flops * len(slots) // size,
        )

    between = list(range(2, size - 1))
    middle = far_grad(between, "middle_grad")
    for d, part in zip(between, middle):
        got[d] = along(part, [(i, (i - d) % size) for i in range(size)])
    first[-1], second[-1], middle, tables, mods = lax.optimization_barrier(
        (first[-1], second[-1], middle, tables, mods)
    )
    latents, sel, styles, scales = tables
    (far,) = call(
        functools.partial(far_grad_kernel, 1, height, width),
        "far_grad",
        [message],
        first[-1],
        second[-1],
        wide,
        scratch=[((ch, pixels), BF16), ((3, ch, 3 * ch), F32)],
        flops=flops // size,
    )
    far_got = lax.ppermute(far, "chan", [(0, size - 1), (size - 1, 0)])

    parts = call(
        functools.partial(collect_kernel, rows, size),
        "collect",
        [((TAPS + 1, out_ch, in_ch), BF16)] * rows,
        place,
        scale,
        whole_mod,
        far_got,
        *got,
        scalars=1,
        scratch=[((size, *message[0]), F32), ((rows, TAPS, out_ch, in_ch), BF16)],
    )
    parts = [parts[0]] + [
        lax.ppermute(parts[r], "rows", [(i, (i + r) % rows) for i in range(rows)])
        for r in range(1, rows)
    ]
    (own,) = call(row_sum_kernel, "row_sum", [((TAPS + 1, out_ch, in_ch), BF16)], *parts)
    every = exchange(own, "samples")

    own, mods = lax.optimization_barrier((own, mods))
    main, before, after = call(
        functools.partial(input_grad_kernel, rows, size, shares, height, width),
        "input_grad",
        [((ch, pixels), F32), ((ch, width), F32), ((ch, width), F32)],
        place,
        cotan,
        *first,
        *second,
        *mods,
        scalars=1,
        scratch=[
            ((all_ch, pixels), BF16),
            ((size, shares, *share), F32),
            ((TAPS * ch, all_ch), BF16),
            ((height + 2, 3 * ch, width), F32),
        ],
        flops=flops,
    )
    every, main, before, after = lax.optimization_barrier((every, main, before, after))
    from_above, from_below = from_sides(before, after, "rows")
    edge = jnp.concatenate(
        [from_above[:, None], jnp.zeros((ch, height - 2, width), F32), from_below[:, None]], axis=1
    )
    feature_grad = (main.reshape(ch, height, width) + edge).astype(BF16)[None]

    bank_grad, style_part = call(
        functools.partial(bank_grad_kernel, samples),
        "bank_grad",
        [(bank.shape, F32), ((samples, in_ch), F32)],
        place,
        sel,
        bank,
        styles,
        scales,
        *every,
        scalars=2,
        scratch=[((samples, TAPS + 1, out_ch, in_ch), BF16)],
    )
    affine_w_grad, affine_b_grad = call(
        functools.partial(affine_kernel, size),
        "affine",
        [(affine_w.shape, F32), ((1, in_ch), F32)],
        place,
        latents,
        *exchange(style_part, "chan"),
        scalars=1,
        scratch=[((size, samples, in_ch), F32)],
    )
    return (feature_grad, bank_grad, affine_w_grad, affine_b_grad[0])


def solution(mesh):
    return jax.shard_map(
        on_device,
        mesh=mesh,
        in_specs=(
            P("samples", "chan", "rows", None),
            P("samples", "chan", "rows", None),
            P(None, None, "chan", "rows"),
            P("samples", None),
            P("samples", None),
            P(None, "rows"),
            P("rows"),
        ),
        out_specs=(
            P("samples", "chan", "rows", None),
            P(None, None, "chan", "rows"),
            P(None, "rows"),
            P("rows"),
        ),
        check_vma=False,
    )
```

```python
import functools

import jax
import jax.numpy as jnp
from jax import lax
from jax.experimental import pallas as pl
from jax.experimental.pallas import tpu as pltpu
from jax.sharding import PartitionSpec as P

EPS = 1e-08
TAPS = 9
F32 = jnp.float32
BF16 = jnp.bfloat16
VMEM_LIMIT = 16 * 2**20


def params():
    return pltpu.CompilerParams(vmem_limit_bytes=VMEM_LIMIT)


def vspec(n):
    return [pl.BlockSpec(memory_space=pltpu.VMEM)] * n


def sspec(n):
    return [pl.BlockSpec(memory_space=pltpu.SMEM)] * n


def cost(flops, moved):
    return pl.CostEstimate(flops=flops, bytes_accessed=moved, transcendentals=0)


def beside(pieces):
    return pieces[0] if len(pieces) == 1 else jnp.concatenate(pieces, axis=1)


def mixed(bank_ref, sel, sample, tap):
    total = sel[sample][0] * bank_ref[0, tap]
    for k in range(1, bank_ref.shape[0]):
        total = total + sel[sample][k] * bank_ref[k, tap]
    return total


def own_select(sel_ref):
    return [[sel_ref[0, k].astype(F32) for k in range(sel_ref.shape[1])]]


def energy_kernel(sel, bank, latent, affine_w, affine_b, style_out, energy_out):
    style = (
        jnp.dot(latent[...], affine_w[...], precision=lax.Precision.HIGHEST, preferred_element_type=F32)
        + affine_b[...]
    )
    style_out[...] = style
    total = jnp.zeros(bank.shape[2:], F32)
    sel = own_select(sel)
    for tap in range(TAPS):
        plain = mixed(bank, sel, 0, tap) * style
        total = total + plain * plain
    energy_out[...] = jnp.broadcast_to(jnp.sum(total, axis=1, keepdims=True), energy_out.shape)


def modulated_kernel(sel, bank, style, *refs):
    energies, (mod_out, scale_out, row_out) = refs[:-3], refs[-3:]
    energy = energies[0][...]
    for other in energies[1:]:
        energy = energy + other[...]
    scales = lax.rsqrt(energy + EPS)
    scale_out[...] = scales
    row_out[...] = scales.T[0:1]
    scale = scales[:, 0:1]
    sel = own_select(sel)
    for tap in range(TAPS):
        mod_out[tap] = (mixed(bank, sel, 0, tap) * style[...] * scale).astype(BF16)


def blocks_kernel(rows, size, shares, place, *refs):
    parts, whole, out, by_row, by_share = refs[:rows], *refs[rows:]
    row_at = place[2]
    for r in range(rows):
        by_row[lax.rem(row_at - r + rows, rows)] = parts[r][...]
    ch = whole.shape[2] // size
    share = out.shape[1]
    taps = []
    for tap in range(TAPS):
        value = beside([by_row[r, tap].astype(F32) for r in range(rows)])
        whole[tap] = value.astype(BF16)
        taps.append(value)
    for z in range(size):
        value = beside([value[:, z * ch : (z + 1) * ch] for value in taps]).astype(BF16)
        for k in range(shares):
            by_share[k, z] = value[k * share : (k + 1) * share]
    out[...] = by_share[row_at if shares > 1 else 0]


def shifted(x, by):
    width = x.shape[1]
    lane = lax.broadcasted_iota(jnp.int32, x.shape, 1)
    moved = pltpu.roll(x, by % width, 1)
    return jnp.where(lane == (0 if by == 1 else width - 1), 0.0, moved)


def tap_products(g_ref, wide, total, height, width):
    total[...] = jnp.zeros(total.shape, F32)

    def body(row, _):
        g = g_ref[:, pl.ds(pl.multiple_of(row * width, width), width)]
        for kh in range(3):
            x = wide[:, pl.ds(pl.multiple_of((row + kh) * width, width), width)]
            total[kh] += lax.dot_general(g, x, (((1,), (1,)), ((), ())), preferred_element_type=F32)
        return 0

    lax.fori_loop(0, height, body, 0)
    return jnp.concatenate([total[kh] for kh in range(3)], axis=1)


def near_grad_kernel(size, height, width, *refs):
    cotans, (feat, feat_before, feat_after) = refs[:3], refs[3:6]
    outs, (wide, gathered, total) = refs[6:9], refs[9:]
    ch = feat.shape[0]
    for at, cotan in enumerate(cotans):
        gathered[at * ch : (at + 1) * ch] = cotan[...]
    for row in range(height + 2):
        if row == 0:
            x = feat_before[...]
        elif row == height + 1:
            x = feat_after[...]
        else:
            x = feat[:, (row - 1) * width : row * width]
        wide[ch : 2 * ch, row * width : (row + 1) * width] = x
        x = x.astype(F32)
        wide[0:ch, row * width : (row + 1) * width] = shifted(x, 1).astype(BF16)
        wide[2 * ch : 3 * ch, row * width : (row + 1) * width] = shifted(x, -1).astype(BF16)
    whole = tap_products(gathered, wide, total, height, width).astype(BF16)
    for at, out in enumerate(outs):
        out[...] = whole[at * ch : (at + 1) * ch]


def far_grad_kernel(height, width, first, second, wide, out, gathered, total):
    gathered[...] = first[...] + second[...]
    out[...] = tap_products(gathered, wide, total, height, width).astype(BF16)


def input_grad_kernel(rows, size, shares, height, width, place, *refs):
    cotan_own, first, second = refs[0], refs[1:size], refs[size : 2 * size - 1]
    mods = refs[2 * size - 1 : 2 * size - 1 + shares]
    main, before, after, gathered, taps, taps_t, total = refs[2 * size - 1 + shares :]
    ch = cotan_own.shape[0]
    gathered[0:ch] = cotan_own[...]
    for d in range(1, size):
        gathered[d * ch : (d + 1) * ch] = first[d - 1][...] + second[size - d - 1][...]
    for k in range(shares):
        share = lax.rem(place[2] - k + rows, rows) if shares > 1 else 0
        for d in range(size):
            taps[d, share] = mods[k][lax.rem(place[1] - place[3] * d + size, size)].astype(F32)
    taps_t[...] = taps[...].reshape(size * ch, taps.shape[3]).T.astype(BF16)
    total[...] = jnp.zeros(total.shape, F32)

    def body(row, _):
        g = gathered[:, pl.ds(pl.multiple_of(row * width, width), width)]
        for kh in range(3):
            y = jnp.dot(taps_t[kh * 3 * ch : (kh + 1) * 3 * ch], g, preferred_element_type=F32)
            total[row + kh] += y
        return 0

    lax.fori_loop(0, height, body, 0)
    for row in range(height + 2):
        value = total[row, ch : 2 * ch]
        value = value + shifted(total[row, 0:ch], -1) + shifted(total[row, 2 * ch : 3 * ch], 1)
        if row == 0:
            before[...] = value
        elif row == height + 1:
            after[...] = value
        else:
            main[:, (row - 1) * width : row * width] = value


def split3(x):
    high = x.astype(BF16).astype(F32)
    mid = (x - high).astype(BF16).astype(F32)
    return high, mid, x - high - mid


def middle_grad_kernel(size, height, width, place, *refs):
    count = size - 3
    first, second, (wide, own, before, after) = refs[:count], refs[count : 2 * count], refs[2 * count : 2 * count + 4]
    out, gathered, total = refs[2 * count + 4 :]
    ch = own.shape[0]
    for at in range(count):
        gathered[at * ch : (at + 1) * ch] = first[at][...] + second[at][...]
    whole = tap_products(gathered, wide, total, height, width).astype(BF16)
    slots = [own[...], before[...]] + [whole[at * ch : (at + 1) * ch] for at in range(count)] + [after[...]]
    for d, value in enumerate(slots):
        out[lax.rem(place[1] - place[3] * d + size, size)] = value


def put_fall(out, fall):
    lane = lax.broadcasted_iota(jnp.int32, out.shape[1:], 1)
    last = jnp.zeros(out.shape[1:], F32)
    for at, piece in enumerate(split3(fall)):
        last = jnp.where(lane == at, piece, last)
    out[TAPS] = last.astype(BF16)


def get_fall(last):
    last = last.astype(F32)
    return last[:, 0:1] + last[:, 1:2] + last[:, 2:3]


def collect_kernel(rows, size, place, scale, whole_mod, far, near, *refs):
    outs, (by_chan, by_row) = refs[:rows], refs[rows:]
    chan_at, row_at = place[1], place[2]
    by_chan[...] = near[...].astype(F32)
    by_chan[jnp.where(chan_at == 0, size - 1, 0)] += far[...].astype(F32)
    ch = whole_mod.shape[2] // size
    in_ch = outs[0].shape[2]
    product = jnp.zeros(whole_mod.shape[1:], F32)
    for tap in range(TAPS):
        value = beside([by_chan[z, :, tap * ch : (tap + 1) * ch] for z in range(size)])
        product = product + value * whole_mod[tap].astype(F32)
        for r in range(rows):
            by_row[r, tap] = value[:, r * in_ch : (r + 1) * in_ch].astype(BF16)
    fall = jnp.sum(product, axis=1, keepdims=True) * (scale[:, 0:1] * scale[:, 0:1])
    for r in range(rows):
        outs[r][0:TAPS] = by_row[lax.rem(row_at + r, rows)]
        put_fall(outs[r], fall)


def row_sum_kernel(*refs):
    parts, out = refs[:-1], refs[-1]
    fall = get_fall(parts[0][TAPS])
    for part in parts[1:]:
        fall = fall + get_fall(part[TAPS])
    for tap in range(TAPS):
        value = parts[0][tap].astype(F32)
        for part in parts[1:]:
            value = value + part[tap].astype(F32)
        out[tap] = value.astype(BF16)
    put_fall(out, fall)


def bank_grad_kernel(samples, starts, place, bank, *refs):
    parts, smalls = refs[:samples], refs[samples : 2 * samples]
    bank_grad, style_grad, held, small = refs[2 * samples :]
    sample = place[0]
    for s in range(samples):
        held[lax.rem(sample - s + samples, samples)] = parts[s][...]
        small[lax.rem(sample - s + samples, samples)] = smalls[s][...]
    filters, out_ch, in_ch = bank.shape[0], bank.shape[2], bank.shape[3]
    at_style, at_scale, at_sel = starts
    sel, styles, scales, falls = [], [], [], []
    for b in range(samples):
        row = small[b]
        sel.append([row[:, at_sel + k : at_sel + k + 1] for k in range(filters)])
        styles.append(row[:, at_style : at_style + in_ch])
        across = jnp.broadcast_to(row[:, at_scale : at_scale + 128], (128, 128))
        scales.append(across.T[:out_ch, 0:1])
        falls.append(get_fall(held[b, TAPS]))
    sums = [jnp.zeros(bank.shape[2:], F32) for _ in range(samples)]
    for tap in range(TAPS):
        totals = [None] * filters
        for b in range(samples):
            kern = mixed(bank, sel, b, tap)
            plain_grad = held[b, tap].astype(F32) * scales[b] - kern * styles[b] * falls[b]
            sums[b] = sums[b] + plain_grad * kern
            kernel_grad = plain_grad * styles[b]
            for k in range(filters):
                term = sel[b][k] * kernel_grad
                totals[k] = term if totals[k] is None else totals[k] + term
        for k in range(filters):
            bank_grad[k, tap] = totals[k]
    for b in range(samples):
        value = jnp.sum(sums[b], axis=0, keepdims=True)
        for z in range(style_grad.shape[0]):
            style_grad[z, b : b + 1] = value


def affine_kernel(samples, place, parts, *refs):
    smalls, w_grad, b_grad, latents = refs[:samples], *refs[samples:]
    for s in range(samples):
        at = lax.rem(place[0] - s + samples, samples)
        latents[pl.ds(at, 1)] = smalls[s][:, : latents.shape[1]]
    style_grad = parts[0]
    for z in range(1, parts.shape[0]):
        style_grad = style_grad + parts[z]
    w_grad[...] = lax.dot_general(
        latents[...],
        style_grad,
        (((0,), (0,)), ((), ())),
        precision=lax.Precision.HIGHEST,
        preferred_element_type=F32,
    )
    bias = style_grad[0:1]
    for b in range(1, samples):
        bias = bias + style_grad[b : b + 1]
    b_grad[...] = bias


def call(kernel, name, outs, *operands, scalars=0, fetched=0, scratch=(), flops=10**6):
    outs = tuple(jax.ShapeDtypeStruct(*o) for o in outs)
    moved = sum(o.size * o.dtype.itemsize for o in (*outs, *operands))
    return pl.pallas_call(
        kernel,
        out_shape=outs,
        in_specs=sspec(scalars) + [pl.BlockSpec()] * fetched + vspec(len(operands) - scalars - fetched),
        out_specs=tuple(vspec(len(outs))),
        scratch_shapes=[pltpu.VMEM(*s) for s in scratch],
        compiler_params=params(),
        cost_estimate=cost(flops, moved),
        name=name,
    )(*operands)


def exchange(x, axis):
    size = lax.axis_size(axis)
    return [x] + [
        lax.ppermute(x, axis, [(i, (i + s) % size) for i in range(size)]) for s in range(1, size)
    ]


def from_sides(first, last, axis):
    size, at = lax.axis_size(axis), lax.axis_index(axis)
    if size == 2:
        got = lax.ppermute(jnp.where(at == 0, last, first), axis, [(0, 1), (1, 0)])
        nothing = jnp.zeros_like(got)
        return jnp.where(at == 1, got, nothing), jnp.where(at == 0, got, nothing)
    up = [(i, i + 1) for i in range(size - 1)]
    down = [(i + 1, i) for i in range(size - 1)]
    return lax.ppermute(last, axis, up), lax.ppermute(first, axis, down)


def on_device(feature, out_grad, bank, select, latent, affine_w, affine_b):
    rows, samples, size = (lax.axis_size(a) for a in ("rows", "samples", "chan"))
    row_at, sample_at, chan_at = (lax.axis_index(a) for a in ("rows", "samples", "chan"))
    _, ch, height, width = feature.shape
    out_ch, in_ch = bank.shape[2:]
    pixels, all_ch = height * width, ch * size
    sign = 1 - 2 * jnp.remainder(sample_at, 2)
    place = jnp.stack([sample_at, chan_at, row_at, sign]).astype(jnp.int32)
    flops = 2 * TAPS * ch * ch * size * pixels

    def along(x, pairs):
        whole = []
        for b in range(samples):
            for i, j in pairs:
                if b % 2:
                    i, j = size - 1 - i, size - 1 - j
                whole.append((b * size + i, b * size + j))
        return lax.ppermute(x, ("samples", "chan"), whole)

    cotan = out_grad[0].reshape(ch, pixels)
    first, second = [], []

    def step(number, x, y):
        first.append(along(x, [(i, i + 1) for i in range(number - 1, size - 1)]))
        second.append(along(y, [(i + 1, i) for i in range(size - number)]))

    step(1, cotan, cotan)

    feat = feature[0].reshape(ch, pixels)
    feat_before, feat_after = from_sides(feat[:, :width], feat[:, pixels - width :], "rows")
    style, energy = call(
        energy_kernel,
        "energy",
        [((1, in_ch), F32), ((out_ch, 128), F32)],
        select,
        bank,
        latent,
        affine_w,
        affine_b[None],
        scalars=1,
        fetched=4,
    )
    mod_own, scale, scale_row = call(
        modulated_kernel,
        "modulated",
        [((TAPS, out_ch, in_ch), BF16), ((out_ch, 128), F32), ((1, out_ch), F32)],
        select,
        bank,
        style,
        *exchange(energy, "rows"),
        scalars=1,
        fetched=1,
    )
    pieces, starts, at = [], [], 0
    for piece in (latent, style, scale_row, select.astype(F32)):
        length = -(-piece.shape[1] // 128) * 128
        pieces.append(jnp.pad(piece, ((0, 0), (0, length - piece.shape[1]))))
        starts.append(at)
        at += length
    smalls = exchange(jnp.concatenate(pieces, axis=1), "samples")
    first[0], second[0], smalls, feat_before, feat_after = lax.optimization_barrier(
        (first[0], second[0], smalls, feat_before, feat_after)
    )

    step(2, first[0], second[0])
    message = ((ch, TAPS * ch), BF16)
    whole_mod, to_send = call(
        functools.partial(blocks_kernel, rows, size, 1),
        "mod_blocks",
        [((TAPS, out_ch, all_ch), BF16), ((size, *message[0]), BF16)],
        place,
        *exchange(mod_own, "rows"),
        scalars=1,
        scratch=[((rows, TAPS, out_ch, in_ch), BF16), ((1, size, *message[0]), BF16)],
    )
    *near, wide = call(
        functools.partial(near_grad_kernel, size, height, width),
        "near_grad",
        [message] * 3 + [((3 * ch, (height + 2) * width), BF16)],
        cotan,
        first[0],
        second[0],
        feat,
        feat_before,
        feat_after,
        scratch=[((3 * ch, pixels), BF16), ((3, 3 * ch, 3 * ch), F32)],
        flops=flops * 3 // size,
    )
    first[1], second[1], near, to_send, whole_mod = lax.optimization_barrier(
        (first[1], second[1], near, to_send, whole_mod)
    )

    for number in range(3, size):
        step(number, first[number - 2], second[number - 2])
    between = range(2, size - 1)
    (near,) = call(
        functools.partial(middle_grad_kernel, size, height, width),
        "middle_grad",
        [((size, *message[0]), BF16)],
        place,
        *[first[d - 1] for d in between],
        *[second[size - d - 1] for d in between],
        wide,
        *near,
        scalars=1,
        scratch=[((len(between) * ch, pixels), BF16), ((3, len(between) * ch, 3 * ch), F32)],
        flops=flops * len(between) // size,
    )
    near_got = lax.all_to_all(near, "chan", 0, 0)
    first[-1], second[-1], near = lax.optimization_barrier((first[-1], second[-1], near))
    (far,) = call(
        functools.partial(far_grad_kernel, height, width),
        "far_grad",
        [message],
        first[-1],
        second[-1],
        wide,
        scratch=[((ch, pixels), BF16), ((3, ch, 3 * ch), F32)],
        flops=flops // size,
    )
    far_got = lax.ppermute(far, "chan", [(0, size - 1), (size - 1, 0)])

    far_got, to_send = lax.optimization_barrier((far_got, to_send))
    mods = lax.all_to_all(to_send, "chan", 0, 0)
    parts = call(
        functools.partial(collect_kernel, rows, size),
        "collect",
        [((TAPS + 1, out_ch, in_ch), BF16)] * rows,
        place,
        scale,
        whole_mod,
        far_got,
        near_got,
        scalars=1,
        scratch=[((size, *message[0]), F32), ((rows, TAPS, out_ch, in_ch), BF16)],
    )
    parts = [parts[0]] + [
        lax.ppermute(parts[r], "rows", [(i, (i + r) % rows) for i in range(rows)])
        for r in range(1, rows)
    ]
    (own,) = call(row_sum_kernel, "row_sum", [((TAPS + 1, out_ch, in_ch), BF16)], *parts)
    every = exchange(own, "samples")

    own, mods = lax.optimization_barrier((own, mods))
    main, before, after = call(
        functools.partial(input_grad_kernel, rows, size, 1, height, width),
        "input_grad",
        [((ch, pixels), F32), ((ch, width), F32), ((ch, width), F32)],
        place,
        cotan,
        *first,
        *second,
        mods,
        scalars=1,
        scratch=[
            ((all_ch, pixels), BF16),
            ((size, 1, *message[0]), F32),
            ((TAPS * ch, all_ch), BF16),
            ((height + 2, 3 * ch, width), F32),
        ],
        flops=flops,
    )
    every, main, before, after = lax.optimization_barrier((every, main, before, after))
    bank_grad, style_parts = call(
        functools.partial(bank_grad_kernel, samples, starts[1:]),
        "bank_grad",
        [(bank.shape, F32), ((size, samples, in_ch), F32)],
        place,
        bank,
        *every,
        *smalls,
        scalars=1,
        fetched=1,
        scratch=[((samples, TAPS + 1, out_ch, in_ch), BF16), ((samples, *smalls[0].shape), F32)],
    )
    style_parts, before, after = lax.optimization_barrier((style_parts, before, after))
    style_parts = lax.all_to_all(style_parts, "chan", 0, 0)
    from_above, from_below = from_sides(before, after, "rows")
    edge = jnp.concatenate(
        [from_above[:, None], jnp.zeros((ch, height - 2, width), F32), from_below[:, None]], axis=1
    )
    feature_grad = (main.reshape(ch, height, width) + edge).astype(BF16)[None]
    affine_w_grad, affine_b_grad = call(
        functools.partial(affine_kernel, samples),
        "affine",
        [(affine_w.shape, F32), ((1, in_ch), F32)],
        place,
        style_parts,
        *smalls,
        scalars=1,
        scratch=[((samples, latent.shape[1]), F32)],
    )
    return (feature_grad, bank_grad, affine_w_grad, affine_b_grad[0])


def solution(mesh):
    return jax.shard_map(
        on_device,
        mesh=mesh,
        in_specs=(
            P("samples", "chan", "rows", None),
            P("samples", "chan", "rows", None),
            P(None, None, "chan", "rows"),
            P("samples", None),
            P("samples", None),
            P(None, "rows"),
            P("rows"),
        ),
        out_specs=(
            P("samples", "chan", "rows", None),
            P(None, None, "chan", "rows"),
            P(None, "rows"),
            P("rows"),
        ),
        check_vma=False,
    )
```

```python
import functools

import jax
import jax.numpy as jnp
from jax import lax
from jax.experimental import pallas as pl
from jax.experimental.pallas import tpu as pltpu
from jax.sharding import PartitionSpec as P

EPS = 1e-08
TAPS = 9
F32 = jnp.float32
BF16 = jnp.bfloat16
VMEM_LIMIT = 16 * 2**20


def params():
    return pltpu.CompilerParams(vmem_limit_bytes=VMEM_LIMIT)


def vspec(n):
    return [pl.BlockSpec(memory_space=pltpu.VMEM)] * n


def sspec(n):
    return [pl.BlockSpec(memory_space=pltpu.SMEM)] * n


def cost(flops, moved):
    return pl.CostEstimate(flops=flops, bytes_accessed=moved, transcendentals=0)


def beside(pieces):
    return pieces[0] if len(pieces) == 1 else jnp.concatenate(pieces, axis=1)


def mixed(bank_ref, sel, sample, tap):
    total = sel[sample][0] * bank_ref[0, tap]
    for k in range(1, bank_ref.shape[0]):
        total = total + sel[sample][k] * bank_ref[k, tap]
    return total


def own_select(sel_ref):
    return [[sel_ref[0, k].astype(F32) for k in range(sel_ref.shape[1])]]


def energy_kernel(sel, latent, affine_b, bank_hbm, w_hbm, style_out, kernel_out, energy_out, bank, affine_w, sems):
    copies = [
        pltpu.make_async_copy(w_hbm, affine_w, sems.at[0]),
        pltpu.make_async_copy(bank_hbm, bank, sems.at[1]),
    ]
    for copy in copies:
        copy.start()
    copies[0].wait()
    style = (
        jnp.dot(latent[...], affine_w[...], precision=lax.Precision.HIGHEST, preferred_element_type=F32)
        + affine_b[...]
    )
    style_out[...] = style
    total = jnp.zeros(bank.shape[2:], F32)
    sel = own_select(sel)
    copies[1].wait()
    for tap in range(TAPS):
        kernel = mixed(bank, sel, 0, tap)
        kernel_out[tap] = kernel
        plain = kernel * style
        total = total + plain * plain
    energy_out[...] = jnp.broadcast_to(jnp.sum(total, axis=1, keepdims=True), energy_out.shape)


def modulated_kernel(kernel, style, *refs):
    energies, (mod_out, scale_out, row_out) = refs[:-3], refs[-3:]
    energy = energies[0][...]
    for other in energies[1:]:
        energy = energy + other[...]
    scales = lax.rsqrt(energy + EPS)
    scale_out[...] = scales
    row_out[...] = scales.T[0:1]
    scale = scales[:, 0:1]
    for tap in range(TAPS):
        mod_out[tap] = (kernel[tap] * style[...] * scale).astype(BF16)


def blocks_kernel(rows, size, shares, place, *refs):
    parts, whole, own, ahead, behind, others, by_row, by_share = refs[:rows], *refs[rows:]
    chan_at, row_at, sign = place[1], place[2], place[3]
    for r in range(rows):
        by_row[lax.rem(row_at - r + rows, rows)] = parts[r][...]
    ch = whole.shape[2] // size
    share = ch // shares
    taps = []
    for tap in range(TAPS):
        value = beside([by_row[r, tap].astype(F32) for r in range(rows)])
        whole[tap] = value.astype(BF16)
        taps.append(value)
    for z in range(size):
        value = beside([value[:, z * ch : (z + 1) * ch] for value in taps]).astype(BF16)
        for k in range(shares):
            by_share[k, z] = value[k * share : (k + 1) * share]
    for k in range(shares):
        own[k * share : (k + 1) * share] = by_share[k, chan_at]
    k = row_at if shares > 1 else 0
    ahead[...] = by_share[k, lax.rem(chan_at + sign + size, size)]
    behind[...] = by_share[k, lax.rem(chan_at - sign + size, size)]
    for d in range(2, size - 1):
        others[(d - 2) * share : (d - 1) * share] = by_share[k, lax.rem(chan_at + sign * d + size, size)]
    others[(size - 3) * share :] = by_share[k, size - 1 - chan_at]


def shifted(x, by):
    width = x.shape[1]
    lane = lax.broadcasted_iota(jnp.int32, x.shape, 1)
    moved = pltpu.roll(x, by % width, 1)
    return jnp.where(lane == (0 if by == 1 else width - 1), 0.0, moved)


def spread(wide, row, x):
    ch, width = x.shape
    wide[ch : 2 * ch, row * width : (row + 1) * width] = x
    x = x.astype(F32)
    wide[0:ch, row * width : (row + 1) * width] = shifted(x, 1).astype(BF16)
    wide[2 * ch : 3 * ch, row * width : (row + 1) * width] = shifted(x, -1).astype(BF16)


def rows_kernel(height, width, feat, feat_before, feat_after, out):
    out[:, 0:width] = feat_before[...]
    out[:, width : (height + 1) * width] = feat[...]
    out[:, (height + 1) * width :] = feat_after[...]


def tap_products(g_ref, wides, totals, height, width):
    for total in totals:
        total[...] = jnp.zeros(total.shape, F32)

    def body(row, _):
        g = g_ref[:, pl.ds(pl.multiple_of(row * width, width), width)]
        for wide, total in zip(wides, totals):
            for kh in range(3):
                x = wide[:, pl.ds(pl.multiple_of((row + kh) * width, width), width)]
                total[kh] += lax.dot_general(g, x, (((1,), (1,)), ((), ())), preferred_element_type=F32)
        return 0

    lax.fori_loop(0, height, body, 0)
    return [jnp.concatenate([total[kh] for kh in range(3)], axis=1).astype(BF16) for total in totals]


def near_grad_kernel(height, width, *refs):
    cotans, feat, outs, (wide, gathered, total) = refs[:3], refs[3], refs[4:7], refs[7:]
    ch = feat.shape[0]
    for at, cotan in enumerate(cotans):
        gathered[at * ch : (at + 1) * ch] = cotan[...]
    for row in range(height + 2):
        spread(wide, row, feat[:, row * width : (row + 1) * width])
    (whole,) = tap_products(gathered, [wide], [total], height, width)
    for at, out in enumerate(outs):
        out[...] = whole[at * ch : (at + 1) * ch]


def far_grad_kernel(count, height, width, *refs):
    first, second, (wide, feat) = refs[:count], refs[count : 2 * count], refs[2 * count : 2 * count + 2]
    outs, (wide_end, gathered, end_block, total, end_total) = refs[2 * count + 2 : -5], refs[-5:]
    ch = feat.shape[0]
    for at in range(count):
        gathered[at * ch : (at + 1) * ch] = first[at][...] + second[count - 1 - at][...]
    for row in range(height + 2):
        spread(wide_end, row, feat[:, row * width : (row + 1) * width])
    if count == 1:
        whole, end = tap_products(gathered, [wide, wide_end], [total, end_total], height, width)
    else:
        end_block[...] = first[-1][...] + second[-1][...]
        (whole,) = tap_products(gathered, [wide], [total], height, width)
        (end,) = tap_products(end_block, [wide_end], [end_total], height, width)
    out = outs[0]
    out[0 : count * ch] = whole
    out[count * ch :] = end


def input_products(cotan, taps_t, total, outs, height, width):
    main, before, after = outs
    ch = main.shape[0]
    total[...] = jnp.zeros(total.shape, F32)

    def body(row, _):
        g = cotan[:, pl.ds(pl.multiple_of(row * width, width), width)]
        for kh in range(3):
            y = jnp.dot(taps_t[kh * 3 * ch : (kh + 1) * 3 * ch], g, preferred_element_type=F32)
            total[row + kh] += y
        return 0

    lax.fori_loop(0, height, body, 0)
    for row in range(height + 2):
        value = total[row, ch : 2 * ch]
        value = value + shifted(total[row, 0:ch], -1) + shifted(total[row, 2 * ch : 3 * ch], 1)
        value = value.astype(main.dtype)
        if row == 0:
            before[...] = value
        elif row == height + 1:
            after[...] = value
        else:
            main[:, (row - 1) * width : row * width] = value


def input_grad_kernel(rows, count, height, width, place, *refs):
    cotans, first, second = refs[:3], refs[3 : 3 + count], refs[3 + count : 3 + 2 * count]
    own_mod, mods, outs = refs[3 + 2 * count], refs[4 + 2 * count : -7], refs[-7:-4]
    gathered, taps, taps_t, total = refs[-4:]
    ch = own_mod.shape[0]
    shares, share = len(mods), ch // len(mods)
    for at, cotan in enumerate(cotans):
        gathered[at * ch : (at + 1) * ch] = cotan[...]
    for at in range(count):
        gathered[(3 + at) * ch : (4 + at) * ch] = first[at][...] + second[count - 1 - at][...]
    for k in range(shares):
        taps[0, k] = own_mod[k * share : (k + 1) * share].astype(F32)
        owner = lax.rem(place[2] - k + rows, rows) if shares > 1 else 0
        for at in range(2 + count):
            taps[1 + at, owner] = mods[k][at * share : (at + 1) * share].astype(F32)
    taps_t[...] = taps[...].reshape((3 + count) * ch, taps.shape[3]).T.astype(BF16)
    input_products(gathered, taps_t, total, outs, height, width)


def end_input_kernel(rows, count, height, width, place, first, second, *refs):
    mods, outs, (gathered, taps, taps_t, total) = refs[:-7], refs[-7:-4], refs[-4:]
    ch = outs[0].shape[0]
    shares, share = len(mods), ch // len(mods)
    gathered[...] = first[...] + second[...]
    for k in range(shares):
        owner = lax.rem(place[2] - k + rows, rows) if shares > 1 else 0
        taps[owner] = mods[k][(2 + count) * share :].astype(F32)
    taps_t[...] = taps[...].reshape(ch, taps.shape[2]).T.astype(BF16)
    input_products(gathered, taps_t, total, outs, height, width)


def split3(x):
    high = x.astype(BF16).astype(F32)
    mid = (x - high).astype(BF16).astype(F32)
    return high, mid, x - high - mid


def put_fall(out, fall):
    lane = lax.broadcasted_iota(jnp.int32, out.shape[1:], 1)
    last = jnp.zeros(out.shape[1:], F32)
    for at, piece in enumerate(split3(fall)):
        last = jnp.where(lane == at, piece, last)
    out[TAPS] = last.astype(BF16)


def get_fall(last):
    last = last.astype(F32)
    return last[:, 0:1] + last[:, 1:2] + last[:, 2:3]


def collect_kernel(rows, size, place, scale, whole_mod, own, ahead, behind, others, *refs):
    outs, (by_chan, by_row) = refs[:rows], refs[rows:]
    chan_at, row_at, sign = place[1], place[2], place[3]
    ch = own.shape[0]
    by_chan[chan_at] = own[...].astype(F32)
    by_chan[lax.rem(chan_at + sign + size, size)] = ahead[...].astype(F32)
    by_chan[lax.rem(chan_at - sign + size, size)] = behind[...].astype(F32)
    for d in range(2, size - 1):
        value = others[(d - 2) * ch : (d - 1) * ch].astype(F32)
        by_chan[lax.rem(chan_at + sign * d + size, size)] = value
    by_chan[jnp.where(chan_at == 0, size - 1, 0)] += others[(size - 3) * ch :].astype(F32)
    in_ch = outs[0].shape[2]
    product = jnp.zeros(whole_mod.shape[1:], F32)
    for tap in range(TAPS):
        value = beside([by_chan[z, :, tap * ch : (tap + 1) * ch] for z in range(size)])
        product = product + value * whole_mod[tap].astype(F32)
        for r in range(rows):
            by_row[r, tap] = value[:, r * in_ch : (r + 1) * in_ch].astype(BF16)
    fall = jnp.sum(product, axis=1, keepdims=True) * (scale[:, 0:1] * scale[:, 0:1])
    for r in range(rows):
        outs[r][0:TAPS] = by_row[lax.rem(row_at + r, rows)]
        put_fall(outs[r], fall)


def row_sum_kernel(*refs):
    parts, out = refs[:-1], refs[-1]
    fall = get_fall(parts[0][TAPS])
    for part in parts[1:]:
        fall = fall + get_fall(part[TAPS])
    for tap in range(TAPS):
        value = parts[0][tap].astype(F32)
        for part in parts[1:]:
            value = value + part[tap].astype(F32)
        out[tap] = value.astype(BF16)
    put_fall(out, fall)


def bank_grad_kernel(samples, starts, place, bank, *refs):
    parts, smalls = refs[:samples], refs[samples : 2 * samples]
    bank_grad, style_grad, held, small = refs[2 * samples :]
    sample = place[0]
    for s in range(samples):
        held[lax.rem(sample - s + samples, samples)] = parts[s][...]
        small[lax.rem(sample - s + samples, samples)] = smalls[s][...]
    filters, out_ch, in_ch = bank.shape[0], bank.shape[2], bank.shape[3]
    at_style, at_scale, at_sel = starts
    sel, styles, scales, falls = [], [], [], []
    for b in range(samples):
        row = small[b]
        sel.append([row[:, at_sel + k : at_sel + k + 1] for k in range(filters)])
        styles.append(row[:, at_style : at_style + in_ch])
        across = jnp.broadcast_to(row[:, at_scale : at_scale + 128], (128, 128))
        scales.append(across.T[:out_ch, 0:1])
        falls.append(get_fall(held[b, TAPS]))
    sums = [jnp.zeros(bank.shape[2:], F32) for _ in range(samples)]
    for tap in range(TAPS):
        totals = [None] * filters
        for b in range(samples):
            kern = mixed(bank, sel, b, tap)
            plain_grad = held[b, tap].astype(F32) * scales[b] - kern * styles[b] * falls[b]
            sums[b] = sums[b] + plain_grad * kern
            kernel_grad = plain_grad * styles[b]
            for k in range(filters):
                term = sel[b][k] * kernel_grad
                totals[k] = term if totals[k] is None else totals[k] + term
        for k in range(filters):
            bank_grad[k, tap] = totals[k]
    for b in range(samples):
        value = jnp.sum(sums[b], axis=0, keepdims=True)
        style_grad[b : b + 1] = value


def affine_kernel(samples, size, place, *refs):
    parts, smalls = refs[:size], refs[size : size + samples]
    w_grad, b_grad, latents, held = refs[size + samples :]
    for s in range(samples):
        at = lax.rem(place[0] - s + samples, samples)
        latents[pl.ds(at, 1)] = smalls[s][:, : latents.shape[1]]
    for d in range(size):
        held[lax.rem(place[1] - d + size, size)] = parts[d][...]
    style_grad = held[0]
    for z in range(1, size):
        style_grad = style_grad + held[z]
    w_grad[...] = lax.dot_general(
        latents[...],
        style_grad,
        (((0,), (0,)), ((), ())),
        precision=lax.Precision.HIGHEST,
        preferred_element_type=F32,
    )
    bias = style_grad[0:1]
    for b in range(1, samples):
        bias = bias + style_grad[b : b + 1]
    b_grad[...] = bias


def call(kernel, name, outs, *operands, scalars=0, fetched=0, scratch=(), copies=0, flops=10**6):
    outs = tuple(jax.ShapeDtypeStruct(*o) for o in outs)
    moved = sum(o.size * o.dtype.itemsize for o in (*outs, *operands))
    return pl.pallas_call(
        kernel,
        out_shape=outs,
        in_specs=sspec(scalars)
        + vspec(len(operands) - scalars - fetched)
        + [pl.BlockSpec(memory_space=pltpu.HBM)] * fetched,
        out_specs=tuple(vspec(len(outs))),
        scratch_shapes=[pltpu.VMEM(*s) for s in scratch] + [pltpu.SemaphoreType.DMA((copies,))] * (copies > 0),
        compiler_params=params(),
        cost_estimate=cost(flops, moved),
        name=name,
    )(*operands)


def exchange(x, axis):
    size = lax.axis_size(axis)
    return [x] + [
        lax.ppermute(x, axis, [(i, (i + s) % size) for i in range(size)]) for s in range(1, size)
    ]


def from_sides(first, last, lines):
    size, chans, at = lax.axis_size("rows"), lax.axis_size("chan"), lax.axis_index("rows")

    def send(x, pairs):
        return lax.ppermute(
            x, ("rows", "chan"), [(r * chans + i, q * chans + j) for r, q in pairs for i, j in lines]
        )

    if size == 2:
        got = send(jnp.where(at == 0, last, first), [(0, 1), (1, 0)])
        nothing = jnp.zeros_like(got)
        return jnp.where(at == 1, got, nothing), jnp.where(at == 0, got, nothing)
    up = [(i, i + 1) for i in range(size - 1)]
    down = [(i + 1, i) for i in range(size - 1)]
    return send(last, up), send(first, down)


def on_device(feature, out_grad, bank, select, latent, affine_w, affine_b):
    rows, samples, size = (lax.axis_size(a) for a in ("rows", "samples", "chan"))
    row_at, sample_at, chan_at = (lax.axis_index(a) for a in ("rows", "samples", "chan"))
    _, ch, height, width = feature.shape
    out_ch, in_ch = bank.shape[2:]
    pixels, all_ch = height * width, ch * size
    sign = 1 - 2 * jnp.remainder(sample_at, 2)
    place = jnp.stack([sample_at, chan_at, row_at, sign]).astype(jnp.int32)
    flops = 2 * TAPS * ch * ch * size * pixels

    def along(x, pairs):
        whole = []
        for b in range(samples):
            for i, j in pairs:
                if b % 2:
                    i, j = size - 1 - i, size - 1 - j
                whole.append((b * size + i, b * size + j))
        return lax.ppermute(x, ("samples", "chan"), whole)

    cotan = out_grad[0].reshape(ch, pixels)
    first, second = [], []

    def step(number, x, y):
        first.append(along(x, [(i, i + 1) for i in range(number - 1, size - 1)]))
        second.append(along(y, [(i + 1, i) for i in range(size - number)]))

    step(1, cotan, cotan)

    same = [(i, i) for i in range(size)]
    feat = feature[0].reshape(ch, pixels)
    feat_before, feat_after = from_sides(feat[:, :width], feat[:, pixels - width :], same)
    style, kernel, energy = call(
        energy_kernel,
        "energy",
        [((1, in_ch), F32), ((TAPS, out_ch, in_ch), F32), ((out_ch, 128), F32)],
        select,
        latent,
        affine_b[None],
        bank,
        affine_w,
        scalars=1,
        fetched=2,
        scratch=[(bank.shape, F32), (affine_w.shape, F32)],
        copies=2,
    )
    mod_own, scale, scale_row = call(
        modulated_kernel,
        "modulated",
        [((TAPS, out_ch, in_ch), BF16), ((out_ch, 128), F32), ((1, out_ch), F32)],
        kernel,
        style,
        *exchange(energy, "rows"),
    )
    extended = ((ch, (height + 2) * width), BF16)
    (feat,) = call(
        functools.partial(rows_kernel, height, width), "feat_rows", [extended], feat, feat_before, feat_after
    )
    message = ((ch, TAPS * ch), BF16)
    shares = rows if ch % (16 * rows) == 0 else 1
    share = ((ch // shares, TAPS * ch), BF16)
    count = size - 3
    whole_mod, own_mod, mod_ahead, mod_behind, mod_others = call(
        functools.partial(blocks_kernel, rows, size, shares),
        "mod_blocks",
        [
            ((TAPS, out_ch, all_ch), BF16),
            message,
            share,
            share,
            (((count + 1) * share[0][0], share[0][1]), BF16),
        ],
        place,
        *exchange(mod_own, "rows"),
        scalars=1,
        scratch=[((rows, TAPS, out_ch, in_ch), BF16), ((shares, size, *share[0]), BF16)],
    )
    first[0], second[0], feat, mod_ahead, mod_behind, mod_others = lax.optimization_barrier(
        (first[0], second[0], feat, mod_ahead, mod_behind, mod_others)
    )

    step(2, first[0], second[0])
    feat_end = lax.ppermute(feat, "chan", [(0, 1), (size - 1, size - 2)])
    forth = [(i, i + 1) for i in range(size - 1)]
    back = [(i + 1, i) for i in range(size - 1)]
    ring = [(i, (i + 2) % size) for i in range(size)]
    mods = [along(mod_ahead, forth), along(mod_behind, back), along(mod_others, ring)]
    pieces, starts, at = [], [], 0
    for piece in (latent, style, scale_row, select.astype(F32)):
        length = -(-piece.shape[1] // 128) * 128
        pieces.append(jnp.pad(piece, ((0, 0), (0, length - piece.shape[1]))))
        starts.append(at)
        at += length
    smalls = exchange(jnp.concatenate(pieces, axis=1), "samples")
    own_grad, grad_behind, grad_ahead, wide = call(
        functools.partial(near_grad_kernel, height, width),
        "near_grad",
        [message] * 3 + [((3 * ch, (height + 2) * width), BF16)],
        cotan,
        first[0],
        second[0],
        feat,
        scratch=[((3 * ch, pixels), BF16), ((3, 3 * ch, 3 * ch), F32)],
        flops=flops * 3 // size,
    )
    from_ahead, from_behind = along(grad_behind, back), along(grad_ahead, forth)
    first[1], second[1], feat_end, mods, smalls, wide = lax.optimization_barrier(
        (first[1], second[1], feat_end, mods, smalls, wide)
    )

    (grad_others,) = call(
        functools.partial(far_grad_kernel, count, height, width),
        "far_grad",
        [(((count + 1) * ch, TAPS * ch), BF16)],
        *first[1:],
        *second[1:],
        wide,
        feat_end,
        scratch=[
            ((3 * ch, (height + 2) * width), BF16),
            ((count * ch, pixels), BF16),
            ((ch, pixels), BF16),
            ((3, count * ch, 3 * ch), F32),
            ((3, ch, 3 * ch), F32),
        ],
        flops=flops * 2 // size,
    )
    from_others = along(grad_others, ring)
    mods = jnp.concatenate(mods, axis=0)
    mods = exchange(mods, "rows") if shares > 1 else [mods]
    parts = call(
        functools.partial(collect_kernel, rows, size),
        "collect",
        [((TAPS + 1, out_ch, in_ch), BF16)] * rows,
        place,
        scale,
        whole_mod,
        own_grad,
        from_ahead,
        from_behind,
        from_others,
        scalars=1,
        scratch=[((size, *message[0]), F32), ((rows, TAPS, out_ch, in_ch), BF16)],
    )
    parts, mods = lax.optimization_barrier((parts, mods))
    parts = [parts[0]] + [
        lax.ppermute(parts[r], "rows", [(i, (i + r) % rows) for i in range(rows)])
        for r in range(1, rows)
    ]
    end_main, end_before, end_after = call(
        functools.partial(end_input_kernel, rows, count, height, width),
        "end_input_grad",
        [((ch, pixels), BF16), ((ch, width), BF16), ((ch, width), BF16)],
        place,
        first[-1],
        second[-1],
        *mods,
        scalars=1,
        scratch=[
            ((ch, pixels), BF16),
            ((shares, *share[0]), F32),
            ((TAPS * ch, ch), BF16),
            ((height + 2, 3 * ch, width), F32),
        ],
        flops=flops // size,
    )
    (own,) = call(row_sum_kernel, "row_sum", [((TAPS + 1, out_ch, in_ch), BF16)], *parts)
    every = exchange(own, "samples")
    outward = [(1, 0), (size - 2, size - 1)]
    far_main = lax.ppermute(end_main, "chan", outward)

    own, mods = lax.optimization_barrier((own, mods))
    main, before, after = call(
        functools.partial(input_grad_kernel, rows, count, height, width),
        "input_grad",
        [((ch, pixels), F32), ((ch, width), F32), ((ch, width), F32)],
        place,
        cotan,
        first[0],
        second[0],
        *first[1:],
        *second[1:],
        own_mod,
        *mods,
        scalars=1,
        scratch=[
            (((3 + count) * ch, pixels), BF16),
            ((3 + count, shares, *share[0]), F32),
            ((TAPS * ch, (3 + count) * ch), BF16),
            ((height + 2, 3 * ch, width), F32),
        ],
        flops=flops,
    )
    every, main, before, after = lax.optimization_barrier((every, main, before, after))
    bank_grad, style_part = call(
        functools.partial(bank_grad_kernel, samples, starts[1:]),
        "bank_grad",
        [(bank.shape, F32), ((samples, in_ch), F32)],
        place,
        bank,
        *every,
        *smalls,
        scalars=1,
        scratch=[((samples, TAPS + 1, out_ch, in_ch), BF16), ((samples, *smalls[0].shape), F32)],
    )
    style_part, sides = lax.optimization_barrier((style_part, (before, after, end_before, end_after)))
    style_parts = exchange(style_part, "chan")
    above, below = from_sides(*sides[:2], same)
    end_above, end_below = from_sides(*sides[2:], outward)
    from_above, from_below = above + end_above.astype(F32), below + end_below.astype(F32)
    edge = jnp.concatenate(
        [from_above[:, None], jnp.zeros((ch, height - 2, width), F32), from_below[:, None]], axis=1
    )
    total = (main + far_main.astype(F32)).reshape(ch, height, width) + edge
    feature_grad = total.astype(BF16)[None]
    affine_w_grad, affine_b_grad = call(
        functools.partial(affine_kernel, samples, size),
        "affine",
        [(affine_w.shape, F32), ((1, in_ch), F32)],
        place,
        *style_parts,
        *smalls,
        scalars=1,
        scratch=[((samples, latent.shape[1]), F32), ((size, samples, in_ch), F32)],
    )
    return (feature_grad, bank_grad, affine_w_grad, affine_b_grad[0])


def solution(mesh):
    return jax.shard_map(
        on_device,
        mesh=mesh,
        in_specs=(
            P("samples", "chan", "rows", None),
            P("samples", "chan", "rows", None),
            P(None, None, "chan", "rows"),
            P("samples", None),
            P("samples", None),
            P(None, "rows"),
            P("rows"),
        ),
        out_specs=(
            P("samples", "chan", "rows", None),
            P(None, None, "chan", "rows"),
            P(None, "rows"),
            P("rows"),
        ),
        check_vma=False,
    )
```

```python
import functools

import jax
import jax.numpy as jnp
from jax import lax
from jax.experimental import pallas as pl
from jax.experimental.pallas import tpu as pltpu
from jax.sharding import PartitionSpec as P

EPS = 1e-08
TAPS = 9
F32 = jnp.float32
BF16 = jnp.bfloat16
VMEM_LIMIT = 16 * 2**20


def params():
    return pltpu.CompilerParams(vmem_limit_bytes=VMEM_LIMIT)


def vspec(n):
    return [pl.BlockSpec(memory_space=pltpu.VMEM)] * n


def sspec(n):
    return [pl.BlockSpec(memory_space=pltpu.SMEM)] * n


def cost(flops, moved):
    return pl.CostEstimate(flops=flops, bytes_accessed=moved, transcendentals=0)


def beside(pieces):
    return pieces[0] if len(pieces) == 1 else jnp.concatenate(pieces, axis=1)


def mixed(bank_ref, weights, tap):
    total = weights[0] * bank_ref[0, tap]
    for k in range(1, bank_ref.shape[0]):
        total = total + weights[k] * bank_ref[k, tap]
    return total


def energy_kernel(*refs):
    given, (style_out, kernel_out, energy_out, small), held, sems = refs[:5], refs[5:9], refs[9:14], refs[14]
    copies = [pltpu.make_async_copy(x, y, sems.at[n]) for n, (x, y) in enumerate(zip(given, held))]
    for copy in copies:
        copy.start()
    for copy in copies:
        copy.wait()
    select, latent, affine_b, affine_w, bank = held
    style = (
        jnp.dot(latent[...], affine_w[...], precision=lax.Precision.HIGHEST, preferred_element_type=F32)
        + affine_b[...]
    )
    style_out[...] = style
    filters, in_ch = bank.shape[0], bank.shape[3]
    weights = [select[0, k].astype(F32) for k in range(filters)]
    total = jnp.zeros(bank.shape[2:], F32)
    for tap in range(TAPS):
        kernel = mixed(bank, weights, tap)
        kernel_out[tap] = kernel
        plain = kernel * style
        total = total + plain * plain
    energy_out[...] = jnp.broadcast_to(jnp.sum(total, axis=1, keepdims=True), energy_out.shape)
    small[...] = jnp.zeros(small.shape, F32)
    last = latent.shape[1] // in_ch
    for n in range(last):
        small[n : n + 1] = latent[:, n * in_ch : (n + 1) * in_ch]
    small[last : last + 1] = style
    lane = lax.broadcasted_iota(jnp.int32, (1, in_ch), 1)
    row = jnp.zeros((1, in_ch), F32)
    for k in range(filters):
        row = jnp.where(lane == k, weights[k], row)
    small[last + 1 : last + 2] = row


def modulated_kernel(kernel, style, *refs):
    energies, (mod_out, scale_out) = refs[:-2], refs[-2:]
    energy = energies[0][...]
    for other in energies[1:]:
        energy = energy + other[...]
    scales = lax.rsqrt(energy + EPS)
    scale_out[...] = scales
    scale = scales[:, 0:1]
    for tap in range(TAPS):
        mod_out[tap] = (kernel[tap] * style[...] * scale).astype(BF16)


def blocks_kernel(rows, size, place, *refs):
    parts, whole, outs, (by_row, by_chan) = refs[:rows], refs[rows], refs[rows + 1 : rows + 1 + size], refs[-2:]
    row_at, chan_at, sign = place[2], place[1], place[3]
    for r in range(rows):
        by_row[lax.rem(row_at - r + rows, rows)] = parts[r][...]
    ch = whole.shape[2] // size
    taps = []
    for tap in range(TAPS):
        value = beside([by_row[r, tap].astype(F32) for r in range(rows)])
        whole[tap] = value.astype(BF16)
        taps.append(value)
    for z in range(size):
        by_chan[z] = beside([value[:, z * ch : (z + 1) * ch] for value in taps]).astype(BF16)
    for d in range(size):
        outs[d][...] = by_chan[lax.rem(chan_at + sign * d + size, size)]


def shifted(x, by):
    width = x.shape[1]
    lane = lax.broadcasted_iota(jnp.int32, x.shape, 1)
    moved = pltpu.roll(x, by % width, 1)
    return jnp.where(lane == (0 if by == 1 else width - 1), 0.0, moved)


def spread(wide, row, x):
    ch, width = x.shape
    wide[ch : 2 * ch, row * width : (row + 1) * width] = x
    x = x.astype(F32)
    wide[0:ch, row * width : (row + 1) * width] = shifted(x, 1).astype(BF16)
    wide[2 * ch : 3 * ch, row * width : (row + 1) * width] = shifted(x, -1).astype(BF16)


def rows_kernel(height, width, feat, feat_before, feat_after, out):
    out[:, 0:width] = feat_before[...]
    out[:, width : (height + 1) * width] = feat[...]
    out[:, (height + 1) * width :] = feat_after[...]


def tap_products(g_ref, wides, totals, height, width):
    for total in totals:
        total[...] = jnp.zeros(total.shape, F32)

    def body(row, _):
        g = g_ref[:, pl.ds(pl.multiple_of(row * width, width), width)]
        for wide, total in zip(wides, totals):
            for kh in range(3):
                x = wide[:, pl.ds(pl.multiple_of((row + kh) * width, width), width)]
                total[kh] += lax.dot_general(g, x, (((1,), (1,)), ((), ())), preferred_element_type=F32)
        return 0

    lax.fori_loop(0, height, body, 0)
    return [jnp.concatenate([total[kh] for kh in range(3)], axis=1).astype(BF16) for total in totals]


def near_grad_kernel(height, width, *refs):
    cotans, feat, outs, (wide, gathered, total) = refs[:3], refs[3], refs[4:7], refs[7:]
    ch = feat.shape[0]
    for at, cotan in enumerate(cotans):
        gathered[at * ch : (at + 1) * ch] = cotan[...]
    for row in range(height + 2):
        spread(wide, row, feat[:, row * width : (row + 1) * width])
    (whole,) = tap_products(gathered, [wide], [total], height, width)
    for at, out in enumerate(outs):
        out[...] = whole[at * ch : (at + 1) * ch]


def far_grad_kernel(count, height, width, *refs):
    first, second, (wide, feat) = refs[:count], refs[count : 2 * count], refs[2 * count : 2 * count + 2]
    (out, middle, end_block), (wide_end, total, end_total) = refs[2 * count + 2 : -3], refs[-3:]
    ch = feat.shape[0]
    for at in range(count):
        middle[at * ch : (at + 1) * ch] = first[at][...] + second[count - 1 - at][...]
    end_block[...] = first[-1][...] + second[-1][...]
    for row in range(height + 2):
        spread(wide_end, row, feat[:, row * width : (row + 1) * width])
    if count == 1:
        whole, end = tap_products(end_block, [wide, wide_end], [total, end_total], height, width)
    else:
        (whole,) = tap_products(middle, [wide], [total], height, width)
        (end,) = tap_products(end_block, [wide_end], [end_total], height, width)
    out[0 : count * ch] = whole
    out[count * ch :] = end


def input_grad_kernel(size, height, width, place, cotan, first, second, middle, far, *refs):
    mods, (main, before, after, gathered, taps_t, total) = refs[:size], refs[size:]
    ch = main.shape[0]
    spot = jnp.where(place[3] > 0, place[1], size - 1 - place[1])
    gathered[0:ch] = cotan[...]
    gathered[ch : 2 * ch] = jnp.where(spot == 0, far[...], first[...])
    gathered[2 * ch : (size - 1) * ch] = middle[...]
    gathered[(size - 1) * ch :] = jnp.where(spot == size - 1, far[...], second[...])
    every = jnp.concatenate([mod[...].astype(F32) for mod in mods], axis=0)
    taps_t[...] = every.T.astype(BF16)
    total[...] = jnp.zeros(total.shape, F32)

    def body(row, _):
        g = gathered[:, pl.ds(pl.multiple_of(row * width, width), width)]
        for kh in range(3):
            y = jnp.dot(taps_t[kh * 3 * ch : (kh + 1) * 3 * ch], g, preferred_element_type=F32)
            total[row + kh] += y
        return 0

    lax.fori_loop(0, height, body, 0)
    for row in range(height + 2):
        value = total[row, ch : 2 * ch]
        value = value + shifted(total[row, 0:ch], -1) + shifted(total[row, 2 * ch : 3 * ch], 1)
        if row == 0:
            before[...] = value
        elif row == height + 1:
            after[...] = value
        else:
            main[:, (row - 1) * width : row * width] = value


def split3(x):
    high = x.astype(BF16).astype(F32)
    mid = (x - high).astype(BF16).astype(F32)
    return high, mid, x - high - mid


def put_columns(out, columns):
    lane = lax.broadcasted_iota(jnp.int32, out.shape[1:], 1)
    last = jnp.zeros(out.shape[1:], F32)
    for n, column in enumerate(columns):
        for at, piece in enumerate(split3(column)):
            last = jnp.where(lane == 3 * n + at, piece, last)
    out[TAPS] = last.astype(BF16)


def get_column(last, n=0):
    last = last.astype(F32)
    return last[:, 3 * n : 3 * n + 1] + last[:, 3 * n + 1 : 3 * n + 2] + last[:, 3 * n + 2 : 3 * n + 3]


def collect_kernel(rows, size, place, scale, whole_mod, own, ahead, behind, others, *refs):
    outs, (by_chan, by_row) = refs[:rows], refs[rows:]
    chan_at, row_at, sign = place[1], place[2], place[3]
    ch = own.shape[0]
    by_chan[chan_at] = own[...].astype(F32)
    by_chan[lax.rem(chan_at + sign + size, size)] = ahead[...].astype(F32)
    by_chan[lax.rem(chan_at - sign + size, size)] = behind[...].astype(F32)
    for d in range(2, size - 1):
        value = others[(d - 2) * ch : (d - 1) * ch].astype(F32)
        by_chan[lax.rem(chan_at + sign * d + size, size)] = value
    by_chan[jnp.where(chan_at == 0, size - 1, 0)] += others[(size - 3) * ch :].astype(F32)
    in_ch = outs[0].shape[2]
    product = jnp.zeros(whole_mod.shape[1:], F32)
    for tap in range(TAPS):
        value = beside([by_chan[z, :, tap * ch : (tap + 1) * ch] for z in range(size)])
        product = product + value * whole_mod[tap].astype(F32)
        for r in range(rows):
            by_row[r, tap] = value[:, r * in_ch : (r + 1) * in_ch].astype(BF16)
    fall = jnp.sum(product, axis=1, keepdims=True) * (scale[:, 0:1] * scale[:, 0:1])
    for r in range(rows):
        outs[r][0:TAPS] = by_row[lax.rem(row_at + r, rows)]
        put_columns(outs[r], [fall])


def row_sum_kernel(scale, small, *refs):
    parts, out = refs[:-1], refs[-1]
    fall = get_column(parts[0][TAPS])
    for part in parts[1:]:
        fall = fall + get_column(part[TAPS])
    for tap in range(TAPS):
        value = parts[0][tap].astype(F32)
        for part in parts[1:]:
            value = value + part[tap].astype(F32)
        out[tap] = value.astype(BF16)
    put_columns(out, [fall, scale[:, 0:1]])
    out_ch, in_ch = out.shape[1:]
    pieces = list(split3(small[...]))
    spare = (out.shape[0] - TAPS - 1) * out_ch - 3 * small.shape[0]
    if spare:
        pieces.append(jnp.zeros((spare, in_ch), F32))
    pieces = jnp.concatenate(pieces, axis=0).astype(BF16)
    for n in range(out.shape[0] - TAPS - 1):
        out[TAPS + 1 + n] = pieces[n * out_ch : (n + 1) * out_ch]


def bank_grad_kernel(samples, small_rows, place, bank, *refs):
    parts, (bank_grad, style_grad, latents, held) = refs[:samples], refs[samples:]
    for s in range(samples):
        held[lax.rem(place[0] - s + samples, samples)] = parts[s][...]
    filters, in_ch = bank.shape[0], bank.shape[3]
    last = latents.shape[1] // in_ch
    sel, styles, scales, falls = [], [], [], []
    for b in range(samples):
        rows = jnp.concatenate([held[b, n].astype(F32) for n in range(TAPS + 1, held.shape[1])], axis=0)
        small = rows[:small_rows] + rows[small_rows : 2 * small_rows] + rows[2 * small_rows : 3 * small_rows]
        latents[b : b + 1] = beside([small[n : n + 1] for n in range(last)])
        styles.append(small[last : last + 1])
        sel.append([small[last + 1 : last + 2, k : k + 1] for k in range(filters)])
        falls.append(get_column(held[b, TAPS]))
        scales.append(get_column(held[b, TAPS], 1))
    sums = [jnp.zeros(bank.shape[2:], F32) for _ in range(samples)]
    for tap in range(TAPS):
        totals = [None] * filters
        for b in range(samples):
            kern = mixed(bank, sel[b], tap)
            plain_grad = held[b, tap].astype(F32) * scales[b] - kern * styles[b] * falls[b]
            sums[b] = sums[b] + plain_grad * kern
            kernel_grad = plain_grad * styles[b]
            for k in range(filters):
                term = sel[b][k] * kernel_grad
                totals[k] = term if totals[k] is None else totals[k] + term
        for k in range(filters):
            bank_grad[k, tap] = totals[k]
    for b in range(samples):
        value = jnp.sum(sums[b], axis=0, keepdims=True)
        style_grad[b : b + 1] = value


def affine_kernel(samples, size, place, latents, *refs):
    parts, (w_grad, b_grad, held) = refs[:size], refs[size:]
    for d in range(size):
        held[lax.rem(place[1] - d + size, size)] = parts[d][...]
    style_grad = held[0]
    for z in range(1, size):
        style_grad = style_grad + held[z]
    w_grad[...] = lax.dot_general(
        latents[...],
        style_grad,
        (((0,), (0,)), ((), ())),
        precision=lax.Precision.HIGHEST,
        preferred_element_type=F32,
    )
    bias = style_grad[0:1]
    for b in range(1, samples):
        bias = bias + style_grad[b : b + 1]
    b_grad[...] = bias


def call(kernel, name, outs, *operands, scalars=0, fetched=0, scratch=(), flops=10**6):
    outs = tuple(jax.ShapeDtypeStruct(*o) for o in outs)
    moved = sum(o.size * o.dtype.itemsize for o in (*outs, *operands))
    return pl.pallas_call(
        kernel,
        out_shape=outs,
        in_specs=sspec(scalars)
        + vspec(len(operands) - scalars - fetched)
        + [pl.BlockSpec(memory_space=pltpu.HBM)] * fetched,
        out_specs=tuple(vspec(len(outs))),
        scratch_shapes=[pltpu.VMEM(*s) if isinstance(s, tuple) else s for s in scratch],
        compiler_params=params(),
        cost_estimate=cost(flops, moved),
        name=name,
    )(*operands)


def exchange(x, axis):
    size = lax.axis_size(axis)
    return [x] + [
        lax.ppermute(x, axis, [(i, (i + s) % size) for i in range(size)]) for s in range(1, size)
    ]


def from_sides(first, last, axis):
    size, at = lax.axis_size(axis), lax.axis_index(axis)
    if size == 2:
        got = lax.ppermute(jnp.where(at == 0, last, first), axis, [(0, 1), (1, 0)])
        nothing = jnp.zeros_like(got)
        return jnp.where(at == 1, got, nothing), jnp.where(at == 0, got, nothing)
    up = [(i, i + 1) for i in range(size - 1)]
    down = [(i + 1, i) for i in range(size - 1)]
    return lax.ppermute(last, axis, up), lax.ppermute(first, axis, down)


def on_device(feature, out_grad, bank, select, latent, affine_w, affine_b):
    rows, samples, size = (lax.axis_size(a) for a in ("rows", "samples", "chan"))
    row_at, sample_at, chan_at = (lax.axis_index(a) for a in ("rows", "samples", "chan"))
    _, ch, height, width = feature.shape
    out_ch, in_ch = bank.shape[2:]
    pixels, all_ch = height * width, ch * size
    sign = 1 - 2 * jnp.remainder(sample_at, 2)
    place = jnp.stack([sample_at, chan_at, row_at, sign]).astype(jnp.int32)
    flops = 2 * TAPS * ch * ch * size * pixels

    def along(x, pairs):
        whole = []
        for b in range(samples):
            for i, j in pairs:
                if b % 2:
                    i, j = size - 1 - i, size - 1 - j
                whole.append((b * size + i, b * size + j))
        return lax.ppermute(x, ("samples", "chan"), whole)

    cotan = out_grad[0].reshape(ch, pixels)
    first, second = [], []

    def step(number, x, y):
        first.append(along(x, [(i, i + 1) for i in range(number - 1, size - 1)]))
        second.append(along(y, [(i + 1, i) for i in range(size - number)]))

    step(1, cotan, cotan)

    feat = feature[0].reshape(ch, pixels)
    feat_before, feat_after = from_sides(feat[:, :width], feat[:, pixels - width :], "rows")
    small_rows = -(-(latent.shape[1] // in_ch + 2) // 8) * 8
    style, kernel, energy, small = call(
        energy_kernel,
        "energy",
        [((1, in_ch), F32), ((TAPS, out_ch, in_ch), F32), ((out_ch, 128), F32), ((small_rows, in_ch), F32)],
        select,
        latent,
        affine_b[None],
        affine_w,
        bank,
        fetched=5,
        scratch=[
            pltpu.SMEM(select.shape, jnp.int32),
            (latent.shape, F32),
            ((1, in_ch), F32),
            (affine_w.shape, F32),
            (bank.shape, F32),
            pltpu.SemaphoreType.DMA((5,)),
        ],
    )
    extended = ((ch, (height + 2) * width), BF16)
    (feat,) = call(
        functools.partial(rows_kernel, height, width), "feat_rows", [extended], feat, feat_before, feat_after
    )
    feat_end = lax.ppermute(feat, "chan", [(0, 1), (size - 1, size - 2)])
    mod_own, scale = call(
        modulated_kernel,
        "modulated",
        [((TAPS, out_ch, in_ch), BF16), ((out_ch, 128), F32)],
        kernel,
        style,
        *exchange(energy, "rows"),
    )
    message = ((ch, TAPS * ch), BF16)
    whole_mod, *mods = call(
        functools.partial(blocks_kernel, rows, size),
        "mod_blocks",
        [((TAPS, out_ch, all_ch), BF16)] + [message] * size,
        place,
        *exchange(mod_own, "rows"),
        scalars=1,
        scratch=[((rows, TAPS, out_ch, in_ch), BF16), ((size, *message[0]), BF16)],
    )
    first[0], second[0], energy, mod_own = lax.optimization_barrier((first[0], second[0], energy, mod_own))

    step(2, first[0], second[0])
    own_grad, grad_behind, grad_ahead, wide = call(
        functools.partial(near_grad_kernel, height, width),
        "near_grad",
        [message] * 3 + [((3 * ch, (height + 2) * width), BF16)],
        cotan,
        first[0],
        second[0],
        feat,
        scratch=[((3 * ch, pixels), BF16), ((3, 3 * ch, 3 * ch), F32)],
        flops=flops * 3 // size,
    )
    forth = [(i, i + 1) for i in range(size - 1)]
    back = [(i + 1, i) for i in range(size - 1)]
    from_ahead, from_behind = along(grad_behind, back), along(grad_ahead, forth)
    first[1], second[1], feat_end, wide, mods, whole_mod, from_ahead, from_behind = lax.optimization_barrier(
        (first[1], second[1], feat_end, wide, mods, whole_mod, from_ahead, from_behind)
    )

    count = size - 3
    grad_others, middle, end_block = call(
        functools.partial(far_grad_kernel, count, height, width),
        "far_grad",
        [(((count + 1) * ch, TAPS * ch), BF16), ((count * ch, pixels), BF16), ((ch, pixels), BF16)],
        *first[1:],
        *second[1:],
        wide,
        feat_end,
        scratch=[
            ((3 * ch, (height + 2) * width), BF16),
            ((3, count * ch, 3 * ch), F32),
            ((3, ch, 3 * ch), F32),
        ],
        flops=flops * 2 // size,
    )
    from_others = along(grad_others, [(i, (i + 2) % size) for i in range(size)])
    far = lax.ppermute(end_block, "chan", [(1, 0), (size - 2, size - 1)])
    parts = call(
        functools.partial(collect_kernel, rows, size),
        "collect",
        [((TAPS + 1, out_ch, in_ch), BF16)] * rows,
        place,
        scale,
        whole_mod,
        own_grad,
        from_ahead,
        from_behind,
        from_others,
        scalars=1,
        scratch=[((size, *message[0]), F32), ((rows, TAPS, out_ch, in_ch), BF16)],
    )
    parts, mods = lax.optimization_barrier((parts, mods))
    mods = [mods[0]] + [along(mods[d], [(i, (i + d) % size) for i in range(size)]) for d in range(1, size)]
    parts = [parts[0]] + [
        lax.ppermute(parts[r], "rows", [(i, (i + r) % rows) for i in range(rows)])
        for r in range(1, rows)
    ]
    slots = TAPS + 1 - (-3 * small_rows // out_ch)
    (own,) = call(row_sum_kernel, "row_sum", [((slots, out_ch, in_ch), BF16)], scale, small, *parts)
    every = exchange(own, "samples")

    own, mods, far = lax.optimization_barrier((own, mods, far))
    main, before, after = call(
        functools.partial(input_grad_kernel, size, height, width),
        "input_grad",
        [((ch, pixels), F32), ((ch, width), F32), ((ch, width), F32)],
        place,
        cotan,
        first[0],
        second[0],
        middle,
        far,
        *mods,
        scalars=1,
        scratch=[
            ((all_ch, pixels), BF16),
            ((TAPS * ch, all_ch), BF16),
            ((height + 2, 3 * ch, width), F32),
        ],
        flops=flops,
    )
    every, main, before, after = lax.optimization_barrier((every, main, before, after))
    from_above, from_below = from_sides(before, after, "rows")
    bank_grad, style_part, latents = call(
        functools.partial(bank_grad_kernel, samples, small_rows),
        "bank_grad",
        [(bank.shape, F32), ((samples, in_ch), F32), ((samples, latent.shape[1]), F32)],
        place,
        bank,
        *every,
        scalars=1,
        scratch=[((samples, slots, out_ch, in_ch), BF16)],
    )
    style_parts = exchange(style_part, "chan")
    edge = jnp.concatenate(
        [from_above[:, None], jnp.zeros((ch, height - 2, width), F32), from_below[:, None]], axis=1
    )
    feature_grad = (main.reshape(ch, height, width) + edge).astype(BF16)[None]
    affine_w_grad, affine_b_grad = call(
        functools.partial(affine_kernel, samples, size),
        "affine",
        [(affine_w.shape, F32), ((1, in_ch), F32)],
        place,
        latents,
        *style_parts,
        scalars=1,
        scratch=[((size, samples, in_ch), F32)],
    )
    return (feature_grad, bank_grad, affine_w_grad, affine_b_grad[0])


def solution(mesh):
    return jax.shard_map(
        on_device,
        mesh=mesh,
        in_specs=(
            P("samples", "chan", "rows", None),
            P("samples", "chan", "rows", None),
            P(None, None, "chan", "rows"),
            P("samples", None),
            P("samples", None),
            P(None, "rows"),
            P("rows"),
        ),
        out_specs=(
            P("samples", "chan", "rows", None),
            P(None, None, "chan", "rows"),
            P(None, "rows"),
            P("rows"),
        ),
        check_vma=False,
    )
```

```python
import functools

import jax
import jax.numpy as jnp
from jax import lax
from jax.experimental import pallas as pl
from jax.experimental.pallas import tpu as pltpu
from jax.sharding import PartitionSpec as P

EPS = 1e-08
TAPS = 9
F32 = jnp.float32
BF16 = jnp.bfloat16
VMEM_LIMIT = 16 * 2**20
COLLECT_FLOPS = 3 * 10**9


def params():
    return pltpu.CompilerParams(vmem_limit_bytes=VMEM_LIMIT)


def vspec(n):
    return [pl.BlockSpec(memory_space=pltpu.VMEM)] * n


def sspec(n):
    return [pl.BlockSpec(memory_space=pltpu.SMEM)] * n


def cost(flops, moved):
    return pl.CostEstimate(flops=flops, bytes_accessed=moved, transcendentals=0)


def beside(pieces):
    return pieces[0] if len(pieces) == 1 else jnp.concatenate(pieces, axis=1)


def mixed(bank_ref, weights, tap):
    total = weights[0] * bank_ref[0, tap]
    for k in range(1, bank_ref.shape[0]):
        total = total + weights[k] * bank_ref[k, tap]
    return total


def energy_kernel(*refs):
    given, (style_out, kernel_out, energy_out, small), held, sems = refs[:5], refs[5:9], refs[9:14], refs[14]
    copies = [pltpu.make_async_copy(x, y, sems.at[n]) for n, (x, y) in enumerate(zip(given, held))]
    for copy in copies:
        copy.start()
    for copy in copies:
        copy.wait()
    select, latent, affine_b, affine_w, bank = held
    style = (
        jnp.dot(latent[...], affine_w[...], precision=lax.Precision.HIGHEST, preferred_element_type=F32)
        + affine_b[...]
    )
    style_out[...] = style
    filters, in_ch = bank.shape[0], bank.shape[3]
    weights = [select[0, k].astype(F32) for k in range(filters)]
    total = jnp.zeros(bank.shape[2:], F32)
    for tap in range(TAPS):
        kernel = mixed(bank, weights, tap)
        kernel_out[tap] = kernel
        plain = kernel * style
        total = total + plain * plain
    energy_out[...] = jnp.broadcast_to(jnp.sum(total, axis=1, keepdims=True), energy_out.shape)
    small[...] = jnp.zeros(small.shape, F32)
    last = latent.shape[1] // in_ch
    for n in range(last):
        small[n : n + 1] = latent[:, n * in_ch : (n + 1) * in_ch]
    small[last : last + 1] = style
    lane = lax.broadcasted_iota(jnp.int32, (1, in_ch), 1)
    row = jnp.zeros((1, in_ch), F32)
    for k in range(filters):
        row = jnp.where(lane == k, weights[k], row)
    small[last + 1 : last + 2] = row


def modulated_kernel(kernel, style, *refs):
    energies, (mod_out, scale_out) = refs[:-2], refs[-2:]
    energy = energies[0][...]
    for other in energies[1:]:
        energy = energy + other[...]
    scales = lax.rsqrt(energy + EPS)
    scale_out[...] = scales
    scale = scales[:, 0:1]
    for tap in range(TAPS):
        mod_out[tap] = (kernel[tap] * style[...] * scale).astype(BF16)


def blocks_kernel(rows, size, place, *refs):
    parts, whole, outs, (by_row, by_chan) = refs[:rows], refs[rows], refs[rows + 1 : rows + 1 + size], refs[-2:]
    row_at, chan_at, sign = place[2], place[1], place[3]
    for r in range(rows):
        by_row[lax.rem(row_at - r + rows, rows)] = parts[r][...]
    ch = whole.shape[2] // size
    taps = []
    for tap in range(TAPS):
        value = beside([by_row[r, tap].astype(F32) for r in range(rows)])
        whole[tap] = value.astype(BF16)
        taps.append(value)
    for z in range(size):
        by_chan[z] = beside([value[:, z * ch : (z + 1) * ch] for value in taps]).astype(BF16)
    for d in range(size):
        outs[d][...] = by_chan[lax.rem(chan_at + sign * d + size, size)]


def shifted(x, by):
    width = x.shape[1]
    lane = lax.broadcasted_iota(jnp.int32, x.shape, 1)
    moved = pltpu.roll(x, by % width, 1)
    return jnp.where(lane == (0 if by == 1 else width - 1), 0.0, moved)


def spread(wide, row, x):
    ch, width = x.shape
    wide[ch : 2 * ch, row * width : (row + 1) * width] = x
    x = x.astype(F32)
    wide[0:ch, row * width : (row + 1) * width] = shifted(x, 1).astype(BF16)
    wide[2 * ch : 3 * ch, row * width : (row + 1) * width] = shifted(x, -1).astype(BF16)


def rows_kernel(height, width, feat, feat_before, feat_after, out):
    out[:, 0:width] = feat_before[...]
    out[:, width : (height + 1) * width] = feat[...]
    out[:, (height + 1) * width :] = feat_after[...]


def tap_products(g_ref, wides, totals, height, width):
    for total in totals:
        total[...] = jnp.zeros(total.shape, F32)

    def body(row, _):
        g = g_ref[:, pl.ds(pl.multiple_of(row * width, width), width)]
        for wide, total in zip(wides, totals):
            for kh in range(3):
                x = wide[:, pl.ds(pl.multiple_of((row + kh) * width, width), width)]
                total[kh] += lax.dot_general(g, x, (((1,), (1,)), ((), ())), preferred_element_type=F32)
        return 0

    lax.fori_loop(0, height, body, 0)
    return [jnp.concatenate([total[kh] for kh in range(3)], axis=1).astype(BF16) for total in totals]


def near_grad_kernel(height, width, *refs):
    cotans, feat, outs, (wide, gathered, total) = refs[:3], refs[3], refs[4:7], refs[7:]
    ch = feat.shape[0]
    for at, cotan in enumerate(cotans):
        gathered[at * ch : (at + 1) * ch] = cotan[...]
    for row in range(height + 2):
        spread(wide, row, feat[:, row * width : (row + 1) * width])
    (whole,) = tap_products(gathered, [wide], [total], height, width)
    for at, out in enumerate(outs):
        out[...] = whole[at * ch : (at + 1) * ch]


def middle_grad_kernel(count, height, width, *refs):
    first, second, wide = refs[:count], refs[count : 2 * count], refs[2 * count]
    out, middle, end_block, total = refs[2 * count + 1 :]
    ch = end_block.shape[0]
    for at in range(count):
        middle[at * ch : (at + 1) * ch] = first[at][...] + second[count - 1 - at][...]
    end_block[...] = first[-1][...] + second[-1][...]
    (out[...],) = tap_products(middle, [wide], [total], height, width)


def end_grad_kernel(height, width, end_block, feat, out, wide, total):
    for row in range(height + 2):
        spread(wide, row, feat[:, row * width : (row + 1) * width])
    (out[...],) = tap_products(end_block, [wide], [total], height, width)


def input_grad_kernel(size, height, width, place, cotan, first, second, middle, far, *refs):
    mods, (main, before, after, gathered, taps_t, total) = refs[:size], refs[size:]
    ch = main.shape[0]
    spot = jnp.where(place[3] > 0, place[1], size - 1 - place[1])
    gathered[0:ch] = cotan[...]
    gathered[ch : 2 * ch] = jnp.where(spot == 0, far[...], first[...])
    gathered[2 * ch : (size - 1) * ch] = middle[...]
    gathered[(size - 1) * ch :] = jnp.where(spot == size - 1, far[...], second[...])
    every = jnp.concatenate([mod[...].astype(F32) for mod in mods], axis=0)
    taps_t[...] = every.T.astype(BF16)
    total[...] = jnp.zeros(total.shape, F32)

    def body(row, _):
        g = gathered[:, pl.ds(pl.multiple_of(row * width, width), width)]
        for kh in range(3):
            y = jnp.dot(taps_t[kh * 3 * ch : (kh + 1) * 3 * ch], g, preferred_element_type=F32)
            total[row + kh] += y
        return 0

    lax.fori_loop(0, height, body, 0)
    for row in range(height + 2):
        value = total[row, ch : 2 * ch]
        value = value + shifted(total[row, 0:ch], -1) + shifted(total[row, 2 * ch : 3 * ch], 1)
        if row == 0:
            before[...] = value
        elif row == height + 1:
            after[...] = value
        else:
            main[:, (row - 1) * width : row * width] = value


def split3(x):
    high = x.astype(BF16).astype(F32)
    mid = (x - high).astype(BF16).astype(F32)
    return high, mid, x - high - mid


def put_columns(out, columns):
    lane = lax.broadcasted_iota(jnp.int32, out.shape[1:], 1)
    last = jnp.zeros(out.shape[1:], F32)
    for n, column in enumerate(columns):
        for at, piece in enumerate(split3(column)):
            last = jnp.where(lane == 3 * n + at, piece, last)
    out[TAPS] = last.astype(BF16)


def get_column(last, n=0):
    last = last.astype(F32)
    return last[:, 3 * n : 3 * n + 1] + last[:, 3 * n + 1 : 3 * n + 2] + last[:, 3 * n + 2 : 3 * n + 3]


def collect_kernel(rows, size, place, scale, whole_mod, own, ahead, behind, others, end, *refs):
    outs, (by_chan, by_row) = refs[:rows], refs[rows:]
    chan_at, row_at, sign = place[1], place[2], place[3]
    ch = own.shape[0]
    by_chan[chan_at] = own[...].astype(F32)
    by_chan[lax.rem(chan_at + sign + size, size)] = ahead[...].astype(F32)
    by_chan[lax.rem(chan_at - sign + size, size)] = behind[...].astype(F32)
    for d in range(2, size - 1):
        value = others[(d - 2) * ch : (d - 1) * ch].astype(F32)
        by_chan[lax.rem(chan_at + sign * d + size, size)] = value
    by_chan[jnp.where(chan_at == 0, size - 1, 0)] += end[...].astype(F32)
    in_ch = outs[0].shape[2]
    product = jnp.zeros(whole_mod.shape[1:], F32)
    for tap in range(TAPS):
        value = beside([by_chan[z, :, tap * ch : (tap + 1) * ch] for z in range(size)])
        product = product + value * whole_mod[tap].astype(F32)
        for r in range(rows):
            by_row[r, tap] = value[:, r * in_ch : (r + 1) * in_ch].astype(BF16)
    fall = jnp.sum(product, axis=1, keepdims=True) * (scale[:, 0:1] * scale[:, 0:1])
    for r in range(rows):
        outs[r][0:TAPS] = by_row[lax.rem(row_at + r, rows)]
        put_columns(outs[r], [fall])


def row_sum_kernel(scale, small, *refs):
    parts, out = refs[:-1], refs[-1]
    fall = get_column(parts[0][TAPS])
    for part in parts[1:]:
        fall = fall + get_column(part[TAPS])
    for tap in range(TAPS):
        value = parts[0][tap].astype(F32)
        for part in parts[1:]:
            value = value + part[tap].astype(F32)
        out[tap] = value.astype(BF16)
    put_columns(out, [fall, scale[:, 0:1]])
    out_ch, in_ch = out.shape[1:]
    pieces = list(split3(small[...]))
    spare = (out.shape[0] - TAPS - 1) * out_ch - 3 * small.shape[0]
    if spare:
        pieces.append(jnp.zeros((spare, in_ch), F32))
    pieces = jnp.concatenate(pieces, axis=0).astype(BF16)
    for n in range(out.shape[0] - TAPS - 1):
        out[TAPS + 1 + n] = pieces[n * out_ch : (n + 1) * out_ch]


def bank_grad_kernel(samples, small_rows, place, bank, *refs):
    parts, (bank_grad, style_grad, latents, held) = refs[:samples], refs[samples:]
    for s in range(samples):
        held[lax.rem(place[0] - s + samples, samples)] = parts[s][...]
    filters, in_ch = bank.shape[0], bank.shape[3]
    last = latents.shape[1] // in_ch
    sel, styles, scales, falls = [], [], [], []
    for b in range(samples):
        rows = jnp.concatenate([held[b, n].astype(F32) for n in range(TAPS + 1, held.shape[1])], axis=0)
        small = rows[:small_rows] + rows[small_rows : 2 * small_rows] + rows[2 * small_rows : 3 * small_rows]
        latents[b : b + 1] = beside([small[n : n + 1] for n in range(last)])
        styles.append(small[last : last + 1])
        sel.append([small[last + 1 : last + 2, k : k + 1] for k in range(filters)])
        falls.append(get_column(held[b, TAPS]))
        scales.append(get_column(held[b, TAPS], 1))
    sums = [jnp.zeros(bank.shape[2:], F32) for _ in range(samples)]
    for tap in range(TAPS):
        totals = [None] * filters
        for b in range(samples):
            kern = mixed(bank, sel[b], tap)
            plain_grad = held[b, tap].astype(F32) * scales[b] - kern * styles[b] * falls[b]
            sums[b] = sums[b] + plain_grad * kern
            kernel_grad = plain_grad * styles[b]
            for k in range(filters):
                term = sel[b][k] * kernel_grad
                totals[k] = term if totals[k] is None else totals[k] + term
        for k in range(filters):
            bank_grad[k, tap] = totals[k]
    for b in range(samples):
        value = jnp.sum(sums[b], axis=0, keepdims=True)
        style_grad[b : b + 1] = value


def affine_kernel(samples, size, place, latents, *refs):
    parts, (w_grad, b_grad, held) = refs[:size], refs[size:]
    for d in range(size):
        held[lax.rem(place[1] - d + size, size)] = parts[d][...]
    style_grad = held[0]
    for z in range(1, size):
        style_grad = style_grad + held[z]
    w_grad[...] = lax.dot_general(
        latents[...],
        style_grad,
        (((0,), (0,)), ((), ())),
        precision=lax.Precision.HIGHEST,
        preferred_element_type=F32,
    )
    bias = style_grad[0:1]
    for b in range(1, samples):
        bias = bias + style_grad[b : b + 1]
    b_grad[...] = bias


def call(kernel, name, outs, *operands, scalars=0, fetched=0, scratch=(), flops=10**6):
    outs = tuple(jax.ShapeDtypeStruct(*o) for o in outs)
    moved = sum(o.size * o.dtype.itemsize for o in (*outs, *operands))
    return pl.pallas_call(
        kernel,
        out_shape=outs,
        in_specs=sspec(scalars)
        + vspec(len(operands) - scalars - fetched)
        + [pl.BlockSpec(memory_space=pltpu.HBM)] * fetched,
        out_specs=tuple(vspec(len(outs))),
        scratch_shapes=[pltpu.VMEM(*s) if isinstance(s, tuple) else s for s in scratch],
        compiler_params=params(),
        cost_estimate=cost(flops, moved),
        name=name,
    )(*operands)


def exchange(x, axis):
    size = lax.axis_size(axis)
    return [x] + [
        lax.ppermute(x, axis, [(i, (i + s) % size) for i in range(size)]) for s in range(1, size)
    ]


def from_sides(first, last, axis):
    size, at = lax.axis_size(axis), lax.axis_index(axis)
    if size == 2:
        got = lax.ppermute(jnp.where(at == 0, last, first), axis, [(0, 1), (1, 0)])
        nothing = jnp.zeros_like(got)
        return jnp.where(at == 1, got, nothing), jnp.where(at == 0, got, nothing)
    up = [(i, i + 1) for i in range(size - 1)]
    down = [(i + 1, i) for i in range(size - 1)]
    return lax.ppermute(last, axis, up), lax.ppermute(first, axis, down)


def on_device(feature, out_grad, bank, select, latent, affine_w, affine_b):
    rows, samples, size = (lax.axis_size(a) for a in ("rows", "samples", "chan"))
    row_at, sample_at, chan_at = (lax.axis_index(a) for a in ("rows", "samples", "chan"))
    _, ch, height, width = feature.shape
    out_ch, in_ch = bank.shape[2:]
    pixels, all_ch = height * width, ch * size
    sign = 1 - 2 * jnp.remainder(sample_at, 2)
    place = jnp.stack([sample_at, chan_at, row_at, sign]).astype(jnp.int32)
    flops = 2 * TAPS * ch * ch * size * pixels

    def along(x, pairs):
        whole = []
        for b in range(samples):
            for i, j in pairs:
                if b % 2:
                    i, j = size - 1 - i, size - 1 - j
                whole.append((b * size + i, b * size + j))
        return lax.ppermute(x, ("samples", "chan"), whole)

    cotan = out_grad[0].reshape(ch, pixels)
    first, second = [], []

    def step(number, x, y):
        first.append(along(x, [(i, i + 1) for i in range(number - 1, size - 1)]))
        second.append(along(y, [(i + 1, i) for i in range(size - number)]))

    step(1, cotan, cotan)

    feat = feature[0].reshape(ch, pixels)
    feat_before, feat_after = from_sides(feat[:, :width], feat[:, pixels - width :], "rows")
    small_rows = -(-(latent.shape[1] // in_ch + 2) // 8) * 8
    style, kernel, energy, small = call(
        energy_kernel,
        "energy",
        [((1, in_ch), F32), ((TAPS, out_ch, in_ch), F32), ((out_ch, 128), F32), ((small_rows, in_ch), F32)],
        select,
        latent,
        affine_b[None],
        affine_w,
        bank,
        fetched=5,
        scratch=[
            pltpu.SMEM(select.shape, jnp.int32),
            (latent.shape, F32),
            ((1, in_ch), F32),
            (affine_w.shape, F32),
            (bank.shape, F32),
            pltpu.SemaphoreType.DMA((5,)),
        ],
    )
    extended = ((ch, (height + 2) * width), BF16)
    (feat,) = call(
        functools.partial(rows_kernel, height, width), "feat_rows", [extended], feat, feat_before, feat_after
    )
    mod_own, scale = call(
        modulated_kernel,
        "modulated",
        [((TAPS, out_ch, in_ch), BF16), ((out_ch, 128), F32)],
        kernel,
        style,
        *exchange(energy, "rows"),
    )
    feat, mod_own = lax.optimization_barrier((feat, mod_own))
    feat_end = lax.ppermute(feat, "chan", [(0, 1), (size - 1, size - 2)])
    message = ((ch, TAPS * ch), BF16)
    whole_mod, *mods = call(
        functools.partial(blocks_kernel, rows, size),
        "mod_blocks",
        [((TAPS, out_ch, all_ch), BF16)] + [message] * size,
        place,
        *exchange(mod_own, "rows"),
        scalars=1,
        scratch=[((rows, TAPS, out_ch, in_ch), BF16), ((size, *message[0]), BF16)],
    )
    first[0], second[0], energy, mod_own = lax.optimization_barrier((first[0], second[0], energy, mod_own))

    step(2, first[0], second[0])
    own_grad, grad_behind, grad_ahead, wide = call(
        functools.partial(near_grad_kernel, height, width),
        "near_grad",
        [message] * 3 + [((3 * ch, (height + 2) * width), BF16)],
        cotan,
        first[0],
        second[0],
        feat,
        scratch=[((3 * ch, pixels), BF16), ((3, 3 * ch, 3 * ch), F32)],
        flops=flops * 3 // size,
    )
    forth = [(i, i + 1) for i in range(size - 1)]
    back = [(i + 1, i) for i in range(size - 1)]
    from_ahead, from_behind = along(grad_behind, back), along(grad_ahead, forth)
    first[1], second[1], feat_end, wide, mods, whole_mod, from_ahead, from_behind = lax.optimization_barrier(
        (first[1], second[1], feat_end, wide, mods, whole_mod, from_ahead, from_behind)
    )

    count = size - 3
    grad_others, middle, end_block = call(
        functools.partial(middle_grad_kernel, count, height, width),
        "middle_grad",
        [((count * ch, TAPS * ch), BF16), ((count * ch, pixels), BF16), ((ch, pixels), BF16)],
        *first[1:],
        *second[1:],
        wide,
        scratch=[((3, count * ch, 3 * ch), F32)],
        flops=flops // size,
    )
    (grad_end,) = call(
        functools.partial(end_grad_kernel, height, width),
        "end_grad",
        [message],
        end_block,
        feat_end,
        scratch=[((3 * ch, (height + 2) * width), BF16), ((3, ch, 3 * ch), F32)],
        flops=flops // size,
    )
    from_others = along(grad_others, [(i, (i + 2) % size) for i in range(size)])
    from_end = lax.ppermute(grad_end, "chan", [(1, size - 1), (size - 2, 0)])
    far = lax.ppermute(end_block, "chan", [(1, 0), (size - 2, size - 1)])
    parts = call(
        functools.partial(collect_kernel, rows, size),
        "collect",
        [((TAPS + 1, out_ch, in_ch), BF16)] * rows,
        place,
        scale,
        whole_mod,
        own_grad,
        from_ahead,
        from_behind,
        from_others,
        from_end,
        scalars=1,
        scratch=[((size, *message[0]), F32), ((rows, TAPS, out_ch, in_ch), BF16)],
        flops=COLLECT_FLOPS,
    )
    parts, mods = lax.optimization_barrier((parts, mods))
    mods = [mods[0]] + [along(mods[d], [(i, (i + d) % size) for i in range(size)]) for d in range(1, size)]
    parts = [parts[0]] + [
        lax.ppermute(parts[r], "rows", [(i, (i + r) % rows) for i in range(rows)])
        for r in range(1, rows)
    ]
    slots = TAPS + 1 - (-3 * small_rows // out_ch)
    (own,) = call(row_sum_kernel, "row_sum", [((slots, out_ch, in_ch), BF16)], scale, small, *parts)
    every = exchange(own, "samples")

    own, mods, far = lax.optimization_barrier((own, mods, far))
    main, before, after = call(
        functools.partial(input_grad_kernel, size, height, width),
        "input_grad",
        [((ch, pixels), F32), ((ch, width), F32), ((ch, width), F32)],
        place,
        cotan,
        first[0],
        second[0],
        middle,
        far,
        *mods,
        scalars=1,
        scratch=[
            ((all_ch, pixels), BF16),
            ((TAPS * ch, all_ch), BF16),
            ((height + 2, 3 * ch, width), F32),
        ],
        flops=flops,
    )
    every, main, before, after = lax.optimization_barrier((every, main, before, after))
    from_above, from_below = from_sides(before, after, "rows")
    bank_grad, style_part, latents = call(
        functools.partial(bank_grad_kernel, samples, small_rows),
        "bank_grad",
        [(bank.shape, F32), ((samples, in_ch), F32), ((samples, latent.shape[1]), F32)],
        place,
        bank,
        *every,
        scalars=1,
        scratch=[((samples, slots, out_ch, in_ch), BF16)],
    )
    style_parts = exchange(style_part, "chan")
    edge = jnp.concatenate(
        [from_above[:, None], jnp.zeros((ch, height - 2, width), F32), from_below[:, None]], axis=1
    )
    feature_grad = (main.reshape(ch, height, width) + edge).astype(BF16)[None]
    style_parts, feature_grad = lax.optimization_barrier((style_parts, feature_grad))
    affine_w_grad, affine_b_grad = call(
        functools.partial(affine_kernel, samples, size),
        "affine",
        [(affine_w.shape, F32), ((1, in_ch), F32)],
        place,
        latents,
        *style_parts,
        scalars=1,
        scratch=[((size, samples, in_ch), F32)],
    )
    return (feature_grad, bank_grad, affine_w_grad, affine_b_grad[0])


def solution(mesh):
    return jax.shard_map(
        on_device,
        mesh=mesh,
        in_specs=(
            P("samples", "chan", "rows", None),
            P("samples", "chan", "rows", None),
            P(None, None, "chan", "rows"),
            P("samples", None),
            P("samples", None),
            P(None, "rows"),
            P("rows"),
        ),
        out_specs=(
            P("samples", "chan", "rows", None),
            P(None, None, "chan", "rows"),
            P(None, "rows"),
            P("rows"),
        ),
        check_vma=False,
    )
```

```python
import functools

import jax
import jax.numpy as jnp
from jax import lax
from jax.experimental import pallas as pl
from jax.experimental.pallas import tpu as pltpu
from jax.sharding import PartitionSpec as P

EPS = 1e-08
TAPS = 9
F32 = jnp.float32
BF16 = jnp.bfloat16
VMEM_LIMIT = 16 * 2**20
COLLECT_FLOPS = 3 * 10**9
INPUT_FLOPS = 2 * 10**9


def params():
    return pltpu.CompilerParams(vmem_limit_bytes=VMEM_LIMIT)


def vspec(n):
    return [pl.BlockSpec(memory_space=pltpu.VMEM)] * n


def sspec(n):
    return [pl.BlockSpec(memory_space=pltpu.SMEM)] * n


def cost(flops, moved):
    return pl.CostEstimate(flops=flops, bytes_accessed=moved, transcendentals=0)


def beside(pieces):
    return pieces[0] if len(pieces) == 1 else jnp.concatenate(pieces, axis=1)


def mixed(bank_ref, weights, tap):
    total = weights[0] * bank_ref[0, tap]
    for k in range(1, bank_ref.shape[0]):
        total = total + weights[k] * bank_ref[k, tap]
    return total


def energy_kernel(*refs):
    given, (style_out, kernel_out, energy_out, small), held, sems = refs[:5], refs[5:9], refs[9:14], refs[14]
    copies = [pltpu.make_async_copy(x, y, sems.at[n]) for n, (x, y) in enumerate(zip(given, held))]
    for copy in copies:
        copy.start()
    for copy in copies:
        copy.wait()
    select, latent, affine_b, affine_w, bank = held
    style = (
        jnp.dot(latent[...], affine_w[...], precision=lax.Precision.HIGHEST, preferred_element_type=F32)
        + affine_b[...]
    )
    style_out[...] = style
    filters, in_ch = bank.shape[0], bank.shape[3]
    weights = [select[0, k].astype(F32) for k in range(filters)]
    total = jnp.zeros(bank.shape[2:], F32)
    for tap in range(TAPS):
        kernel = mixed(bank, weights, tap)
        kernel_out[tap] = kernel
        plain = kernel * style
        total = total + plain * plain
    energy_out[...] = jnp.broadcast_to(jnp.sum(total, axis=1, keepdims=True), energy_out.shape)
    small[...] = jnp.zeros(small.shape, F32)
    last = latent.shape[1] // in_ch
    for n in range(last):
        small[n : n + 1] = latent[:, n * in_ch : (n + 1) * in_ch]
    small[last : last + 1] = style
    lane = lax.broadcasted_iota(jnp.int32, (1, in_ch), 1)
    row = jnp.zeros((1, in_ch), F32)
    for k in range(filters):
        row = jnp.where(lane == k, weights[k], row)
    small[last + 1 : last + 2] = row


def modulated_kernel(kernel, style, *refs):
    energies, (mod_out, scale_out) = refs[:-2], refs[-2:]
    energy = energies[0][...]
    for other in energies[1:]:
        energy = energy + other[...]
    scales = lax.rsqrt(energy + EPS)
    scale_out[...] = scales
    scale = scales[:, 0:1]
    for tap in range(TAPS):
        mod_out[tap] = (kernel[tap] * style[...] * scale).astype(BF16)


def blocks_kernel(rows, size, place, *refs):
    parts, whole, outs, (by_row, by_chan) = refs[:rows], refs[rows], refs[rows + 1 : rows + 1 + size], refs[-2:]
    row_at, chan_at, sign = place[2], place[1], place[3]
    for r in range(rows):
        by_row[lax.rem(row_at - r + rows, rows)] = parts[r][...]
    ch = whole.shape[2] // size
    taps = []
    for tap in range(TAPS):
        value = beside([by_row[r, tap].astype(F32) for r in range(rows)])
        whole[tap] = value.astype(BF16)
        taps.append(value)
    for z in range(size):
        by_chan[z] = beside([value[:, z * ch : (z + 1) * ch] for value in taps]).astype(BF16)
    for d in range(size):
        outs[d][...] = by_chan[lax.rem(chan_at + sign * d + size, size)]


def shifted(x, by):
    width = x.shape[1]
    lane = lax.broadcasted_iota(jnp.int32, x.shape, 1)
    moved = pltpu.roll(x, by % width, 1)
    return jnp.where(lane == (0 if by == 1 else width - 1), 0.0, moved)


def spread(wide, row, x):
    ch, width = x.shape
    wide[ch : 2 * ch, row * width : (row + 1) * width] = x
    x = x.astype(F32)
    wide[0:ch, row * width : (row + 1) * width] = shifted(x, 1).astype(BF16)
    wide[2 * ch : 3 * ch, row * width : (row + 1) * width] = shifted(x, -1).astype(BF16)


def rows_kernel(height, width, feat, feat_before, feat_after, out):
    out[:, 0:width] = feat_before[...]
    out[:, width : (height + 1) * width] = feat[...]
    out[:, (height + 1) * width :] = feat_after[...]


def tap_products(g_ref, wides, totals, height, width):
    for total in totals:
        total[...] = jnp.zeros(total.shape, F32)

    def body(row, _):
        g = g_ref[:, pl.ds(pl.multiple_of(row * width, width), width)]
        for wide, total in zip(wides, totals):
            for kh in range(3):
                x = wide[:, pl.ds(pl.multiple_of((row + kh) * width, width), width)]
                total[kh] += lax.dot_general(g, x, (((1,), (1,)), ((), ())), preferred_element_type=F32)
        return 0

    lax.fori_loop(0, height, body, 0)
    return [jnp.concatenate([total[kh] for kh in range(3)], axis=1).astype(BF16) for total in totals]


def near_grad_kernel(height, width, *refs):
    cotans, feat, mods, (own, behind, ahead), (wide, gathered, total) = refs[:3], refs[3], refs[4:6], refs[6:9], refs[9:]
    ch = feat.shape[0]
    for at, cotan in enumerate(cotans):
        gathered[at * ch : (at + 1) * ch] = cotan[...]
    for row in range(height + 2):
        spread(wide, row, feat[:, row * width : (row + 1) * width])
    (whole,) = tap_products(gathered, [wide], [total], height, width)
    own[...] = whole[0:ch]
    for at, (out, mod) in enumerate(zip((behind, ahead), mods)):
        out[0:ch] = whole[(at + 1) * ch : (at + 2) * ch]
        out[ch : 2 * ch] = mod[...]
        out[2 * ch :] = mods[1 - at][...]


def middle_grad_kernel(count, height, width, *refs):
    first, second, wide = refs[:count], refs[count : 2 * count], refs[2 * count]
    out, middle, end_block, total = refs[2 * count + 1 :]
    ch = end_block.shape[0]
    for at in range(count):
        middle[at * ch : (at + 1) * ch] = first[at][...] + second[count - 1 - at][...]
    end_block[...] = first[-1][...] + second[-1][...]
    (out[...],) = tap_products(middle, [wide], [total], height, width)


def end_grad_kernel(height, width, place, end_block, feat, ahead, behind, out, wide, total):
    ch = feat.shape[0]
    second = place[1] == jnp.where(place[3] > 0, 1, place[4] - 2)
    out[ch:] = jnp.where(second, behind[2 * ch :], ahead[2 * ch :])
    for row in range(height + 2):
        spread(wide, row, feat[:, row * width : (row + 1) * width])
    (out[0:ch],) = tap_products(end_block, [wide], [total], height, width)


def input_grad_kernel(size, height, width, place, cotan, first, second, middle, far, own_mod, behind, ahead, end, *refs):
    others, (main, before, after, gathered, taps_t, total) = refs[: size - 3], refs[size - 3 :]
    ch = main.shape[0]
    spot = jnp.where(place[3] > 0, place[1], size - 1 - place[1])
    gathered[0:ch] = cotan[...]
    gathered[ch : 2 * ch] = jnp.where(spot == 0, far[...], first[...])
    gathered[2 * ch : (size - 1) * ch] = middle[...]
    gathered[(size - 1) * ch :] = jnp.where(spot == size - 1, far[...], second[...])
    mods = [own_mod[...], jnp.where(spot == 0, end[ch:], behind[ch : 2 * ch])]
    mods += [other[...] for other in others]
    mods.append(jnp.where(spot == size - 1, end[ch:], ahead[ch : 2 * ch]))
    every = jnp.concatenate([mod.astype(F32) for mod in mods], axis=0)
    taps_t[...] = every.T.astype(BF16)
    total[...] = jnp.zeros(total.shape, F32)

    def body(row, _):
        g = gathered[:, pl.ds(pl.multiple_of(row * width, width), width)]
        for kh in range(3):
            y = jnp.dot(taps_t[kh * 3 * ch : (kh + 1) * 3 * ch], g, preferred_element_type=F32)
            total[row + kh] += y
        return 0

    lax.fori_loop(0, height, body, 0)
    for row in range(height + 2):
        value = total[row, ch : 2 * ch]
        value = value + shifted(total[row, 0:ch], -1) + shifted(total[row, 2 * ch : 3 * ch], 1)
        if row == 0:
            before[...] = value
        elif row == height + 1:
            after[...] = value
        else:
            main[:, (row - 1) * width : row * width] = value


def split3(x):
    high = x.astype(BF16).astype(F32)
    mid = (x - high).astype(BF16).astype(F32)
    return high, mid, x - high - mid


def put_columns(out, columns):
    lane = lax.broadcasted_iota(jnp.int32, out.shape[1:], 1)
    last = jnp.zeros(out.shape[1:], F32)
    for n, column in enumerate(columns):
        for at, piece in enumerate(split3(column)):
            last = jnp.where(lane == 3 * n + at, piece, last)
    out[TAPS] = last.astype(BF16)


def get_column(last, n=0):
    last = last.astype(F32)
    return last[:, 3 * n : 3 * n + 1] + last[:, 3 * n + 1 : 3 * n + 2] + last[:, 3 * n + 2 : 3 * n + 3]


def collect_kernel(rows, size, place, scale, whole_mod, own, ahead, behind, others, end, *refs):
    outs, (by_chan, by_row) = refs[:rows], refs[rows:]
    chan_at, row_at, sign = place[1], place[2], place[3]
    ch = own.shape[0]
    by_chan[chan_at] = own[...].astype(F32)
    by_chan[lax.rem(chan_at + sign + size, size)] = ahead[0:ch].astype(F32)
    by_chan[lax.rem(chan_at - sign + size, size)] = behind[0:ch].astype(F32)
    for d in range(2, size - 1):
        value = others[(d - 2) * ch : (d - 1) * ch].astype(F32)
        by_chan[lax.rem(chan_at + sign * d + size, size)] = value
    by_chan[jnp.where(chan_at == 0, size - 1, 0)] += end[0:ch].astype(F32)
    in_ch = outs[0].shape[2]
    product = jnp.zeros(whole_mod.shape[1:], F32)
    for tap in range(TAPS):
        value = beside([by_chan[z, :, tap * ch : (tap + 1) * ch] for z in range(size)])
        product = product + value * whole_mod[tap].astype(F32)
        for r in range(rows):
            by_row[r, tap] = value[:, r * in_ch : (r + 1) * in_ch].astype(BF16)
    fall = jnp.sum(product, axis=1, keepdims=True) * (scale[:, 0:1] * scale[:, 0:1])
    for r in range(rows):
        outs[r][0:TAPS] = by_row[lax.rem(row_at + r, rows)]
        put_columns(outs[r], [fall])


def row_sum_kernel(scale, small, *refs):
    parts, out = refs[:-1], refs[-1]
    fall = get_column(parts[0][TAPS])
    for part in parts[1:]:
        fall = fall + get_column(part[TAPS])
    for tap in range(TAPS):
        value = parts[0][tap].astype(F32)
        for part in parts[1:]:
            value = value + part[tap].astype(F32)
        out[tap] = value.astype(BF16)
    put_columns(out, [fall, scale[:, 0:1]])
    out_ch, in_ch = out.shape[1:]
    pieces = list(split3(small[...]))
    spare = (out.shape[0] - TAPS - 1) * out_ch - 3 * small.shape[0]
    if spare:
        pieces.append(jnp.zeros((spare, in_ch), F32))
    pieces = jnp.concatenate(pieces, axis=0).astype(BF16)
    for n in range(out.shape[0] - TAPS - 1):
        out[TAPS + 1 + n] = pieces[n * out_ch : (n + 1) * out_ch]


def bank_grad_kernel(samples, small_rows, place, bank, *refs):
    parts, (bank_grad, style_grad, latents, held) = refs[:samples], refs[samples:]
    for s in range(samples):
        held[lax.rem(place[0] - s + samples, samples)] = parts[s][...]
    filters, in_ch = bank.shape[0], bank.shape[3]
    last = latents.shape[1] // in_ch
    sel, styles, scales, falls = [], [], [], []
    for b in range(samples):
        rows = jnp.concatenate([held[b, n].astype(F32) for n in range(TAPS + 1, held.shape[1])], axis=0)
        small = rows[:small_rows] + rows[small_rows : 2 * small_rows] + rows[2 * small_rows : 3 * small_rows]
        latents[b : b + 1] = beside([small[n : n + 1] for n in range(last)])
        styles.append(small[last : last + 1])
        sel.append([small[last + 1 : last + 2, k : k + 1] for k in range(filters)])
        falls.append(get_column(held[b, TAPS]))
        scales.append(get_column(held[b, TAPS], 1))
    sums = [jnp.zeros(bank.shape[2:], F32) for _ in range(samples)]
    for tap in range(TAPS):
        totals = [None] * filters
        for b in range(samples):
            kern = mixed(bank, sel[b], tap)
            plain_grad = held[b, tap].astype(F32) * scales[b] - kern * styles[b] * falls[b]
            sums[b] = sums[b] + plain_grad * kern
            kernel_grad = plain_grad * styles[b]
            for k in range(filters):
                term = sel[b][k] * kernel_grad
                totals[k] = term if totals[k] is None else totals[k] + term
        for k in range(filters):
            bank_grad[k, tap] = totals[k]
    for b in range(samples):
        value = jnp.sum(sums[b], axis=0, keepdims=True)
        style_grad[b : b + 1] = value


def affine_kernel(samples, size, place, latents, *refs):
    parts, (w_grad, b_grad, held) = refs[:size], refs[size:]
    for d in range(size):
        held[lax.rem(place[1] - d + size, size)] = parts[d][...]
    style_grad = held[0]
    for z in range(1, size):
        style_grad = style_grad + held[z]
    w_grad[...] = lax.dot_general(
        latents[...],
        style_grad,
        (((0,), (0,)), ((), ())),
        precision=lax.Precision.HIGHEST,
        preferred_element_type=F32,
    )
    bias = style_grad[0:1]
    for b in range(1, samples):
        bias = bias + style_grad[b : b + 1]
    b_grad[...] = bias


def call(kernel, name, outs, *operands, scalars=0, fetched=0, scratch=(), flops=10**6):
    outs = tuple(jax.ShapeDtypeStruct(*o) for o in outs)
    moved = sum(o.size * o.dtype.itemsize for o in (*outs, *operands))
    return pl.pallas_call(
        kernel,
        out_shape=outs,
        in_specs=sspec(scalars)
        + vspec(len(operands) - scalars - fetched)
        + [pl.BlockSpec(memory_space=pltpu.HBM)] * fetched,
        out_specs=tuple(vspec(len(outs))),
        scratch_shapes=[pltpu.VMEM(*s) if isinstance(s, tuple) else s for s in scratch],
        compiler_params=params(),
        cost_estimate=cost(flops, moved),
        name=name,
    )(*operands)


def exchange(x, axis):
    size = lax.axis_size(axis)
    return [x] + [
        lax.ppermute(x, axis, [(i, (i + s) % size) for i in range(size)]) for s in range(1, size)
    ]


def from_sides(first, last, axis):
    size, at = lax.axis_size(axis), lax.axis_index(axis)
    if size == 2:
        got = lax.ppermute(jnp.where(at == 0, last, first), axis, [(0, 1), (1, 0)])
        nothing = jnp.zeros_like(got)
        return jnp.where(at == 1, got, nothing), jnp.where(at == 0, got, nothing)
    up = [(i, i + 1) for i in range(size - 1)]
    down = [(i + 1, i) for i in range(size - 1)]
    return lax.ppermute(last, axis, up), lax.ppermute(first, axis, down)


def on_device(feature, out_grad, bank, select, latent, affine_w, affine_b):
    rows, samples, size = (lax.axis_size(a) for a in ("rows", "samples", "chan"))
    row_at, sample_at, chan_at = (lax.axis_index(a) for a in ("rows", "samples", "chan"))
    _, ch, height, width = feature.shape
    out_ch, in_ch = bank.shape[2:]
    pixels, all_ch = height * width, ch * size
    sign = 1 - 2 * jnp.remainder(sample_at, 2)
    place = jnp.stack([sample_at, chan_at, row_at, sign, size]).astype(jnp.int32)
    flops = 2 * TAPS * ch * ch * size * pixels

    def along(x, pairs):
        whole = []
        for b in range(samples):
            for i, j in pairs:
                if b % 2:
                    i, j = size - 1 - i, size - 1 - j
                whole.append((b * size + i, b * size + j))
        return lax.ppermute(x, ("samples", "chan"), whole)

    cotan = out_grad[0].reshape(ch, pixels)
    first, second = [], []

    def step(number, x, y):
        first.append(along(x, [(i, i + 1) for i in range(number - 1, size - 1)]))
        second.append(along(y, [(i + 1, i) for i in range(size - number)]))

    step(1, cotan, cotan)

    feat = feature[0].reshape(ch, pixels)
    feat_before, feat_after = from_sides(feat[:, :width], feat[:, pixels - width :], "rows")
    small_rows = -(-(latent.shape[1] // in_ch + 2) // 8) * 8
    style, kernel, energy, small = call(
        energy_kernel,
        "energy",
        [((1, in_ch), F32), ((TAPS, out_ch, in_ch), F32), ((out_ch, 128), F32), ((small_rows, in_ch), F32)],
        select,
        latent,
        affine_b[None],
        affine_w,
        bank,
        fetched=5,
        scratch=[
            pltpu.SMEM(select.shape, jnp.int32),
            (latent.shape, F32),
            ((1, in_ch), F32),
            (affine_w.shape, F32),
            (bank.shape, F32),
            pltpu.SemaphoreType.DMA((5,)),
        ],
    )
    extended = ((ch, (height + 2) * width), BF16)
    (feat,) = call(
        functools.partial(rows_kernel, height, width), "feat_rows", [extended], feat, feat_before, feat_after
    )
    mod_own, scale = call(
        modulated_kernel,
        "modulated",
        [((TAPS, out_ch, in_ch), BF16), ((out_ch, 128), F32)],
        kernel,
        style,
        *exchange(energy, "rows"),
    )
    feat, mod_own = lax.optimization_barrier((feat, mod_own))
    feat_end = lax.ppermute(feat, "chan", [(0, 1), (size - 1, size - 2)])
    message = ((ch, TAPS * ch), BF16)
    whole_mod, *mods = call(
        functools.partial(blocks_kernel, rows, size),
        "mod_blocks",
        [((TAPS, out_ch, all_ch), BF16)] + [message] * size,
        place,
        *exchange(mod_own, "rows"),
        scalars=1,
        scratch=[((rows, TAPS, out_ch, in_ch), BF16), ((size, *message[0]), BF16)],
    )
    first[0], second[0], energy, mod_own = lax.optimization_barrier((first[0], second[0], energy, mod_own))

    step(2, first[0], second[0])
    triple, double = ((3 * ch, TAPS * ch), BF16), ((2 * ch, TAPS * ch), BF16)
    own_grad, to_behind, to_ahead, wide = call(
        functools.partial(near_grad_kernel, height, width),
        "near_grad",
        [message, triple, triple, ((3 * ch, (height + 2) * width), BF16)],
        cotan,
        first[0],
        second[0],
        feat,
        mods[size - 1],
        mods[1],
        scratch=[((3 * ch, pixels), BF16), ((3, 3 * ch, 3 * ch), F32)],
        flops=flops * 3 // size,
    )
    from_ahead = along(to_behind, [(i + 1, i) for i in range(size - 1)])
    from_behind = along(to_ahead, [(i, i + 1) for i in range(size - 1)])
    first[1], second[1], feat_end, wide, whole_mod = lax.optimization_barrier(
        (first[1], second[1], feat_end, wide, whole_mod)
    )

    count = size - 3
    grad_others, middle, end_block = call(
        functools.partial(middle_grad_kernel, count, height, width),
        "middle_grad",
        [((count * ch, TAPS * ch), BF16), ((count * ch, pixels), BF16), ((ch, pixels), BF16)],
        *first[1:],
        *second[1:],
        wide,
        scratch=[((3, count * ch, 3 * ch), F32)],
        flops=flops // size,
    )
    (grad_end,) = call(
        functools.partial(end_grad_kernel, height, width),
        "end_grad",
        [double],
        place,
        end_block,
        feat_end,
        from_ahead,
        from_behind,
        scalars=1,
        scratch=[((3 * ch, (height + 2) * width), BF16), ((3, ch, 3 * ch), F32)],
        flops=flops // size,
    )
    from_others = along(grad_others, [(i, (i + 2) % size) for i in range(size)])
    from_others, grad_end = lax.optimization_barrier((from_others, grad_end))
    from_end = lax.ppermute(grad_end, "chan", [(1, size - 1), (size - 2, 0)])
    far = lax.ppermute(end_block, "chan", [(1, 0), (size - 2, size - 1)])
    parts = call(
        functools.partial(collect_kernel, rows, size),
        "collect",
        [((TAPS + 1, out_ch, in_ch), BF16)] * rows,
        place,
        scale,
        whole_mod,
        own_grad,
        from_ahead,
        from_behind,
        from_others,
        from_end,
        scalars=1,
        scratch=[((size, *message[0]), F32), ((rows, TAPS, out_ch, in_ch), BF16)],
        flops=COLLECT_FLOPS,
    )
    parts, mods = lax.optimization_barrier((parts, mods))
    others = [along(mods[d], [(i, (i + d) % size) for i in range(size)]) for d in range(2, size - 1)]
    parts = [parts[0]] + [
        lax.ppermute(parts[r], "rows", [(i, (i + r) % rows) for i in range(rows)])
        for r in range(1, rows)
    ]
    slots = TAPS + 1 - (-3 * small_rows // out_ch)
    (own,) = call(row_sum_kernel, "row_sum", [((slots, out_ch, in_ch), BF16)], scale, small, *parts)
    every = exchange(own, "samples")

    own, others, far = lax.optimization_barrier((own, others, far))
    main, before, after = call(
        functools.partial(input_grad_kernel, size, height, width),
        "input_grad",
        [((ch, pixels), F32), ((ch, width), F32), ((ch, width), F32)],
        place,
        cotan,
        first[0],
        second[0],
        middle,
        far,
        mods[0],
        from_behind,
        from_ahead,
        from_end,
        *others,
        scalars=1,
        scratch=[
            ((all_ch, pixels), BF16),
            ((TAPS * ch, all_ch), BF16),
            ((height + 2, 3 * ch, width), F32),
        ],
        flops=INPUT_FLOPS,
    )
    every, main, before, after = lax.optimization_barrier((every, main, before, after))
    from_above, from_below = from_sides(before, after, "rows")
    bank_grad, style_part, latents = call(
        functools.partial(bank_grad_kernel, samples, small_rows),
        "bank_grad",
        [(bank.shape, F32), ((samples, in_ch), F32), ((samples, latent.shape[1]), F32)],
        place,
        bank,
        *every,
        scalars=1,
        scratch=[((samples, slots, out_ch, in_ch), BF16)],
    )
    style_parts = exchange(style_part, "chan")
    edge = jnp.concatenate(
        [from_above[:, None], jnp.zeros((ch, height - 2, width), F32), from_below[:, None]], axis=1
    )
    feature_grad = (main.reshape(ch, height, width) + edge).astype(BF16)[None]
    style_parts, feature_grad = lax.optimization_barrier((style_parts, feature_grad))
    affine_w_grad, affine_b_grad = call(
        functools.partial(affine_kernel, samples, size),
        "affine",
        [(affine_w.shape, F32), ((1, in_ch), F32)],
        place,
        latents,
        *style_parts,
        scalars=1,
        scratch=[((size, samples, in_ch), F32)],
    )
    return (feature_grad, bank_grad, affine_w_grad, affine_b_grad[0])


def solution(mesh):
    return jax.shard_map(
        on_device,
        mesh=mesh,
        in_specs=(
            P("samples", "chan", "rows", None),
            P("samples", "chan", "rows", None),
            P(None, None, "chan", "rows"),
            P("samples", None),
            P("samples", None),
            P(None, "rows"),
            P("rows"),
        ),
        out_specs=(
            P("samples", "chan", "rows", None),
            P(None, None, "chan", "rows"),
            P(None, "rows"),
            P("rows"),
        ),
        check_vma=False,
    )
```

```python
import functools

import jax
import jax.numpy as jnp
from jax import lax
from jax.experimental import pallas as pl
from jax.experimental.pallas import tpu as pltpu
from jax.sharding import PartitionSpec as P

EPS = 1e-08
TAPS = 9
F32 = jnp.float32
BF16 = jnp.bfloat16
VMEM_LIMIT = 16 * 2**20
COLLECT_FLOPS = 3 * 10**9
INPUT_FLOPS = 2 * 10**9


def params():
    return pltpu.CompilerParams(vmem_limit_bytes=VMEM_LIMIT)


def vspec(n):
    return [pl.BlockSpec(memory_space=pltpu.VMEM)] * n


def sspec(n):
    return [pl.BlockSpec(memory_space=pltpu.SMEM)] * n


def cost(flops, moved):
    return pl.CostEstimate(flops=flops, bytes_accessed=moved, transcendentals=0)


def beside(pieces):
    return pieces[0] if len(pieces) == 1 else jnp.concatenate(pieces, axis=1)


def mixed(bank_ref, weights, tap):
    total = weights[0] * bank_ref[0, tap]
    for k in range(1, bank_ref.shape[0]):
        total = total + weights[k] * bank_ref[k, tap]
    return total


def plain_kernel(*refs):
    given, (plain_out, small), held, sems = refs[:5], refs[5:7], refs[7:12], refs[12]
    copies = [pltpu.make_async_copy(x, y, sems.at[n]) for n, (x, y) in enumerate(zip(given, held))]
    for copy in copies:
        copy.start()
    for copy in copies:
        copy.wait()
    select, latent, affine_b, affine_w, bank = held
    style = (
        jnp.dot(latent[...], affine_w[...], precision=lax.Precision.HIGHEST, preferred_element_type=F32)
        + affine_b[...]
    )
    filters, in_ch = bank.shape[0], bank.shape[3]
    weights = [select[0, k].astype(F32) for k in range(filters)]
    total = jnp.zeros(bank.shape[2:], F32)
    for tap in range(TAPS):
        plain = mixed(bank, weights, tap) * style
        plain_out[tap] = plain
        total = total + plain * plain
    plain_out[TAPS] = jnp.broadcast_to(jnp.sum(total, axis=1, keepdims=True), total.shape)
    small[...] = jnp.zeros(small.shape, F32)
    last = latent.shape[1] // in_ch
    for n in range(last):
        small[n : n + 1] = latent[:, n * in_ch : (n + 1) * in_ch]
    small[last : last + 1] = style
    lane = lax.broadcasted_iota(jnp.int32, (1, in_ch), 1)
    row = jnp.zeros((1, in_ch), F32)
    for k in range(filters):
        row = jnp.where(lane == k, weights[k], row)
    small[last + 1 : last + 2] = row


def blocks_kernel(rows, size, place, *refs):
    parts, (whole, scale_out), outs, (by_row, by_chan) = refs[:rows], refs[rows : rows + 2], refs[rows + 2 : -2], refs[-2:]
    row_at, chan_at, sign = place[2], place[1], place[3]
    energy = parts[0][TAPS]
    for part in parts[1:]:
        energy = energy + part[TAPS]
    scale = lax.rsqrt(energy[:, 0:1] + EPS)
    scale_out[...] = jnp.broadcast_to(scale, scale_out.shape)
    for r in range(rows):
        by_row[lax.rem(row_at - r + rows, rows)] = parts[r][0:TAPS]
    ch = whole.shape[2] // size
    taps = []
    for tap in range(TAPS):
        value = beside([by_row[r, tap] for r in range(rows)]) * scale
        whole[tap] = value.astype(BF16)
        taps.append(value)
    for z in range(size):
        by_chan[z] = beside([value[:, z * ch : (z + 1) * ch] for value in taps]).astype(BF16)
    for d in range(size):
        outs[d][...] = by_chan[lax.rem(chan_at + sign * d + size, size)]


def shifted(x, by):
    width = x.shape[1]
    lane = lax.broadcasted_iota(jnp.int32, x.shape, 1)
    moved = pltpu.roll(x, by % width, 1)
    return jnp.where(lane == (0 if by == 1 else width - 1), 0.0, moved)


def spread(wide, row, x):
    ch, width = x.shape
    wide[ch : 2 * ch, row * width : (row + 1) * width] = x
    x = x.astype(F32)
    wide[0:ch, row * width : (row + 1) * width] = shifted(x, 1).astype(BF16)
    wide[2 * ch : 3 * ch, row * width : (row + 1) * width] = shifted(x, -1).astype(BF16)


def rows_kernel(height, width, feat, feat_before, feat_after, out):
    out[:, 0:width] = feat_before[...]
    out[:, width : (height + 1) * width] = feat[...]
    out[:, (height + 1) * width :] = feat_after[...]


def tap_products(g_ref, wides, totals, height, width):
    for total in totals:
        total[...] = jnp.zeros(total.shape, F32)

    def body(row, _):
        g = g_ref[:, pl.ds(pl.multiple_of(row * width, width), width)]
        for wide, total in zip(wides, totals):
            for kh in range(3):
                x = wide[:, pl.ds(pl.multiple_of((row + kh) * width, width), width)]
                total[kh] += lax.dot_general(g, x, (((1,), (1,)), ((), ())), preferred_element_type=F32)
        return 0

    lax.fori_loop(0, height, body, 0)
    return [jnp.concatenate([total[kh] for kh in range(3)], axis=1).astype(BF16) for total in totals]


def near_grad_kernel(height, width, *refs):
    cotans, feat, mods, (own, behind, ahead), (wide, gathered, total) = refs[:3], refs[3], refs[4:6], refs[6:9], refs[9:]
    ch = feat.shape[0]
    for at, cotan in enumerate(cotans):
        gathered[at * ch : (at + 1) * ch] = cotan[...]
    for row in range(height + 2):
        spread(wide, row, feat[:, row * width : (row + 1) * width])
    (whole,) = tap_products(gathered, [wide], [total], height, width)
    own[...] = whole[0:ch]
    for at, (out, mod) in enumerate(zip((behind, ahead), mods)):
        out[0:ch] = whole[(at + 1) * ch : (at + 2) * ch]
        out[ch : 2 * ch] = mod[...]
        out[2 * ch :] = mods[1 - at][...]


def middle_grad_kernel(count, height, width, *refs):
    first, second, wide = refs[:count], refs[count : 2 * count], refs[2 * count]
    out, middle, end_block, total = refs[2 * count + 1 :]
    ch = end_block.shape[0]
    for at in range(count):
        middle[at * ch : (at + 1) * ch] = first[at][...] + second[count - 1 - at][...]
    end_block[...] = first[-1][...] + second[-1][...]
    (out[...],) = tap_products(middle, [wide], [total], height, width)


def end_grad_kernel(height, width, place, end_block, feat, ahead, behind, out, wide, total):
    ch = feat.shape[0]
    second = place[1] == jnp.where(place[3] > 0, 1, place[4] - 2)
    out[ch:] = jnp.where(second, behind[2 * ch :], ahead[2 * ch :])
    for row in range(height + 2):
        spread(wide, row, feat[:, row * width : (row + 1) * width])
    (out[0:ch],) = tap_products(end_block, [wide], [total], height, width)


def input_grad_kernel(size, height, width, place, cotan, first, second, middle, far, own_mod, behind, ahead, end, *refs):
    others, (main, before, after, gathered, taps_t, total) = refs[: size - 3], refs[size - 3 :]
    ch = main.shape[0]
    spot = jnp.where(place[3] > 0, place[1], size - 1 - place[1])
    gathered[0:ch] = cotan[...]
    gathered[ch : 2 * ch] = jnp.where(spot == 0, far[...], first[...])
    gathered[2 * ch : (size - 1) * ch] = middle[...]
    gathered[(size - 1) * ch :] = jnp.where(spot == size - 1, far[...], second[...])
    mods = [own_mod[...], jnp.where(spot == 0, end[ch:], behind[ch : 2 * ch])]
    mods += [other[...] for other in others]
    mods.append(jnp.where(spot == size - 1, end[ch:], ahead[ch : 2 * ch]))
    every = jnp.concatenate([mod.astype(F32) for mod in mods], axis=0)
    taps_t[...] = every.T.astype(BF16)
    total[...] = jnp.zeros(total.shape, F32)

    def body(row, _):
        g = gathered[:, pl.ds(pl.multiple_of(row * width, width), width)]
        for kh in range(3):
            y = jnp.dot(taps_t[kh * 3 * ch : (kh + 1) * 3 * ch], g, preferred_element_type=F32)
            total[row + kh] += y
        return 0

    lax.fori_loop(0, height, body, 0)
    for row in range(height + 2):
        value = total[row, ch : 2 * ch]
        value = value + shifted(total[row, 0:ch], -1) + shifted(total[row, 2 * ch : 3 * ch], 1)
        if row == 0:
            before[...] = value
        elif row == height + 1:
            after[...] = value
        else:
            main[:, (row - 1) * width : row * width] = value


def split3(x):
    high = x.astype(BF16).astype(F32)
    mid = (x - high).astype(BF16).astype(F32)
    return high, mid, x - high - mid


def put_columns(out, columns):
    lane = lax.broadcasted_iota(jnp.int32, out.shape[1:], 1)
    last = jnp.zeros(out.shape[1:], F32)
    for n, column in enumerate(columns):
        for at, piece in enumerate(split3(column)):
            last = jnp.where(lane == 3 * n + at, piece, last)
    out[TAPS] = last.astype(BF16)


def get_column(last, n=0):
    last = last.astype(F32)
    return last[:, 3 * n : 3 * n + 1] + last[:, 3 * n + 1 : 3 * n + 2] + last[:, 3 * n + 2 : 3 * n + 3]


def collect_kernel(rows, size, place, scale, whole_mod, own, ahead, behind, others, end, *refs):
    outs, (by_chan, by_row) = refs[:rows], refs[rows:]
    chan_at, row_at, sign = place[1], place[2], place[3]
    ch = own.shape[0]
    by_chan[chan_at] = own[...].astype(F32)
    by_chan[lax.rem(chan_at + sign + size, size)] = ahead[0:ch].astype(F32)
    by_chan[lax.rem(chan_at - sign + size, size)] = behind[0:ch].astype(F32)
    for d in range(2, size - 1):
        value = others[(d - 2) * ch : (d - 1) * ch].astype(F32)
        by_chan[lax.rem(chan_at + sign * d + size, size)] = value
    by_chan[jnp.where(chan_at == 0, size - 1, 0)] += end[0:ch].astype(F32)
    in_ch = outs[0].shape[2]
    product = jnp.zeros(whole_mod.shape[1:], F32)
    for tap in range(TAPS):
        value = beside([by_chan[z, :, tap * ch : (tap + 1) * ch] for z in range(size)])
        product = product + value * whole_mod[tap].astype(F32)
        for r in range(rows):
            by_row[r, tap] = value[:, r * in_ch : (r + 1) * in_ch].astype(BF16)
    fall = jnp.sum(product, axis=1, keepdims=True) * (scale[:, 0:1] * scale[:, 0:1])
    for r in range(rows):
        outs[r][0:TAPS] = by_row[lax.rem(row_at + r, rows)]
        put_columns(outs[r], [fall])


def row_sum_kernel(scale, small, *refs):
    parts, out = refs[:-1], refs[-1]
    fall = get_column(parts[0][TAPS])
    for part in parts[1:]:
        fall = fall + get_column(part[TAPS])
    for tap in range(TAPS):
        value = parts[0][tap].astype(F32)
        for part in parts[1:]:
            value = value + part[tap].astype(F32)
        out[tap] = value.astype(BF16)
    put_columns(out, [fall, scale[:, 0:1]])
    out_ch, in_ch = out.shape[1:]
    pieces = list(split3(small[...]))
    spare = (out.shape[0] - TAPS - 1) * out_ch - 3 * small.shape[0]
    if spare:
        pieces.append(jnp.zeros((spare, in_ch), F32))
    pieces = jnp.concatenate(pieces, axis=0).astype(BF16)
    for n in range(out.shape[0] - TAPS - 1):
        out[TAPS + 1 + n] = pieces[n * out_ch : (n + 1) * out_ch]


def bank_grad_kernel(samples, small_rows, place, bank, *refs):
    parts, (bank_grad, style_grad, latents, held) = refs[:samples], refs[samples:]
    for s in range(samples):
        held[lax.rem(place[0] - s + samples, samples)] = parts[s][...]
    filters, in_ch = bank.shape[0], bank.shape[3]
    last = latents.shape[1] // in_ch
    sel, styles, scales, falls = [], [], [], []
    for b in range(samples):
        rows = jnp.concatenate([held[b, n].astype(F32) for n in range(TAPS + 1, held.shape[1])], axis=0)
        small = rows[:small_rows] + rows[small_rows : 2 * small_rows] + rows[2 * small_rows : 3 * small_rows]
        latents[b : b + 1] = beside([small[n : n + 1] for n in range(last)])
        styles.append(small[last : last + 1])
        sel.append([small[last + 1 : last + 2, k : k + 1] for k in range(filters)])
        falls.append(get_column(held[b, TAPS]))
        scales.append(get_column(held[b, TAPS], 1))
    sums = [jnp.zeros(bank.shape[2:], F32) for _ in range(samples)]
    for tap in range(TAPS):
        totals = [None] * filters
        for b in range(samples):
            kern = mixed(bank, sel[b], tap)
            plain_grad = held[b, tap].astype(F32) * scales[b] - kern * styles[b] * falls[b]
            sums[b] = sums[b] + plain_grad * kern
            kernel_grad = plain_grad * styles[b]
            for k in range(filters):
                term = sel[b][k] * kernel_grad
                totals[k] = term if totals[k] is None else totals[k] + term
        for k in range(filters):
            bank_grad[k, tap] = totals[k]
    for b in range(samples):
        value = jnp.sum(sums[b], axis=0, keepdims=True)
        style_grad[b : b + 1] = value


def affine_kernel(samples, size, place, latents, *refs):
    parts, (w_grad, b_grad, held) = refs[:size], refs[size:]
    for d in range(size):
        held[lax.rem(place[1] - d + size, size)] = parts[d][...]
    style_grad = held[0]
    for z in range(1, size):
        style_grad = style_grad + held[z]
    w_grad[...] = lax.dot_general(
        latents[...],
        style_grad,
        (((0,), (0,)), ((), ())),
        precision=lax.Precision.HIGHEST,
        preferred_element_type=F32,
    )
    bias = style_grad[0:1]
    for b in range(1, samples):
        bias = bias + style_grad[b : b + 1]
    b_grad[...] = bias


def call(kernel, name, outs, *operands, scalars=0, fetched=0, scratch=(), flops=10**6):
    outs = tuple(jax.ShapeDtypeStruct(*o) for o in outs)
    moved = sum(o.size * o.dtype.itemsize for o in (*outs, *operands))
    return pl.pallas_call(
        kernel,
        out_shape=outs,
        in_specs=sspec(scalars)
        + vspec(len(operands) - scalars - fetched)
        + [pl.BlockSpec(memory_space=pltpu.HBM)] * fetched,
        out_specs=tuple(vspec(len(outs))),
        scratch_shapes=[pltpu.VMEM(*s) if isinstance(s, tuple) else s for s in scratch],
        compiler_params=params(),
        cost_estimate=cost(flops, moved),
        name=name,
    )(*operands)


def exchange(x, axis):
    size = lax.axis_size(axis)
    return [x] + [
        lax.ppermute(x, axis, [(i, (i + s) % size) for i in range(size)]) for s in range(1, size)
    ]


def from_sides(first, last, axis):
    size, at = lax.axis_size(axis), lax.axis_index(axis)
    if size == 2:
        got = lax.ppermute(jnp.where(at == 0, last, first), axis, [(0, 1), (1, 0)])
        nothing = jnp.zeros_like(got)
        return jnp.where(at == 1, got, nothing), jnp.where(at == 0, got, nothing)
    up = [(i, i + 1) for i in range(size - 1)]
    down = [(i + 1, i) for i in range(size - 1)]
    return lax.ppermute(last, axis, up), lax.ppermute(first, axis, down)


def on_device(feature, out_grad, bank, select, latent, affine_w, affine_b):
    rows, samples, size = (lax.axis_size(a) for a in ("rows", "samples", "chan"))
    row_at, sample_at, chan_at = (lax.axis_index(a) for a in ("rows", "samples", "chan"))
    _, ch, height, width = feature.shape
    out_ch, in_ch = bank.shape[2:]
    pixels, all_ch = height * width, ch * size
    sign = 1 - 2 * jnp.remainder(sample_at, 2)
    place = jnp.stack([sample_at, chan_at, row_at, sign, size]).astype(jnp.int32)
    flops = 2 * TAPS * ch * ch * size * pixels

    def along(x, pairs):
        whole = []
        for b in range(samples):
            for i, j in pairs:
                if b % 2:
                    i, j = size - 1 - i, size - 1 - j
                whole.append((b * size + i, b * size + j))
        return lax.ppermute(x, ("samples", "chan"), whole)

    cotan = out_grad[0].reshape(ch, pixels)
    first, second = [], []

    def step(number, x, y):
        first.append(along(x, [(i, i + 1) for i in range(number - 1, size - 1)]))
        second.append(along(y, [(i + 1, i) for i in range(size - number)]))

    step(1, cotan, cotan)

    small_rows = -(-(latent.shape[1] // in_ch + 2) // 8) * 8
    plain, small = call(
        plain_kernel,
        "plain",
        [((TAPS + 1, out_ch, in_ch), F32), ((small_rows, in_ch), F32)],
        select,
        latent,
        affine_b[None],
        affine_w,
        bank,
        fetched=5,
        scratch=[
            pltpu.SMEM(select.shape, jnp.int32),
            (latent.shape, F32),
            ((1, in_ch), F32),
            (affine_w.shape, F32),
            (bank.shape, F32),
            pltpu.SemaphoreType.DMA((5,)),
        ],
    )
    plains = exchange(plain, "rows")
    feature, plain = lax.optimization_barrier((feature, plain))
    feat = feature[0].reshape(ch, pixels)
    feat_before, feat_after = from_sides(feat[:, :width], feat[:, pixels - width :], "rows")
    extended = ((ch, (height + 2) * width), BF16)
    (feat,) = call(
        functools.partial(rows_kernel, height, width), "feat_rows", [extended], feat, feat_before, feat_after
    )
    feat, plains = lax.optimization_barrier((feat, plains))
    feat_end = lax.ppermute(feat, "chan", [(0, 1), (size - 1, size - 2)])
    message = ((ch, TAPS * ch), BF16)
    whole_mod, scale, *mods = call(
        functools.partial(blocks_kernel, rows, size),
        "mod_blocks",
        [((TAPS, out_ch, all_ch), BF16), ((out_ch, 128), F32)] + [message] * size,
        place,
        *plains,
        scalars=1,
        scratch=[((rows, TAPS, out_ch, in_ch), F32), ((size, *message[0]), BF16)],
    )
    first[0], second[0], plains = lax.optimization_barrier((first[0], second[0], plains))

    step(2, first[0], second[0])
    triple, double = ((3 * ch, TAPS * ch), BF16), ((2 * ch, TAPS * ch), BF16)
    own_grad, to_behind, to_ahead, wide = call(
        functools.partial(near_grad_kernel, height, width),
        "near_grad",
        [message, triple, triple, ((3 * ch, (height + 2) * width), BF16)],
        cotan,
        first[0],
        second[0],
        feat,
        mods[size - 1],
        mods[1],
        scratch=[((3 * ch, pixels), BF16), ((3, 3 * ch, 3 * ch), F32)],
        flops=flops * 3 // size,
    )
    from_ahead = along(to_behind, [(i + 1, i) for i in range(size - 1)])
    from_behind = along(to_ahead, [(i, i + 1) for i in range(size - 1)])
    first[1], second[1], feat_end, wide, whole_mod = lax.optimization_barrier(
        (first[1], second[1], feat_end, wide, whole_mod)
    )

    count = size - 3
    grad_others, middle, end_block = call(
        functools.partial(middle_grad_kernel, count, height, width),
        "middle_grad",
        [((count * ch, TAPS * ch), BF16), ((count * ch, pixels), BF16), ((ch, pixels), BF16)],
        *first[1:],
        *second[1:],
        wide,
        scratch=[((3, count * ch, 3 * ch), F32)],
        flops=flops // size,
    )
    (grad_end,) = call(
        functools.partial(end_grad_kernel, height, width),
        "end_grad",
        [double],
        place,
        end_block,
        feat_end,
        from_ahead,
        from_behind,
        scalars=1,
        scratch=[((3 * ch, (height + 2) * width), BF16), ((3, ch, 3 * ch), F32)],
        flops=flops // size,
    )
    from_others = along(grad_others, [(i, (i + 2) % size) for i in range(size)])
    from_others, grad_end = lax.optimization_barrier((from_others, grad_end))
    from_end = lax.ppermute(grad_end, "chan", [(1, size - 1), (size - 2, 0)])
    far = lax.ppermute(end_block, "chan", [(1, 0), (size - 2, size - 1)])
    parts = call(
        functools.partial(collect_kernel, rows, size),
        "collect",
        [((TAPS + 1, out_ch, in_ch), BF16)] * rows,
        place,
        scale,
        whole_mod,
        own_grad,
        from_ahead,
        from_behind,
        from_others,
        from_end,
        scalars=1,
        scratch=[((size, *message[0]), F32), ((rows, TAPS, out_ch, in_ch), BF16)],
        flops=COLLECT_FLOPS,
    )
    parts, mods = lax.optimization_barrier((parts, mods))
    others = [along(mods[d], [(i, (i + d) % size) for i in range(size)]) for d in range(2, size - 1)]
    parts = [parts[0]] + [
        lax.ppermute(parts[r], "rows", [(i, (i + r) % rows) for i in range(rows)])
        for r in range(1, rows)
    ]
    slots = TAPS + 1 - (-3 * small_rows // out_ch)
    (own,) = call(row_sum_kernel, "row_sum", [((slots, out_ch, in_ch), BF16)], scale, small, *parts)
    every = exchange(own, "samples")

    own, others, far = lax.optimization_barrier((own, others, far))
    main, before, after = call(
        functools.partial(input_grad_kernel, size, height, width),
        "input_grad",
        [((ch, pixels), F32), ((ch, width), F32), ((ch, width), F32)],
        place,
        cotan,
        first[0],
        second[0],
        middle,
        far,
        mods[0],
        from_behind,
        from_ahead,
        from_end,
        *others,
        scalars=1,
        scratch=[
            ((all_ch, pixels), BF16),
            ((TAPS * ch, all_ch), BF16),
            ((height + 2, 3 * ch, width), F32),
        ],
        flops=INPUT_FLOPS,
    )
    every, main, before, after = lax.optimization_barrier((every, main, before, after))
    from_above, from_below = from_sides(before, after, "rows")
    bank_grad, style_part, latents = call(
        functools.partial(bank_grad_kernel, samples, small_rows),
        "bank_grad",
        [(bank.shape, F32), ((samples, in_ch), F32), ((samples, latent.shape[1]), F32)],
        place,
        bank,
        *every,
        scalars=1,
        scratch=[((samples, slots, out_ch, in_ch), BF16)],
    )
    style_parts = exchange(style_part, "chan")
    edge = jnp.concatenate(
        [from_above[:, None], jnp.zeros((ch, height - 2, width), F32), from_below[:, None]], axis=1
    )
    feature_grad = (main.reshape(ch, height, width) + edge).astype(BF16)[None]
    style_parts, feature_grad = lax.optimization_barrier((style_parts, feature_grad))
    affine_w_grad, affine_b_grad = call(
        functools.partial(affine_kernel, samples, size),
        "affine",
        [(affine_w.shape, F32), ((1, in_ch), F32)],
        place,
        latents,
        *style_parts,
        scalars=1,
        scratch=[((size, samples, in_ch), F32)],
    )
    return (feature_grad, bank_grad, affine_w_grad, affine_b_grad[0])


def solution(mesh):
    return jax.shard_map(
        on_device,
        mesh=mesh,
        in_specs=(
            P("samples", "chan", "rows", None),
            P("samples", "chan", "rows", None),
            P(None, None, "chan", "rows"),
            P("samples", None),
            P("samples", None),
            P(None, "rows"),
            P("rows"),
        ),
        out_specs=(
            P("samples", "chan", "rows", None),
            P(None, None, "chan", "rows"),
            P(None, "rows"),
            P("rows"),
        ),
        check_vma=False,
    )
```

```python
import functools

import jax
import jax.numpy as jnp
from jax import lax
from jax.experimental import pallas as pl
from jax.experimental.pallas import tpu as pltpu
from jax.sharding import PartitionSpec as P

EPS = 1e-08
TAPS = 9
F32 = jnp.float32
BF16 = jnp.bfloat16
VMEM_LIMIT = 16 * 2**20
COLLECT_FLOPS = 3 * 10**9
INPUT_FLOPS = 2 * 10**9


def params():
    return pltpu.CompilerParams(vmem_limit_bytes=VMEM_LIMIT)


def vspec(n):
    return [pl.BlockSpec(memory_space=pltpu.VMEM)] * n


def sspec(n):
    return [pl.BlockSpec(memory_space=pltpu.SMEM)] * n


def cost(flops, moved):
    return pl.CostEstimate(flops=flops, bytes_accessed=moved, transcendentals=0)


def beside(pieces):
    return pieces[0] if len(pieces) == 1 else jnp.concatenate(pieces, axis=1)


def mixed(bank_ref, weights, tap):
    total = weights[0] * bank_ref[0, tap]
    for k in range(1, bank_ref.shape[0]):
        total = total + weights[k] * bank_ref[k, tap]
    return total


def plain_kernel(*refs):
    given, (plain_out, small), held, sems = refs[:5], refs[5:7], refs[7:12], refs[12]
    copies = [pltpu.make_async_copy(x, y, sems.at[n]) for n, (x, y) in enumerate(zip(given, held))]
    for copy in copies:
        copy.start()
    for copy in copies:
        copy.wait()
    select, latent, affine_b, affine_w, bank = held
    style = (
        jnp.dot(latent[...], affine_w[...], precision=lax.Precision.HIGHEST, preferred_element_type=F32)
        + affine_b[...]
    )
    filters, in_ch = bank.shape[0], bank.shape[3]
    weights = [select[0, k].astype(F32) for k in range(filters)]
    total = jnp.zeros(bank.shape[2:], F32)
    for tap in range(TAPS):
        plain = mixed(bank, weights, tap) * style
        plain_out[tap] = plain
        total = total + plain * plain
    plain_out[TAPS] = jnp.broadcast_to(jnp.sum(total, axis=1, keepdims=True), total.shape)
    small[...] = jnp.zeros(small.shape, F32)
    last = latent.shape[1] // in_ch
    for n in range(last):
        small[n : n + 1] = latent[:, n * in_ch : (n + 1) * in_ch]
    small[last : last + 1] = style
    lane = lax.broadcasted_iota(jnp.int32, (1, in_ch), 1)
    row = jnp.zeros((1, in_ch), F32)
    for k in range(filters):
        row = jnp.where(lane == k, weights[k], row)
    small[last + 1 : last + 2] = row


def blocks_kernel(rows, size, place, *refs):
    parts, (whole, scale_out), outs, (by_row, by_chan) = refs[:rows], refs[rows : rows + 2], refs[rows + 2 : -2], refs[-2:]
    row_at, chan_at, sign = place[2], place[1], place[3]
    energy = parts[0][TAPS]
    for part in parts[1:]:
        energy = energy + part[TAPS]
    scale = lax.rsqrt(energy[:, 0:1] + EPS)
    scale_out[...] = jnp.broadcast_to(scale, scale_out.shape)
    for r in range(rows):
        by_row[lax.rem(row_at - r + rows, rows)] = parts[r][0:TAPS]
    ch = whole.shape[2] // size
    taps = []
    for tap in range(TAPS):
        value = beside([by_row[r, tap] for r in range(rows)]) * scale
        whole[tap] = value.astype(BF16)
        taps.append(value)
    for z in range(size):
        by_chan[z] = beside([value[:, z * ch : (z + 1) * ch] for value in taps]).astype(BF16)
    for d in range(size):
        outs[d][...] = by_chan[lax.rem(chan_at + sign * d + size, size)]
    outs[size][...] = by_chan[size - 1 - chan_at]


def shifted(x, by):
    width = x.shape[1]
    lane = lax.broadcasted_iota(jnp.int32, x.shape, 1)
    moved = pltpu.roll(x, by % width, 1)
    return jnp.where(lane == (0 if by == 1 else width - 1), 0.0, moved)


def spread(wide, row, x):
    ch, width = x.shape
    wide[ch : 2 * ch, row * width : (row + 1) * width] = x
    x = x.astype(F32)
    wide[0:ch, row * width : (row + 1) * width] = shifted(x, 1).astype(BF16)
    wide[2 * ch : 3 * ch, row * width : (row + 1) * width] = shifted(x, -1).astype(BF16)


def rows_kernel(height, width, feat, feat_before, feat_after, out):
    out[:, 0:width] = feat_before[...]
    out[:, width : (height + 1) * width] = feat[...]
    out[:, (height + 1) * width :] = feat_after[...]


def tap_products(g_ref, wides, totals, height, width):
    for total in totals:
        total[...] = jnp.zeros(total.shape, F32)

    def body(row, _):
        g = g_ref[:, pl.ds(pl.multiple_of(row * width, width), width)]
        for wide, total in zip(wides, totals):
            for kh in range(3):
                x = wide[:, pl.ds(pl.multiple_of((row + kh) * width, width), width)]
                total[kh] += lax.dot_general(g, x, (((1,), (1,)), ((), ())), preferred_element_type=F32)
        return 0

    lax.fori_loop(0, height, body, 0)
    return [jnp.concatenate([total[kh] for kh in range(3)], axis=1).astype(BF16) for total in totals]


def near_grad_kernel(height, width, *refs):
    cotans, feat, mods, (own, behind, ahead), (wide, gathered, total) = refs[:3], refs[3], refs[4:6], refs[6:9], refs[9:]
    ch = feat.shape[0]
    for at, cotan in enumerate(cotans):
        gathered[at * ch : (at + 1) * ch] = cotan[...]
    for row in range(height + 2):
        spread(wide, row, feat[:, row * width : (row + 1) * width])
    (whole,) = tap_products(gathered, [wide], [total], height, width)
    own[...] = whole[0:ch]
    for at, (out, mod) in enumerate(zip((behind, ahead), mods)):
        out[0:ch] = whole[(at + 1) * ch : (at + 2) * ch]
        out[ch:] = mod[...]


def middle_grad_kernel(count, height, width, *refs):
    first, second, wide = refs[:count], refs[count : 2 * count], refs[2 * count]
    out, middle, end_block, total = refs[2 * count + 1 :]
    ch = end_block.shape[0]
    for at in range(count):
        middle[at * ch : (at + 1) * ch] = first[at][...] + second[count - 1 - at][...]
    end_block[...] = first[-1][...] + second[-1][...]
    (out[...],) = tap_products(middle, [wide], [total], height, width)


def end_grad_kernel(height, width, end_block, feat, out, wide, total):
    for row in range(height + 2):
        spread(wide, row, feat[:, row * width : (row + 1) * width])
    (out[...],) = tap_products(end_block, [wide], [total], height, width)


def input_grad_kernel(size, height, width, place, cotan, first, second, middle, far, own_mod, behind, ahead, *refs):
    others, (main, before, after, gathered, taps_t, total) = refs[: size - 2], refs[size - 2 :]
    ch = main.shape[0]
    spot = jnp.where(place[3] > 0, place[1], size - 1 - place[1])
    gathered[0:ch] = cotan[...]
    gathered[ch : 2 * ch] = jnp.where(spot == 0, far[...], first[...])
    gathered[2 * ch : (size - 1) * ch] = middle[...]
    gathered[(size - 1) * ch :] = jnp.where(spot == size - 1, far[...], second[...])
    end_mod = others[-1][...]
    mods = [own_mod[...], jnp.where(spot == 0, end_mod, behind[ch:])]
    mods += [other[...] for other in others[:-1]]
    mods.append(jnp.where(spot == size - 1, end_mod, ahead[ch:]))
    every = jnp.concatenate([mod.astype(F32) for mod in mods], axis=0)
    taps_t[...] = every.T.astype(BF16)
    total[...] = jnp.zeros(total.shape, F32)

    def body(row, _):
        g = gathered[:, pl.ds(pl.multiple_of(row * width, width), width)]
        for kh in range(3):
            y = jnp.dot(taps_t[kh * 3 * ch : (kh + 1) * 3 * ch], g, preferred_element_type=F32)
            total[row + kh] += y
        return 0

    lax.fori_loop(0, height, body, 0)
    for row in range(height + 2):
        value = total[row, ch : 2 * ch]
        value = value + shifted(total[row, 0:ch], -1) + shifted(total[row, 2 * ch : 3 * ch], 1)
        if row == 0:
            before[...] = value
        elif row == height + 1:
            after[...] = value
        else:
            main[:, (row - 1) * width : row * width] = value


def split3(x):
    high = x.astype(BF16).astype(F32)
    mid = (x - high).astype(BF16).astype(F32)
    return high, mid, x - high - mid


def put_columns(out, columns):
    lane = lax.broadcasted_iota(jnp.int32, out.shape[1:], 1)
    last = jnp.zeros(out.shape[1:], F32)
    for n, column in enumerate(columns):
        for at, piece in enumerate(split3(column)):
            last = jnp.where(lane == 3 * n + at, piece, last)
    out[TAPS] = last.astype(BF16)


def get_column(last, n=0):
    last = last.astype(F32)
    return last[:, 3 * n : 3 * n + 1] + last[:, 3 * n + 1 : 3 * n + 2] + last[:, 3 * n + 2 : 3 * n + 3]


def collect_kernel(rows, size, place, scale, whole_mod, own, ahead, behind, others, end, *refs):
    outs, (by_chan, by_row) = refs[:rows], refs[rows:]
    chan_at, row_at, sign = place[1], place[2], place[3]
    ch = own.shape[0]
    by_chan[chan_at] = own[...].astype(F32)
    by_chan[lax.rem(chan_at + sign + size, size)] = ahead[0:ch].astype(F32)
    by_chan[lax.rem(chan_at - sign + size, size)] = behind[0:ch].astype(F32)
    for d in range(2, size - 1):
        value = others[(d - 2) * ch : (d - 1) * ch].astype(F32)
        by_chan[lax.rem(chan_at + sign * d + size, size)] = value
    by_chan[jnp.where(chan_at == 0, size - 1, 0)] += end[...].astype(F32)
    in_ch = outs[0].shape[2]
    product = jnp.zeros(whole_mod.shape[1:], F32)
    for tap in range(TAPS):
        value = beside([by_chan[z, :, tap * ch : (tap + 1) * ch] for z in range(size)])
        product = product + value * whole_mod[tap].astype(F32)
        for r in range(rows):
            by_row[r, tap] = value[:, r * in_ch : (r + 1) * in_ch].astype(BF16)
    fall = jnp.sum(product, axis=1, keepdims=True) * (scale[:, 0:1] * scale[:, 0:1])
    for r in range(rows):
        outs[r][0:TAPS] = by_row[lax.rem(row_at + r, rows)]
        put_columns(outs[r], [fall])


def row_sum_kernel(scale, small, *refs):
    parts, out = refs[:-1], refs[-1]
    fall = get_column(parts[0][TAPS])
    for part in parts[1:]:
        fall = fall + get_column(part[TAPS])
    for tap in range(TAPS):
        value = parts[0][tap].astype(F32)
        for part in parts[1:]:
            value = value + part[tap].astype(F32)
        out[tap] = value.astype(BF16)
    put_columns(out, [fall, scale[:, 0:1]])
    out_ch, in_ch = out.shape[1:]
    pieces = list(split3(small[...]))
    spare = (out.shape[0] - TAPS - 1) * out_ch - 3 * small.shape[0]
    if spare:
        pieces.append(jnp.zeros((spare, in_ch), F32))
    pieces = jnp.concatenate(pieces, axis=0).astype(BF16)
    for n in range(out.shape[0] - TAPS - 1):
        out[TAPS + 1 + n] = pieces[n * out_ch : (n + 1) * out_ch]


def bank_grad_kernel(samples, small_rows, place, bank, *refs):
    parts, (bank_grad, style_grad, latents, held) = refs[:samples], refs[samples:]
    for s in range(samples):
        held[lax.rem(place[0] - s + samples, samples)] = parts[s][...]
    filters, in_ch = bank.shape[0], bank.shape[3]
    last = latents.shape[1] // in_ch
    sel, styles, scales, falls = [], [], [], []
    for b in range(samples):
        rows = jnp.concatenate([held[b, n].astype(F32) for n in range(TAPS + 1, held.shape[1])], axis=0)
        small = rows[:small_rows] + rows[small_rows : 2 * small_rows] + rows[2 * small_rows : 3 * small_rows]
        latents[b : b + 1] = beside([small[n : n + 1] for n in range(last)])
        styles.append(small[last : last + 1])
        sel.append([small[last + 1 : last + 2, k : k + 1] for k in range(filters)])
        falls.append(get_column(held[b, TAPS]))
        scales.append(get_column(held[b, TAPS], 1))
    sums = [jnp.zeros(bank.shape[2:], F32) for _ in range(samples)]
    for tap in range(TAPS):
        totals = [None] * filters
        for b in range(samples):
            kern = mixed(bank, sel[b], tap)
            plain_grad = held[b, tap].astype(F32) * scales[b] - kern * styles[b] * falls[b]
            sums[b] = sums[b] + plain_grad * kern
            kernel_grad = plain_grad * styles[b]
            for k in range(filters):
                term = sel[b][k] * kernel_grad
                totals[k] = term if totals[k] is None else totals[k] + term
        for k in range(filters):
            bank_grad[k, tap] = totals[k]
    for b in range(samples):
        value = jnp.sum(sums[b], axis=0, keepdims=True)
        style_grad[b : b + 1] = value


def affine_kernel(samples, size, place, latents, *refs):
    parts, (w_grad, b_grad, held) = refs[:size], refs[size:]
    for d in range(size):
        held[lax.rem(place[1] - d + size, size)] = parts[d][...]
    style_grad = held[0]
    for z in range(1, size):
        style_grad = style_grad + held[z]
    w_grad[...] = lax.dot_general(
        latents[...],
        style_grad,
        (((0,), (0,)), ((), ())),
        precision=lax.Precision.HIGHEST,
        preferred_element_type=F32,
    )
    bias = style_grad[0:1]
    for b in range(1, samples):
        bias = bias + style_grad[b : b + 1]
    b_grad[...] = bias


def call(kernel, name, outs, *operands, scalars=0, fetched=0, scratch=(), flops=10**6):
    outs = tuple(jax.ShapeDtypeStruct(*o) for o in outs)
    moved = sum(o.size * o.dtype.itemsize for o in (*outs, *operands))
    return pl.pallas_call(
        kernel,
        out_shape=outs,
        in_specs=sspec(scalars)
        + vspec(len(operands) - scalars - fetched)
        + [pl.BlockSpec(memory_space=pltpu.HBM)] * fetched,
        out_specs=tuple(vspec(len(outs))),
        scratch_shapes=[pltpu.VMEM(*s) if isinstance(s, tuple) else s for s in scratch],
        compiler_params=params(),
        cost_estimate=cost(flops, moved),
        name=name,
    )(*operands)


def exchange(x, axis):
    size = lax.axis_size(axis)
    return [x] + [
        lax.ppermute(x, axis, [(i, (i + s) % size) for i in range(size)]) for s in range(1, size)
    ]


def from_sides(first, last, axis):
    size, at = lax.axis_size(axis), lax.axis_index(axis)
    if size == 2:
        got = lax.ppermute(jnp.where(at == 0, last, first), axis, [(0, 1), (1, 0)])
        nothing = jnp.zeros_like(got)
        return jnp.where(at == 1, got, nothing), jnp.where(at == 0, got, nothing)
    up = [(i, i + 1) for i in range(size - 1)]
    down = [(i + 1, i) for i in range(size - 1)]
    return lax.ppermute(last, axis, up), lax.ppermute(first, axis, down)


def on_device(feature, out_grad, bank, select, latent, affine_w, affine_b):
    rows, samples, size = (lax.axis_size(a) for a in ("rows", "samples", "chan"))
    row_at, sample_at, chan_at = (lax.axis_index(a) for a in ("rows", "samples", "chan"))
    _, ch, height, width = feature.shape
    out_ch, in_ch = bank.shape[2:]
    pixels, all_ch = height * width, ch * size
    sign = 1 - 2 * jnp.remainder(sample_at, 2)
    place = jnp.stack([sample_at, chan_at, row_at, sign]).astype(jnp.int32)
    flops = 2 * TAPS * ch * ch * size * pixels

    def along(x, pairs):
        whole = []
        for b in range(samples):
            for i, j in pairs:
                if b % 2:
                    i, j = size - 1 - i, size - 1 - j
                whole.append((b * size + i, b * size + j))
        return lax.ppermute(x, ("samples", "chan"), whole)

    cotan = out_grad[0].reshape(ch, pixels)
    first, second = [], []

    def step(number, x, y):
        first.append(along(x, [(i, i + 1) for i in range(number - 1, size - 1)]))
        second.append(along(y, [(i + 1, i) for i in range(size - number)]))

    step(1, cotan, cotan)

    small_rows = -(-(latent.shape[1] // in_ch + 2) // 8) * 8
    plain, small = call(
        plain_kernel,
        "plain",
        [((TAPS + 1, out_ch, in_ch), F32), ((small_rows, in_ch), F32)],
        select,
        latent,
        affine_b[None],
        affine_w,
        bank,
        fetched=5,
        scratch=[
            pltpu.SMEM(select.shape, jnp.int32),
            (latent.shape, F32),
            ((1, in_ch), F32),
            (affine_w.shape, F32),
            (bank.shape, F32),
            pltpu.SemaphoreType.DMA((5,)),
        ],
    )
    plains = exchange(plain, "rows")
    feature, cotan = lax.optimization_barrier((feature, cotan))
    feat = feature[0].reshape(ch, pixels)
    feat_before, feat_after = from_sides(feat[:, :width], feat[:, pixels - width :], "rows")
    extended = ((ch, (height + 2) * width), BF16)
    (feat,) = call(
        functools.partial(rows_kernel, height, width), "feat_rows", [extended], feat, feat_before, feat_after
    )
    feat, plain = lax.optimization_barrier((feat, plain))
    feat_end = lax.ppermute(feat, "chan", [(0, 1), (size - 1, size - 2)])
    message = ((ch, TAPS * ch), BF16)
    whole_mod, scale, *mods = call(
        functools.partial(blocks_kernel, rows, size),
        "mod_blocks",
        [((TAPS, out_ch, all_ch), BF16), ((out_ch, 128), F32)] + [message] * (size + 1),
        place,
        *plains,
        scalars=1,
        scratch=[((rows, TAPS, out_ch, in_ch), F32), ((size, *message[0]), BF16)],
    )
    first[0], second[0], plains = lax.optimization_barrier((first[0], second[0], plains))

    step(2, first[0], second[0])
    double = ((2 * ch, TAPS * ch), BF16)
    own_grad, to_behind, to_ahead, wide = call(
        functools.partial(near_grad_kernel, height, width),
        "near_grad",
        [message, double, double, ((3 * ch, (height + 2) * width), BF16)],
        cotan,
        first[0],
        second[0],
        feat,
        mods[size - 1],
        mods[1],
        scratch=[((3 * ch, pixels), BF16), ((3, 3 * ch, 3 * ch), F32)],
        flops=flops * 3 // size,
    )
    from_ahead = along(to_behind, [(i + 1, i) for i in range(size - 1)])
    from_behind = along(to_ahead, [(i, i + 1) for i in range(size - 1)])
    first[1], second[1], feat_end, wide, whole_mod = lax.optimization_barrier(
        (first[1], second[1], feat_end, wide, whole_mod)
    )

    count = size - 3
    grad_others, middle, end_block = call(
        functools.partial(middle_grad_kernel, count, height, width),
        "middle_grad",
        [((count * ch, TAPS * ch), BF16), ((count * ch, pixels), BF16), ((ch, pixels), BF16)],
        *first[1:],
        *second[1:],
        wide,
        scratch=[((3, count * ch, 3 * ch), F32)],
        flops=flops // size,
    )
    (grad_end,) = call(
        functools.partial(end_grad_kernel, height, width),
        "end_grad",
        [message],
        end_block,
        feat_end,
        scratch=[((3 * ch, (height + 2) * width), BF16), ((3, ch, 3 * ch), F32)],
        flops=flops // size,
    )
    from_others = along(grad_others, [(i, (i + 2) % size) for i in range(size)])
    from_end = lax.ppermute(grad_end, "chan", [(1, size - 1), (size - 2, 0)])
    far = lax.ppermute(end_block, "chan", [(1, 0), (size - 2, size - 1)])
    parts = call(
        functools.partial(collect_kernel, rows, size),
        "collect",
        [((TAPS + 1, out_ch, in_ch), BF16)] * rows,
        place,
        scale,
        whole_mod,
        own_grad,
        from_ahead,
        from_behind,
        from_others,
        from_end,
        scalars=1,
        scratch=[((size, *message[0]), F32), ((rows, TAPS, out_ch, in_ch), BF16)],
        flops=COLLECT_FLOPS,
    )
    parts, mods = lax.optimization_barrier((parts, mods))
    others = [along(mods[d], [(i, (i + d) % size) for i in range(size)]) for d in range(2, size - 1)]
    others.append(lax.ppermute(mods[size], "chan", [(0, size - 1), (size - 1, 0)]))
    parts = [parts[0]] + [
        lax.ppermute(parts[r], "rows", [(i, (i + r) % rows) for i in range(rows)])
        for r in range(1, rows)
    ]
    slots = TAPS + 1 - (-3 * small_rows // out_ch)
    (own,) = call(row_sum_kernel, "row_sum", [((slots, out_ch, in_ch), BF16)], scale, small, *parts)
    every = exchange(own, "samples")

    own, others, far = lax.optimization_barrier((own, others, far))
    main, before, after = call(
        functools.partial(input_grad_kernel, size, height, width),
        "input_grad",
        [((ch, pixels), F32), ((ch, width), F32), ((ch, width), F32)],
        place,
        cotan,
        first[0],
        second[0],
        middle,
        far,
        mods[0],
        from_behind,
        from_ahead,
        *others,
        scalars=1,
        scratch=[
            ((all_ch, pixels), BF16),
            ((TAPS * ch, all_ch), BF16),
            ((height + 2, 3 * ch, width), F32),
        ],
        flops=INPUT_FLOPS,
    )
    every, main, before, after = lax.optimization_barrier((every, main, before, after))
    from_above, from_below = from_sides(before, after, "rows")
    bank_grad, style_part, latents = call(
        functools.partial(bank_grad_kernel, samples, small_rows),
        "bank_grad",
        [(bank.shape, F32), ((samples, in_ch), F32), ((samples, latent.shape[1]), F32)],
        place,
        bank,
        *every,
        scalars=1,
        scratch=[((samples, slots, out_ch, in_ch), BF16)],
    )
    style_parts = exchange(style_part, "chan")
    edge = jnp.concatenate(
        [from_above[:, None], jnp.zeros((ch, height - 2, width), F32), from_below[:, None]], axis=1
    )
    feature_grad = (main.reshape(ch, height, width) + edge).astype(BF16)[None]
    style_parts, feature_grad = lax.optimization_barrier((style_parts, feature_grad))
    affine_w_grad, affine_b_grad = call(
        functools.partial(affine_kernel, samples, size),
        "affine",
        [(affine_w.shape, F32), ((1, in_ch), F32)],
        place,
        latents,
        *style_parts,
        scalars=1,
        scratch=[((size, samples, in_ch), F32)],
    )
    return (feature_grad, bank_grad, affine_w_grad, affine_b_grad[0])


def solution(mesh):
    return jax.shard_map(
        on_device,
        mesh=mesh,
        in_specs=(
            P("samples", "chan", "rows", None),
            P("samples", "chan", "rows", None),
            P(None, None, "chan", "rows"),
            P("samples", None),
            P("samples", None),
            P(None, "rows"),
            P("rows"),
        ),
        out_specs=(
            P("samples", "chan", "rows", None),
            P(None, None, "chan", "rows"),
            P(None, "rows"),
            P("rows"),
        ),
        check_vma=False,
    )
```

```python
import functools

import jax
import jax.numpy as jnp
from jax import lax
from jax.experimental import pallas as pl
from jax.experimental.pallas import tpu as pltpu
from jax.sharding import PartitionSpec as P

EPS = 1e-08
TAPS = 9
F32 = jnp.float32
BF16 = jnp.bfloat16
VMEM_LIMIT = 16 * 2**20
COLLECT_FLOPS = 6 * 10**9
INPUT_FLOPS = 2 * 10**9


def params():
    return pltpu.CompilerParams(vmem_limit_bytes=VMEM_LIMIT)


def vspec(n):
    return [pl.BlockSpec(memory_space=pltpu.VMEM)] * n


def sspec(n):
    return [pl.BlockSpec(memory_space=pltpu.SMEM)] * n


def cost(flops, moved):
    return pl.CostEstimate(flops=flops, bytes_accessed=moved, transcendentals=0)


def beside(pieces):
    return pieces[0] if len(pieces) == 1 else jnp.concatenate(pieces, axis=1)


def mixed(bank_ref, weights, tap):
    total = weights[0] * bank_ref[0, tap]
    for k in range(1, bank_ref.shape[0]):
        total = total + weights[k] * bank_ref[k, tap]
    return total


def plain_kernel(*refs):
    given, (plain_out, small), held, sems = refs[:5], refs[5:7], refs[7:12], refs[12]
    copies = [pltpu.make_async_copy(x, y, sems.at[n]) for n, (x, y) in enumerate(zip(given, held))]
    for copy in copies:
        copy.start()
    for copy in copies:
        copy.wait()
    select, latent, affine_b, affine_w, bank = held
    style = (
        jnp.dot(latent[...], affine_w[...], precision=lax.Precision.HIGHEST, preferred_element_type=F32)
        + affine_b[...]
    )
    filters, in_ch = bank.shape[0], bank.shape[3]
    weights = [select[0, k].astype(F32) for k in range(filters)]
    total = jnp.zeros(bank.shape[2:], F32)
    for tap in range(TAPS):
        plain = mixed(bank, weights, tap) * style
        plain_out[tap] = plain
        total = total + plain * plain
    plain_out[TAPS] = jnp.broadcast_to(jnp.sum(total, axis=1, keepdims=True), total.shape)
    small[...] = jnp.zeros(small.shape, F32)
    last = latent.shape[1] // in_ch
    for n in range(last):
        small[n : n + 1] = latent[:, n * in_ch : (n + 1) * in_ch]
    small[last : last + 1] = style
    lane = lax.broadcasted_iota(jnp.int32, (1, in_ch), 1)
    row = jnp.zeros((1, in_ch), F32)
    for k in range(filters):
        row = jnp.where(lane == k, weights[k], row)
    small[last + 1 : last + 2] = row


def blocks_kernel(rows, size, place, *refs):
    parts, (whole, scale_out), outs, (by_row, by_chan) = refs[:rows], refs[rows : rows + 2], refs[rows + 2 : -2], refs[-2:]
    row_at, chan_at, sign = place[2], place[1], place[3]
    energy = parts[0][TAPS]
    for part in parts[1:]:
        energy = energy + part[TAPS]
    scale = lax.rsqrt(energy[:, 0:1] + EPS)
    scale_out[...] = jnp.broadcast_to(scale, scale_out.shape)
    for r in range(rows):
        by_row[lax.rem(row_at - r + rows, rows)] = parts[r][0:TAPS]
    ch = whole.shape[2] // size
    taps = []
    for tap in range(TAPS):
        value = beside([by_row[r, tap] for r in range(rows)]) * scale
        whole[tap] = value.astype(BF16)
        taps.append(value)
    for z in range(size):
        by_chan[z] = beside([value[:, z * ch : (z + 1) * ch] for value in taps]).astype(BF16)
    for d in range(size):
        outs[d][...] = by_chan[lax.rem(chan_at + sign * d + size, size)]
    outs[size][...] = by_chan[size - 1 - chan_at]


def shifted(x, by):
    width = x.shape[1]
    lane = lax.broadcasted_iota(jnp.int32, x.shape, 1)
    moved = pltpu.roll(x, by % width, 1)
    return jnp.where(lane == (0 if by == 1 else width - 1), 0.0, moved)


def spread(wide, row, x):
    ch, width = x.shape
    wide[ch : 2 * ch, row * width : (row + 1) * width] = x
    x = x.astype(F32)
    wide[0:ch, row * width : (row + 1) * width] = shifted(x, 1).astype(BF16)
    wide[2 * ch : 3 * ch, row * width : (row + 1) * width] = shifted(x, -1).astype(BF16)


def rows_kernel(height, width, feat, feat_before, feat_after, out):
    out[:, 0:width] = feat_before[...]
    out[:, width : (height + 1) * width] = feat[...]
    out[:, (height + 1) * width :] = feat_after[...]


def tap_products(g_ref, wides, totals, height, width):
    for total in totals:
        total[...] = jnp.zeros(total.shape, F32)

    def body(row, _):
        g = g_ref[:, pl.ds(pl.multiple_of(row * width, width), width)]
        for wide, total in zip(wides, totals):
            for kh in range(3):
                x = wide[:, pl.ds(pl.multiple_of((row + kh) * width, width), width)]
                total[kh] += lax.dot_general(g, x, (((1,), (1,)), ((), ())), preferred_element_type=F32)
        return 0

    lax.fori_loop(0, height, body, 0)
    return [jnp.concatenate([total[kh] for kh in range(3)], axis=1).astype(BF16) for total in totals]


def near_grad_kernel(height, width, *refs):
    cotans, feat, mods, (own, behind, ahead), (wide, gathered, total) = refs[:3], refs[3], refs[4:6], refs[6:9], refs[9:]
    ch = feat.shape[0]
    for at, cotan in enumerate(cotans):
        gathered[at * ch : (at + 1) * ch] = cotan[...]
    for row in range(height + 2):
        spread(wide, row, feat[:, row * width : (row + 1) * width])
    (whole,) = tap_products(gathered, [wide], [total], height, width)
    own[...] = whole[0:ch]
    for at, (out, mod) in enumerate(zip((behind, ahead), mods)):
        out[0:ch] = whole[(at + 1) * ch : (at + 2) * ch]
        out[ch:] = mod[...]


def middle_grad_kernel(count, height, width, *refs):
    first, second, wide = refs[:count], refs[count : 2 * count], refs[2 * count]
    out, middle, end_block, total = refs[2 * count + 1 :]
    ch = end_block.shape[0]
    for at in range(count):
        middle[at * ch : (at + 1) * ch] = first[at][...] + second[count - 1 - at][...]
    end_block[...] = first[-1][...] + second[-1][...]
    (out[...],) = tap_products(middle, [wide], [total], height, width)


def end_grad_kernel(height, width, end_block, feat, out, wide, total):
    for row in range(height + 2):
        spread(wide, row, feat[:, row * width : (row + 1) * width])
    (out[...],) = tap_products(end_block, [wide], [total], height, width)


def input_grad_kernel(size, height, width, place, cotan, first, second, middle, far, own_mod, behind, ahead, *refs):
    others, (main, before, after, gathered, taps_t, total) = refs[: size - 2], refs[size - 2 :]
    ch = main.shape[0]
    spot = jnp.where(place[3] > 0, place[1], size - 1 - place[1])
    gathered[0:ch] = cotan[...]
    gathered[ch : 2 * ch] = jnp.where(spot == 0, far[...], first[...])
    gathered[2 * ch : (size - 1) * ch] = middle[...]
    gathered[(size - 1) * ch :] = jnp.where(spot == size - 1, far[...], second[...])
    end_mod = others[-1][...]
    mods = [own_mod[...], jnp.where(spot == 0, end_mod, behind[ch:])]
    mods += [other[...] for other in others[:-1]]
    mods.append(jnp.where(spot == size - 1, end_mod, ahead[ch:]))
    every = jnp.concatenate([mod.astype(F32) for mod in mods], axis=0)
    taps_t[...] = every.T.astype(BF16)
    total[...] = jnp.zeros(total.shape, F32)

    def body(row, _):
        g = gathered[:, pl.ds(pl.multiple_of(row * width, width), width)]
        for kh in range(3):
            y = jnp.dot(taps_t[kh * 3 * ch : (kh + 1) * 3 * ch], g, preferred_element_type=F32)
            total[row + kh] += y
        return 0

    lax.fori_loop(0, height, body, 0)
    for row in range(height + 2):
        value = total[row, ch : 2 * ch]
        value = value + shifted(total[row, 0:ch], -1) + shifted(total[row, 2 * ch : 3 * ch], 1)
        if row == 0:
            before[...] = value
        elif row == height + 1:
            after[...] = value
        else:
            main[:, (row - 1) * width : row * width] = value


def split3(x):
    high = x.astype(BF16).astype(F32)
    mid = (x - high).astype(BF16).astype(F32)
    return high, mid, x - high - mid


def put_columns(out, columns):
    lane = lax.broadcasted_iota(jnp.int32, out.shape[1:], 1)
    last = jnp.zeros(out.shape[1:], F32)
    for n, column in enumerate(columns):
        for at, piece in enumerate(split3(column)):
            last = jnp.where(lane == 3 * n + at, piece, last)
    out[TAPS] = last.astype(BF16)


def get_column(last, n=0):
    last = last.astype(F32)
    return last[:, 3 * n : 3 * n + 1] + last[:, 3 * n + 1 : 3 * n + 2] + last[:, 3 * n + 2 : 3 * n + 3]


def collect_kernel(rows, size, place, scale, whole_mod, own, ahead, behind, others, end, *refs):
    outs, (by_chan, by_row) = refs[:rows], refs[rows:]
    chan_at, row_at, sign = place[1], place[2], place[3]
    ch = own.shape[0]
    by_chan[chan_at] = own[...].astype(F32)
    by_chan[lax.rem(chan_at + sign + size, size)] = ahead[0:ch].astype(F32)
    by_chan[lax.rem(chan_at - sign + size, size)] = behind[0:ch].astype(F32)
    for d in range(2, size - 1):
        value = others[(d - 2) * ch : (d - 1) * ch].astype(F32)
        by_chan[lax.rem(chan_at + sign * d + size, size)] = value
    by_chan[jnp.where(chan_at == 0, size - 1, 0)] += end[...].astype(F32)
    in_ch = outs[0].shape[2]
    product = jnp.zeros(whole_mod.shape[1:], F32)
    for tap in range(TAPS):
        value = beside([by_chan[z, :, tap * ch : (tap + 1) * ch] for z in range(size)])
        product = product + value * whole_mod[tap].astype(F32)
        for r in range(rows):
            by_row[r, tap] = value[:, r * in_ch : (r + 1) * in_ch].astype(BF16)
    fall = jnp.sum(product, axis=1, keepdims=True) * (scale[:, 0:1] * scale[:, 0:1])
    for r in range(rows):
        outs[r][0:TAPS] = by_row[lax.rem(row_at + r, rows)]
        put_columns(outs[r], [fall])


def row_sum_kernel(scale, small, *refs):
    parts, out = refs[:-1], refs[-1]
    fall = get_column(parts[0][TAPS])
    for part in parts[1:]:
        fall = fall + get_column(part[TAPS])
    for tap in range(TAPS):
        value = parts[0][tap].astype(F32)
        for part in parts[1:]:
            value = value + part[tap].astype(F32)
        out[tap] = value.astype(BF16)
    put_columns(out, [fall, scale[:, 0:1]])
    out_ch, in_ch = out.shape[1:]
    pieces = list(split3(small[...]))
    spare = (out.shape[0] - TAPS - 1) * out_ch - 3 * small.shape[0]
    if spare:
        pieces.append(jnp.zeros((spare, in_ch), F32))
    pieces = jnp.concatenate(pieces, axis=0).astype(BF16)
    for n in range(out.shape[0] - TAPS - 1):
        out[TAPS + 1 + n] = pieces[n * out_ch : (n + 1) * out_ch]


def bank_grad_kernel(samples, small_rows, place, bank, *refs):
    parts, (bank_grad, style_grad, latents, held) = refs[:samples], refs[samples:]
    for s in range(samples):
        held[lax.rem(place[0] - s + samples, samples)] = parts[s][...]
    filters, in_ch = bank.shape[0], bank.shape[3]
    last = latents.shape[1] // in_ch
    sel, styles, scales, falls = [], [], [], []
    for b in range(samples):
        rows = jnp.concatenate([held[b, n].astype(F32) for n in range(TAPS + 1, held.shape[1])], axis=0)
        small = rows[:small_rows] + rows[small_rows : 2 * small_rows] + rows[2 * small_rows : 3 * small_rows]
        latents[b : b + 1] = beside([small[n : n + 1] for n in range(last)])
        styles.append(small[last : last + 1])
        sel.append([small[last + 1 : last + 2, k : k + 1] for k in range(filters)])
        falls.append(get_column(held[b, TAPS]))
        scales.append(get_column(held[b, TAPS], 1))
    sums = [jnp.zeros(bank.shape[2:], F32) for _ in range(samples)]
    for tap in range(TAPS):
        totals = [None] * filters
        for b in range(samples):
            kern = mixed(bank, sel[b], tap)
            plain_grad = held[b, tap].astype(F32) * scales[b] - kern * styles[b] * falls[b]
            sums[b] = sums[b] + plain_grad * kern
            kernel_grad = plain_grad * styles[b]
            for k in range(filters):
                term = sel[b][k] * kernel_grad
                totals[k] = term if totals[k] is None else totals[k] + term
        for k in range(filters):
            bank_grad[k, tap] = totals[k]
    for b in range(samples):
        value = jnp.sum(sums[b], axis=0, keepdims=True)
        style_grad[b : b + 1] = value


def affine_kernel(samples, size, place, latents, *refs):
    parts, (w_grad, b_grad, held) = refs[:size], refs[size:]
    for d in range(size):
        held[lax.rem(place[1] - d + size, size)] = parts[d][...]
    style_grad = held[0]
    for z in range(1, size):
        style_grad = style_grad + held[z]
    w_grad[...] = lax.dot_general(
        latents[...],
        style_grad,
        (((0,), (0,)), ((), ())),
        precision=lax.Precision.HIGHEST,
        preferred_element_type=F32,
    )
    bias = style_grad[0:1]
    for b in range(1, samples):
        bias = bias + style_grad[b : b + 1]
    b_grad[...] = bias


def call(kernel, name, outs, *operands, scalars=0, fetched=0, scratch=(), flops=10**6):
    outs = tuple(jax.ShapeDtypeStruct(*o) for o in outs)
    moved = sum(o.size * o.dtype.itemsize for o in (*outs, *operands))
    return pl.pallas_call(
        kernel,
        out_shape=outs,
        in_specs=sspec(scalars)
        + vspec(len(operands) - scalars - fetched)
        + [pl.BlockSpec(memory_space=pltpu.HBM)] * fetched,
        out_specs=tuple(vspec(len(outs))),
        scratch_shapes=[pltpu.VMEM(*s) if isinstance(s, tuple) else s for s in scratch],
        compiler_params=params(),
        cost_estimate=cost(flops, moved),
        name=name,
    )(*operands)


def exchange(x, axis):
    size = lax.axis_size(axis)
    return [x] + [
        lax.ppermute(x, axis, [(i, (i + s) % size) for i in range(size)]) for s in range(1, size)
    ]


def from_sides(first, last, axis):
    size, at = lax.axis_size(axis), lax.axis_index(axis)
    if size == 2:
        got = lax.ppermute(jnp.where(at == 0, last, first), axis, [(0, 1), (1, 0)])
        nothing = jnp.zeros_like(got)
        return jnp.where(at == 1, got, nothing), jnp.where(at == 0, got, nothing)
    up = [(i, i + 1) for i in range(size - 1)]
    down = [(i + 1, i) for i in range(size - 1)]
    return lax.ppermute(last, axis, up), lax.ppermute(first, axis, down)


def on_device(feature, out_grad, bank, select, latent, affine_w, affine_b):
    rows, samples, size = (lax.axis_size(a) for a in ("rows", "samples", "chan"))
    row_at, sample_at, chan_at = (lax.axis_index(a) for a in ("rows", "samples", "chan"))
    _, ch, height, width = feature.shape
    out_ch, in_ch = bank.shape[2:]
    pixels, all_ch = height * width, ch * size
    sign = 1 - 2 * jnp.remainder(sample_at, 2)
    place = jnp.stack([sample_at, chan_at, row_at, sign]).astype(jnp.int32)
    flops = 2 * TAPS * ch * ch * size * pixels

    def along(x, pairs):
        whole = []
        for b in range(samples):
            for i, j in pairs:
                if b % 2:
                    i, j = size - 1 - i, size - 1 - j
                whole.append((b * size + i, b * size + j))
        return lax.ppermute(x, ("samples", "chan"), whole)

    cotan = out_grad[0].reshape(ch, pixels)
    first, second = [], []

    def step(number, x, y):
        first.append(along(x, [(i, i + 1) for i in range(number - 1, size - 1)]))
        second.append(along(y, [(i + 1, i) for i in range(size - number)]))

    step(1, cotan, cotan)

    small_rows = -(-(latent.shape[1] // in_ch + 2) // 8) * 8
    plain, small = call(
        plain_kernel,
        "plain",
        [((TAPS + 1, out_ch, in_ch), F32), ((small_rows, in_ch), F32)],
        select,
        latent,
        affine_b[None],
        affine_w,
        bank,
        fetched=5,
        scratch=[
            pltpu.SMEM(select.shape, jnp.int32),
            (latent.shape, F32),
            ((1, in_ch), F32),
            (affine_w.shape, F32),
            (bank.shape, F32),
            pltpu.SemaphoreType.DMA((5,)),
        ],
    )
    plains = exchange(plain, "rows")
    feature, cotan = lax.optimization_barrier((feature, cotan))
    feat = feature[0].reshape(ch, pixels)
    feat_before, feat_after = from_sides(feat[:, :width], feat[:, pixels - width :], "rows")
    extended = ((ch, (height + 2) * width), BF16)
    (feat,) = call(
        functools.partial(rows_kernel, height, width), "feat_rows", [extended], feat, feat_before, feat_after
    )
    feat, plain = lax.optimization_barrier((feat, plain))
    feat_end = lax.ppermute(feat, "chan", [(0, 1), (size - 1, size - 2)])
    message = ((ch, TAPS * ch), BF16)
    whole_mod, scale, *mods = call(
        functools.partial(blocks_kernel, rows, size),
        "mod_blocks",
        [((TAPS, out_ch, all_ch), BF16), ((out_ch, 128), F32)] + [message] * (size + 1),
        place,
        *plains,
        scalars=1,
        scratch=[((rows, TAPS, out_ch, in_ch), F32), ((size, *message[0]), BF16)],
    )
    first[0], second[0], plains = lax.optimization_barrier((first[0], second[0], plains))

    step(2, first[0], second[0])
    double = ((2 * ch, TAPS * ch), BF16)
    own_grad, to_behind, to_ahead, wide = call(
        functools.partial(near_grad_kernel, height, width),
        "near_grad",
        [message, double, double, ((3 * ch, (height + 2) * width), BF16)],
        cotan,
        first[0],
        second[0],
        feat,
        mods[size - 1],
        mods[1],
        scratch=[((3 * ch, pixels), BF16), ((3, 3 * ch, 3 * ch), F32)],
        flops=flops * 3 // size,
    )
    from_ahead = along(to_behind, [(i + 1, i) for i in range(size - 1)])
    from_behind = along(to_ahead, [(i, i + 1) for i in range(size - 1)])
    first[1], second[1], feat_end, wide, whole_mod = lax.optimization_barrier(
        (first[1], second[1], feat_end, wide, whole_mod)
    )

    count = size - 3
    grad_others, middle, end_block = call(
        functools.partial(middle_grad_kernel, count, height, width),
        "middle_grad",
        [((count * ch, TAPS * ch), BF16), ((count * ch, pixels), BF16), ((ch, pixels), BF16)],
        *first[1:],
        *second[1:],
        wide,
        scratch=[((3, count * ch, 3 * ch), F32)],
        flops=flops // size,
    )
    (grad_end,) = call(
        functools.partial(end_grad_kernel, height, width),
        "end_grad",
        [message],
        end_block,
        feat_end,
        scratch=[((3 * ch, (height + 2) * width), BF16), ((3, ch, 3 * ch), F32)],
        flops=flops // size,
    )
    from_others = along(grad_others, [(i, (i + 2) % size) for i in range(size)])
    from_end = lax.ppermute(grad_end, "chan", [(1, size - 1), (size - 2, 0)])
    end_block, grad_end = lax.optimization_barrier((end_block, grad_end))
    far = lax.ppermute(end_block, "chan", [(1, 0), (size - 2, size - 1)])
    parts = call(
        functools.partial(collect_kernel, rows, size),
        "collect",
        [((TAPS + 1, out_ch, in_ch), BF16)] * rows,
        place,
        scale,
        whole_mod,
        own_grad,
        from_ahead,
        from_behind,
        from_others,
        from_end,
        scalars=1,
        scratch=[((size, *message[0]), F32), ((rows, TAPS, out_ch, in_ch), BF16)],
        flops=COLLECT_FLOPS,
    )
    parts, mods = lax.optimization_barrier((parts, mods))
    others = [along(mods[d], [(i, (i + d) % size) for i in range(size)]) for d in range(2, size - 1)]
    others.append(lax.ppermute(mods[size], "chan", [(0, size - 1), (size - 1, 0)]))
    parts = [parts[0]] + [
        lax.ppermute(parts[r], "rows", [(i, (i + r) % rows) for i in range(rows)])
        for r in range(1, rows)
    ]
    slots = TAPS + 1 - (-3 * small_rows // out_ch)
    (own,) = call(row_sum_kernel, "row_sum", [((slots, out_ch, in_ch), BF16)], scale, small, *parts)
    every = exchange(own, "samples")

    own, others, far = lax.optimization_barrier((own, others, far))
    main, before, after = call(
        functools.partial(input_grad_kernel, size, height, width),
        "input_grad",
        [((ch, pixels), F32), ((ch, width), F32), ((ch, width), F32)],
        place,
        cotan,
        first[0],
        second[0],
        middle,
        far,
        mods[0],
        from_behind,
        from_ahead,
        *others,
        scalars=1,
        scratch=[
            ((all_ch, pixels), BF16),
            ((TAPS * ch, all_ch), BF16),
            ((height + 2, 3 * ch, width), F32),
        ],
        flops=INPUT_FLOPS,
    )
    every, main, before, after = lax.optimization_barrier((every, main, before, after))
    from_above, from_below = from_sides(before, after, "rows")
    bank_grad, style_part, latents = call(
        functools.partial(bank_grad_kernel, samples, small_rows),
        "bank_grad",
        [(bank.shape, F32), ((samples, in_ch), F32), ((samples, latent.shape[1]), F32)],
        place,
        bank,
        *every,
        scalars=1,
        scratch=[((samples, slots, out_ch, in_ch), BF16)],
    )
    style_parts = exchange(style_part, "chan")
    edge = jnp.concatenate(
        [from_above[:, None], jnp.zeros((ch, height - 2, width), F32), from_below[:, None]], axis=1
    )
    feature_grad = (main.reshape(ch, height, width) + edge).astype(BF16)[None]
    style_parts, feature_grad = lax.optimization_barrier((style_parts, feature_grad))
    affine_w_grad, affine_b_grad = call(
        functools.partial(affine_kernel, samples, size),
        "affine",
        [(affine_w.shape, F32), ((1, in_ch), F32)],
        place,
        latents,
        *style_parts,
        scalars=1,
        scratch=[((size, samples, in_ch), F32)],
    )
    return (feature_grad, bank_grad, affine_w_grad, affine_b_grad[0])


def solution(mesh):
    return jax.shard_map(
        on_device,
        mesh=mesh,
        in_specs=(
            P("samples", "chan", "rows", None),
            P("samples", "chan", "rows", None),
            P(None, None, "chan", "rows"),
            P("samples", None),
            P("samples", None),
            P(None, "rows"),
            P("rows"),
        ),
        out_specs=(
            P("samples", "chan", "rows", None),
            P(None, None, "chan", "rows"),
            P(None, "rows"),
            P("rows"),
        ),
        check_vma=False,
    )
```

```python
import functools

import jax
import jax.numpy as jnp
from jax import lax
from jax.experimental import pallas as pl
from jax.experimental.pallas import tpu as pltpu
from jax.sharding import PartitionSpec as P

EPS = 1e-08
TAPS = 9
F32 = jnp.float32
BF16 = jnp.bfloat16
VMEM_LIMIT = 16 * 2**20
COLLECT_FLOPS = 6 * 10**9
INPUT_FLOPS = 2 * 10**9


def params():
    return pltpu.CompilerParams(vmem_limit_bytes=VMEM_LIMIT)


def vspec(n):
    return [pl.BlockSpec(memory_space=pltpu.VMEM)] * n


def sspec(n):
    return [pl.BlockSpec(memory_space=pltpu.SMEM)] * n


def cost(flops, moved):
    return pl.CostEstimate(flops=flops, bytes_accessed=moved, transcendentals=0)


def beside(pieces):
    return pieces[0] if len(pieces) == 1 else jnp.concatenate(pieces, axis=1)


def mixed(bank_ref, weights, tap):
    total = weights[0] * bank_ref[0, tap]
    for k in range(1, bank_ref.shape[0]):
        total = total + weights[k] * bank_ref[k, tap]
    return total


def plain_kernel(*refs):
    given, (plain_out, small), held, sems = refs[:5], refs[5:7], refs[7:12], refs[12]
    copies = [pltpu.make_async_copy(x, y, sems.at[n]) for n, (x, y) in enumerate(zip(given, held))]
    for copy in copies:
        copy.start()
    for copy in copies:
        copy.wait()
    select, latent, affine_b, affine_w, bank = held
    style = (
        jnp.dot(latent[...], affine_w[...], precision=lax.Precision.HIGHEST, preferred_element_type=F32)
        + affine_b[...]
    )
    filters, in_ch = bank.shape[0], bank.shape[3]
    weights = [select[0, k].astype(F32) for k in range(filters)]
    total = jnp.zeros(bank.shape[2:], F32)
    for tap in range(TAPS):
        plain = mixed(bank, weights, tap) * style
        plain_out[tap] = plain
        total = total + plain * plain
    plain_out[TAPS] = jnp.broadcast_to(jnp.sum(total, axis=1, keepdims=True), total.shape)
    small[...] = jnp.zeros(small.shape, F32)
    last = latent.shape[1] // in_ch
    for n in range(last):
        small[n : n + 1] = latent[:, n * in_ch : (n + 1) * in_ch]
    small[last : last + 1] = style
    lane = lax.broadcasted_iota(jnp.int32, (1, in_ch), 1)
    row = jnp.zeros((1, in_ch), F32)
    for k in range(filters):
        row = jnp.where(lane == k, weights[k], row)
    small[last + 1 : last + 2] = row


def blocks_kernel(rows, size, place, *refs):
    parts, (whole, scale_out), outs, (by_row, by_chan) = refs[:rows], refs[rows : rows + 2], refs[rows + 2 : -2], refs[-2:]
    row_at, chan_at, sign = place[2], place[1], place[3]
    energy = parts[0][TAPS]
    for part in parts[1:]:
        energy = energy + part[TAPS]
    scale = lax.rsqrt(energy[:, 0:1] + EPS)
    scale_out[...] = jnp.broadcast_to(scale, scale_out.shape)
    for r in range(rows):
        by_row[lax.rem(row_at - r + rows, rows)] = parts[r][0:TAPS]
    ch = whole.shape[2] // size
    taps = []
    for tap in range(TAPS):
        value = beside([by_row[r, tap] for r in range(rows)]) * scale
        whole[tap] = value.astype(BF16)
        taps.append(value)
    for z in range(size):
        by_chan[z] = beside([value[:, z * ch : (z + 1) * ch] for value in taps]).astype(BF16)
    for d in range(size):
        outs[d][...] = by_chan[lax.rem(chan_at + sign * d + size, size)]
    outs[size][...] = by_chan[size - 1 - chan_at]


def shifted(x, by):
    width = x.shape[1]
    lane = lax.broadcasted_iota(jnp.int32, x.shape, 1)
    moved = pltpu.roll(x, by % width, 1)
    return jnp.where(lane == (0 if by == 1 else width - 1), 0.0, moved)


def spread(wide, row, x):
    ch, width = x.shape
    wide[ch : 2 * ch, row * width : (row + 1) * width] = x
    x = x.astype(F32)
    wide[0:ch, row * width : (row + 1) * width] = shifted(x, 1).astype(BF16)
    wide[2 * ch : 3 * ch, row * width : (row + 1) * width] = shifted(x, -1).astype(BF16)


def rows_kernel(height, width, feat, feat_before, feat_after, out):
    out[:, 0:width] = feat_before[...]
    out[:, width : (height + 1) * width] = feat[...]
    out[:, (height + 1) * width :] = feat_after[...]


def tap_products(g_ref, wides, totals, height, width):
    for total in totals:
        total[...] = jnp.zeros(total.shape, F32)

    def body(row, _):
        g = g_ref[:, pl.ds(pl.multiple_of(row * width, width), width)]
        for wide, total in zip(wides, totals):
            for kh in range(3):
                x = wide[:, pl.ds(pl.multiple_of((row + kh) * width, width), width)]
                total[kh] += lax.dot_general(g, x, (((1,), (1,)), ((), ())), preferred_element_type=F32)
        return 0

    lax.fori_loop(0, height, body, 0)
    return [jnp.concatenate([total[kh] for kh in range(3)], axis=1).astype(BF16) for total in totals]


def own_grad_kernel(height, width, cotan, feat, out, wide, total):
    for row in range(height + 2):
        spread(wide, row, feat[:, row * width : (row + 1) * width])
    (out[...],) = tap_products(cotan, [wide], [total], height, width)


def near_grad_kernel(height, width, *refs):
    cotans, wide, mods, outs, (gathered, total) = refs[:2], refs[2], refs[3:5], refs[5:7], refs[7:]
    ch = cotans[0].shape[0]
    for at, cotan in enumerate(cotans):
        gathered[at * ch : (at + 1) * ch] = cotan[...]
    (whole,) = tap_products(gathered, [wide], [total], height, width)
    for at, (out, mod) in enumerate(zip(outs, mods)):
        out[0:ch] = whole[at * ch : (at + 1) * ch]
        out[ch:] = mod[...]


def middle_grad_kernel(count, height, width, *refs):
    first, second, wide = refs[:count], refs[count : 2 * count], refs[2 * count]
    out, middle, end_block, total = refs[2 * count + 1 :]
    ch = end_block.shape[0]
    for at in range(count):
        middle[at * ch : (at + 1) * ch] = first[at][...] + second[count - 1 - at][...]
    end_block[...] = first[-1][...] + second[-1][...]
    (out[...],) = tap_products(middle, [wide], [total], height, width)


def end_grad_kernel(height, width, end_block, feat, out, wide, total):
    for row in range(height + 2):
        spread(wide, row, feat[:, row * width : (row + 1) * width])
    (out[...],) = tap_products(end_block, [wide], [total], height, width)


def input_grad_kernel(size, height, width, place, cotan, first, second, middle, far, own_mod, behind, ahead, *refs):
    others, (main, before, after, gathered, taps_t, total) = refs[: size - 2], refs[size - 2 :]
    ch = main.shape[0]
    spot = jnp.where(place[3] > 0, place[1], size - 1 - place[1])
    gathered[0:ch] = cotan[...]
    gathered[ch : 2 * ch] = jnp.where(spot == 0, far[...], first[...])
    gathered[2 * ch : (size - 1) * ch] = middle[...]
    gathered[(size - 1) * ch :] = jnp.where(spot == size - 1, far[...], second[...])
    end_mod = others[-1][...]
    mods = [own_mod[...], jnp.where(spot == 0, end_mod, behind[ch:])]
    mods += [other[...] for other in others[:-1]]
    mods.append(jnp.where(spot == size - 1, end_mod, ahead[ch:]))
    every = jnp.concatenate([mod.astype(F32) for mod in mods], axis=0)
    taps_t[...] = every.T.astype(BF16)
    total[...] = jnp.zeros(total.shape, F32)

    def body(row, _):
        g = gathered[:, pl.ds(pl.multiple_of(row * width, width), width)]
        for kh in range(3):
            y = jnp.dot(taps_t[kh * 3 * ch : (kh + 1) * 3 * ch], g, preferred_element_type=F32)
            total[row + kh] += y
        return 0

    lax.fori_loop(0, height, body, 0)
    for row in range(height + 2):
        value = total[row, ch : 2 * ch]
        value = value + shifted(total[row, 0:ch], -1) + shifted(total[row, 2 * ch : 3 * ch], 1)
        if row == 0:
            before[...] = value
        elif row == height + 1:
            after[...] = value
        else:
            main[:, (row - 1) * width : row * width] = value


def split3(x):
    high = x.astype(BF16).astype(F32)
    mid = (x - high).astype(BF16).astype(F32)
    return high, mid, x - high - mid


def put_columns(out, columns):
    lane = lax.broadcasted_iota(jnp.int32, out.shape[1:], 1)
    last = jnp.zeros(out.shape[1:], F32)
    for n, column in enumerate(columns):
        for at, piece in enumerate(split3(column)):
            last = jnp.where(lane == 3 * n + at, piece, last)
    out[TAPS] = last.astype(BF16)


def get_column(last, n=0):
    last = last.astype(F32)
    return last[:, 3 * n : 3 * n + 1] + last[:, 3 * n + 1 : 3 * n + 2] + last[:, 3 * n + 2 : 3 * n + 3]


def collect_kernel(rows, size, place, scale, whole_mod, own, ahead, behind, others, end, *refs):
    outs, (by_chan, by_row) = refs[:rows], refs[rows:]
    chan_at, row_at, sign = place[1], place[2], place[3]
    ch = own.shape[0]
    by_chan[chan_at] = own[...].astype(F32)
    by_chan[lax.rem(chan_at + sign + size, size)] = ahead[0:ch].astype(F32)
    by_chan[lax.rem(chan_at - sign + size, size)] = behind[0:ch].astype(F32)
    for d in range(2, size - 1):
        value = others[(d - 2) * ch : (d - 1) * ch].astype(F32)
        by_chan[lax.rem(chan_at + sign * d + size, size)] = value
    by_chan[jnp.where(chan_at == 0, size - 1, 0)] += end[...].astype(F32)
    in_ch = outs[0].shape[2]
    product = jnp.zeros(whole_mod.shape[1:], F32)
    for tap in range(TAPS):
        value = beside([by_chan[z, :, tap * ch : (tap + 1) * ch] for z in range(size)])
        product = product + value * whole_mod[tap].astype(F32)
        for r in range(rows):
            by_row[r, tap] = value[:, r * in_ch : (r + 1) * in_ch].astype(BF16)
    fall = jnp.sum(product, axis=1, keepdims=True) * (scale[:, 0:1] * scale[:, 0:1])
    for r in range(rows):
        outs[r][0:TAPS] = by_row[lax.rem(row_at + r, rows)]
        put_columns(outs[r], [fall])


def row_sum_kernel(scale, small, *refs):
    parts, out = refs[:-1], refs[-1]
    fall = get_column(parts[0][TAPS])
    for part in parts[1:]:
        fall = fall + get_column(part[TAPS])
    for tap in range(TAPS):
        value = parts[0][tap].astype(F32)
        for part in parts[1:]:
            value = value + part[tap].astype(F32)
        out[tap] = value.astype(BF16)
    put_columns(out, [fall, scale[:, 0:1]])
    out_ch, in_ch = out.shape[1:]
    pieces = list(split3(small[...]))
    spare = (out.shape[0] - TAPS - 1) * out_ch - 3 * small.shape[0]
    if spare:
        pieces.append(jnp.zeros((spare, in_ch), F32))
    pieces = jnp.concatenate(pieces, axis=0).astype(BF16)
    for n in range(out.shape[0] - TAPS - 1):
        out[TAPS + 1 + n] = pieces[n * out_ch : (n + 1) * out_ch]


def bank_grad_kernel(samples, small_rows, place, bank, *refs):
    parts, (bank_grad, style_grad, latents, held) = refs[:samples], refs[samples:]
    for s in range(samples):
        held[lax.rem(place[0] - s + samples, samples)] = parts[s][...]
    filters, in_ch = bank.shape[0], bank.shape[3]
    last = latents.shape[1] // in_ch
    sel, styles, scales, falls = [], [], [], []
    for b in range(samples):
        rows = jnp.concatenate([held[b, n].astype(F32) for n in range(TAPS + 1, held.shape[1])], axis=0)
        small = rows[:small_rows] + rows[small_rows : 2 * small_rows] + rows[2 * small_rows : 3 * small_rows]
        latents[b : b + 1] = beside([small[n : n + 1] for n in range(last)])
        styles.append(small[last : last + 1])
        sel.append([small[last + 1 : last + 2, k : k + 1] for k in range(filters)])
        falls.append(get_column(held[b, TAPS]))
        scales.append(get_column(held[b, TAPS], 1))
    sums = [jnp.zeros(bank.shape[2:], F32) for _ in range(samples)]
    for tap in range(TAPS):
        totals = [None] * filters
        for b in range(samples):
            kern = mixed(bank, sel[b], tap)
            plain_grad = held[b, tap].astype(F32) * scales[b] - kern * styles[b] * falls[b]
            sums[b] = sums[b] + plain_grad * kern
            kernel_grad = plain_grad * styles[b]
            for k in range(filters):
                term = sel[b][k] * kernel_grad
                totals[k] = term if totals[k] is None else totals[k] + term
        for k in range(filters):
            bank_grad[k, tap] = totals[k]
    for b in range(samples):
        value = jnp.sum(sums[b], axis=0, keepdims=True)
        style_grad[b : b + 1] = value


def affine_kernel(samples, size, place, latents, *refs):
    parts, (w_grad, b_grad, held) = refs[:size], refs[size:]
    for d in range(size):
        held[lax.rem(place[1] - d + size, size)] = parts[d][...]
    style_grad = held[0]
    for z in range(1, size):
        style_grad = style_grad + held[z]
    w_grad[...] = lax.dot_general(
        latents[...],
        style_grad,
        (((0,), (0,)), ((), ())),
        precision=lax.Precision.HIGHEST,
        preferred_element_type=F32,
    )
    bias = style_grad[0:1]
    for b in range(1, samples):
        bias = bias + style_grad[b : b + 1]
    b_grad[...] = bias


def call(kernel, name, outs, *operands, scalars=0, fetched=0, scratch=(), flops=10**6):
    outs = tuple(jax.ShapeDtypeStruct(*o) for o in outs)
    moved = sum(o.size * o.dtype.itemsize for o in (*outs, *operands))
    return pl.pallas_call(
        kernel,
        out_shape=outs,
        in_specs=sspec(scalars)
        + vspec(len(operands) - scalars - fetched)
        + [pl.BlockSpec(memory_space=pltpu.HBM)] * fetched,
        out_specs=tuple(vspec(len(outs))),
        scratch_shapes=[pltpu.VMEM(*s) if isinstance(s, tuple) else s for s in scratch],
        compiler_params=params(),
        cost_estimate=cost(flops, moved),
        name=name,
    )(*operands)


def exchange(x, axis):
    size = lax.axis_size(axis)
    return [x] + [
        lax.ppermute(x, axis, [(i, (i + s) % size) for i in range(size)]) for s in range(1, size)
    ]


def from_sides(first, last, axis):
    size, at = lax.axis_size(axis), lax.axis_index(axis)
    if size == 2:
        got = lax.ppermute(jnp.where(at == 0, last, first), axis, [(0, 1), (1, 0)])
        nothing = jnp.zeros_like(got)
        return jnp.where(at == 1, got, nothing), jnp.where(at == 0, got, nothing)
    up = [(i, i + 1) for i in range(size - 1)]
    down = [(i + 1, i) for i in range(size - 1)]
    return lax.ppermute(last, axis, up), lax.ppermute(first, axis, down)


def on_device(feature, out_grad, bank, select, latent, affine_w, affine_b):
    rows, samples, size = (lax.axis_size(a) for a in ("rows", "samples", "chan"))
    row_at, sample_at, chan_at = (lax.axis_index(a) for a in ("rows", "samples", "chan"))
    _, ch, height, width = feature.shape
    out_ch, in_ch = bank.shape[2:]
    pixels, all_ch = height * width, ch * size
    sign = 1 - 2 * jnp.remainder(sample_at, 2)
    place = jnp.stack([sample_at, chan_at, row_at, sign]).astype(jnp.int32)
    flops = 2 * TAPS * ch * ch * size * pixels

    def along(x, pairs):
        whole = []
        for b in range(samples):
            for i, j in pairs:
                if b % 2:
                    i, j = size - 1 - i, size - 1 - j
                whole.append((b * size + i, b * size + j))
        return lax.ppermute(x, ("samples", "chan"), whole)

    cotan = out_grad[0].reshape(ch, pixels)
    first, second = [], []

    def step(number, x, y):
        first.append(along(x, [(i, i + 1) for i in range(number - 1, size - 1)]))
        second.append(along(y, [(i + 1, i) for i in range(size - number)]))

    step(1, cotan, cotan)

    small_rows = -(-(latent.shape[1] // in_ch + 2) // 8) * 8
    plain, small = call(
        plain_kernel,
        "plain",
        [((TAPS + 1, out_ch, in_ch), F32), ((small_rows, in_ch), F32)],
        select,
        latent,
        affine_b[None],
        affine_w,
        bank,
        fetched=5,
        scratch=[
            pltpu.SMEM(select.shape, jnp.int32),
            (latent.shape, F32),
            ((1, in_ch), F32),
            (affine_w.shape, F32),
            (bank.shape, F32),
            pltpu.SemaphoreType.DMA((5,)),
        ],
    )
    plains = exchange(plain, "rows")
    feature, cotan = lax.optimization_barrier((feature, cotan))
    feat = feature[0].reshape(ch, pixels)
    feat_before, feat_after = from_sides(feat[:, :width], feat[:, pixels - width :], "rows")
    extended = ((ch, (height + 2) * width), BF16)
    (feat,) = call(
        functools.partial(rows_kernel, height, width), "feat_rows", [extended], feat, feat_before, feat_after
    )
    feat, plain = lax.optimization_barrier((feat, plain))
    feat_end = lax.ppermute(feat, "chan", [(0, 1), (size - 1, size - 2)])
    message = ((ch, TAPS * ch), BF16)
    whole_mod, scale, *mods = call(
        functools.partial(blocks_kernel, rows, size),
        "mod_blocks",
        [((TAPS, out_ch, all_ch), BF16), ((out_ch, 128), F32)] + [message] * (size + 1),
        place,
        *plains,
        scalars=1,
        scratch=[((rows, TAPS, out_ch, in_ch), F32), ((size, *message[0]), BF16)],
    )
    own_grad, wide = call(
        functools.partial(own_grad_kernel, height, width),
        "own_grad",
        [message, ((3 * ch, (height + 2) * width), BF16)],
        cotan,
        feat,
        scratch=[((3, ch, 3 * ch), F32)],
        flops=flops // size,
    )
    first[0], second[0], plains, own_grad, wide = lax.optimization_barrier(
        (first[0], second[0], plains, own_grad, wide)
    )

    step(2, first[0], second[0])
    double = ((2 * ch, TAPS * ch), BF16)
    to_behind, to_ahead = call(
        functools.partial(near_grad_kernel, height, width),
        "near_grad",
        [double, double],
        first[0],
        second[0],
        wide,
        mods[size - 1],
        mods[1],
        scratch=[((2 * ch, pixels), BF16), ((3, 2 * ch, 3 * ch), F32)],
        flops=flops * 2 // size,
    )
    from_ahead = along(to_behind, [(i + 1, i) for i in range(size - 1)])
    first[1], second[1], feat_end, to_ahead, whole_mod = lax.optimization_barrier(
        (first[1], second[1], feat_end, to_ahead, whole_mod)
    )

    count = size - 3
    grad_others, middle, end_block = call(
        functools.partial(middle_grad_kernel, count, height, width),
        "middle_grad",
        [((count * ch, TAPS * ch), BF16), ((count * ch, pixels), BF16), ((ch, pixels), BF16)],
        *first[1:],
        *second[1:],
        wide,
        scratch=[((3, count * ch, 3 * ch), F32)],
        flops=flops // size,
    )
    (grad_end,) = call(
        functools.partial(end_grad_kernel, height, width),
        "end_grad",
        [message],
        end_block,
        feat_end,
        scratch=[((3 * ch, (height + 2) * width), BF16), ((3, ch, 3 * ch), F32)],
        flops=flops // size,
    )
    to_ahead, grad_others = lax.optimization_barrier((to_ahead, grad_others))
    from_behind = along(to_ahead, [(i, i + 1) for i in range(size - 1)])
    from_others = along(grad_others, [(i, (i + 2) % size) for i in range(size)])
    from_end = lax.ppermute(grad_end, "chan", [(1, size - 1), (size - 2, 0)])
    end_block, grad_end = lax.optimization_barrier((end_block, grad_end))
    far = lax.ppermute(end_block, "chan", [(1, 0), (size - 2, size - 1)])
    parts = call(
        functools.partial(collect_kernel, rows, size),
        "collect",
        [((TAPS + 1, out_ch, in_ch), BF16)] * rows,
        place,
        scale,
        whole_mod,
        own_grad,
        from_ahead,
        from_behind,
        from_others,
        from_end,
        scalars=1,
        scratch=[((size, *message[0]), F32), ((rows, TAPS, out_ch, in_ch), BF16)],
        flops=COLLECT_FLOPS,
    )
    parts, mods = lax.optimization_barrier((parts, mods))
    others = [along(mods[d], [(i, (i + d) % size) for i in range(size)]) for d in range(2, size - 1)]
    others.append(lax.ppermute(mods[size], "chan", [(0, size - 1), (size - 1, 0)]))
    parts = [parts[0]] + [
        lax.ppermute(parts[r], "rows", [(i, (i + r) % rows) for i in range(rows)])
        for r in range(1, rows)
    ]
    slots = TAPS + 1 - (-3 * small_rows // out_ch)
    (own,) = call(row_sum_kernel, "row_sum", [((slots, out_ch, in_ch), BF16)], scale, small, *parts)
    every = exchange(own, "samples")

    own, others, far = lax.optimization_barrier((own, others, far))
    main, before, after = call(
        functools.partial(input_grad_kernel, size, height, width),
        "input_grad",
        [((ch, pixels), F32), ((ch, width), F32), ((ch, width), F32)],
        place,
        cotan,
        first[0],
        second[0],
        middle,
        far,
        mods[0],
        from_behind,
        from_ahead,
        *others,
        scalars=1,
        scratch=[
            ((all_ch, pixels), BF16),
            ((TAPS * ch, all_ch), BF16),
            ((height + 2, 3 * ch, width), F32),
        ],
        flops=INPUT_FLOPS,
    )
    every, main, before, after = lax.optimization_barrier((every, main, before, after))
    from_above, from_below = from_sides(before, after, "rows")
    bank_grad, style_part, latents = call(
        functools.partial(bank_grad_kernel, samples, small_rows),
        "bank_grad",
        [(bank.shape, F32), ((samples, in_ch), F32), ((samples, latent.shape[1]), F32)],
        place,
        bank,
        *every,
        scalars=1,
        scratch=[((samples, slots, out_ch, in_ch), BF16)],
    )
    style_parts = exchange(style_part, "chan")
    edge = jnp.concatenate(
        [from_above[:, None], jnp.zeros((ch, height - 2, width), F32), from_below[:, None]], axis=1
    )
    feature_grad = (main.reshape(ch, height, width) + edge).astype(BF16)[None]
    style_parts, feature_grad = lax.optimization_barrier((style_parts, feature_grad))
    affine_w_grad, affine_b_grad = call(
        functools.partial(affine_kernel, samples, size),
        "affine",
        [(affine_w.shape, F32), ((1, in_ch), F32)],
        place,
        latents,
        *style_parts,
        scalars=1,
        scratch=[((size, samples, in_ch), F32)],
    )
    return (feature_grad, bank_grad, affine_w_grad, affine_b_grad[0])


def solution(mesh):
    return jax.shard_map(
        on_device,
        mesh=mesh,
        in_specs=(
            P("samples", "chan", "rows", None),
            P("samples", "chan", "rows", None),
            P(None, None, "chan", "rows"),
            P("samples", None),
            P("samples", None),
            P(None, "rows"),
            P("rows"),
        ),
        out_specs=(
            P("samples", "chan", "rows", None),
            P(None, None, "chan", "rows"),
            P(None, "rows"),
            P("rows"),
        ),
        check_vma=False,
    )
```

```python
import functools

import jax
import jax.numpy as jnp
from jax import lax
from jax.experimental import pallas as pl
from jax.experimental.pallas import tpu as pltpu
from jax.sharding import PartitionSpec as P

EPS = 1e-08
TAPS = 9
F32 = jnp.float32
BF16 = jnp.bfloat16
VMEM_LIMIT = 16 * 2**20
COLLECT_FLOPS = 6 * 10**9
INPUT_FLOPS = 2 * 10**9


def params():
    return pltpu.CompilerParams(vmem_limit_bytes=VMEM_LIMIT)


def vspec(n):
    return [pl.BlockSpec(memory_space=pltpu.VMEM)] * n


def sspec(n):
    return [pl.BlockSpec(memory_space=pltpu.SMEM)] * n


def cost(flops, moved):
    return pl.CostEstimate(flops=flops, bytes_accessed=moved, transcendentals=0)


def beside(pieces):
    return pieces[0] if len(pieces) == 1 else jnp.concatenate(pieces, axis=1)


def mixed(bank_ref, weights, tap):
    total = weights[0] * bank_ref[0, tap]
    for k in range(1, bank_ref.shape[0]):
        total = total + weights[k] * bank_ref[k, tap]
    return total


def plain_kernel(*refs):
    given, (plain_out, small), held, sems = refs[:5], refs[5:7], refs[7:12], refs[12]
    copies = [pltpu.make_async_copy(x, y, sems.at[n]) for n, (x, y) in enumerate(zip(given, held))]
    for copy in copies:
        copy.start()
    for copy in copies:
        copy.wait()
    select, latent, affine_b, affine_w, bank = held
    style = (
        jnp.dot(latent[...], affine_w[...], precision=lax.Precision.HIGHEST, preferred_element_type=F32)
        + affine_b[...]
    )
    filters, in_ch = bank.shape[0], bank.shape[3]
    weights = [select[0, k].astype(F32) for k in range(filters)]
    total = jnp.zeros(bank.shape[2:], F32)
    for tap in range(TAPS):
        plain = mixed(bank, weights, tap) * style
        plain_out[tap] = plain
        total = total + plain * plain
    plain_out[TAPS] = jnp.broadcast_to(jnp.sum(total, axis=1, keepdims=True), total.shape)
    small[...] = jnp.zeros(small.shape, F32)
    last = latent.shape[1] // in_ch
    for n in range(last):
        small[n : n + 1] = latent[:, n * in_ch : (n + 1) * in_ch]
    small[last : last + 1] = style
    lane = lax.broadcasted_iota(jnp.int32, (1, in_ch), 1)
    row = jnp.zeros((1, in_ch), F32)
    for k in range(filters):
        row = jnp.where(lane == k, weights[k], row)
    small[last + 1 : last + 2] = row


def blocks_kernel(rows, size, place, *refs):
    parts, (whole, scale_out), outs, (by_row, by_chan) = refs[:rows], refs[rows : rows + 2], refs[rows + 2 : -2], refs[-2:]
    row_at, chan_at, sign = place[2], place[1], place[3]
    energy = parts[0][TAPS]
    for part in parts[1:]:
        energy = energy + part[TAPS]
    scale = lax.rsqrt(energy[:, 0:1] + EPS)
    scale_out[...] = jnp.broadcast_to(scale, scale_out.shape)
    for r in range(rows):
        by_row[lax.rem(row_at - r + rows, rows)] = parts[r][0:TAPS]
    ch = whole.shape[2] // size
    taps = []
    for tap in range(TAPS):
        value = beside([by_row[r, tap] for r in range(rows)]) * scale
        whole[tap] = value.astype(BF16)
        taps.append(value)
    for z in range(size):
        by_chan[z] = beside([value[:, z * ch : (z + 1) * ch] for value in taps]).astype(BF16)
    for d in range(size):
        outs[d][...] = by_chan[lax.rem(chan_at + sign * d + size, size)]
    outs[size][...] = by_chan[size - 1 - chan_at]


def shifted(x, by):
    width = x.shape[1]
    lane = lax.broadcasted_iota(jnp.int32, x.shape, 1)
    moved = pltpu.roll(x, by % width, 1)
    return jnp.where(lane == (0 if by == 1 else width - 1), 0.0, moved)


def spread(wide, row, x):
    ch, width = x.shape
    wide[ch : 2 * ch, row * width : (row + 1) * width] = x
    x = x.astype(F32)
    wide[0:ch, row * width : (row + 1) * width] = shifted(x, 1).astype(BF16)
    wide[2 * ch : 3 * ch, row * width : (row + 1) * width] = shifted(x, -1).astype(BF16)


def rows_kernel(height, width, feat, feat_before, feat_after, out):
    out[:, 0:width] = feat_before[...]
    out[:, width : (height + 1) * width] = feat[...]
    out[:, (height + 1) * width :] = feat_after[...]


def tap_products(g_ref, wides, totals, height, width):
    for total in totals:
        total[...] = jnp.zeros(total.shape, F32)

    def body(row, _):
        g = g_ref[:, pl.ds(pl.multiple_of(row * width, width), width)]
        for wide, total in zip(wides, totals):
            for kh in range(3):
                x = wide[:, pl.ds(pl.multiple_of((row + kh) * width, width), width)]
                total[kh] += lax.dot_general(g, x, (((1,), (1,)), ((), ())), preferred_element_type=F32)
        return 0

    lax.fori_loop(0, height, body, 0)
    return [jnp.concatenate([total[kh] for kh in range(3)], axis=1).astype(BF16) for total in totals]


def near_grad_kernel(height, width, *refs):
    cotans, feat, mods, (own, behind, ahead), (wide, gathered, total) = refs[:3], refs[3], refs[4:6], refs[6:9], refs[9:]
    ch = feat.shape[0]
    for at, cotan in enumerate(cotans):
        gathered[at * ch : (at + 1) * ch] = cotan[...]
    for row in range(height + 2):
        spread(wide, row, feat[:, row * width : (row + 1) * width])
    (whole,) = tap_products(gathered, [wide], [total], height, width)
    own[...] = whole[0:ch]
    for at, (out, mod) in enumerate(zip((behind, ahead), mods)):
        out[0:ch] = whole[(at + 1) * ch : (at + 2) * ch]
        out[ch:] = mod[...]


def middle_grad_kernel(count, height, width, *refs):
    first, second, wide = refs[:count], refs[count : 2 * count], refs[2 * count]
    out, middle, end_block, total = refs[2 * count + 1 :]
    ch = end_block.shape[0]
    for at in range(count):
        middle[at * ch : (at + 1) * ch] = first[at][...] + second[count - 1 - at][...]
    end_block[...] = first[-1][...] + second[-1][...]
    (out[...],) = tap_products(middle, [wide], [total], height, width)


def end_grad_kernel(height, width, end_block, feat, out, wide, total):
    for row in range(height + 2):
        spread(wide, row, feat[:, row * width : (row + 1) * width])
    (out[...],) = tap_products(end_block, [wide], [total], height, width)


def input_grad_kernel(rows, size, height, width, place, cotan, first, second, middle, far, own_mod, behind, ahead, *refs):
    others, (main, before, after, gathered, taps_t, total) = refs[: size - 2], refs[size - 2 :]
    ch = main.shape[0]
    spot = jnp.where(place[3] > 0, place[1], size - 1 - place[1])
    gathered[0:ch] = cotan[...]
    gathered[ch : 2 * ch] = jnp.where(spot == 0, far[...], first[...])
    gathered[2 * ch : (size - 1) * ch] = middle[...]
    gathered[(size - 1) * ch :] = jnp.where(spot == size - 1, far[...], second[...])
    end_mod = others[-1][...]
    mods = [own_mod[...], jnp.where(spot == 0, end_mod, behind[ch:])]
    mods += [other[...] for other in others[:-1]]
    mods.append(jnp.where(spot == size - 1, end_mod, ahead[ch:]))
    every = jnp.concatenate([mod.astype(F32) for mod in mods], axis=0)
    taps_t[...] = every.T.astype(BF16)
    total[...] = jnp.zeros(total.shape, F32)

    def body(row, _):
        g = gathered[:, pl.ds(pl.multiple_of(row * width, width), width)]
        for kh in range(3):
            y = jnp.dot(taps_t[kh * 3 * ch : (kh + 1) * 3 * ch], g, preferred_element_type=F32)
            total[row + kh] += y
        return 0

    lax.fori_loop(0, height, body, 0)
    for row in range(height + 2):
        value = total[row, ch : 2 * ch]
        value = value + shifted(total[row, 0:ch], -1) + shifted(total[row, 2 * ch : 3 * ch], 1)
        if row == 0:
            before[...] = value
        elif row == height + 1:
            after[...] = jnp.where(place[2] == 1, before[...], value) if rows == 2 else value
        else:
            main[:, (row - 1) * width : row * width] = value


def split3(x):
    high = x.astype(BF16).astype(F32)
    mid = (x - high).astype(BF16).astype(F32)
    return high, mid, x - high - mid


def put_columns(out, columns):
    lane = lax.broadcasted_iota(jnp.int32, out.shape[1:], 1)
    last = jnp.zeros(out.shape[1:], F32)
    for n, column in enumerate(columns):
        for at, piece in enumerate(split3(column)):
            last = jnp.where(lane == 3 * n + at, piece, last)
    out[TAPS] = last.astype(BF16)


def get_column(last, n=0):
    last = last.astype(F32)
    return last[:, 3 * n : 3 * n + 1] + last[:, 3 * n + 1 : 3 * n + 2] + last[:, 3 * n + 2 : 3 * n + 3]


def collect_kernel(rows, size, place, scale, whole_mod, own, ahead, behind, others, end, *refs):
    outs, (by_chan, by_row) = refs[:rows], refs[rows:]
    chan_at, row_at, sign = place[1], place[2], place[3]
    ch = own.shape[0]
    by_chan[chan_at] = own[...].astype(F32)
    by_chan[lax.rem(chan_at + sign + size, size)] = ahead[0:ch].astype(F32)
    by_chan[lax.rem(chan_at - sign + size, size)] = behind[0:ch].astype(F32)
    for d in range(2, size - 1):
        value = others[(d - 2) * ch : (d - 1) * ch].astype(F32)
        by_chan[lax.rem(chan_at + sign * d + size, size)] = value
    by_chan[jnp.where(chan_at == 0, size - 1, 0)] += end[...].astype(F32)
    in_ch = outs[0].shape[2]
    product = jnp.zeros(whole_mod.shape[1:], F32)
    for tap in range(TAPS):
        value = beside([by_chan[z, :, tap * ch : (tap + 1) * ch] for z in range(size)])
        product = product + value * whole_mod[tap].astype(F32)
        for r in range(rows):
            by_row[r, tap] = value[:, r * in_ch : (r + 1) * in_ch].astype(BF16)
    fall = jnp.sum(product, axis=1, keepdims=True) * (scale[:, 0:1] * scale[:, 0:1])
    for r in range(rows):
        outs[r][0:TAPS] = by_row[lax.rem(row_at + r, rows)]
        put_columns(outs[r], [fall])


def row_sum_kernel(scale, small, *refs):
    parts, out = refs[:-1], refs[-1]
    fall = get_column(parts[0][TAPS])
    for part in parts[1:]:
        fall = fall + get_column(part[TAPS])
    for tap in range(TAPS):
        value = parts[0][tap].astype(F32)
        for part in parts[1:]:
            value = value + part[tap].astype(F32)
        out[tap] = value.astype(BF16)
    put_columns(out, [fall, scale[:, 0:1]])
    out_ch, in_ch = out.shape[1:]
    pieces = list(split3(small[...]))
    spare = (out.shape[0] - TAPS - 1) * out_ch - 3 * small.shape[0]
    if spare:
        pieces.append(jnp.zeros((spare, in_ch), F32))
    pieces = jnp.concatenate(pieces, axis=0).astype(BF16)
    for n in range(out.shape[0] - TAPS - 1):
        out[TAPS + 1 + n] = pieces[n * out_ch : (n + 1) * out_ch]


def bank_grad_kernel(samples, small_rows, place, bank, *refs):
    parts, (bank_out, style_grad, latents, held, bank_grad, sems) = refs[:samples], refs[samples:]
    copies = [pltpu.make_async_copy(bank_grad.at[:, tap], bank_out.at[:, tap], sems.at[tap]) for tap in range(TAPS)]
    for s in range(samples):
        held[partner(place[0], s, samples)] = parts[s][...]
    filters, in_ch = bank.shape[0], bank.shape[3]
    last = latents.shape[1] // in_ch
    sel, styles, scales, falls = [], [], [], []
    for b in range(samples):
        rows = jnp.concatenate([held[b, n].astype(F32) for n in range(TAPS + 1, held.shape[1])], axis=0)
        small = rows[:small_rows] + rows[small_rows : 2 * small_rows] + rows[2 * small_rows : 3 * small_rows]
        latents[b : b + 1] = beside([small[n : n + 1] for n in range(last)])
        styles.append(small[last : last + 1])
        sel.append([small[last + 1 : last + 2, k : k + 1] for k in range(filters)])
        falls.append(get_column(held[b, TAPS]))
        scales.append(get_column(held[b, TAPS], 1))
    sums = [jnp.zeros(bank.shape[2:], F32) for _ in range(samples)]
    for tap in range(TAPS):
        totals = [None] * filters
        for b in range(samples):
            kern = mixed(bank, sel[b], tap)
            plain_grad = held[b, tap].astype(F32) * scales[b] - kern * styles[b] * falls[b]
            sums[b] = sums[b] + plain_grad * kern
            kernel_grad = plain_grad * styles[b]
            for k in range(filters):
                term = sel[b][k] * kernel_grad
                totals[k] = term if totals[k] is None else totals[k] + term
        for k in range(filters):
            bank_grad[k, tap] = totals[k]
        copies[tap].start()
    for b in range(samples):
        value = jnp.sum(sums[b], axis=0, keepdims=True)
        style_grad[b : b + 1] = value
    for copy in copies:
        copy.wait()


def affine_kernel(samples, size, place, latents, *refs):
    parts, (w_grad, b_grad, held) = refs[:size], refs[size:]
    for d in range(size):
        held[lax.rem(place[1] - d + size, size)] = parts[d][...]
    style_grad = held[0]
    for z in range(1, size):
        style_grad = style_grad + held[z]
    high, mid, low = split3(latents[...])
    top, middle, bottom = split3(style_grad)
    w_grad[...] = lax.dot_general(
        jnp.concatenate([high, high, mid, high, mid, low], axis=0).astype(BF16),
        jnp.concatenate([top, middle, top, bottom, middle, top], axis=0).astype(BF16),
        (((0,), (0,)), ((), ())),
        preferred_element_type=F32,
    )
    bias = style_grad[0:1]
    for b in range(1, samples):
        bias = bias + style_grad[b : b + 1]
    b_grad[...] = bias


def call(kernel, name, outs, *operands, scalars=0, fetched=0, kept=0, scratch=(), flops=10**6):
    outs = tuple(jax.ShapeDtypeStruct(*o) for o in outs)
    moved = sum(o.size * o.dtype.itemsize for o in (*outs, *operands))
    return pl.pallas_call(
        kernel,
        out_shape=outs,
        in_specs=sspec(scalars)
        + vspec(len(operands) - scalars - fetched)
        + [pl.BlockSpec(memory_space=pltpu.HBM)] * fetched,
        out_specs=tuple([pl.BlockSpec(memory_space=pltpu.HBM)] * kept + vspec(len(outs) - kept)),
        scratch_shapes=[pltpu.VMEM(*s) if isinstance(s, tuple) else s for s in scratch],
        compiler_params=params(),
        cost_estimate=cost(flops, moved),
        name=name,
    )(*operands)


def partner(at, step, size):
    return at ^ step if size & (size - 1) == 0 else (at - step + size) % size


def exchange_pairs(x, axis):
    size = lax.axis_size(axis)
    got = {0: x}
    for step in sorted(range(1, size), key=lambda n: (n < 2, n)):
        got[step] = lax.ppermute(x, axis, [(partner(i, step, size), i) for i in range(size)])
    return [got[step] for step in range(size)]


def exchange(x, axis):
    size = lax.axis_size(axis)
    return [x] + [
        lax.ppermute(x, axis, [(i, (i + s) % size) for i in range(size)]) for s in range(1, size)
    ]


def from_sides(first, last, axis):
    size, at = lax.axis_size(axis), lax.axis_index(axis)
    if size == 2:
        edge = last if first is None else jnp.where(at == 0, last, first)
        got = lax.ppermute(edge, axis, [(0, 1), (1, 0)])
        nothing = jnp.zeros_like(got)
        return jnp.where(at == 1, got, nothing), jnp.where(at == 0, got, nothing)
    up = [(i, i + 1) for i in range(size - 1)]
    down = [(i + 1, i) for i in range(size - 1)]
    return lax.ppermute(last, axis, up), lax.ppermute(first, axis, down)


def on_device(feature, out_grad, bank, select, latent, affine_w, affine_b):
    rows, samples, size = (lax.axis_size(a) for a in ("rows", "samples", "chan"))
    row_at, sample_at, chan_at = (lax.axis_index(a) for a in ("rows", "samples", "chan"))
    _, ch, height, width = feature.shape
    out_ch, in_ch = bank.shape[2:]
    pixels, all_ch = height * width, ch * size
    sign = 1 - 2 * jnp.remainder(sample_at, 2)
    place = jnp.stack([sample_at, chan_at, row_at, sign]).astype(jnp.int32)
    flops = 2 * TAPS * ch * ch * size * pixels

    def along(x, pairs):
        whole = []
        for b in range(samples):
            for i, j in pairs:
                if b % 2:
                    i, j = size - 1 - i, size - 1 - j
                whole.append((b * size + i, b * size + j))
        return lax.ppermute(x, ("samples", "chan"), whole)

    cotan = out_grad[0].reshape(ch, pixels)
    first, second = [], []

    def step(number, x, y):
        first.append(along(x, [(i, i + 1) for i in range(number - 1, size - 1)]))
        second.append(along(y, [(i + 1, i) for i in range(size - number)]))

    step(1, cotan, cotan)

    small_rows = -(-(latent.shape[1] // in_ch + 2) // 8) * 8
    plain, small = call(
        plain_kernel,
        "plain",
        [((TAPS + 1, out_ch, in_ch), F32), ((small_rows, in_ch), F32)],
        select,
        latent,
        affine_b[None],
        affine_w,
        bank,
        fetched=5,
        scratch=[
            pltpu.SMEM(select.shape, jnp.int32),
            (latent.shape, F32),
            ((1, in_ch), F32),
            (affine_w.shape, F32),
            (bank.shape, F32),
            pltpu.SemaphoreType.DMA((5,)),
        ],
    )
    plains = exchange(plain, "rows")
    feature, cotan = lax.optimization_barrier((feature, cotan))
    feat = feature[0].reshape(ch, pixels)
    feat_before, feat_after = from_sides(feat[:, :width], feat[:, pixels - width :], "rows")
    extended = ((ch, (height + 2) * width), BF16)
    (feat,) = call(
        functools.partial(rows_kernel, height, width), "feat_rows", [extended], feat, feat_before, feat_after
    )
    feat, plain = lax.optimization_barrier((feat, plain))
    feat_end = lax.ppermute(feat, "chan", [(0, 1), (size - 1, size - 2)])
    message = ((ch, TAPS * ch), BF16)
    whole_mod, scale, *mods = call(
        functools.partial(blocks_kernel, rows, size),
        "mod_blocks",
        [((TAPS, out_ch, all_ch), BF16), ((out_ch, 128), F32)] + [message] * (size + 1),
        place,
        *plains,
        scalars=1,
        scratch=[((rows, TAPS, out_ch, in_ch), F32), ((size, *message[0]), BF16)],
    )
    first[0], second[0], plains = lax.optimization_barrier((first[0], second[0], plains))

    step(2, first[0], second[0])
    double = ((2 * ch, TAPS * ch), BF16)
    own_grad, to_behind, to_ahead, wide = call(
        functools.partial(near_grad_kernel, height, width),
        "near_grad",
        [message, double, double, ((3 * ch, (height + 2) * width), BF16)],
        cotan,
        first[0],
        second[0],
        feat,
        mods[size - 1],
        mods[1],
        scratch=[((3 * ch, pixels), BF16), ((3, 3 * ch, 3 * ch), F32)],
        flops=flops * 3 // size,
    )
    from_ahead = along(to_behind, [(i + 1, i) for i in range(size - 1)])
    from_behind = along(to_ahead, [(i, i + 1) for i in range(size - 1)])
    first[1], second[1], feat_end, wide, whole_mod = lax.optimization_barrier(
        (first[1], second[1], feat_end, wide, whole_mod)
    )

    count = size - 3
    grad_others, middle, end_block = call(
        functools.partial(middle_grad_kernel, count, height, width),
        "middle_grad",
        [((count * ch, TAPS * ch), BF16), ((count * ch, pixels), BF16), ((ch, pixels), BF16)],
        *first[1:],
        *second[1:],
        wide,
        scratch=[((3, count * ch, 3 * ch), F32)],
        flops=flops // size,
    )
    (grad_end,) = call(
        functools.partial(end_grad_kernel, height, width),
        "end_grad",
        [message],
        end_block,
        feat_end,
        scratch=[((3 * ch, (height + 2) * width), BF16), ((3, ch, 3 * ch), F32)],
        flops=flops // size,
    )
    from_others = along(grad_others, [(i, (i + 2) % size) for i in range(size)])
    from_end = lax.ppermute(grad_end, "chan", [(1, size - 1), (size - 2, 0)])
    end_block, grad_end = lax.optimization_barrier((end_block, grad_end))
    far = lax.ppermute(end_block, "chan", [(1, 0), (size - 2, size - 1)])
    parts = call(
        functools.partial(collect_kernel, rows, size),
        "collect",
        [((TAPS + 1, out_ch, in_ch), BF16)] * rows,
        place,
        scale,
        whole_mod,
        own_grad,
        from_ahead,
        from_behind,
        from_others,
        from_end,
        scalars=1,
        scratch=[((size, *message[0]), F32), ((rows, TAPS, out_ch, in_ch), BF16)],
        flops=COLLECT_FLOPS,
    )
    parts, mods = lax.optimization_barrier((parts, mods))
    others = [along(mods[d], [(i, (i + d) % size) for i in range(size)]) for d in range(2, size - 1)]
    others.append(lax.ppermute(mods[size], "chan", [(0, size - 1), (size - 1, 0)]))
    parts = [parts[0]] + [
        lax.ppermute(parts[r], "rows", [(i, (i + r) % rows) for i in range(rows)])
        for r in range(1, rows)
    ]
    slots = TAPS + 1 - (-3 * small_rows // out_ch)
    (own,) = call(row_sum_kernel, "row_sum", [((slots, out_ch, in_ch), BF16)], scale, small, *parts)
    every = exchange_pairs(own, "samples")

    own, others, far = lax.optimization_barrier((own, others, far))
    main, before, after = call(
        functools.partial(input_grad_kernel, rows, size, height, width),
        "input_grad",
        [((ch, pixels), F32), ((ch, width), F32), ((ch, width), F32)],
        place,
        cotan,
        first[0],
        second[0],
        middle,
        far,
        mods[0],
        from_behind,
        from_ahead,
        *others,
        scalars=1,
        scratch=[
            ((all_ch, pixels), BF16),
            ((TAPS * ch, all_ch), BF16),
            ((height + 2, 3 * ch, width), F32),
        ],
        flops=INPUT_FLOPS,
    )
    every, main, before, after = lax.optimization_barrier((every, main, before, after))
    from_above, from_below = from_sides(None if rows == 2 else before, after, "rows")
    bank_grad, style_part, latents = call(
        functools.partial(bank_grad_kernel, samples, small_rows),
        "bank_grad",
        [(bank.shape, F32), ((samples, in_ch), F32), ((samples, latent.shape[1]), F32)],
        place,
        bank,
        *every,
        scalars=1,
        scratch=[((samples, slots, out_ch, in_ch), BF16), (bank.shape, F32), pltpu.SemaphoreType.DMA((TAPS,))],
        kept=1,
    )
    style_parts = exchange(style_part, "chan")
    edge = jnp.concatenate(
        [from_above[:, None], jnp.zeros((ch, height - 2, width), F32), from_below[:, None]], axis=1
    )
    feature_grad = (main.reshape(ch, height, width) + edge).astype(BF16)[None]
    style_parts, feature_grad = lax.optimization_barrier((style_parts, feature_grad))
    affine_w_grad, affine_b_grad = call(
        functools.partial(affine_kernel, samples, size),
        "affine",
        [(affine_w.shape, F32), ((1, in_ch), F32)],
        place,
        latents,
        *style_parts,
        scalars=1,
        scratch=[((size, samples, in_ch), F32)],
    )
    return (feature_grad, bank_grad, affine_w_grad, affine_b_grad[0])


def solution(mesh):
    return jax.shard_map(
        on_device,
        mesh=mesh,
        in_specs=(
            P("samples", "chan", "rows", None),
            P("samples", "chan", "rows", None),
            P(None, None, "chan", "rows"),
            P("samples", None),
            P("samples", None),
            P(None, "rows"),
            P("rows"),
        ),
        out_specs=(
            P("samples", "chan", "rows", None),
            P(None, None, "chan", "rows"),
            P(None, "rows"),
            P("rows"),
        ),
        check_vma=False,
    )
```

```python
import functools

import jax
import jax.numpy as jnp
from jax import lax
from jax.experimental import pallas as pl
from jax.experimental.pallas import tpu as pltpu
from jax.sharding import PartitionSpec as P

EPS = 1e-08
TAPS = 9
F32 = jnp.float32
BF16 = jnp.bfloat16
VMEM_LIMIT = 16 * 2**20
COLLECT_FLOPS = 6 * 10**9
INPUT_FLOPS = 2 * 10**9


def params():
    return pltpu.CompilerParams(vmem_limit_bytes=VMEM_LIMIT)


def vspec(n):
    return [pl.BlockSpec(memory_space=pltpu.VMEM)] * n


def sspec(n):
    return [pl.BlockSpec(memory_space=pltpu.SMEM)] * n


def cost(flops, moved):
    return pl.CostEstimate(flops=flops, bytes_accessed=moved, transcendentals=0)


def beside(pieces):
    return pieces[0] if len(pieces) == 1 else jnp.concatenate(pieces, axis=1)


def mixed(bank_ref, weights, tap):
    total = weights[0] * bank_ref[0, tap]
    for k in range(1, bank_ref.shape[0]):
        total = total + weights[k] * bank_ref[k, tap]
    return total


def plain_kernel(*refs):
    given, (plain_out, small), held, sems = refs[:5], refs[5:7], refs[7:12], refs[12]
    copies = [pltpu.make_async_copy(x, y, sems.at[n]) for n, (x, y) in enumerate(zip(given, held))]
    for copy in copies:
        copy.start()
    for copy in copies:
        copy.wait()
    select, latent, affine_b, affine_w, bank = held
    style = (
        jnp.dot(latent[...], affine_w[...], precision=lax.Precision.HIGHEST, preferred_element_type=F32)
        + affine_b[...]
    )
    filters, in_ch = bank.shape[0], bank.shape[3]
    weights = [select[0, k].astype(F32) for k in range(filters)]
    total = jnp.zeros(bank.shape[2:], F32)
    for tap in range(TAPS):
        plain = mixed(bank, weights, tap) * style
        plain_out[tap] = plain
        total = total + plain * plain
    plain_out[TAPS] = jnp.broadcast_to(jnp.sum(total, axis=1, keepdims=True), total.shape)
    small[...] = jnp.zeros(small.shape, F32)
    last = latent.shape[1] // in_ch
    for n in range(last):
        small[n : n + 1] = latent[:, n * in_ch : (n + 1) * in_ch]
    small[last : last + 1] = style
    lane = lax.broadcasted_iota(jnp.int32, (1, in_ch), 1)
    row = jnp.zeros((1, in_ch), F32)
    for k in range(filters):
        row = jnp.where(lane == k, weights[k], row)
    small[last + 1 : last + 2] = row


def blocks_kernel(rows, size, place, *refs):
    parts, (whole, scale_out), outs, (by_row, by_chan) = refs[:rows], refs[rows : rows + 2], refs[rows + 2 : -2], refs[-2:]
    row_at, chan_at, sign = place[2], place[1], place[3]
    energy = parts[0][TAPS]
    for part in parts[1:]:
        energy = energy + part[TAPS]
    scale = lax.rsqrt(energy[:, 0:1] + EPS)
    scale_out[...] = jnp.broadcast_to(scale, scale_out.shape)
    for r in range(rows):
        by_row[lax.rem(row_at - r + rows, rows)] = parts[r][0:TAPS]
    ch = whole.shape[2] // size
    taps = []
    for tap in range(TAPS):
        value = beside([by_row[r, tap] for r in range(rows)]) * scale
        whole[tap] = value.astype(BF16)
        taps.append(value)
    for z in range(size):
        by_chan[z] = beside([value[:, z * ch : (z + 1) * ch] for value in taps]).astype(BF16)
    for d in range(size):
        outs[d][...] = by_chan[lax.rem(chan_at + sign * d + size, size)]
    outs[size][...] = by_chan[size - 1 - chan_at]


def shifted(x, by):
    width = x.shape[1]
    lane = lax.broadcasted_iota(jnp.int32, x.shape, 1)
    moved = pltpu.roll(x, by % width, 1)
    return jnp.where(lane == (0 if by == 1 else width - 1), 0.0, moved)


def spread(wide, row, x):
    ch, width = x.shape
    wide[ch : 2 * ch, row * width : (row + 1) * width] = x
    x = x.astype(F32)
    wide[0:ch, row * width : (row + 1) * width] = shifted(x, 1).astype(BF16)
    wide[2 * ch : 3 * ch, row * width : (row + 1) * width] = shifted(x, -1).astype(BF16)


def rows_kernel(height, width, feat, feat_before, feat_after, out):
    out[:, 0:width] = feat_before[...]
    out[:, width : (height + 1) * width] = feat[...]
    out[:, (height + 1) * width :] = feat_after[...]


def tap_products(g_ref, wides, totals, height, width):
    for total in totals:
        total[...] = jnp.zeros(total.shape, F32)

    def body(row, _):
        g = g_ref[:, pl.ds(pl.multiple_of(row * width, width), width)]
        for wide, total in zip(wides, totals):
            for kh in range(3):
                x = wide[:, pl.ds(pl.multiple_of((row + kh) * width, width), width)]
                total[kh] += lax.dot_general(g, x, (((1,), (1,)), ((), ())), preferred_element_type=F32)
        return 0

    lax.fori_loop(0, height, body, 0)
    return [jnp.concatenate([total[kh] for kh in range(3)], axis=1).astype(BF16) for total in totals]


def near_grad_kernel(height, width, *refs):
    cotans, feat, mods, (own, behind, ahead), (wide, gathered, total) = refs[:3], refs[3], refs[4:6], refs[6:9], refs[9:]
    ch = feat.shape[0]
    for at, cotan in enumerate(cotans):
        gathered[at * ch : (at + 1) * ch] = cotan[...]
    for row in range(height + 2):
        spread(wide, row, feat[:, row * width : (row + 1) * width])
    (whole,) = tap_products(gathered, [wide], [total], height, width)
    own[...] = whole[0:ch]
    for at, (out, mod) in enumerate(zip((behind, ahead), mods)):
        out[0:ch] = whole[(at + 1) * ch : (at + 2) * ch]
        out[ch:] = mod[...]


def middle_grad_kernel(count, height, width, *refs):
    first, second, wide = refs[:count], refs[count : 2 * count], refs[2 * count]
    out, middle, end_block, total = refs[2 * count + 1 :]
    ch = end_block.shape[0]
    for at in range(count):
        middle[at * ch : (at + 1) * ch] = first[at][...] + second[count - 1 - at][...]
    end_block[...] = first[-1][...] + second[-1][...]
    (out[...],) = tap_products(middle, [wide], [total], height, width)


def end_grad_kernel(height, width, end_block, feat, out, wide, total):
    for row in range(height + 2):
        spread(wide, row, feat[:, row * width : (row + 1) * width])
    (out[...],) = tap_products(end_block, [wide], [total], height, width)


def input_grad_kernel(rows, size, height, width, place, cotan, first, second, middle, far, own_mod, behind, ahead, *refs):
    others, (main, before, after, gathered, taps_t, total) = refs[: size - 2], refs[size - 2 :]
    ch = main.shape[0]
    spot = jnp.where(place[3] > 0, place[1], size - 1 - place[1])
    gathered[0:ch] = cotan[...]
    gathered[ch : 2 * ch] = jnp.where(spot == 0, far[...], first[...])
    gathered[2 * ch : (size - 1) * ch] = middle[...]
    gathered[(size - 1) * ch :] = jnp.where(spot == size - 1, far[...], second[...])
    end_mod = others[-1][...]
    mods = [own_mod[...], jnp.where(spot == 0, end_mod, behind[ch:])]
    mods += [other[...] for other in others[:-1]]
    mods.append(jnp.where(spot == size - 1, end_mod, ahead[ch:]))
    every = jnp.concatenate([mod.astype(F32) for mod in mods], axis=0)
    taps_t[...] = every.T.astype(BF16)
    total[...] = jnp.zeros(total.shape, F32)

    def body(row, _):
        g = gathered[:, pl.ds(pl.multiple_of(row * width, width), width)]
        for kh in range(3):
            y = jnp.dot(taps_t[kh * 3 * ch : (kh + 1) * 3 * ch], g, preferred_element_type=F32)
            total[row + kh] += y
        return 0

    lax.fori_loop(0, height, body, 0)
    for row in range(height + 2):
        value = total[row, ch : 2 * ch]
        value = value + shifted(total[row, 0:ch], -1) + shifted(total[row, 2 * ch : 3 * ch], 1)
        if row == 0:
            before[...] = value
        elif row == height + 1:
            after[...] = jnp.where(place[2] == 1, before[...], value) if rows == 2 else value
        else:
            main[:, (row - 1) * width : row * width] = value


def split3(x):
    high = x.astype(BF16).astype(F32)
    mid = (x - high).astype(BF16).astype(F32)
    return high, mid, x - high - mid


def put_columns(out, columns):
    lane = lax.broadcasted_iota(jnp.int32, out.shape[1:], 1)
    last = jnp.zeros(out.shape[1:], F32)
    for n, column in enumerate(columns):
        for at, piece in enumerate(split3(column)):
            last = jnp.where(lane == 3 * n + at, piece, last)
    out[TAPS] = last.astype(BF16)


def get_column(last, n=0):
    last = last.astype(F32)
    return last[:, 3 * n : 3 * n + 1] + last[:, 3 * n + 1 : 3 * n + 2] + last[:, 3 * n + 2 : 3 * n + 3]


def collect_kernel(rows, size, place, scale, whole_mod, own, ahead, behind, others, end, *refs):
    outs, (by_chan, by_row) = refs[:rows], refs[rows:]
    chan_at, row_at, sign = place[1], place[2], place[3]
    ch = own.shape[0]
    by_chan[chan_at] = own[...].astype(F32)
    by_chan[lax.rem(chan_at + sign + size, size)] = ahead[0:ch].astype(F32)
    by_chan[lax.rem(chan_at - sign + size, size)] = behind[0:ch].astype(F32)
    for d in range(2, size - 1):
        value = others[(d - 2) * ch : (d - 1) * ch].astype(F32)
        by_chan[lax.rem(chan_at + sign * d + size, size)] = value
    by_chan[jnp.where(chan_at == 0, size - 1, 0)] += end[...].astype(F32)
    in_ch = outs[0].shape[2]
    product = jnp.zeros(whole_mod.shape[1:], F32)
    for tap in range(TAPS):
        value = beside([by_chan[z, :, tap * ch : (tap + 1) * ch] for z in range(size)])
        product = product + value * whole_mod[tap].astype(F32)
        for r in range(rows):
            by_row[r, tap] = value[:, r * in_ch : (r + 1) * in_ch].astype(BF16)
    fall = jnp.sum(product, axis=1, keepdims=True) * (scale[:, 0:1] * scale[:, 0:1])
    for r in range(rows):
        outs[r][0:TAPS] = by_row[lax.rem(row_at + r, rows)]
        put_columns(outs[r], [fall])


def row_sum_kernel(scale, small, *refs):
    parts, out = refs[:-1], refs[-1]
    fall = get_column(parts[0][TAPS])
    for part in parts[1:]:
        fall = fall + get_column(part[TAPS])
    for tap in range(TAPS):
        value = parts[0][tap].astype(F32)
        for part in parts[1:]:
            value = value + part[tap].astype(F32)
        out[tap] = value.astype(BF16)
    put_columns(out, [fall, scale[:, 0:1]])
    out_ch, in_ch = out.shape[1:]
    pieces = list(split3(small[...]))
    spare = (out.shape[0] - TAPS - 1) * out_ch - 3 * small.shape[0]
    if spare:
        pieces.append(jnp.zeros((spare, in_ch), F32))
    pieces = jnp.concatenate(pieces, axis=0).astype(BF16)
    for n in range(out.shape[0] - TAPS - 1):
        out[TAPS + 1 + n] = pieces[n * out_ch : (n + 1) * out_ch]


def bank_grad_kernel(samples, small_rows, place, bank, *refs):
    parts, (bank_out, style_grad, latents, held, bank_grad, sems) = refs[:samples], refs[samples:]
    copies = [pltpu.make_async_copy(bank_grad.at[:, tap], bank_out.at[:, tap], sems.at[tap]) for tap in range(TAPS)]
    for part, step in zip(parts, steps_of(samples)):
        held[partner(place[0], step, samples)] = part[...]
    filters, in_ch = bank.shape[0], bank.shape[3]
    last = latents.shape[1] // in_ch
    sel, styles, scales, falls = [], [], [], []
    for b in range(samples):
        rows = jnp.concatenate([held[b, n].astype(F32) for n in range(TAPS + 1, held.shape[1])], axis=0)
        small = rows[:small_rows] + rows[small_rows : 2 * small_rows] + rows[2 * small_rows : 3 * small_rows]
        latents[b : b + 1] = beside([small[n : n + 1] for n in range(last)])
        styles.append(small[last : last + 1])
        sel.append([small[last + 1 : last + 2, k : k + 1] for k in range(filters)])
        falls.append(get_column(held[b, TAPS]))
        scales.append(get_column(held[b, TAPS], 1))
    sums = [jnp.zeros(bank.shape[2:], F32) for _ in range(samples)]
    for tap in range(TAPS):
        totals = [None] * filters
        for b in range(samples):
            kern = mixed(bank, sel[b], tap)
            plain_grad = held[b, tap].astype(F32) * scales[b] - kern * styles[b] * falls[b]
            sums[b] = sums[b] + plain_grad * kern
            kernel_grad = plain_grad * styles[b]
            for k in range(filters):
                term = sel[b][k] * kernel_grad
                totals[k] = term if totals[k] is None else totals[k] + term
        for k in range(filters):
            bank_grad[k, tap] = totals[k]
        copies[tap].start()
    for b in range(samples):
        value = jnp.sum(sums[b], axis=0, keepdims=True)
        style_grad[b : b + 1] = value
    for copy in copies:
        copy.wait()


def affine_kernel(samples, latents, *refs):
    parts, (w_grad, b_grad) = refs[:-2], refs[-2:]
    style_grad = parts[0][...]
    for part in parts[1:]:
        style_grad = style_grad + part[...]
    high, mid, low = split3(latents[...])
    top, middle, bottom = split3(style_grad)
    w_grad[...] = lax.dot_general(
        jnp.concatenate([high, high, mid, high, mid, low], axis=0).astype(BF16),
        jnp.concatenate([top, middle, top, bottom, middle, top], axis=0).astype(BF16),
        (((0,), (0,)), ((), ())),
        preferred_element_type=F32,
    )
    bias = style_grad[0:1]
    for b in range(1, samples):
        bias = bias + style_grad[b : b + 1]
    b_grad[...] = bias


def call(kernel, name, outs, *operands, scalars=0, fetched=0, kept=0, scratch=(), flops=10**6):
    outs = tuple(jax.ShapeDtypeStruct(*o) for o in outs)
    moved = sum(o.size * o.dtype.itemsize for o in (*outs, *operands))
    return pl.pallas_call(
        kernel,
        out_shape=outs,
        in_specs=sspec(scalars)
        + vspec(len(operands) - scalars - fetched)
        + [pl.BlockSpec(memory_space=pltpu.HBM)] * fetched,
        out_specs=tuple([pl.BlockSpec(memory_space=pltpu.HBM)] * kept + vspec(len(outs) - kept)),
        scratch_shapes=[pltpu.VMEM(*s) if isinstance(s, tuple) else s for s in scratch],
        compiler_params=params(),
        cost_estimate=cost(flops, moved),
        name=name,
    )(*operands)


def partner(at, step, size):
    return at ^ step if size & (size - 1) == 0 else (at - step + size) % size


def steps_of(size):
    return [0] + sorted(range(1, size), key=lambda n: (n < 2, n))


def exchange_pairs(x, axis):
    size = lax.axis_size(axis)
    return [x] + [
        lax.ppermute(x, axis, [(partner(i, step, size), i) for i in range(size)]) for step in steps_of(size)[1:]
    ]


def exchange(x, axis):
    size = lax.axis_size(axis)
    return [x] + [
        lax.ppermute(x, axis, [(i, (i + s) % size) for i in range(size)]) for s in range(1, size)
    ]


def halves_of_sum(x, axis):
    size = lax.axis_size(axis)
    if size & (size - 1):
        return [lax.psum(x, axis)]
    step, parts = 1, [x]
    while step < size:
        x = sum(parts[1:], parts[0])
        parts = [x, lax.ppermute(x, axis, [(i, i ^ step) for i in range(size)])]
        step *= 2
    return parts


def from_sides(first, last, axis):
    size, at = lax.axis_size(axis), lax.axis_index(axis)
    if size == 2:
        edge = last if first is None else jnp.where(at == 0, last, first)
        got = lax.ppermute(edge, axis, [(0, 1), (1, 0)])
        nothing = jnp.zeros_like(got)
        return jnp.where(at == 1, got, nothing), jnp.where(at == 0, got, nothing)
    up = [(i, i + 1) for i in range(size - 1)]
    down = [(i + 1, i) for i in range(size - 1)]
    return lax.ppermute(last, axis, up), lax.ppermute(first, axis, down)


def on_device(feature, out_grad, bank, select, latent, affine_w, affine_b):
    rows, samples, size = (lax.axis_size(a) for a in ("rows", "samples", "chan"))
    row_at, sample_at, chan_at = (lax.axis_index(a) for a in ("rows", "samples", "chan"))
    _, ch, height, width = feature.shape
    out_ch, in_ch = bank.shape[2:]
    pixels, all_ch = height * width, ch * size
    sign = 1 - 2 * jnp.remainder(sample_at, 2)
    place = jnp.stack([sample_at, chan_at, row_at, sign]).astype(jnp.int32)
    flops = 2 * TAPS * ch * ch * size * pixels

    def along(x, pairs):
        whole = []
        for b in range(samples):
            for i, j in pairs:
                if b % 2:
                    i, j = size - 1 - i, size - 1 - j
                whole.append((b * size + i, b * size + j))
        return lax.ppermute(x, ("samples", "chan"), whole)

    cotan = out_grad[0].reshape(ch, pixels)
    first, second = [], []

    def step(number, x, y):
        first.append(along(x, [(i, i + 1) for i in range(number - 1, size - 1)]))
        second.append(along(y, [(i + 1, i) for i in range(size - number)]))

    step(1, cotan, cotan)

    small_rows = -(-(latent.shape[1] // in_ch + 2) // 8) * 8
    plain, small = call(
        plain_kernel,
        "plain",
        [((TAPS + 1, out_ch, in_ch), F32), ((small_rows, in_ch), F32)],
        select,
        latent,
        affine_b[None],
        affine_w,
        bank,
        fetched=5,
        scratch=[
            pltpu.SMEM(select.shape, jnp.int32),
            (latent.shape, F32),
            ((1, in_ch), F32),
            (affine_w.shape, F32),
            (bank.shape, F32),
            pltpu.SemaphoreType.DMA((5,)),
        ],
    )
    plains = exchange(plain, "rows")
    feature, cotan = lax.optimization_barrier((feature, cotan))
    feat = feature[0].reshape(ch, pixels)
    feat_before, feat_after = from_sides(feat[:, :width], feat[:, pixels - width :], "rows")
    extended = ((ch, (height + 2) * width), BF16)
    (feat,) = call(
        functools.partial(rows_kernel, height, width), "feat_rows", [extended], feat, feat_before, feat_after
    )
    feat, plain = lax.optimization_barrier((feat, plain))
    feat_end = lax.ppermute(feat, "chan", [(0, 1), (size - 1, size - 2)])
    message = ((ch, TAPS * ch), BF16)
    whole_mod, scale, *mods = call(
        functools.partial(blocks_kernel, rows, size),
        "mod_blocks",
        [((TAPS, out_ch, all_ch), BF16), ((out_ch, 128), F32)] + [message] * (size + 1),
        place,
        *plains,
        scalars=1,
        scratch=[((rows, TAPS, out_ch, in_ch), F32), ((size, *message[0]), BF16)],
    )
    first[0], second[0], plains = lax.optimization_barrier((first[0], second[0], plains))

    step(2, first[0], second[0])
    double = ((2 * ch, TAPS * ch), BF16)
    own_grad, to_behind, to_ahead, wide = call(
        functools.partial(near_grad_kernel, height, width),
        "near_grad",
        [message, double, double, ((3 * ch, (height + 2) * width), BF16)],
        cotan,
        first[0],
        second[0],
        feat,
        mods[size - 1],
        mods[1],
        scratch=[((3 * ch, pixels), BF16), ((3, 3 * ch, 3 * ch), F32)],
        flops=flops * 3 // size,
    )
    from_ahead = along(to_behind, [(i + 1, i) for i in range(size - 1)])
    from_behind = along(to_ahead, [(i, i + 1) for i in range(size - 1)])
    first[1], second[1], feat_end, wide, whole_mod = lax.optimization_barrier(
        (first[1], second[1], feat_end, wide, whole_mod)
    )

    count = size - 3
    grad_others, middle, end_block = call(
        functools.partial(middle_grad_kernel, count, height, width),
        "middle_grad",
        [((count * ch, TAPS * ch), BF16), ((count * ch, pixels), BF16), ((ch, pixels), BF16)],
        *first[1:],
        *second[1:],
        wide,
        scratch=[((3, count * ch, 3 * ch), F32)],
        flops=flops // size,
    )
    (grad_end,) = call(
        functools.partial(end_grad_kernel, height, width),
        "end_grad",
        [message],
        end_block,
        feat_end,
        scratch=[((3 * ch, (height + 2) * width), BF16), ((3, ch, 3 * ch), F32)],
        flops=flops // size,
    )
    from_others = along(grad_others, [(i, (i + 2) % size) for i in range(size)])
    from_end = lax.ppermute(grad_end, "chan", [(1, size - 1), (size - 2, 0)])
    end_block, grad_end = lax.optimization_barrier((end_block, grad_end))
    far = lax.ppermute(end_block, "chan", [(1, 0), (size - 2, size - 1)])
    parts = call(
        functools.partial(collect_kernel, rows, size),
        "collect",
        [((TAPS + 1, out_ch, in_ch), BF16)] * rows,
        place,
        scale,
        whole_mod,
        own_grad,
        from_ahead,
        from_behind,
        from_others,
        from_end,
        scalars=1,
        scratch=[((size, *message[0]), F32), ((rows, TAPS, out_ch, in_ch), BF16)],
        flops=COLLECT_FLOPS,
    )
    parts, mods = lax.optimization_barrier((parts, mods))
    others = [along(mods[d], [(i, (i + d) % size) for i in range(size)]) for d in range(2, size - 1)]
    others.append(lax.ppermute(mods[size], "chan", [(0, size - 1), (size - 1, 0)]))
    parts = [parts[0]] + [
        lax.ppermute(parts[r], "rows", [(i, (i + r) % rows) for i in range(rows)])
        for r in range(1, rows)
    ]
    slots = TAPS + 1 - (-3 * small_rows // out_ch)
    (own,) = call(row_sum_kernel, "row_sum", [((slots, out_ch, in_ch), BF16)], scale, small, *parts)
    every = exchange_pairs(own, "samples")

    own, others, far = lax.optimization_barrier((own, others, far))
    main, before, after = call(
        functools.partial(input_grad_kernel, rows, size, height, width),
        "input_grad",
        [((ch, pixels), F32), ((ch, width), F32), ((ch, width), F32)],
        place,
        cotan,
        first[0],
        second[0],
        middle,
        far,
        mods[0],
        from_behind,
        from_ahead,
        *others,
        scalars=1,
        scratch=[
            ((all_ch, pixels), BF16),
            ((TAPS * ch, all_ch), BF16),
            ((height + 2, 3 * ch, width), F32),
        ],
        flops=INPUT_FLOPS,
    )
    every, main, before, after = lax.optimization_barrier((every, main, before, after))
    from_above, from_below = from_sides(None if rows == 2 else before, after, "rows")
    bank_grad, style_part, latents = call(
        functools.partial(bank_grad_kernel, samples, small_rows),
        "bank_grad",
        [(bank.shape, F32), ((samples, in_ch), F32), ((samples, latent.shape[1]), F32)],
        place,
        bank,
        *every,
        scalars=1,
        scratch=[((samples, slots, out_ch, in_ch), BF16), (bank.shape, F32), pltpu.SemaphoreType.DMA((TAPS,))],
        kept=1,
    )
    style_parts = halves_of_sum(style_part, "chan")
    edge = jnp.concatenate(
        [from_above[:, None], jnp.zeros((ch, height - 2, width), F32), from_below[:, None]], axis=1
    )
    feature_grad = (main.reshape(ch, height, width) + edge).astype(BF16)[None]
    style_parts, feature_grad = lax.optimization_barrier((style_parts, feature_grad))
    affine_w_grad, affine_b_grad = call(
        functools.partial(affine_kernel, samples),
        "affine",
        [(affine_w.shape, F32), ((1, in_ch), F32)],
        latents,
        *style_parts,
    )
    return (feature_grad, bank_grad, affine_w_grad, affine_b_grad[0])


def solution(mesh):
    return jax.shard_map(
        on_device,
        mesh=mesh,
        in_specs=(
            P("samples", "chan", "rows", None),
            P("samples", "chan", "rows", None),
            P(None, None, "chan", "rows"),
            P("samples", None),
            P("samples", None),
            P(None, "rows"),
            P("rows"),
        ),
        out_specs=(
            P("samples", "chan", "rows", None),
            P(None, None, "chan", "rows"),
            P(None, "rows"),
            P("rows"),
        ),
        check_vma=False,
    )
```

```python
import functools

import jax
import jax.numpy as jnp
from jax import lax
from jax.experimental import pallas as pl
from jax.experimental.pallas import tpu as pltpu
from jax.sharding import PartitionSpec as P

EPS = 1e-08
TAPS = 9
F32 = jnp.float32
BF16 = jnp.bfloat16
VMEM_LIMIT = 16 * 2**20
COLLECT_FLOPS = 6 * 10**9
INPUT_FLOPS = 2 * 10**9


def params():
    return pltpu.CompilerParams(vmem_limit_bytes=VMEM_LIMIT)


def vspec(n):
    return [pl.BlockSpec(memory_space=pltpu.VMEM)] * n


def sspec(n):
    return [pl.BlockSpec(memory_space=pltpu.SMEM)] * n


def cost(flops, moved):
    return pl.CostEstimate(flops=flops, bytes_accessed=moved, transcendentals=0)


def beside(pieces):
    return pieces[0] if len(pieces) == 1 else jnp.concatenate(pieces, axis=1)


def mixed(bank_ref, weights, tap):
    total = weights[0] * bank_ref[0, tap]
    for k in range(1, bank_ref.shape[0]):
        total = total + weights[k] * bank_ref[k, tap]
    return total


def plain_kernel(*refs):
    given, (plain_out, small), held, sems = refs[:5], refs[5:7], refs[7:12], refs[12]
    copies = [pltpu.make_async_copy(x, y, sems.at[n]) for n, (x, y) in enumerate(zip(given, held))]
    for copy in copies:
        copy.start()
    for copy in copies:
        copy.wait()
    select, latent, affine_b, affine_w, bank = held
    style = (
        jnp.dot(latent[...], affine_w[...], precision=lax.Precision.HIGHEST, preferred_element_type=F32)
        + affine_b[...]
    )
    filters, in_ch = bank.shape[0], bank.shape[3]
    weights = [select[0, k].astype(F32) for k in range(filters)]
    total = jnp.zeros(bank.shape[2:], F32)
    for tap in range(TAPS):
        plain = mixed(bank, weights, tap) * style
        plain_out[tap] = plain
        total = total + plain * plain
    plain_out[TAPS] = jnp.broadcast_to(jnp.sum(total, axis=1, keepdims=True), total.shape)
    small[...] = jnp.zeros(small.shape, F32)
    last = latent.shape[1] // in_ch
    for n in range(last):
        small[n : n + 1] = latent[:, n * in_ch : (n + 1) * in_ch]
    small[last : last + 1] = style
    lane = lax.broadcasted_iota(jnp.int32, (1, in_ch), 1)
    row = jnp.zeros((1, in_ch), F32)
    for k in range(filters):
        row = jnp.where(lane == k, weights[k], row)
    small[last + 1 : last + 2] = row


def blocks_kernel(rows, size, place, *refs):
    parts, (whole, scale_out), outs, (by_row, by_chan) = refs[:rows], refs[rows : rows + 2], refs[rows + 2 : -2], refs[-2:]
    row_at, chan_at, sign = place[2], place[1], place[3]
    energy = parts[0][TAPS]
    for part in parts[1:]:
        energy = energy + part[TAPS]
    scale = lax.rsqrt(energy[:, 0:1] + EPS)
    scale_out[...] = jnp.broadcast_to(scale, scale_out.shape)
    for r in range(rows):
        by_row[lax.rem(row_at - r + rows, rows)] = parts[r][0:TAPS]
    ch = whole.shape[2] // size
    taps = []
    for tap in range(TAPS):
        value = beside([by_row[r, tap] for r in range(rows)]) * scale
        whole[tap] = value.astype(BF16)
        taps.append(value)
    for z in range(size):
        by_chan[z] = beside([value[:, z * ch : (z + 1) * ch] for value in taps]).astype(BF16)
    for d in range(size):
        outs[d][...] = by_chan[lax.rem(chan_at + sign * d + size, size)]
    outs[size][...] = by_chan[size - 1 - chan_at]


def shifted(x, by):
    width = x.shape[1]
    lane = lax.broadcasted_iota(jnp.int32, x.shape, 1)
    moved = pltpu.roll(x, by % width, 1)
    return jnp.where(lane == (0 if by == 1 else width - 1), 0.0, moved)


def spread(wide, row, x):
    ch, width = x.shape
    wide[ch : 2 * ch, row * width : (row + 1) * width] = x
    x = x.astype(F32)
    wide[0:ch, row * width : (row + 1) * width] = shifted(x, 1).astype(BF16)
    wide[2 * ch : 3 * ch, row * width : (row + 1) * width] = shifted(x, -1).astype(BF16)


def rows_kernel(height, width, feat, feat_before, feat_after, out):
    out[:, 0:width] = feat_before[...]
    out[:, width : (height + 1) * width] = feat[...]
    out[:, (height + 1) * width :] = feat_after[...]


def tap_products(g_ref, wides, totals, height, width):
    for total in totals:
        total[...] = jnp.zeros(total.shape, F32)

    def body(row, _):
        g = g_ref[:, pl.ds(pl.multiple_of(row * width, width), width)]
        for wide, total in zip(wides, totals):
            for kh in range(3):
                x = wide[:, pl.ds(pl.multiple_of((row + kh) * width, width), width)]
                total[kh] += lax.dot_general(g, x, (((1,), (1,)), ((), ())), preferred_element_type=F32)
        return 0

    lax.fori_loop(0, height, body, 0)
    return [jnp.concatenate([total[kh] for kh in range(3)], axis=1).astype(BF16) for total in totals]


def near_grad_kernel(height, width, *refs):
    cotans, feat, mods, (own, behind, ahead), (wide, gathered, total) = refs[:3], refs[3], refs[4:6], refs[6:9], refs[9:]
    ch = feat.shape[0]
    for at, cotan in enumerate(cotans):
        gathered[at * ch : (at + 1) * ch] = cotan[...]
    for row in range(height + 2):
        spread(wide, row, feat[:, row * width : (row + 1) * width])
    (whole,) = tap_products(gathered, [wide], [total], height, width)
    own[...] = whole[0:ch]
    for at, (out, mod) in enumerate(zip((behind, ahead), mods)):
        out[0:ch] = whole[(at + 1) * ch : (at + 2) * ch]
        out[ch:] = mod[...]


def middle_grad_kernel(count, height, width, *refs):
    first, second, wide, mods = refs[:count], refs[count : 2 * count], refs[2 * count], refs[2 * count + 1 : 3 * count + 1]
    out, middle, end_block, total = refs[3 * count + 1 :]
    ch = end_block.shape[0]
    for at in range(count):
        middle[at * ch : (at + 1) * ch] = first[at][...] + second[count - 1 - at][...]
    end_block[...] = first[-1][...] + second[-1][...]
    (out[0 : count * ch],) = tap_products(middle, [wide], [total], height, width)
    for at, mod in enumerate(mods):
        out[(count + at) * ch : (count + at + 1) * ch] = mod[...]


def end_grad_kernel(height, width, end_block, feat, out, wide, total):
    for row in range(height + 2):
        spread(wide, row, feat[:, row * width : (row + 1) * width])
    (out[...],) = tap_products(end_block, [wide], [total], height, width)


def input_grad_kernel(rows, size, height, width, place, cotan, first, second, middle, far, own_mod, behind, ahead, others, end_mod, *refs):
    main, before, after, gathered, taps_t, total = refs
    ch = main.shape[0]
    spot = jnp.where(place[3] > 0, place[1], size - 1 - place[1])
    gathered[0:ch] = cotan[...]
    gathered[ch : 2 * ch] = jnp.where(spot == 0, far[...], first[...])
    gathered[2 * ch : (size - 1) * ch] = middle[...]
    gathered[(size - 1) * ch :] = jnp.where(spot == size - 1, far[...], second[...])
    mods = [own_mod[...], jnp.where(spot == 0, end_mod[...], behind[ch:])]
    mods.append(others[(size - 3) * ch :])
    mods.append(jnp.where(spot == size - 1, end_mod[...], ahead[ch:]))
    every = jnp.concatenate([mod.astype(F32) for mod in mods], axis=0)
    taps_t[...] = every.T.astype(BF16)
    total[...] = jnp.zeros(total.shape, F32)

    def body(row, _):
        g = gathered[:, pl.ds(pl.multiple_of(row * width, width), width)]
        for kh in range(3):
            y = jnp.dot(taps_t[kh * 3 * ch : (kh + 1) * 3 * ch], g, preferred_element_type=F32)
            total[row + kh] += y
        return 0

    lax.fori_loop(0, height, body, 0)
    for row in range(height + 2):
        value = total[row, ch : 2 * ch]
        value = value + shifted(total[row, 0:ch], -1) + shifted(total[row, 2 * ch : 3 * ch], 1)
        if row == 0:
            before[...] = value
        elif row == height + 1:
            after[...] = jnp.where(place[2] == 1, before[...], value) if rows == 2 else value
        else:
            main[:, (row - 1) * width : row * width] = value


def split3(x):
    high = x.astype(BF16).astype(F32)
    mid = (x - high).astype(BF16).astype(F32)
    return high, mid, x - high - mid


def put_columns(out, columns):
    lane = lax.broadcasted_iota(jnp.int32, out.shape[1:], 1)
    last = jnp.zeros(out.shape[1:], F32)
    for n, column in enumerate(columns):
        for at, piece in enumerate(split3(column)):
            last = jnp.where(lane == 3 * n + at, piece, last)
    out[TAPS] = last.astype(BF16)


def get_column(last, n=0):
    last = last.astype(F32)
    return last[:, 3 * n : 3 * n + 1] + last[:, 3 * n + 1 : 3 * n + 2] + last[:, 3 * n + 2 : 3 * n + 3]


def collect_kernel(rows, size, place, scale, whole_mod, own, ahead, behind, others, end, *refs):
    outs, (by_chan, by_row) = refs[:rows], refs[rows:]
    chan_at, row_at, sign = place[1], place[2], place[3]
    ch = own.shape[0]
    by_chan[chan_at] = own[...].astype(F32)
    by_chan[lax.rem(chan_at + sign + size, size)] = ahead[0:ch].astype(F32)
    by_chan[lax.rem(chan_at - sign + size, size)] = behind[0:ch].astype(F32)
    for d in range(2, size - 1):
        value = others[(d - 2) * ch : (d - 1) * ch].astype(F32)
        by_chan[lax.rem(chan_at + sign * d + size, size)] = value
    by_chan[jnp.where(chan_at == 0, size - 1, 0)] += end[...].astype(F32)
    in_ch = outs[0].shape[2]
    product = jnp.zeros(whole_mod.shape[1:], F32)
    for tap in range(TAPS):
        value = beside([by_chan[z, :, tap * ch : (tap + 1) * ch] for z in range(size)])
        product = product + value * whole_mod[tap].astype(F32)
        for r in range(rows):
            by_row[r, tap] = value[:, r * in_ch : (r + 1) * in_ch].astype(BF16)
    fall = jnp.sum(product, axis=1, keepdims=True) * (scale[:, 0:1] * scale[:, 0:1])
    for r in range(rows):
        outs[r][0:TAPS] = by_row[lax.rem(row_at + r, rows)]
        put_columns(outs[r], [fall])


def row_sum_kernel(scale, small, *refs):
    parts, out = refs[:-1], refs[-1]
    fall = get_column(parts[0][TAPS])
    for part in parts[1:]:
        fall = fall + get_column(part[TAPS])
    for tap in range(TAPS):
        value = parts[0][tap].astype(F32)
        for part in parts[1:]:
            value = value + part[tap].astype(F32)
        out[tap] = value.astype(BF16)
    put_columns(out, [fall, scale[:, 0:1]])
    out_ch, in_ch = out.shape[1:]
    pieces = list(split3(small[...]))
    spare = (out.shape[0] - TAPS - 1) * out_ch - 3 * small.shape[0]
    if spare:
        pieces.append(jnp.zeros((spare, in_ch), F32))
    pieces = jnp.concatenate(pieces, axis=0).astype(BF16)
    for n in range(out.shape[0] - TAPS - 1):
        out[TAPS + 1 + n] = pieces[n * out_ch : (n + 1) * out_ch]


def bank_grad_kernel(samples, small_rows, place, bank, *refs):
    parts, (bank_out, style_grad, latents, held, bank_grad, sems) = refs[:samples], refs[samples:]
    copies = [pltpu.make_async_copy(bank_grad.at[:, tap], bank_out.at[:, tap], sems.at[tap]) for tap in range(TAPS)]
    for part, step in zip(parts, steps_of(samples)):
        held[partner(place[0], step, samples)] = part[...]
    filters, in_ch = bank.shape[0], bank.shape[3]
    last = latents.shape[1] // in_ch
    sel, styles, scales, falls = [], [], [], []
    for b in range(samples):
        rows = jnp.concatenate([held[b, n].astype(F32) for n in range(TAPS + 1, held.shape[1])], axis=0)
        small = rows[:small_rows] + rows[small_rows : 2 * small_rows] + rows[2 * small_rows : 3 * small_rows]
        latents[b : b + 1] = beside([small[n : n + 1] for n in range(last)])
        styles.append(small[last : last + 1])
        sel.append([small[last + 1 : last + 2, k : k + 1] for k in range(filters)])
        falls.append(get_column(held[b, TAPS]))
        scales.append(get_column(held[b, TAPS], 1))
    sums = [jnp.zeros(bank.shape[2:], F32) for _ in range(samples)]
    for tap in range(TAPS):
        totals = [None] * filters
        for b in range(samples):
            kern = mixed(bank, sel[b], tap)
            plain_grad = held[b, tap].astype(F32) * scales[b] - kern * styles[b] * falls[b]
            sums[b] = sums[b] + plain_grad * kern
            kernel_grad = plain_grad * styles[b]
            for k in range(filters):
                term = sel[b][k] * kernel_grad
                totals[k] = term if totals[k] is None else totals[k] + term
        for k in range(filters):
            bank_grad[k, tap] = totals[k]
        copies[tap].start()
    for b in range(samples):
        value = jnp.sum(sums[b], axis=0, keepdims=True)
        style_grad[b : b + 1] = value
    for copy in copies:
        copy.wait()


def pair_sum(parts):
    while len(parts) > 1:
        parts = [x + y for x, y in zip(parts[::2], parts[1::2])]
    return parts[0]


def affine_kernel(samples, latents, *refs):
    parts, (w_grad, b_grad) = refs[:-2], refs[-2:]
    style_grad = pair_sum([part[...] for part in parts])
    high, mid, low = split3(latents[...])
    top, middle, bottom = split3(style_grad)
    w_grad[...] = lax.dot_general(
        jnp.concatenate([high, high, mid, high, mid, low], axis=0).astype(BF16),
        jnp.concatenate([top, middle, top, bottom, middle, top], axis=0).astype(BF16),
        (((0,), (0,)), ((), ())),
        preferred_element_type=F32,
    )
    bias = style_grad[0:1]
    for b in range(1, samples):
        bias = bias + style_grad[b : b + 1]
    b_grad[...] = bias


def call(kernel, name, outs, *operands, scalars=0, fetched=0, kept=0, scratch=(), flops=10**6):
    outs = tuple(jax.ShapeDtypeStruct(*o) for o in outs)
    moved = sum(o.size * o.dtype.itemsize for o in (*outs, *operands))
    return pl.pallas_call(
        kernel,
        out_shape=outs,
        in_specs=sspec(scalars)
        + vspec(len(operands) - scalars - fetched)
        + [pl.BlockSpec(memory_space=pltpu.HBM)] * fetched,
        out_specs=tuple([pl.BlockSpec(memory_space=pltpu.HBM)] * kept + vspec(len(outs) - kept)),
        scratch_shapes=[pltpu.VMEM(*s) if isinstance(s, tuple) else s for s in scratch],
        compiler_params=params(),
        cost_estimate=cost(flops, moved),
        name=name,
    )(*operands)


def partner(at, step, size):
    return at ^ step if size & (size - 1) == 0 else (at - step + size) % size


def steps_of(size):
    return [0] + sorted(range(1, size), key=lambda n: (n < 2, n))


def exchange_pairs(x, axis):
    size = lax.axis_size(axis)
    return [x] + [
        lax.ppermute(x, axis, [(partner(i, step, size), i) for i in range(size)]) for step in steps_of(size)[1:]
    ]


def exchange(x, axis):
    size = lax.axis_size(axis)
    return [x] + [
        lax.ppermute(x, axis, [(i, (i + s) % size) for i in range(size)]) for s in range(1, size)
    ]


def terms_of_sum(x, axis):
    size = lax.axis_size(axis)
    if size & (size - 1):
        return [lax.psum(x, axis)]
    return [x] + [lax.ppermute(x, axis, [(i, i ^ step) for i in range(size)]) for step in range(1, size)]


def from_sides(first, last, axis):
    size, at = lax.axis_size(axis), lax.axis_index(axis)
    if size == 2:
        edge = last if first is None else jnp.where(at == 0, last, first)
        got = lax.ppermute(edge, axis, [(0, 1), (1, 0)])
        nothing = jnp.zeros_like(got)
        return jnp.where(at == 1, got, nothing), jnp.where(at == 0, got, nothing)
    up = [(i, i + 1) for i in range(size - 1)]
    down = [(i + 1, i) for i in range(size - 1)]
    return lax.ppermute(last, axis, up), lax.ppermute(first, axis, down)


def on_device(feature, out_grad, bank, select, latent, affine_w, affine_b):
    rows, samples, size = (lax.axis_size(a) for a in ("rows", "samples", "chan"))
    row_at, sample_at, chan_at = (lax.axis_index(a) for a in ("rows", "samples", "chan"))
    _, ch, height, width = feature.shape
    out_ch, in_ch = bank.shape[2:]
    pixels, all_ch = height * width, ch * size
    sign = 1 - 2 * jnp.remainder(sample_at, 2)
    place = jnp.stack([sample_at, chan_at, row_at, sign]).astype(jnp.int32)
    flops = 2 * TAPS * ch * ch * size * pixels

    def along(x, pairs):
        whole = []
        for b in range(samples):
            for i, j in pairs:
                if b % 2:
                    i, j = size - 1 - i, size - 1 - j
                whole.append((b * size + i, b * size + j))
        return lax.ppermute(x, ("samples", "chan"), whole)

    cotan = out_grad[0].reshape(ch, pixels)
    first, second = [], []

    def step(number, x, y):
        first.append(along(x, [(i, i + 1) for i in range(number - 1, size - 1)]))
        second.append(along(y, [(i + 1, i) for i in range(size - number)]))

    step(1, cotan, cotan)

    small_rows = -(-(latent.shape[1] // in_ch + 2) // 8) * 8
    plain, small = call(
        plain_kernel,
        "plain",
        [((TAPS + 1, out_ch, in_ch), F32), ((small_rows, in_ch), F32)],
        select,
        latent,
        affine_b[None],
        affine_w,
        bank,
        fetched=5,
        scratch=[
            pltpu.SMEM(select.shape, jnp.int32),
            (latent.shape, F32),
            ((1, in_ch), F32),
            (affine_w.shape, F32),
            (bank.shape, F32),
            pltpu.SemaphoreType.DMA((5,)),
        ],
    )
    plains = exchange(plain, "rows")
    feature, cotan = lax.optimization_barrier((feature, cotan))
    feat = feature[0].reshape(ch, pixels)
    feat_before, feat_after = from_sides(feat[:, :width], feat[:, pixels - width :], "rows")
    extended = ((ch, (height + 2) * width), BF16)
    (feat,) = call(
        functools.partial(rows_kernel, height, width), "feat_rows", [extended], feat, feat_before, feat_after
    )
    feat, plain = lax.optimization_barrier((feat, plain))
    feat_end = lax.ppermute(feat, "chan", [(0, 1), (size - 1, size - 2)])
    message = ((ch, TAPS * ch), BF16)
    whole_mod, scale, *mods = call(
        functools.partial(blocks_kernel, rows, size),
        "mod_blocks",
        [((TAPS, out_ch, all_ch), BF16), ((out_ch, 128), F32)] + [message] * (size + 1),
        place,
        *plains,
        scalars=1,
        scratch=[((rows, TAPS, out_ch, in_ch), F32), ((size, *message[0]), BF16)],
    )
    first[0], second[0], plains = lax.optimization_barrier((first[0], second[0], plains))

    step(2, first[0], second[0])
    double = ((2 * ch, TAPS * ch), BF16)
    own_grad, to_behind, to_ahead, wide = call(
        functools.partial(near_grad_kernel, height, width),
        "near_grad",
        [message, double, double, ((3 * ch, (height + 2) * width), BF16)],
        cotan,
        first[0],
        second[0],
        feat,
        mods[size - 1],
        mods[1],
        scratch=[((3 * ch, pixels), BF16), ((3, 3 * ch, 3 * ch), F32)],
        flops=flops * 3 // size,
    )
    from_ahead = along(to_behind, [(i + 1, i) for i in range(size - 1)])
    from_behind = along(to_ahead, [(i, i + 1) for i in range(size - 1)])
    first[1], second[1], feat_end, wide, whole_mod = lax.optimization_barrier(
        (first[1], second[1], feat_end, wide, whole_mod)
    )

    count = size - 3
    grad_others, middle, end_block = call(
        functools.partial(middle_grad_kernel, count, height, width),
        "middle_grad",
        [((2 * count * ch, TAPS * ch), BF16), ((count * ch, pixels), BF16), ((ch, pixels), BF16)],
        *first[1:],
        *second[1:],
        wide,
        *mods[2 : size - 1],
        scratch=[((3, count * ch, 3 * ch), F32)],
        flops=flops // size,
    )
    (grad_end,) = call(
        functools.partial(end_grad_kernel, height, width),
        "end_grad",
        [message],
        end_block,
        feat_end,
        scratch=[((3 * ch, (height + 2) * width), BF16), ((3, ch, 3 * ch), F32)],
        flops=flops // size,
    )
    from_others = along(grad_others, [(i, (i + 2) % size) for i in range(size)])
    from_end = lax.ppermute(grad_end, "chan", [(1, size - 1), (size - 2, 0)])
    end_block, grad_end = lax.optimization_barrier((end_block, grad_end))
    far = lax.ppermute(end_block, "chan", [(1, 0), (size - 2, size - 1)])
    parts = call(
        functools.partial(collect_kernel, rows, size),
        "collect",
        [((TAPS + 1, out_ch, in_ch), BF16)] * rows,
        place,
        scale,
        whole_mod,
        own_grad,
        from_ahead,
        from_behind,
        from_others,
        from_end,
        scalars=1,
        scratch=[((size, *message[0]), F32), ((rows, TAPS, out_ch, in_ch), BF16)],
        flops=COLLECT_FLOPS,
    )
    parts, mods = lax.optimization_barrier((parts, mods))
    end_mod = lax.ppermute(mods[size], "chan", [(0, size - 1), (size - 1, 0)])
    parts = [parts[0]] + [
        lax.ppermute(parts[r], "rows", [(i, (i + r) % rows) for i in range(rows)])
        for r in range(1, rows)
    ]
    slots = TAPS + 1 - (-3 * small_rows // out_ch)
    (own,) = call(row_sum_kernel, "row_sum", [((slots, out_ch, in_ch), BF16)], scale, small, *parts)
    every = exchange_pairs(own, "samples")

    own, end_mod, far = lax.optimization_barrier((own, end_mod, far))
    main, before, after = call(
        functools.partial(input_grad_kernel, rows, size, height, width),
        "input_grad",
        [((ch, pixels), F32), ((ch, width), F32), ((ch, width), F32)],
        place,
        cotan,
        first[0],
        second[0],
        middle,
        far,
        mods[0],
        from_behind,
        from_ahead,
        from_others,
        end_mod,
        scalars=1,
        scratch=[
            ((all_ch, pixels), BF16),
            ((TAPS * ch, all_ch), BF16),
            ((height + 2, 3 * ch, width), F32),
        ],
        flops=INPUT_FLOPS,
    )
    every, main, before, after = lax.optimization_barrier((every, main, before, after))
    from_above, from_below = from_sides(None if rows == 2 else before, after, "rows")
    bank_grad, style_part, latents = call(
        functools.partial(bank_grad_kernel, samples, small_rows),
        "bank_grad",
        [(bank.shape, F32), ((samples, in_ch), F32), ((samples, latent.shape[1]), F32)],
        place,
        bank,
        *every,
        scalars=1,
        scratch=[((samples, slots, out_ch, in_ch), BF16), (bank.shape, F32), pltpu.SemaphoreType.DMA((TAPS,))],
        kept=1,
    )
    style_parts = terms_of_sum(style_part, "chan")
    edge = jnp.concatenate(
        [from_above[:, None], jnp.zeros((ch, height - 2, width), F32), from_below[:, None]], axis=1
    )
    feature_grad = (main.reshape(ch, height, width) + edge).astype(BF16)[None]
    style_parts, feature_grad = lax.optimization_barrier((style_parts, feature_grad))
    affine_w_grad, affine_b_grad = call(
        functools.partial(affine_kernel, samples),
        "affine",
        [(affine_w.shape, F32), ((1, in_ch), F32)],
        latents,
        *style_parts,
    )
    return (feature_grad, bank_grad, affine_w_grad, affine_b_grad[0])


def solution(mesh):
    return jax.shard_map(
        on_device,
        mesh=mesh,
        in_specs=(
            P("samples", "chan", "rows", None),
            P("samples", "chan", "rows", None),
            P(None, None, "chan", "rows"),
            P("samples", None),
            P("samples", None),
            P(None, "rows"),
            P("rows"),
        ),
        out_specs=(
            P("samples", "chan", "rows", None),
            P(None, None, "chan", "rows"),
            P(None, "rows"),
            P("rows"),
        ),
        check_vma=False,
    )
```

```python
import functools

import jax
import jax.numpy as jnp
from jax import lax
from jax.experimental import pallas as pl
from jax.experimental.pallas import tpu as pltpu
from jax.sharding import PartitionSpec as P

EPS = 1e-08
TAPS = 9
F32 = jnp.float32
BF16 = jnp.bfloat16
VMEM_LIMIT = 16 * 2**20
COLLECT_FLOPS = 6 * 10**9
INPUT_FLOPS = 2 * 10**9


def params():
    return pltpu.CompilerParams(vmem_limit_bytes=VMEM_LIMIT)


def vspec(n):
    return [pl.BlockSpec(memory_space=pltpu.VMEM)] * n


def sspec(n):
    return [pl.BlockSpec(memory_space=pltpu.SMEM)] * n


def cost(flops, moved):
    return pl.CostEstimate(flops=flops, bytes_accessed=moved, transcendentals=0)


def beside(pieces):
    return pieces[0] if len(pieces) == 1 else jnp.concatenate(pieces, axis=1)


def mixed(bank_ref, weights, tap):
    total = weights[0] * bank_ref[0, tap]
    for k in range(1, bank_ref.shape[0]):
        total = total + weights[k] * bank_ref[k, tap]
    return total


def plain_kernel(*refs):
    given, (plain_out, message, small), held, sems = refs[:5], refs[5:8], refs[8:13], refs[13]
    copies = [pltpu.make_async_copy(x, y, sems.at[n]) for n, (x, y) in enumerate(zip(given, held))]
    for copy in copies:
        copy.start()
    for copy in copies:
        copy.wait()
    select, latent, affine_b, affine_w, bank = held
    style = (
        jnp.dot(latent[...], affine_w[...], precision=lax.Precision.HIGHEST, preferred_element_type=F32)
        + affine_b[...]
    )
    filters, in_ch = bank.shape[0], bank.shape[3]
    weights = [select[0, k].astype(F32) for k in range(filters)]
    total = jnp.zeros(bank.shape[2:], F32)
    for tap in range(TAPS):
        plain = mixed(bank, weights, tap) * style
        plain_out[tap] = plain
        message[tap] = plain.astype(BF16)
        total = total + plain * plain
    energy = jnp.sum(total, axis=1, keepdims=True)
    plain_out[TAPS] = jnp.broadcast_to(energy, total.shape)
    put_columns(message, [energy])
    small[...] = jnp.zeros(small.shape, F32)
    last = latent.shape[1] // in_ch
    for n in range(last):
        small[n : n + 1] = latent[:, n * in_ch : (n + 1) * in_ch]
    small[last : last + 1] = style
    lane = lax.broadcasted_iota(jnp.int32, (1, in_ch), 1)
    row = jnp.zeros((1, in_ch), F32)
    for k in range(filters):
        row = jnp.where(lane == k, weights[k], row)
    small[last + 1 : last + 2] = row


def blocks_kernel(rows, size, place, *refs):
    parts, (whole, scale_out), outs, (by_row, by_chan) = refs[:rows], refs[rows : rows + 2], refs[rows + 2 : -2], refs[-2:]
    row_at, chan_at, sign = place[2], place[1], place[3]
    energy = parts[0][TAPS][:, 0:1]
    for part in parts[1:]:
        energy = energy + get_column(part[TAPS])
    scale = lax.rsqrt(energy + EPS)
    scale_out[...] = jnp.broadcast_to(scale, scale_out.shape)
    for r in range(rows):
        by_row[lax.rem(row_at - r + rows, rows)] = parts[r][0:TAPS].astype(F32)
    ch = whole.shape[2] // size
    taps = []
    for tap in range(TAPS):
        value = beside([by_row[r, tap] for r in range(rows)]) * scale
        whole[tap] = value.astype(BF16)
        taps.append(value)
    for z in range(size):
        by_chan[z] = beside([value[:, z * ch : (z + 1) * ch] for value in taps]).astype(BF16)
    for d in range(size):
        outs[d][...] = by_chan[lax.rem(chan_at + sign * d + size, size)]
    outs[size][...] = by_chan[size - 1 - chan_at]


def shifted(x, by):
    width = x.shape[1]
    lane = lax.broadcasted_iota(jnp.int32, x.shape, 1)
    moved = pltpu.roll(x, by % width, 1)
    return jnp.where(lane == (0 if by == 1 else width - 1), 0.0, moved)


def spread(wide, row, x):
    ch, width = x.shape
    wide[ch : 2 * ch, row * width : (row + 1) * width] = x
    x = x.astype(F32)
    wide[0:ch, row * width : (row + 1) * width] = shifted(x, 1).astype(BF16)
    wide[2 * ch : 3 * ch, row * width : (row + 1) * width] = shifted(x, -1).astype(BF16)


def rows_kernel(height, width, feat, feat_before, feat_after, out):
    out[:, 0:width] = feat_before[...]
    out[:, width : (height + 1) * width] = feat[...]
    out[:, (height + 1) * width :] = feat_after[...]


def tap_products(g_ref, wides, totals, height, width):
    for total in totals:
        total[...] = jnp.zeros(total.shape, F32)

    def body(row, _):
        g = g_ref[:, pl.ds(pl.multiple_of(row * width, width), width)]
        for wide, total in zip(wides, totals):
            for kh in range(3):
                x = wide[:, pl.ds(pl.multiple_of((row + kh) * width, width), width)]
                total[kh] += lax.dot_general(g, x, (((1,), (1,)), ((), ())), preferred_element_type=F32)
        return 0

    lax.fori_loop(0, height, body, 0)
    return [jnp.concatenate([total[kh] for kh in range(3)], axis=1).astype(BF16) for total in totals]


def near_grad_kernel(height, width, *refs):
    cotans, feat, mods, (own, behind, ahead), (wide, gathered, total) = refs[:3], refs[3], refs[4:6], refs[6:9], refs[9:]
    ch = feat.shape[0]
    for at, cotan in enumerate(cotans):
        gathered[at * ch : (at + 1) * ch] = cotan[...]
    for row in range(height + 2):
        spread(wide, row, feat[:, row * width : (row + 1) * width])
    (whole,) = tap_products(gathered, [wide], [total], height, width)
    own[...] = whole[0:ch]
    for at, (out, mod) in enumerate(zip((behind, ahead), mods)):
        out[0:ch] = whole[(at + 1) * ch : (at + 2) * ch]
        out[ch:] = mod[...]


def middle_grad_kernel(count, height, width, *refs):
    first, second, wide, mods = refs[:count], refs[count : 2 * count], refs[2 * count], refs[2 * count + 1 : 3 * count + 1]
    out, middle, end_block, total = refs[3 * count + 1 :]
    ch = end_block.shape[0]
    for at in range(count):
        middle[at * ch : (at + 1) * ch] = first[at][...] + second[count - 1 - at][...]
    end_block[...] = first[-1][...] + second[-1][...]
    (out[0 : count * ch],) = tap_products(middle, [wide], [total], height, width)
    for at, mod in enumerate(mods):
        out[(count + at) * ch : (count + at + 1) * ch] = mod[...]


def end_grad_kernel(height, width, end_block, feat, out, wide, total):
    for row in range(height + 2):
        spread(wide, row, feat[:, row * width : (row + 1) * width])
    (out[...],) = tap_products(end_block, [wide], [total], height, width)


def input_grad_kernel(rows, size, height, width, place, cotan, first, second, middle, far, own_mod, behind, ahead, others, end_mod, *refs):
    main, before, after, gathered, taps_t, total = refs
    ch = main.shape[0]
    spot = jnp.where(place[3] > 0, place[1], size - 1 - place[1])
    gathered[0:ch] = cotan[...]
    gathered[ch : 2 * ch] = jnp.where(spot == 0, far[...], first[...])
    gathered[2 * ch : (size - 1) * ch] = middle[...]
    gathered[(size - 1) * ch :] = jnp.where(spot == size - 1, far[...], second[...])
    mods = [own_mod[...], jnp.where(spot == 0, end_mod[...], behind[ch:])]
    mods.append(others[(size - 3) * ch :])
    mods.append(jnp.where(spot == size - 1, end_mod[...], ahead[ch:]))
    every = jnp.concatenate([mod.astype(F32) for mod in mods], axis=0)
    taps_t[...] = every.T.astype(BF16)
    total[...] = jnp.zeros(total.shape, F32)

    def body(row, _):
        g = gathered[:, pl.ds(pl.multiple_of(row * width, width), width)]
        for kh in range(3):
            y = jnp.dot(taps_t[kh * 3 * ch : (kh + 1) * 3 * ch], g, preferred_element_type=F32)
            total[row + kh] += y
        return 0

    lax.fori_loop(0, height, body, 0)
    for row in range(height + 2):
        value = total[row, ch : 2 * ch]
        value = value + shifted(total[row, 0:ch], -1) + shifted(total[row, 2 * ch : 3 * ch], 1)
        if row == 0:
            before[...] = value
        elif row == height + 1:
            after[...] = jnp.where(place[2] == 1, before[...], value) if rows == 2 else value
        else:
            main[:, (row - 1) * width : row * width] = value


def split3(x):
    high = x.astype(BF16).astype(F32)
    mid = (x - high).astype(BF16).astype(F32)
    return high, mid, x - high - mid


def put_columns(out, columns):
    lane = lax.broadcasted_iota(jnp.int32, out.shape[1:], 1)
    last = jnp.zeros(out.shape[1:], F32)
    for n, column in enumerate(columns):
        for at, piece in enumerate(split3(column)):
            last = jnp.where(lane == 3 * n + at, piece, last)
    out[TAPS] = last.astype(BF16)


def get_column(last, n=0):
    last = last.astype(F32)
    return last[:, 3 * n : 3 * n + 1] + last[:, 3 * n + 1 : 3 * n + 2] + last[:, 3 * n + 2 : 3 * n + 3]


def collect_kernel(rows, size, place, scale, whole_mod, own, ahead, behind, others, end, *refs):
    outs, (by_chan, by_row) = refs[:rows], refs[rows:]
    chan_at, row_at, sign = place[1], place[2], place[3]
    ch = own.shape[0]
    by_chan[chan_at] = own[...].astype(F32)
    by_chan[lax.rem(chan_at + sign + size, size)] = ahead[0:ch].astype(F32)
    by_chan[lax.rem(chan_at - sign + size, size)] = behind[0:ch].astype(F32)
    for d in range(2, size - 1):
        value = others[(d - 2) * ch : (d - 1) * ch].astype(F32)
        by_chan[lax.rem(chan_at + sign * d + size, size)] = value
    by_chan[jnp.where(chan_at == 0, size - 1, 0)] += end[...].astype(F32)
    in_ch = outs[0].shape[2]
    product = jnp.zeros(whole_mod.shape[1:], F32)
    for tap in range(TAPS):
        value = beside([by_chan[z, :, tap * ch : (tap + 1) * ch] for z in range(size)])
        product = product + value * whole_mod[tap].astype(F32)
        for r in range(rows):
            by_row[r, tap] = value[:, r * in_ch : (r + 1) * in_ch].astype(BF16)
    fall = jnp.sum(product, axis=1, keepdims=True) * (scale[:, 0:1] * scale[:, 0:1])
    for r in range(rows):
        outs[r][0:TAPS] = by_row[lax.rem(row_at + r, rows)]
        put_columns(outs[r], [fall])


def row_sum_kernel(scale, small, *refs):
    parts, out = refs[:-1], refs[-1]
    fall = get_column(parts[0][TAPS])
    for part in parts[1:]:
        fall = fall + get_column(part[TAPS])
    for tap in range(TAPS):
        value = parts[0][tap].astype(F32)
        for part in parts[1:]:
            value = value + part[tap].astype(F32)
        out[tap] = value.astype(BF16)
    put_columns(out, [fall, scale[:, 0:1]])
    out_ch, in_ch = out.shape[1:]
    pieces = list(split3(small[...]))
    spare = (out.shape[0] - TAPS - 1) * out_ch - 3 * small.shape[0]
    if spare:
        pieces.append(jnp.zeros((spare, in_ch), F32))
    pieces = jnp.concatenate(pieces, axis=0).astype(BF16)
    for n in range(out.shape[0] - TAPS - 1):
        out[TAPS + 1 + n] = pieces[n * out_ch : (n + 1) * out_ch]


def bank_grad_kernel(samples, small_rows, place, bank, *refs):
    parts, (bank_out, style_grad, latents, held, bank_grad, sems) = refs[:samples], refs[samples:]
    copies = [pltpu.make_async_copy(bank_grad.at[:, tap], bank_out.at[:, tap], sems.at[tap]) for tap in range(TAPS)]
    for part, step in zip(parts, steps_of(samples)):
        held[partner(place[0], step, samples)] = part[...]
    filters, in_ch = bank.shape[0], bank.shape[3]
    last = latents.shape[1] // in_ch
    sel, styles, scales, falls = [], [], [], []
    for b in range(samples):
        rows = jnp.concatenate([held[b, n].astype(F32) for n in range(TAPS + 1, held.shape[1])], axis=0)
        small = rows[:small_rows] + rows[small_rows : 2 * small_rows] + rows[2 * small_rows : 3 * small_rows]
        latents[b : b + 1] = beside([small[n : n + 1] for n in range(last)])
        styles.append(small[last : last + 1])
        sel.append([small[last + 1 : last + 2, k : k + 1] for k in range(filters)])
        falls.append(get_column(held[b, TAPS]))
        scales.append(get_column(held[b, TAPS], 1))
    sums = [jnp.zeros(bank.shape[2:], F32) for _ in range(samples)]
    for tap in range(TAPS):
        totals = [None] * filters
        for b in range(samples):
            kern = mixed(bank, sel[b], tap)
            plain_grad = held[b, tap].astype(F32) * scales[b] - kern * styles[b] * falls[b]
            sums[b] = sums[b] + plain_grad * kern
            kernel_grad = plain_grad * styles[b]
            for k in range(filters):
                term = sel[b][k] * kernel_grad
                totals[k] = term if totals[k] is None else totals[k] + term
        for k in range(filters):
            bank_grad[k, tap] = totals[k]
        copies[tap].start()
    for b in range(samples):
        value = jnp.sum(sums[b], axis=0, keepdims=True)
        style_grad[b : b + 1] = value
    for copy in copies:
        copy.wait()


def pair_sum(parts):
    while len(parts) > 1:
        parts = [x + y for x, y in zip(parts[::2], parts[1::2])]
    return parts[0]


def affine_kernel(samples, latents, *refs):
    parts, (w_grad, b_grad) = refs[:-2], refs[-2:]
    style_grad = pair_sum([part[...] for part in parts])
    high, mid, low = split3(latents[...])
    top, middle, bottom = split3(style_grad)
    w_grad[...] = lax.dot_general(
        jnp.concatenate([high, high, mid, high, mid, low], axis=0).astype(BF16),
        jnp.concatenate([top, middle, top, bottom, middle, top], axis=0).astype(BF16),
        (((0,), (0,)), ((), ())),
        preferred_element_type=F32,
    )
    bias = style_grad[0:1]
    for b in range(1, samples):
        bias = bias + style_grad[b : b + 1]
    b_grad[...] = bias


def call(kernel, name, outs, *operands, scalars=0, fetched=0, kept=0, scratch=(), flops=10**6):
    outs = tuple(jax.ShapeDtypeStruct(*o) for o in outs)
    moved = sum(o.size * o.dtype.itemsize for o in (*outs, *operands))
    return pl.pallas_call(
        kernel,
        out_shape=outs,
        in_specs=sspec(scalars)
        + vspec(len(operands) - scalars - fetched)
        + [pl.BlockSpec(memory_space=pltpu.HBM)] * fetched,
        out_specs=tuple([pl.BlockSpec(memory_space=pltpu.HBM)] * kept + vspec(len(outs) - kept)),
        scratch_shapes=[pltpu.VMEM(*s) if isinstance(s, tuple) else s for s in scratch],
        compiler_params=params(),
        cost_estimate=cost(flops, moved),
        name=name,
    )(*operands)


def partner(at, step, size):
    return at ^ step if size & (size - 1) == 0 else (at - step + size) % size


def steps_of(size):
    return [0] + sorted(range(1, size), key=lambda n: (n < 2, n))


def exchange_pairs(x, axis):
    size = lax.axis_size(axis)
    return [x] + [
        lax.ppermute(x, axis, [(partner(i, step, size), i) for i in range(size)]) for step in steps_of(size)[1:]
    ]


def exchange(x, axis):
    size = lax.axis_size(axis)
    return [x] + [
        lax.ppermute(x, axis, [(i, (i + s) % size) for i in range(size)]) for s in range(1, size)
    ]


def terms_of_sum(x, axis):
    size = lax.axis_size(axis)
    if size & (size - 1):
        return [lax.psum(x, axis)]
    return [x] + [lax.ppermute(x, axis, [(i, i ^ step) for i in range(size)]) for step in range(1, size)]


def from_sides(first, last, axis):
    size, at = lax.axis_size(axis), lax.axis_index(axis)
    if size == 2:
        edge = last if first is None else jnp.where(at == 0, last, first)
        got = lax.ppermute(edge, axis, [(0, 1), (1, 0)])
        nothing = jnp.zeros_like(got)
        return jnp.where(at == 1, got, nothing), jnp.where(at == 0, got, nothing)
    up = [(i, i + 1) for i in range(size - 1)]
    down = [(i + 1, i) for i in range(size - 1)]
    return lax.ppermute(last, axis, up), lax.ppermute(first, axis, down)


def on_device(feature, out_grad, bank, select, latent, affine_w, affine_b):
    rows, samples, size = (lax.axis_size(a) for a in ("rows", "samples", "chan"))
    row_at, sample_at, chan_at = (lax.axis_index(a) for a in ("rows", "samples", "chan"))
    _, ch, height, width = feature.shape
    out_ch, in_ch = bank.shape[2:]
    pixels, all_ch = height * width, ch * size
    sign = 1 - 2 * jnp.remainder(sample_at, 2)
    place = jnp.stack([sample_at, chan_at, row_at, sign]).astype(jnp.int32)
    flops = 2 * TAPS * ch * ch * size * pixels

    def along(x, pairs):
        whole = []
        for b in range(samples):
            for i, j in pairs:
                if b % 2:
                    i, j = size - 1 - i, size - 1 - j
                whole.append((b * size + i, b * size + j))
        return lax.ppermute(x, ("samples", "chan"), whole)

    cotan = out_grad[0].reshape(ch, pixels)
    first, second = [], []

    def step(number, x, y):
        first.append(along(x, [(i, i + 1) for i in range(number - 1, size - 1)]))
        second.append(along(y, [(i + 1, i) for i in range(size - number)]))

    step(1, cotan, cotan)

    small_rows = -(-(latent.shape[1] // in_ch + 2) // 8) * 8
    plain, plain_message, small = call(
        plain_kernel,
        "plain",
        [((TAPS + 1, out_ch, in_ch), F32), ((TAPS + 1, out_ch, in_ch), BF16), ((small_rows, in_ch), F32)],
        select,
        latent,
        affine_b[None],
        affine_w,
        bank,
        fetched=5,
        scratch=[
            pltpu.SMEM(select.shape, jnp.int32),
            (latent.shape, F32),
            ((1, in_ch), F32),
            (affine_w.shape, F32),
            (bank.shape, F32),
            pltpu.SemaphoreType.DMA((5,)),
        ],
    )
    plains = [plain] + exchange(plain_message, "rows")[1:]
    feature, cotan = lax.optimization_barrier((feature, cotan))
    feat = feature[0].reshape(ch, pixels)
    feat_before, feat_after = from_sides(feat[:, :width], feat[:, pixels - width :], "rows")
    extended = ((ch, (height + 2) * width), BF16)
    (feat,) = call(
        functools.partial(rows_kernel, height, width), "feat_rows", [extended], feat, feat_before, feat_after
    )
    feat, plain = lax.optimization_barrier((feat, plain))
    feat_end = lax.ppermute(feat, "chan", [(0, 1), (size - 1, size - 2)])
    message = ((ch, TAPS * ch), BF16)
    whole_mod, scale, *mods = call(
        functools.partial(blocks_kernel, rows, size),
        "mod_blocks",
        [((TAPS, out_ch, all_ch), BF16), ((out_ch, 128), F32)] + [message] * (size + 1),
        place,
        *plains,
        scalars=1,
        scratch=[((rows, TAPS, out_ch, in_ch), F32), ((size, *message[0]), BF16)],
    )
    first[0], second[0], plains = lax.optimization_barrier((first[0], second[0], plains))

    step(2, first[0], second[0])
    double = ((2 * ch, TAPS * ch), BF16)
    own_grad, to_behind, to_ahead, wide = call(
        functools.partial(near_grad_kernel, height, width),
        "near_grad",
        [message, double, double, ((3 * ch, (height + 2) * width), BF16)],
        cotan,
        first[0],
        second[0],
        feat,
        mods[size - 1],
        mods[1],
        scratch=[((3 * ch, pixels), BF16), ((3, 3 * ch, 3 * ch), F32)],
        flops=flops * 3 // size,
    )
    from_ahead = along(to_behind, [(i + 1, i) for i in range(size - 1)])
    from_behind = along(to_ahead, [(i, i + 1) for i in range(size - 1)])
    first[1], second[1], feat_end, wide, whole_mod = lax.optimization_barrier(
        (first[1], second[1], feat_end, wide, whole_mod)
    )

    count = size - 3
    grad_others, middle, end_block = call(
        functools.partial(middle_grad_kernel, count, height, width),
        "middle_grad",
        [((2 * count * ch, TAPS * ch), BF16), ((count * ch, pixels), BF16), ((ch, pixels), BF16)],
        *first[1:],
        *second[1:],
        wide,
        *mods[2 : size - 1],
        scratch=[((3, count * ch, 3 * ch), F32)],
        flops=flops // size,
    )
    (grad_end,) = call(
        functools.partial(end_grad_kernel, height, width),
        "end_grad",
        [message],
        end_block,
        feat_end,
        scratch=[((3 * ch, (height + 2) * width), BF16), ((3, ch, 3 * ch), F32)],
        flops=flops // size,
    )
    from_others = along(grad_others, [(i, (i + 2) % size) for i in range(size)])
    from_end = lax.ppermute(grad_end, "chan", [(1, size - 1), (size - 2, 0)])
    end_block, grad_end = lax.optimization_barrier((end_block, grad_end))
    far = lax.ppermute(end_block, "chan", [(1, 0), (size - 2, size - 1)])
    parts = call(
        functools.partial(collect_kernel, rows, size),
        "collect",
        [((TAPS + 1, out_ch, in_ch), BF16)] * rows,
        place,
        scale,
        whole_mod,
        own_grad,
        from_ahead,
        from_behind,
        from_others,
        from_end,
        scalars=1,
        scratch=[((size, *message[0]), F32), ((rows, TAPS, out_ch, in_ch), BF16)],
        flops=COLLECT_FLOPS,
    )
    parts, mods = lax.optimization_barrier((parts, mods))
    end_mod = lax.ppermute(mods[size], "chan", [(0, size - 1), (size - 1, 0)])
    parts = [parts[0]] + [
        lax.ppermute(parts[r], "rows", [(i, (i + r) % rows) for i in range(rows)])
        for r in range(1, rows)
    ]
    slots = TAPS + 1 - (-3 * small_rows // out_ch)
    (own,) = call(row_sum_kernel, "row_sum", [((slots, out_ch, in_ch), BF16)], scale, small, *parts)
    every = exchange_pairs(own, "samples")

    own, end_mod, far = lax.optimization_barrier((own, end_mod, far))
    main, before, after = call(
        functools.partial(input_grad_kernel, rows, size, height, width),
        "input_grad",
        [((ch, pixels), F32), ((ch, width), F32), ((ch, width), F32)],
        place,
        cotan,
        first[0],
        second[0],
        middle,
        far,
        mods[0],
        from_behind,
        from_ahead,
        from_others,
        end_mod,
        scalars=1,
        scratch=[
            ((all_ch, pixels), BF16),
            ((TAPS * ch, all_ch), BF16),
            ((height + 2, 3 * ch, width), F32),
        ],
        flops=INPUT_FLOPS,
    )
    every, main, before, after = lax.optimization_barrier((every, main, before, after))
    from_above, from_below = from_sides(None if rows == 2 else before, after, "rows")
    bank_grad, style_part, latents = call(
        functools.partial(bank_grad_kernel, samples, small_rows),
        "bank_grad",
        [(bank.shape, F32), ((samples, in_ch), F32), ((samples, latent.shape[1]), F32)],
        place,
        bank,
        *every,
        scalars=1,
        scratch=[((samples, slots, out_ch, in_ch), BF16), (bank.shape, F32), pltpu.SemaphoreType.DMA((TAPS,))],
        kept=1,
    )
    style_parts = terms_of_sum(style_part, "chan")
    edge = jnp.concatenate(
        [from_above[:, None], jnp.zeros((ch, height - 2, width), F32), from_below[:, None]], axis=1
    )
    feature_grad = (main.reshape(ch, height, width) + edge).astype(BF16)[None]
    style_parts, feature_grad = lax.optimization_barrier((style_parts, feature_grad))
    affine_w_grad, affine_b_grad = call(
        functools.partial(affine_kernel, samples),
        "affine",
        [(affine_w.shape, F32), ((1, in_ch), F32)],
        latents,
        *style_parts,
    )
    return (feature_grad, bank_grad, affine_w_grad, affine_b_grad[0])


def solution(mesh):
    return jax.shard_map(
        on_device,
        mesh=mesh,
        in_specs=(
            P("samples", "chan", "rows", None),
            P("samples", "chan", "rows", None),
            P(None, None, "chan", "rows"),
            P("samples", None),
            P("samples", None),
            P(None, "rows"),
            P("rows"),
        ),
        out_specs=(
            P("samples", "chan", "rows", None),
            P(None, None, "chan", "rows"),
            P(None, "rows"),
            P("rows"),
        ),
        check_vma=False,
    )
```

```python
import functools

import jax
import jax.numpy as jnp
from jax import lax
from jax.experimental import pallas as pl
from jax.experimental.pallas import tpu as pltpu
from jax.sharding import PartitionSpec as P

EPS = 1e-08
TAPS = 9
F32 = jnp.float32
BF16 = jnp.bfloat16
VMEM_LIMIT = 10 * 2**20
COLLECT_FLOPS = 6 * 10**9
INPUT_FLOPS = 2 * 10**9


def params():
    return pltpu.CompilerParams(vmem_limit_bytes=VMEM_LIMIT)


def vspec(n):
    return [pl.BlockSpec(memory_space=pltpu.VMEM)] * n


def sspec(n):
    return [pl.BlockSpec(memory_space=pltpu.SMEM)] * n


def cost(flops, moved):
    return pl.CostEstimate(flops=flops, bytes_accessed=moved, transcendentals=0)


def beside(pieces):
    return pieces[0] if len(pieces) == 1 else jnp.concatenate(pieces, axis=1)


def mixed(bank_ref, weights, tap):
    total = weights[0] * bank_ref[0, tap]
    for k in range(1, bank_ref.shape[0]):
        total = total + weights[k] * bank_ref[k, tap]
    return total


def plain_kernel(*refs):
    given, (plain_out, small), held, sems = refs[:5], refs[5:7], refs[7:12], refs[12]
    copies = [pltpu.make_async_copy(x, y, sems.at[n]) for n, (x, y) in enumerate(zip(given, held))]
    for copy in copies:
        copy.start()
    for copy in copies:
        copy.wait()
    select, latent, affine_b, affine_w, bank = held
    style = (
        jnp.dot(latent[...], affine_w[...], precision=lax.Precision.HIGHEST, preferred_element_type=F32)
        + affine_b[...]
    )
    filters, in_ch = bank.shape[0], bank.shape[3]
    weights = [select[0, k].astype(F32) for k in range(filters)]
    total = jnp.zeros(bank.shape[2:], F32)
    for tap in range(TAPS):
        plain = mixed(bank, weights, tap) * style
        plain_out[tap] = plain
        total = total + plain * plain
    plain_out[TAPS] = jnp.broadcast_to(jnp.sum(total, axis=1, keepdims=True), total.shape)
    small[...] = jnp.zeros(small.shape, F32)
    last = latent.shape[1] // in_ch
    for n in range(last):
        small[n : n + 1] = latent[:, n * in_ch : (n + 1) * in_ch]
    small[last : last + 1] = style
    lane = lax.broadcasted_iota(jnp.int32, (1, in_ch), 1)
    row = jnp.zeros((1, in_ch), F32)
    for k in range(filters):
        row = jnp.where(lane == k, weights[k], row)
    small[last + 1 : last + 2] = row


def blocks_kernel(rows, size, place, *refs):
    parts, (whole, scale_out), outs, (by_row, by_chan) = refs[:rows], refs[rows : rows + 2], refs[rows + 2 : -2], refs[-2:]
    row_at, chan_at, sign = place[2], place[1], place[3]
    energy = parts[0][TAPS]
    for part in parts[1:]:
        energy = energy + part[TAPS]
    scale = lax.rsqrt(energy[:, 0:1] + EPS)
    scale_out[...] = jnp.broadcast_to(scale, scale_out.shape)
    for r in range(rows):
        by_row[lax.rem(row_at - r + rows, rows)] = parts[r][0:TAPS]
    ch = whole.shape[2] // size
    taps = []
    for tap in range(TAPS):
        value = beside([by_row[r, tap] for r in range(rows)]) * scale
        whole[tap] = value.astype(BF16)
        taps.append(value)
    for z in range(size):
        by_chan[z] = beside([value[:, z * ch : (z + 1) * ch] for value in taps]).astype(BF16)
    for d in range(size):
        outs[d][...] = by_chan[lax.rem(chan_at + sign * d + size, size)]
    outs[size][...] = by_chan[size - 1 - chan_at]


def shifted(x, by):
    width = x.shape[1]
    lane = lax.broadcasted_iota(jnp.int32, x.shape, 1)
    moved = pltpu.roll(x, by % width, 1)
    return jnp.where(lane == (0 if by == 1 else width - 1), 0.0, moved)


def spread(wide, row, x):
    ch, width = x.shape
    wide[ch : 2 * ch, row * width : (row + 1) * width] = x
    x = x.astype(F32)
    wide[0:ch, row * width : (row + 1) * width] = shifted(x, 1).astype(BF16)
    wide[2 * ch : 3 * ch, row * width : (row + 1) * width] = shifted(x, -1).astype(BF16)


def rows_kernel(height, width, feat, feat_before, feat_after, out):
    out[:, 0:width] = feat_before[...]
    out[:, width : (height + 1) * width] = feat[...]
    out[:, (height + 1) * width :] = feat_after[...]


def tap_products(g_ref, wides, totals, height, width):
    for total in totals:
        total[...] = jnp.zeros(total.shape, F32)

    def body(row, _):
        g = g_ref[:, pl.ds(pl.multiple_of(row * width, width), width)]
        for wide, total in zip(wides, totals):
            for kh in range(3):
                x = wide[:, pl.ds(pl.multiple_of((row + kh) * width, width), width)]
                total[kh] += lax.dot_general(g, x, (((1,), (1,)), ((), ())), preferred_element_type=F32)
        return 0

    lax.fori_loop(0, height, body, 0)
    return [jnp.concatenate([total[kh] for kh in range(3)], axis=1).astype(BF16) for total in totals]


def near_grad_kernel(height, width, *refs):
    cotans, feat, mods, (own, behind, ahead), (wide, gathered, total) = refs[:3], refs[3], refs[4:6], refs[6:9], refs[9:]
    ch = feat.shape[0]
    for at, cotan in enumerate(cotans):
        gathered[at * ch : (at + 1) * ch] = cotan[...]
    for row in range(height + 2):
        spread(wide, row, feat[:, row * width : (row + 1) * width])
    (whole,) = tap_products(gathered, [wide], [total], height, width)
    own[...] = whole[0:ch]
    for at, (out, mod) in enumerate(zip((behind, ahead), mods)):
        out[0:ch] = whole[(at + 1) * ch : (at + 2) * ch]
        out[ch:] = mod[...]


def middle_grad_kernel(count, height, width, *refs):
    first, second, wide, mods = refs[:count], refs[count : 2 * count], refs[2 * count], refs[2 * count + 1 : 3 * count + 1]
    out, middle, end_block, total = refs[3 * count + 1 :]
    ch = end_block.shape[0]
    for at in range(count):
        middle[at * ch : (at + 1) * ch] = first[at][...] + second[count - 1 - at][...]
    end_block[...] = first[-1][...] + second[-1][...]
    (out[0 : count * ch],) = tap_products(middle, [wide], [total], height, width)
    for at, mod in enumerate(mods):
        out[(count + at) * ch : (count + at + 1) * ch] = mod[...]


def end_grad_kernel(height, width, end_block, feat, out, wide, total):
    for row in range(height + 2):
        spread(wide, row, feat[:, row * width : (row + 1) * width])
    (out[...],) = tap_products(end_block, [wide], [total], height, width)


def input_grad_kernel(rows, size, height, width, place, cotan, first, second, middle, far, own_mod, behind, ahead, others, end_mod, *refs):
    main, before, after, gathered, taps_t, total = refs
    ch = main.shape[0]
    spot = jnp.where(place[3] > 0, place[1], size - 1 - place[1])
    gathered[0:ch] = cotan[...]
    gathered[ch : 2 * ch] = jnp.where(spot == 0, far[...], first[...])
    gathered[2 * ch : (size - 1) * ch] = middle[...]
    gathered[(size - 1) * ch :] = jnp.where(spot == size - 1, far[...], second[...])
    mods = [own_mod[...], jnp.where(spot == 0, end_mod[...], behind[ch:])]
    mods.append(others[(size - 3) * ch :])
    mods.append(jnp.where(spot == size - 1, end_mod[...], ahead[ch:]))
    every = jnp.concatenate([mod.astype(F32) for mod in mods], axis=0)
    taps_t[...] = every.T.astype(BF16)
    total[...] = jnp.zeros(total.shape, F32)

    def body(row, _):
        g = gathered[:, pl.ds(pl.multiple_of(row * width, width), width)]
        for kh in range(3):
            y = jnp.dot(taps_t[kh * 3 * ch : (kh + 1) * 3 * ch], g, preferred_element_type=F32)
            total[row + kh] += y
        return 0

    lax.fori_loop(0, height, body, 0)
    for row in range(height + 2):
        value = total[row, ch : 2 * ch]
        value = value + shifted(total[row, 0:ch], -1) + shifted(total[row, 2 * ch : 3 * ch], 1)
        if row == 0:
            before[...] = value
        elif row == height + 1:
            after[...] = jnp.where(place[2] == 1, before[...], value) if rows == 2 else value
        else:
            main[:, (row - 1) * width : row * width] = value


def split3(x):
    high = x.astype(BF16).astype(F32)
    mid = (x - high).astype(BF16).astype(F32)
    return high, mid, x - high - mid


def put_columns(out, columns):
    lane = lax.broadcasted_iota(jnp.int32, out.shape[1:], 1)
    last = jnp.zeros(out.shape[1:], F32)
    for n, column in enumerate(columns):
        for at, piece in enumerate(split3(column)):
            last = jnp.where(lane == 3 * n + at, piece, last)
    out[TAPS] = last.astype(BF16)


def get_column(last, n=0):
    last = last.astype(F32)
    return last[:, 3 * n : 3 * n + 1] + last[:, 3 * n + 1 : 3 * n + 2] + last[:, 3 * n + 2 : 3 * n + 3]


def collect_kernel(rows, size, place, scale, whole_mod, own, ahead, behind, others, end, *refs):
    outs, (by_chan, by_row) = refs[:rows], refs[rows:]
    chan_at, row_at, sign = place[1], place[2], place[3]
    ch = own.shape[0]
    by_chan[chan_at] = own[...].astype(F32)
    by_chan[lax.rem(chan_at + sign + size, size)] = ahead[0:ch].astype(F32)
    by_chan[lax.rem(chan_at - sign + size, size)] = behind[0:ch].astype(F32)
    for d in range(2, size - 1):
        value = others[(d - 2) * ch : (d - 1) * ch].astype(F32)
        by_chan[lax.rem(chan_at + sign * d + size, size)] = value
    by_chan[jnp.where(chan_at == 0, size - 1, 0)] += end[...].astype(F32)
    in_ch = outs[0].shape[2]
    product = jnp.zeros(whole_mod.shape[1:], F32)
    for tap in range(TAPS):
        value = beside([by_chan[z, :, tap * ch : (tap + 1) * ch] for z in range(size)])
        product = product + value * whole_mod[tap].astype(F32)
        for r in range(rows):
            by_row[r, tap] = value[:, r * in_ch : (r + 1) * in_ch].astype(BF16)
    fall = jnp.sum(product, axis=1, keepdims=True) * (scale[:, 0:1] * scale[:, 0:1])
    for r in range(rows):
        outs[r][0:TAPS] = by_row[lax.rem(row_at + r, rows)]
        put_columns(outs[r], [fall])


def row_sum_kernel(scale, small, *refs):
    parts, out = refs[:-1], refs[-1]
    fall = get_column(parts[0][TAPS])
    for part in parts[1:]:
        fall = fall + get_column(part[TAPS])
    for tap in range(TAPS):
        value = parts[0][tap].astype(F32)
        for part in parts[1:]:
            value = value + part[tap].astype(F32)
        out[tap] = value.astype(BF16)
    put_columns(out, [fall, scale[:, 0:1]])
    out_ch, in_ch = out.shape[1:]
    pieces = list(split3(small[...]))
    spare = (out.shape[0] - TAPS - 1) * out_ch - 3 * small.shape[0]
    if spare:
        pieces.append(jnp.zeros((spare, in_ch), F32))
    pieces = jnp.concatenate(pieces, axis=0).astype(BF16)
    for n in range(out.shape[0] - TAPS - 1):
        out[TAPS + 1 + n] = pieces[n * out_ch : (n + 1) * out_ch]


def bank_grad_kernel(samples, small_rows, place, bank, *refs):
    parts, (bank_out, style_grad, latents, held, bank_grad, sems) = refs[:samples], refs[samples:]
    copies = [pltpu.make_async_copy(bank_grad.at[:, tap], bank_out.at[:, tap], sems.at[tap]) for tap in range(TAPS)]
    for part, step in zip(parts, steps_of(samples)):
        held[partner(place[0], step, samples)] = part[...]
    filters, in_ch = bank.shape[0], bank.shape[3]
    last = latents.shape[1] // in_ch
    sel, styles, scales, falls = [], [], [], []
    for b in range(samples):
        rows = jnp.concatenate([held[b, n].astype(F32) for n in range(TAPS + 1, held.shape[1])], axis=0)
        small = rows[:small_rows] + rows[small_rows : 2 * small_rows] + rows[2 * small_rows : 3 * small_rows]
        latents[b : b + 1] = beside([small[n : n + 1] for n in range(last)])
        styles.append(small[last : last + 1])
        sel.append([small[last + 1 : last + 2, k : k + 1] for k in range(filters)])
        falls.append(get_column(held[b, TAPS]))
        scales.append(get_column(held[b, TAPS], 1))
    sums = [jnp.zeros(bank.shape[2:], F32) for _ in range(samples)]
    for tap in range(TAPS):
        totals = [None] * filters
        for b in range(samples):
            kern = mixed(bank, sel[b], tap)
            plain_grad = held[b, tap].astype(F32) * scales[b] - kern * styles[b] * falls[b]
            sums[b] = sums[b] + plain_grad * kern
            kernel_grad = plain_grad * styles[b]
            for k in range(filters):
                term = sel[b][k] * kernel_grad
                totals[k] = term if totals[k] is None else totals[k] + term
        for k in range(filters):
            bank_grad[k, tap] = totals[k]
        copies[tap].start()
    for b in range(samples):
        value = jnp.sum(sums[b], axis=0, keepdims=True)
        style_grad[b : b + 1] = value
    for copy in copies:
        copy.wait()


def pair_sum(parts):
    while len(parts) > 1:
        parts = [x + y for x, y in zip(parts[::2], parts[1::2])]
    return parts[0]


def affine_kernel(samples, latents, *refs):
    parts, (w_grad, b_grad) = refs[:-2], refs[-2:]
    style_grad = pair_sum([part[...] for part in parts])
    high, mid, low = split3(latents[...])
    top, middle, bottom = split3(style_grad)
    w_grad[...] = lax.dot_general(
        jnp.concatenate([high, high, mid, high, mid, low], axis=0).astype(BF16),
        jnp.concatenate([top, middle, top, bottom, middle, top], axis=0).astype(BF16),
        (((0,), (0,)), ((), ())),
        preferred_element_type=F32,
    )
    bias = style_grad[0:1]
    for b in range(1, samples):
        bias = bias + style_grad[b : b + 1]
    b_grad[...] = bias


def call(kernel, name, outs, *operands, scalars=0, fetched=0, kept=0, scratch=(), flops=10**6):
    outs = tuple(jax.ShapeDtypeStruct(*o) for o in outs)
    moved = sum(o.size * o.dtype.itemsize for o in (*outs, *operands))
    return pl.pallas_call(
        kernel,
        out_shape=outs,
        in_specs=sspec(scalars)
        + vspec(len(operands) - scalars - fetched)
        + [pl.BlockSpec(memory_space=pltpu.HBM)] * fetched,
        out_specs=tuple([pl.BlockSpec(memory_space=pltpu.HBM)] * kept + vspec(len(outs) - kept)),
        scratch_shapes=[pltpu.VMEM(*s) if isinstance(s, tuple) else s for s in scratch],
        compiler_params=params(),
        cost_estimate=cost(flops, moved),
        name=name,
    )(*operands)


def partner(at, step, size):
    return at ^ step if size & (size - 1) == 0 else (at - step + size) % size


def steps_of(size):
    return [0] + sorted(range(1, size), key=lambda n: (n < 2, n))


def exchange_pairs(x, axis):
    size = lax.axis_size(axis)
    return [x] + [
        lax.ppermute(x, axis, [(partner(i, step, size), i) for i in range(size)]) for step in steps_of(size)[1:]
    ]


def exchange(x, axis):
    size = lax.axis_size(axis)
    return [x] + [
        lax.ppermute(x, axis, [(i, (i + s) % size) for i in range(size)]) for s in range(1, size)
    ]


def terms_of_sum(x, axis):
    size = lax.axis_size(axis)
    if size & (size - 1):
        return [lax.psum(x, axis)]
    return [x] + [lax.ppermute(x, axis, [(i, i ^ step) for i in range(size)]) for step in range(1, size)]


def from_sides(first, last, axis):
    size, at = lax.axis_size(axis), lax.axis_index(axis)
    if size == 2:
        edge = last if first is None else jnp.where(at == 0, last, first)
        got = lax.ppermute(edge, axis, [(0, 1), (1, 0)])
        nothing = jnp.zeros_like(got)
        return jnp.where(at == 1, got, nothing), jnp.where(at == 0, got, nothing)
    up = [(i, i + 1) for i in range(size - 1)]
    down = [(i + 1, i) for i in range(size - 1)]
    return lax.ppermute(last, axis, up), lax.ppermute(first, axis, down)


def on_device(feature, out_grad, bank, select, latent, affine_w, affine_b):
    rows, samples, size = (lax.axis_size(a) for a in ("rows", "samples", "chan"))
    row_at, sample_at, chan_at = (lax.axis_index(a) for a in ("rows", "samples", "chan"))
    _, ch, height, width = feature.shape
    out_ch, in_ch = bank.shape[2:]
    pixels, all_ch = height * width, ch * size
    sign = 1 - 2 * jnp.remainder(sample_at, 2)
    place = jnp.stack([sample_at, chan_at, row_at, sign]).astype(jnp.int32)
    flops = 2 * TAPS * ch * ch * size * pixels

    def along(x, pairs):
        whole = []
        for b in range(samples):
            for i, j in pairs:
                if b % 2:
                    i, j = size - 1 - i, size - 1 - j
                whole.append((b * size + i, b * size + j))
        return lax.ppermute(x, ("samples", "chan"), whole)

    cotan = out_grad[0].reshape(ch, pixels)
    first, second = [], []

    def step(number, x, y):
        first.append(along(x, [(i, i + 1) for i in range(number - 1, size - 1)]))
        second.append(along(y, [(i + 1, i) for i in range(size - number)]))

    step(1, cotan, cotan)

    small_rows = -(-(latent.shape[1] // in_ch + 2) // 8) * 8
    plain, small = call(
        plain_kernel,
        "plain",
        [((TAPS + 1, out_ch, in_ch), F32), ((small_rows, in_ch), F32)],
        select,
        latent,
        affine_b[None],
        affine_w,
        bank,
        fetched=5,
        scratch=[
            pltpu.SMEM(select.shape, jnp.int32),
            (latent.shape, F32),
            ((1, in_ch), F32),
            (affine_w.shape, F32),
            (bank.shape, F32),
            pltpu.SemaphoreType.DMA((5,)),
        ],
    )
    plains = exchange(plain, "rows")
    feature, cotan = lax.optimization_barrier((feature, cotan))
    feat = feature[0].reshape(ch, pixels)
    feat_before, feat_after = from_sides(feat[:, :width], feat[:, pixels - width :], "rows")
    extended = ((ch, (height + 2) * width), BF16)
    (feat,) = call(
        functools.partial(rows_kernel, height, width), "feat_rows", [extended], feat, feat_before, feat_after
    )
    feat, plain = lax.optimization_barrier((feat, plain))
    feat_end = lax.ppermute(feat, "chan", [(0, 1), (size - 1, size - 2)])
    message = ((ch, TAPS * ch), BF16)
    whole_mod, scale, *mods = call(
        functools.partial(blocks_kernel, rows, size),
        "mod_blocks",
        [((TAPS, out_ch, all_ch), BF16), ((out_ch, 128), F32)] + [message] * (size + 1),
        place,
        *plains,
        scalars=1,
        scratch=[((rows, TAPS, out_ch, in_ch), F32), ((size, *message[0]), BF16)],
    )
    first[0], second[0], plains = lax.optimization_barrier((first[0], second[0], plains))

    step(2, first[0], second[0])
    double = ((2 * ch, TAPS * ch), BF16)
    own_grad, to_behind, to_ahead, wide = call(
        functools.partial(near_grad_kernel, height, width),
        "near_grad",
        [message, double, double, ((3 * ch, (height + 2) * width), BF16)],
        cotan,
        first[0],
        second[0],
        feat,
        mods[size - 1],
        mods[1],
        scratch=[((3 * ch, pixels), BF16), ((3, 3 * ch, 3 * ch), F32)],
        flops=flops * 3 // size,
    )
    from_ahead = along(to_behind, [(i + 1, i) for i in range(size - 1)])
    from_behind = along(to_ahead, [(i, i + 1) for i in range(size - 1)])
    first[1], second[1], feat_end, wide, whole_mod = lax.optimization_barrier(
        (first[1], second[1], feat_end, wide, whole_mod)
    )

    count = size - 3
    grad_others, middle, end_block = call(
        functools.partial(middle_grad_kernel, count, height, width),
        "middle_grad",
        [((2 * count * ch, TAPS * ch), BF16), ((count * ch, pixels), BF16), ((ch, pixels), BF16)],
        *first[1:],
        *second[1:],
        wide,
        *mods[2 : size - 1],
        scratch=[((3, count * ch, 3 * ch), F32)],
        flops=flops // size,
    )
    (grad_end,) = call(
        functools.partial(end_grad_kernel, height, width),
        "end_grad",
        [message],
        end_block,
        feat_end,
        scratch=[((3 * ch, (height + 2) * width), BF16), ((3, ch, 3 * ch), F32)],
        flops=flops // size,
    )
    from_others = along(grad_others, [(i, (i + 2) % size) for i in range(size)])
    from_end = lax.ppermute(grad_end, "chan", [(1, size - 1), (size - 2, 0)])
    end_block, grad_end = lax.optimization_barrier((end_block, grad_end))
    far = lax.ppermute(end_block, "chan", [(1, 0), (size - 2, size - 1)])
    parts = call(
        functools.partial(collect_kernel, rows, size),
        "collect",
        [((TAPS + 1, out_ch, in_ch), BF16)] * rows,
        place,
        scale,
        whole_mod,
        own_grad,
        from_ahead,
        from_behind,
        from_others,
        from_end,
        scalars=1,
        scratch=[((size, *message[0]), F32), ((rows, TAPS, out_ch, in_ch), BF16)],
        flops=COLLECT_FLOPS,
    )
    parts, mods = lax.optimization_barrier((parts, mods))
    end_mod = lax.ppermute(mods[size], "chan", [(0, size - 1), (size - 1, 0)])
    parts = [parts[0]] + [
        lax.ppermute(parts[r], "rows", [(i, (i + r) % rows) for i in range(rows)])
        for r in range(1, rows)
    ]
    slots = TAPS + 1 - (-3 * small_rows // out_ch)
    (own,) = call(row_sum_kernel, "row_sum", [((slots, out_ch, in_ch), BF16)], scale, small, *parts)
    every = exchange_pairs(own, "samples")

    own, end_mod, far = lax.optimization_barrier((own, end_mod, far))
    main, before, after = call(
        functools.partial(input_grad_kernel, rows, size, height, width),
        "input_grad",
        [((ch, pixels), F32), ((ch, width), F32), ((ch, width), F32)],
        place,
        cotan,
        first[0],
        second[0],
        middle,
        far,
        mods[0],
        from_behind,
        from_ahead,
        from_others,
        end_mod,
        scalars=1,
        scratch=[
            ((all_ch, pixels), BF16),
            ((TAPS * ch, all_ch), BF16),
            ((height + 2, 3 * ch, width), F32),
        ],
        flops=INPUT_FLOPS,
    )
    every, main, before, after = lax.optimization_barrier((every, main, before, after))
    from_above, from_below = from_sides(None if rows == 2 else before, after, "rows")
    bank_grad, style_part, latents = call(
        functools.partial(bank_grad_kernel, samples, small_rows),
        "bank_grad",
        [(bank.shape, F32), ((samples, in_ch), F32), ((samples, latent.shape[1]), F32)],
        place,
        bank,
        *every,
        scalars=1,
        scratch=[((samples, slots, out_ch, in_ch), BF16), (bank.shape, F32), pltpu.SemaphoreType.DMA((TAPS,))],
        kept=1,
    )
    style_parts = terms_of_sum(style_part, "chan")
    edge = jnp.concatenate(
        [from_above[:, None], jnp.zeros((ch, height - 2, width), F32), from_below[:, None]], axis=1
    )
    feature_grad = (main.reshape(ch, height, width) + edge).astype(BF16)[None]
    style_parts, feature_grad = lax.optimization_barrier((style_parts, feature_grad))
    affine_w_grad, affine_b_grad = call(
        functools.partial(affine_kernel, samples),
        "affine",
        [(affine_w.shape, F32), ((1, in_ch), F32)],
        latents,
        *style_parts,
    )
    return (feature_grad, bank_grad, affine_w_grad, affine_b_grad[0])


def solution(mesh):
    return jax.shard_map(
        on_device,
        mesh=mesh,
        in_specs=(
            P("samples", "chan", "rows", None),
            P("samples", "chan", "rows", None),
            P(None, None, "chan", "rows"),
            P("samples", None),
            P("samples", None),
            P(None, "rows"),
            P("rows"),
        ),
        out_specs=(
            P("samples", "chan", "rows", None),
            P(None, None, "chan", "rows"),
            P(None, "rows"),
            P("rows"),
        ),
        check_vma=False,
    )
```

```python
import functools

import jax
import jax.numpy as jnp
from jax import lax
from jax.experimental import pallas as pl
from jax.experimental.pallas import tpu as pltpu
from jax.sharding import PartitionSpec as P

EPS = 1e-08
TAPS = 9
F32 = jnp.float32
BF16 = jnp.bfloat16
VMEM_LIMIT = 10 * 2**20
COLLECT_FLOPS = 6 * 10**9
INPUT_FLOPS = 2 * 10**9


def params():
    return pltpu.CompilerParams(vmem_limit_bytes=VMEM_LIMIT)


def vspec(n):
    return [pl.BlockSpec(memory_space=pltpu.VMEM)] * n


def sspec(n):
    return [pl.BlockSpec(memory_space=pltpu.SMEM)] * n


def cost(flops, moved):
    return pl.CostEstimate(flops=flops, bytes_accessed=moved, transcendentals=0)


def beside(pieces):
    return pieces[0] if len(pieces) == 1 else jnp.concatenate(pieces, axis=1)


def mixed(bank_ref, weights, tap):
    total = weights[0] * bank_ref[0, tap]
    for k in range(1, bank_ref.shape[0]):
        total = total + weights[k] * bank_ref[k, tap]
    return total


def plain_kernel(*refs):
    given, (plain_out, small), held, sems = refs[:5], refs[5:7], refs[7:12], refs[12]
    copies = [pltpu.make_async_copy(x, y, sems.at[n]) for n, (x, y) in enumerate(zip(given, held))]
    for copy in copies:
        copy.start()
    for copy in copies:
        copy.wait()
    select, latent, affine_b, affine_w, bank = held
    style = (
        jnp.dot(latent[...], affine_w[...], precision=lax.Precision.HIGHEST, preferred_element_type=F32)
        + affine_b[...]
    )
    filters, in_ch = bank.shape[0], bank.shape[3]
    weights = [select[0, k].astype(F32) for k in range(filters)]
    total = jnp.zeros(bank.shape[2:], F32)
    for tap in range(TAPS):
        plain = mixed(bank, weights, tap) * style
        plain_out[tap] = plain
        total = total + plain * plain
    plain_out[TAPS] = jnp.broadcast_to(jnp.sum(total, axis=1, keepdims=True), total.shape)
    small[...] = jnp.zeros(small.shape, F32)
    last = latent.shape[1] // in_ch
    for n in range(last):
        small[n : n + 1] = latent[:, n * in_ch : (n + 1) * in_ch]
    small[last : last + 1] = style
    lane = lax.broadcasted_iota(jnp.int32, (1, in_ch), 1)
    row = jnp.zeros((1, in_ch), F32)
    for k in range(filters):
        row = jnp.where(lane == k, weights[k], row)
    small[last + 1 : last + 2] = row


def blocks_kernel(rows, size, place, *refs):
    parts, (whole, scale_out), outs, (by_row, by_chan) = refs[:rows], refs[rows : rows + 2], refs[rows + 2 : -2], refs[-2:]
    row_at, chan_at, sign = place[2], place[1], place[3]
    energy = parts[0][TAPS]
    for part in parts[1:]:
        energy = energy + part[TAPS]
    scale = lax.rsqrt(energy[:, 0:1] + EPS)
    scale_out[...] = jnp.broadcast_to(scale, scale_out.shape)
    for r in range(rows):
        by_row[lax.rem(row_at - r + rows, rows)] = parts[r][0:TAPS]
    ch = whole.shape[2] // size
    taps = []
    for tap in range(TAPS):
        value = beside([by_row[r, tap] for r in range(rows)]) * scale
        whole[tap] = value.astype(BF16)
        taps.append(value)
    for z in range(size):
        by_chan[z] = beside([value[:, z * ch : (z + 1) * ch] for value in taps]).astype(BF16)
    for d in range(size):
        outs[d][...] = by_chan[lax.rem(chan_at + sign * d + size, size)]
    outs[size][...] = by_chan[size - 1 - chan_at]


def shifted(x, by):
    width = x.shape[1]
    lane = lax.broadcasted_iota(jnp.int32, x.shape, 1)
    moved = pltpu.roll(x, by % width, 1)
    return jnp.where(lane == (0 if by == 1 else width - 1), 0.0, moved)


def spread(wide, row, x):
    ch, width = x.shape
    wide[ch : 2 * ch, row * width : (row + 1) * width] = x
    x = x.astype(F32)
    wide[0:ch, row * width : (row + 1) * width] = shifted(x, 1).astype(BF16)
    wide[2 * ch : 3 * ch, row * width : (row + 1) * width] = shifted(x, -1).astype(BF16)


def rows_kernel(height, width, feat, feat_before, feat_after, out):
    out[:, 0:width] = feat_before[...]
    out[:, width : (height + 1) * width] = feat[...]
    out[:, (height + 1) * width :] = feat_after[...]


def tap_products(g_ref, wides, totals, height, width):
    for total in totals:
        total[...] = jnp.zeros(total.shape, F32)

    def body(row, _):
        g = g_ref[:, pl.ds(pl.multiple_of(row * width, width), width)]
        for wide, total in zip(wides, totals):
            for kh in range(3):
                x = wide[:, pl.ds(pl.multiple_of((row + kh) * width, width), width)]
                total[kh] += lax.dot_general(g, x, (((1,), (1,)), ((), ())), preferred_element_type=F32)
        return 0

    lax.fori_loop(0, height, body, 0)
    return [jnp.concatenate([total[kh] for kh in range(3)], axis=1).astype(BF16) for total in totals]


def near_grad_kernel(height, width, *refs):
    cotans, feat, mods, (own, behind, ahead), (wide, gathered, total) = refs[:3], refs[3], refs[4:6], refs[6:9], refs[9:]
    ch = feat.shape[0]
    for at, cotan in enumerate(cotans):
        gathered[at * ch : (at + 1) * ch] = cotan[...]
    for row in range(height + 2):
        spread(wide, row, feat[:, row * width : (row + 1) * width])
    (whole,) = tap_products(gathered, [wide], [total], height, width)
    own[...] = whole[0:ch]
    for at, (out, mod) in enumerate(zip((behind, ahead), mods)):
        out[0:ch] = whole[(at + 1) * ch : (at + 2) * ch]
        out[ch:] = mod[...]


def middle_grad_kernel(count, height, width, *refs):
    first, second, wide, mods = refs[:count], refs[count : 2 * count], refs[2 * count], refs[2 * count + 1 : 3 * count + 1]
    out, middle, end_block, total = refs[3 * count + 1 :]
    ch = end_block.shape[0]
    for at in range(count):
        middle[at * ch : (at + 1) * ch] = first[at][...] + second[count - 1 - at][...]
    end_block[...] = first[-1][...] + second[-1][...]
    (out[0 : count * ch],) = tap_products(middle, [wide], [total], height, width)
    for at, mod in enumerate(mods):
        out[(count + at) * ch : (count + at + 1) * ch] = mod[...]


def end_grad_kernel(height, width, end_block, feat, out, wide, total):
    for row in range(height + 2):
        spread(wide, row, feat[:, row * width : (row + 1) * width])
    (out[...],) = tap_products(end_block, [wide], [total], height, width)


def input_grad_kernel(rows, size, height, width, place, cotan, first, second, middle, far, own_mod, behind, ahead, others, end_mod, *refs):
    main, before, after, gathered, taps_t = refs
    ch = main.shape[0]
    spot = jnp.where(place[3] > 0, place[1], size - 1 - place[1])
    gathered[0:ch] = cotan[...]
    gathered[ch : 2 * ch] = jnp.where(spot == 0, far[...], first[...])
    gathered[2 * ch : (size - 1) * ch] = middle[...]
    gathered[(size - 1) * ch :] = jnp.where(spot == size - 1, far[...], second[...])
    mods = [own_mod[...], jnp.where(spot == 0, end_mod[...], behind[ch:])]
    mods.append(others[(size - 3) * ch :])
    mods.append(jnp.where(spot == size - 1, end_mod[...], ahead[ch:]))
    every = jnp.concatenate([mod.astype(F32) for mod in mods], axis=0)
    taps_t[...] = every.T.astype(BF16)
    for row in range(height + 2):
        total = None
        for kh in range(3):
            if 0 <= row - kh < height:
                g = gathered[:, (row - kh) * width : (row - kh + 1) * width]
                y = jnp.dot(taps_t[kh * 3 * ch : (kh + 1) * 3 * ch], g, preferred_element_type=F32)
                total = y if total is None else total + y
        value = total[ch : 2 * ch]
        value = value + shifted(total[0:ch], -1) + shifted(total[2 * ch : 3 * ch], 1)
        if row == 0:
            before[...] = value
        elif row == height + 1:
            after[...] = jnp.where(place[2] == 1, before[...], value) if rows == 2 else value
        else:
            main[:, (row - 1) * width : row * width] = value


def split3(x):
    high = x.astype(BF16).astype(F32)
    mid = (x - high).astype(BF16).astype(F32)
    return high, mid, x - high - mid


def put_columns(out, columns):
    lane = lax.broadcasted_iota(jnp.int32, out.shape[1:], 1)
    last = jnp.zeros(out.shape[1:], F32)
    for n, column in enumerate(columns):
        for at, piece in enumerate(split3(column)):
            last = jnp.where(lane == 3 * n + at, piece, last)
    out[TAPS] = last.astype(BF16)


def get_column(last, n=0):
    last = last.astype(F32)
    return last[:, 3 * n : 3 * n + 1] + last[:, 3 * n + 1 : 3 * n + 2] + last[:, 3 * n + 2 : 3 * n + 3]


def collect_kernel(rows, size, place, scale, whole_mod, own, ahead, behind, others, end, *refs):
    outs, (by_chan, by_row) = refs[:rows], refs[rows:]
    chan_at, row_at, sign = place[1], place[2], place[3]
    ch = own.shape[0]
    by_chan[chan_at] = own[...].astype(F32)
    by_chan[lax.rem(chan_at + sign + size, size)] = ahead[0:ch].astype(F32)
    by_chan[lax.rem(chan_at - sign + size, size)] = behind[0:ch].astype(F32)
    for d in range(2, size - 1):
        value = others[(d - 2) * ch : (d - 1) * ch].astype(F32)
        by_chan[lax.rem(chan_at + sign * d + size, size)] = value
    by_chan[jnp.where(chan_at == 0, size - 1, 0)] += end[...].astype(F32)
    in_ch = outs[0].shape[2]
    product = jnp.zeros(whole_mod.shape[1:], F32)
    for tap in range(TAPS):
        value = beside([by_chan[z, :, tap * ch : (tap + 1) * ch] for z in range(size)])
        product = product + value * whole_mod[tap].astype(F32)
        for r in range(rows):
            by_row[r, tap] = value[:, r * in_ch : (r + 1) * in_ch].astype(BF16)
    fall = jnp.sum(product, axis=1, keepdims=True) * (scale[:, 0:1] * scale[:, 0:1])
    for r in range(rows):
        outs[r][0:TAPS] = by_row[lax.rem(row_at + r, rows)]
        put_columns(outs[r], [fall])


def row_sum_kernel(scale, small, *refs):
    parts, out = refs[:-1], refs[-1]
    fall = get_column(parts[0][TAPS])
    for part in parts[1:]:
        fall = fall + get_column(part[TAPS])
    for tap in range(TAPS):
        value = parts[0][tap].astype(F32)
        for part in parts[1:]:
            value = value + part[tap].astype(F32)
        out[tap] = value.astype(BF16)
    put_columns(out, [fall, scale[:, 0:1]])
    out_ch, in_ch = out.shape[1:]
    pieces = list(split3(small[...]))
    spare = (out.shape[0] - TAPS - 1) * out_ch - 3 * small.shape[0]
    if spare:
        pieces.append(jnp.zeros((spare, in_ch), F32))
    pieces = jnp.concatenate(pieces, axis=0).astype(BF16)
    for n in range(out.shape[0] - TAPS - 1):
        out[TAPS + 1 + n] = pieces[n * out_ch : (n + 1) * out_ch]


def bank_grad_kernel(samples, small_rows, place, bank, *refs):
    parts, (bank_out, style_grad, latents, held, bank_grad, sems) = refs[:samples], refs[samples:]
    copies = [pltpu.make_async_copy(bank_grad.at[:, tap], bank_out.at[:, tap], sems.at[tap]) for tap in range(TAPS)]
    for part, step in zip(parts, steps_of(samples)):
        held[partner(place[0], step, samples)] = part[...]
    filters, in_ch = bank.shape[0], bank.shape[3]
    last = latents.shape[1] // in_ch
    sel, styles, scales, falls = [], [], [], []
    for b in range(samples):
        rows = jnp.concatenate([held[b, n].astype(F32) for n in range(TAPS + 1, held.shape[1])], axis=0)
        small = rows[:small_rows] + rows[small_rows : 2 * small_rows] + rows[2 * small_rows : 3 * small_rows]
        latents[b : b + 1] = beside([small[n : n + 1] for n in range(last)])
        styles.append(small[last : last + 1])
        sel.append([small[last + 1 : last + 2, k : k + 1] for k in range(filters)])
        falls.append(get_column(held[b, TAPS]))
        scales.append(get_column(held[b, TAPS], 1))
    sums = [jnp.zeros(bank.shape[2:], F32) for _ in range(samples)]
    for tap in range(TAPS):
        totals = [None] * filters
        for b in range(samples):
            kern = mixed(bank, sel[b], tap)
            plain_grad = held[b, tap].astype(F32) * scales[b] - kern * styles[b] * falls[b]
            sums[b] = sums[b] + plain_grad * kern
            kernel_grad = plain_grad * styles[b]
            for k in range(filters):
                term = sel[b][k] * kernel_grad
                totals[k] = term if totals[k] is None else totals[k] + term
        for k in range(filters):
            bank_grad[k, tap] = totals[k]
        copies[tap].start()
    for b in range(samples):
        value = jnp.sum(sums[b], axis=0, keepdims=True)
        style_grad[b : b + 1] = value
    for copy in copies:
        copy.wait()


def pair_sum(parts):
    while len(parts) > 1:
        parts = [x + y for x, y in zip(parts[::2], parts[1::2])]
    return parts[0]


def affine_kernel(samples, latents, *refs):
    parts, (w_grad, b_grad) = refs[:-2], refs[-2:]
    style_grad = pair_sum([part[...] for part in parts])
    high, mid, low = split3(latents[...])
    top, middle, bottom = split3(style_grad)
    w_grad[...] = lax.dot_general(
        jnp.concatenate([high, high, mid, high, mid, low], axis=0).astype(BF16),
        jnp.concatenate([top, middle, top, bottom, middle, top], axis=0).astype(BF16),
        (((0,), (0,)), ((), ())),
        preferred_element_type=F32,
    )
    bias = style_grad[0:1]
    for b in range(1, samples):
        bias = bias + style_grad[b : b + 1]
    b_grad[...] = bias


def call(kernel, name, outs, *operands, scalars=0, fetched=0, kept=0, scratch=(), flops=10**6):
    outs = tuple(jax.ShapeDtypeStruct(*o) for o in outs)
    moved = sum(o.size * o.dtype.itemsize for o in (*outs, *operands))
    return pl.pallas_call(
        kernel,
        out_shape=outs,
        in_specs=sspec(scalars)
        + vspec(len(operands) - scalars - fetched)
        + [pl.BlockSpec(memory_space=pltpu.HBM)] * fetched,
        out_specs=tuple([pl.BlockSpec(memory_space=pltpu.HBM)] * kept + vspec(len(outs) - kept)),
        scratch_shapes=[pltpu.VMEM(*s) if isinstance(s, tuple) else s for s in scratch],
        compiler_params=params(),
        cost_estimate=cost(flops, moved),
        name=name,
    )(*operands)


def partner(at, step, size):
    return at ^ step if size & (size - 1) == 0 else (at - step + size) % size


def steps_of(size):
    return [0] + sorted(range(1, size), key=lambda n: (n < 2, n))


def exchange_pairs(x, axis):
    size = lax.axis_size(axis)
    return [x] + [
        lax.ppermute(x, axis, [(partner(i, step, size), i) for i in range(size)]) for step in steps_of(size)[1:]
    ]


def exchange(x, axis):
    size = lax.axis_size(axis)
    return [x] + [
        lax.ppermute(x, axis, [(i, (i + s) % size) for i in range(size)]) for s in range(1, size)
    ]


def terms_of_sum(x, axis):
    size = lax.axis_size(axis)
    if size & (size - 1):
        return [lax.psum(x, axis)]
    return [x] + [lax.ppermute(x, axis, [(i, i ^ step) for i in range(size)]) for step in range(1, size)]


def from_sides(first, last, axis):
    size, at = lax.axis_size(axis), lax.axis_index(axis)
    if size == 2:
        edge = last if first is None else jnp.where(at == 0, last, first)
        got = lax.ppermute(edge, axis, [(0, 1), (1, 0)])
        nothing = jnp.zeros_like(got)
        return jnp.where(at == 1, got, nothing), jnp.where(at == 0, got, nothing)
    up = [(i, i + 1) for i in range(size - 1)]
    down = [(i + 1, i) for i in range(size - 1)]
    return lax.ppermute(last, axis, up), lax.ppermute(first, axis, down)


def on_device(feature, out_grad, bank, select, latent, affine_w, affine_b):
    rows, samples, size = (lax.axis_size(a) for a in ("rows", "samples", "chan"))
    row_at, sample_at, chan_at = (lax.axis_index(a) for a in ("rows", "samples", "chan"))
    _, ch, height, width = feature.shape
    out_ch, in_ch = bank.shape[2:]
    pixels, all_ch = height * width, ch * size
    sign = 1 - 2 * jnp.remainder(sample_at, 2)
    place = jnp.stack([sample_at, chan_at, row_at, sign]).astype(jnp.int32)
    flops = 2 * TAPS * ch * ch * size * pixels

    def along(x, pairs):
        whole = []
        for b in range(samples):
            for i, j in pairs:
                if b % 2:
                    i, j = size - 1 - i, size - 1 - j
                whole.append((b * size + i, b * size + j))
        return lax.ppermute(x, ("samples", "chan"), whole)

    cotan = out_grad[0].reshape(ch, pixels)
    first, second = [], []

    def step(number, x, y):
        first.append(along(x, [(i, i + 1) for i in range(number - 1, size - 1)]))
        second.append(along(y, [(i + 1, i) for i in range(size - number)]))

    step(1, cotan, cotan)

    small_rows = -(-(latent.shape[1] // in_ch + 2) // 8) * 8
    plain, small = call(
        plain_kernel,
        "plain",
        [((TAPS + 1, out_ch, in_ch), F32), ((small_rows, in_ch), F32)],
        select,
        latent,
        affine_b[None],
        affine_w,
        bank,
        fetched=5,
        scratch=[
            pltpu.SMEM(select.shape, jnp.int32),
            (latent.shape, F32),
            ((1, in_ch), F32),
            (affine_w.shape, F32),
            (bank.shape, F32),
            pltpu.SemaphoreType.DMA((5,)),
        ],
    )
    plains = exchange(plain, "rows")
    feature, cotan = lax.optimization_barrier((feature, cotan))
    feat = feature[0].reshape(ch, pixels)
    feat_before, feat_after = from_sides(feat[:, :width], feat[:, pixels - width :], "rows")
    extended = ((ch, (height + 2) * width), BF16)
    (feat,) = call(
        functools.partial(rows_kernel, height, width), "feat_rows", [extended], feat, feat_before, feat_after
    )
    feat, plain = lax.optimization_barrier((feat, plain))
    feat_end = lax.ppermute(feat, "chan", [(0, 1), (size - 1, size - 2)])
    message = ((ch, TAPS * ch), BF16)
    whole_mod, scale, *mods = call(
        functools.partial(blocks_kernel, rows, size),
        "mod_blocks",
        [((TAPS, out_ch, all_ch), BF16), ((out_ch, 128), F32)] + [message] * (size + 1),
        place,
        *plains,
        scalars=1,
        scratch=[((rows, TAPS, out_ch, in_ch), F32), ((size, *message[0]), BF16)],
    )
    first[0], second[0], plains = lax.optimization_barrier((first[0], second[0], plains))

    step(2, first[0], second[0])
    double = ((2 * ch, TAPS * ch), BF16)
    own_grad, to_behind, to_ahead, wide = call(
        functools.partial(near_grad_kernel, height, width),
        "near_grad",
        [message, double, double, ((3 * ch, (height + 2) * width), BF16)],
        cotan,
        first[0],
        second[0],
        feat,
        mods[size - 1],
        mods[1],
        scratch=[((3 * ch, pixels), BF16), ((3, 3 * ch, 3 * ch), F32)],
        flops=flops * 3 // size,
    )
    from_ahead = along(to_behind, [(i + 1, i) for i in range(size - 1)])
    from_behind = along(to_ahead, [(i, i + 1) for i in range(size - 1)])
    first[1], second[1], feat_end, wide, whole_mod = lax.optimization_barrier(
        (first[1], second[1], feat_end, wide, whole_mod)
    )

    count = size - 3
    grad_others, middle, end_block = call(
        functools.partial(middle_grad_kernel, count, height, width),
        "middle_grad",
        [((2 * count * ch, TAPS * ch), BF16), ((count * ch, pixels), BF16), ((ch, pixels), BF16)],
        *first[1:],
        *second[1:],
        wide,
        *mods[2 : size - 1],
        scratch=[((3, count * ch, 3 * ch), F32)],
        flops=flops // size,
    )
    (grad_end,) = call(
        functools.partial(end_grad_kernel, height, width),
        "end_grad",
        [message],
        end_block,
        feat_end,
        scratch=[((3 * ch, (height + 2) * width), BF16), ((3, ch, 3 * ch), F32)],
        flops=flops // size,
    )
    from_others = along(grad_others, [(i, (i + 2) % size) for i in range(size)])
    from_end = lax.ppermute(grad_end, "chan", [(1, size - 1), (size - 2, 0)])
    end_block, grad_end = lax.optimization_barrier((end_block, grad_end))
    far = lax.ppermute(end_block, "chan", [(1, 0), (size - 2, size - 1)])
    parts = call(
        functools.partial(collect_kernel, rows, size),
        "collect",
        [((TAPS + 1, out_ch, in_ch), BF16)] * rows,
        place,
        scale,
        whole_mod,
        own_grad,
        from_ahead,
        from_behind,
        from_others,
        from_end,
        scalars=1,
        scratch=[((size, *message[0]), F32), ((rows, TAPS, out_ch, in_ch), BF16)],
        flops=COLLECT_FLOPS,
    )
    parts, mods = lax.optimization_barrier((parts, mods))
    end_mod = lax.ppermute(mods[size], "chan", [(0, size - 1), (size - 1, 0)])
    parts = [parts[0]] + [
        lax.ppermute(parts[r], "rows", [(i, (i + r) % rows) for i in range(rows)])
        for r in range(1, rows)
    ]
    slots = TAPS + 1 - (-3 * small_rows // out_ch)
    (own,) = call(row_sum_kernel, "row_sum", [((slots, out_ch, in_ch), BF16)], scale, small, *parts)
    every = exchange_pairs(own, "samples")

    own, end_mod, far = lax.optimization_barrier((own, end_mod, far))
    main, before, after = call(
        functools.partial(input_grad_kernel, rows, size, height, width),
        "input_grad",
        [((ch, pixels), F32), ((ch, width), F32), ((ch, width), F32)],
        place,
        cotan,
        first[0],
        second[0],
        middle,
        far,
        mods[0],
        from_behind,
        from_ahead,
        from_others,
        end_mod,
        scalars=1,
        scratch=[
            ((all_ch, pixels), BF16),
            ((TAPS * ch, all_ch), BF16),
        ],
        flops=INPUT_FLOPS,
    )
    every, main, before, after = lax.optimization_barrier((every, main, before, after))
    from_above, from_below = from_sides(None if rows == 2 else before, after, "rows")
    bank_grad, style_part, latents = call(
        functools.partial(bank_grad_kernel, samples, small_rows),
        "bank_grad",
        [(bank.shape, F32), ((samples, in_ch), F32), ((samples, latent.shape[1]), F32)],
        place,
        bank,
        *every,
        scalars=1,
        scratch=[((samples, slots, out_ch, in_ch), BF16), (bank.shape, F32), pltpu.SemaphoreType.DMA((TAPS,))],
        kept=1,
    )
    style_parts = terms_of_sum(style_part, "chan")
    edge = jnp.concatenate(
        [from_above[:, None], jnp.zeros((ch, height - 2, width), F32), from_below[:, None]], axis=1
    )
    feature_grad = (main.reshape(ch, height, width) + edge).astype(BF16)[None]
    style_parts, feature_grad = lax.optimization_barrier((style_parts, feature_grad))
    affine_w_grad, affine_b_grad = call(
        functools.partial(affine_kernel, samples),
        "affine",
        [(affine_w.shape, F32), ((1, in_ch), F32)],
        latents,
        *style_parts,
    )
    return (feature_grad, bank_grad, affine_w_grad, affine_b_grad[0])


def solution(mesh):
    return jax.shard_map(
        on_device,
        mesh=mesh,
        in_specs=(
            P("samples", "chan", "rows", None),
            P("samples", "chan", "rows", None),
            P(None, None, "chan", "rows"),
            P("samples", None),
            P("samples", None),
            P(None, "rows"),
            P("rows"),
        ),
        out_specs=(
            P("samples", "chan", "rows", None),
            P(None, None, "chan", "rows"),
            P(None, "rows"),
            P("rows"),
        ),
        check_vma=False,
    )
```

```python
import functools

import jax
import jax.numpy as jnp
from jax import lax
from jax.experimental import pallas as pl
from jax.experimental.pallas import tpu as pltpu
from jax.sharding import PartitionSpec as P

EPS = 1e-08
TAPS = 9
F32 = jnp.float32
BF16 = jnp.bfloat16
VMEM_LIMIT = 10 * 2**20
COLLECT_FLOPS = 6 * 10**9
INPUT_FLOPS = 2 * 10**9


def params():
    return pltpu.CompilerParams(vmem_limit_bytes=VMEM_LIMIT)


def vspec(n):
    return [pl.BlockSpec(memory_space=pltpu.VMEM)] * n


def sspec(n):
    return [pl.BlockSpec(memory_space=pltpu.SMEM)] * n


def cost(flops, moved):
    return pl.CostEstimate(flops=flops, bytes_accessed=moved, transcendentals=0)


def beside(pieces):
    return pieces[0] if len(pieces) == 1 else jnp.concatenate(pieces, axis=1)


def mixed(bank_ref, weights, tap):
    total = weights[0] * bank_ref[0, tap]
    for k in range(1, bank_ref.shape[0]):
        total = total + weights[k] * bank_ref[k, tap]
    return total


def plain_kernel(*refs):
    given, (plain_out, small), held, sems = refs[:5], refs[5:7], refs[7:12], refs[12]
    copies = [pltpu.make_async_copy(x, y, sems.at[n]) for n, (x, y) in enumerate(zip(given, held))]
    for copy in copies:
        copy.start()
    for copy in copies:
        copy.wait()
    select, latent, affine_b, affine_w, bank = held
    style = (
        jnp.dot(latent[...], affine_w[...], precision=lax.Precision.HIGHEST, preferred_element_type=F32)
        + affine_b[...]
    )
    filters, in_ch = bank.shape[0], bank.shape[3]
    weights = [select[0, k].astype(F32) for k in range(filters)]
    total = jnp.zeros(bank.shape[2:], F32)
    for tap in range(TAPS):
        plain = mixed(bank, weights, tap) * style
        plain_out[tap] = plain
        total = total + plain * plain
    plain_out[TAPS] = jnp.broadcast_to(jnp.sum(total, axis=1, keepdims=True), total.shape)
    small[...] = jnp.zeros(small.shape, F32)
    last = latent.shape[1] // in_ch
    for n in range(last):
        small[n : n + 1] = latent[:, n * in_ch : (n + 1) * in_ch]
    small[last : last + 1] = style
    lane = lax.broadcasted_iota(jnp.int32, (1, in_ch), 1)
    row = jnp.zeros((1, in_ch), F32)
    for k in range(filters):
        row = jnp.where(lane == k, weights[k], row)
    small[last + 1 : last + 2] = row


def blocks_kernel(rows, size, place, *refs):
    parts, (whole, scale_out), outs, (by_row, by_chan) = refs[:rows], refs[rows : rows + 2], refs[rows + 2 : -2], refs[-2:]
    row_at, chan_at, sign = place[2], place[1], place[3]
    energy = parts[0][TAPS]
    for part in parts[1:]:
        energy = energy + part[TAPS]
    scale = lax.rsqrt(energy[:, 0:1] + EPS)
    scale_out[...] = jnp.broadcast_to(scale, scale_out.shape)
    for r in range(rows):
        by_row[lax.rem(row_at - r + rows, rows)] = parts[r][0:TAPS]
    ch = whole.shape[2] // size
    taps = []
    for tap in range(TAPS):
        value = beside([by_row[r, tap] for r in range(rows)]) * scale
        whole[tap] = value.astype(BF16)
        taps.append(value)
    for z in range(size):
        by_chan[z] = beside([value[:, z * ch : (z + 1) * ch] for value in taps]).astype(BF16)
    for d in range(size):
        outs[d][...] = by_chan[lax.rem(chan_at + sign * d + size, size)]
    outs[size][...] = by_chan[size - 1 - chan_at]


def shifted(x, by):
    width = x.shape[1]
    lane = lax.broadcasted_iota(jnp.int32, x.shape, 1)
    moved = pltpu.roll(x, by % width, 1)
    return jnp.where(lane == (0 if by == 1 else width - 1), 0.0, moved)


def spread(wide, row, x):
    ch, width = x.shape
    wide[ch : 2 * ch, row * width : (row + 1) * width] = x
    x = x.astype(F32)
    wide[0:ch, row * width : (row + 1) * width] = shifted(x, 1).astype(BF16)
    wide[2 * ch : 3 * ch, row * width : (row + 1) * width] = shifted(x, -1).astype(BF16)


def rows_kernel(height, width, feat, feat_before, feat_after, out):
    out[:, 0:width] = feat_before[...]
    out[:, width : (height + 1) * width] = feat[...]
    out[:, (height + 1) * width :] = feat_after[...]


def tap_products(g_ref, wides, totals, height, width):
    g = g_ref[...]
    contract = (((1,), (1,)), ((), ()))
    out = []
    for wide in wides:
        rows = [wide[:, kh * width : (kh + height) * width] for kh in range(3)]
        parts = [lax.dot_general(g, x, contract, preferred_element_type=F32) for x in rows]
        out.append(jnp.concatenate(parts, axis=1).astype(BF16))
    return out


def near_grad_kernel(height, width, *refs):
    cotans, feat, mods, (own, behind, ahead), (wide, gathered, total) = refs[:3], refs[3], refs[4:6], refs[6:9], refs[9:]
    ch = feat.shape[0]
    for at, cotan in enumerate(cotans):
        gathered[at * ch : (at + 1) * ch] = cotan[...]
    for row in range(height + 2):
        spread(wide, row, feat[:, row * width : (row + 1) * width])
    (whole,) = tap_products(gathered, [wide], [total], height, width)
    own[...] = whole[0:ch]
    for at, (out, mod) in enumerate(zip((behind, ahead), mods)):
        out[0:ch] = whole[(at + 1) * ch : (at + 2) * ch]
        out[ch:] = mod[...]


def middle_grad_kernel(count, height, width, *refs):
    first, second, wide, mods = refs[:count], refs[count : 2 * count], refs[2 * count], refs[2 * count + 1 : 3 * count + 1]
    out, middle, end_block, total = refs[3 * count + 1 :]
    ch = end_block.shape[0]
    for at in range(count):
        middle[at * ch : (at + 1) * ch] = first[at][...] + second[count - 1 - at][...]
    end_block[...] = first[-1][...] + second[-1][...]
    (out[0 : count * ch],) = tap_products(middle, [wide], [total], height, width)
    for at, mod in enumerate(mods):
        out[(count + at) * ch : (count + at + 1) * ch] = mod[...]


def end_grad_kernel(height, width, end_block, feat, out, wide, total):
    for row in range(height + 2):
        spread(wide, row, feat[:, row * width : (row + 1) * width])
    (out[...],) = tap_products(end_block, [wide], [total], height, width)


def input_grad_kernel(rows, size, height, width, place, cotan, first, second, middle, far, own_mod, behind, ahead, others, end_mod, *refs):
    main, before, after, gathered, taps_t = refs
    ch = main.shape[0]
    spot = jnp.where(place[3] > 0, place[1], size - 1 - place[1])
    gathered[0:ch] = cotan[...]
    gathered[ch : 2 * ch] = jnp.where(spot == 0, far[...], first[...])
    gathered[2 * ch : (size - 1) * ch] = middle[...]
    gathered[(size - 1) * ch :] = jnp.where(spot == size - 1, far[...], second[...])
    mods = [own_mod[...], jnp.where(spot == 0, end_mod[...], behind[ch:])]
    mods.append(others[(size - 3) * ch :])
    mods.append(jnp.where(spot == size - 1, end_mod[...], ahead[ch:]))
    every = jnp.concatenate([mod.astype(F32) for mod in mods], axis=0)
    taps_t[...] = every.T.astype(BF16)
    for row in range(height + 2):
        total = None
        for kh in range(3):
            if 0 <= row - kh < height:
                g = gathered[:, (row - kh) * width : (row - kh + 1) * width]
                y = jnp.dot(taps_t[kh * 3 * ch : (kh + 1) * 3 * ch], g, preferred_element_type=F32)
                total = y if total is None else total + y
        value = total[ch : 2 * ch]
        value = value + shifted(total[0:ch], -1) + shifted(total[2 * ch : 3 * ch], 1)
        if row == 0:
            before[...] = value
        elif row == height + 1:
            after[...] = jnp.where(place[2] == 1, before[...], value) if rows == 2 else value
        else:
            main[:, (row - 1) * width : row * width] = value


def split3(x):
    high = x.astype(BF16).astype(F32)
    mid = (x - high).astype(BF16).astype(F32)
    return high, mid, x - high - mid


def put_columns(out, columns):
    lane = lax.broadcasted_iota(jnp.int32, out.shape[1:], 1)
    last = jnp.zeros(out.shape[1:], F32)
    for n, column in enumerate(columns):
        for at, piece in enumerate(split3(column)):
            last = jnp.where(lane == 3 * n + at, piece, last)
    out[TAPS] = last.astype(BF16)


def get_column(last, n=0):
    last = last.astype(F32)
    return last[:, 3 * n : 3 * n + 1] + last[:, 3 * n + 1 : 3 * n + 2] + last[:, 3 * n + 2 : 3 * n + 3]


def collect_kernel(rows, size, place, scale, whole_mod, own, ahead, behind, others, end, *refs):
    outs, (by_chan, by_row) = refs[:rows], refs[rows:]
    chan_at, row_at, sign = place[1], place[2], place[3]
    ch = own.shape[0]
    by_chan[chan_at] = own[...].astype(F32)
    by_chan[lax.rem(chan_at + sign + size, size)] = ahead[0:ch].astype(F32)
    by_chan[lax.rem(chan_at - sign + size, size)] = behind[0:ch].astype(F32)
    for d in range(2, size - 1):
        value = others[(d - 2) * ch : (d - 1) * ch].astype(F32)
        by_chan[lax.rem(chan_at + sign * d + size, size)] = value
    by_chan[jnp.where(chan_at == 0, size - 1, 0)] += end[...].astype(F32)
    in_ch = outs[0].shape[2]
    product = jnp.zeros(whole_mod.shape[1:], F32)
    for tap in range(TAPS):
        value = beside([by_chan[z, :, tap * ch : (tap + 1) * ch] for z in range(size)])
        product = product + value * whole_mod[tap].astype(F32)
        for r in range(rows):
            by_row[r, tap] = value[:, r * in_ch : (r + 1) * in_ch].astype(BF16)
    fall = jnp.sum(product, axis=1, keepdims=True) * (scale[:, 0:1] * scale[:, 0:1])
    for r in range(rows):
        outs[r][0:TAPS] = by_row[lax.rem(row_at + r, rows)]
        put_columns(outs[r], [fall])


def row_sum_kernel(scale, small, *refs):
    parts, out = refs[:-1], refs[-1]
    fall = get_column(parts[0][TAPS])
    for part in parts[1:]:
        fall = fall + get_column(part[TAPS])
    for tap in range(TAPS):
        value = parts[0][tap].astype(F32)
        for part in parts[1:]:
            value = value + part[tap].astype(F32)
        out[tap] = value.astype(BF16)
    put_columns(out, [fall, scale[:, 0:1]])
    out_ch, in_ch = out.shape[1:]
    pieces = list(split3(small[...]))
    spare = (out.shape[0] - TAPS - 1) * out_ch - 3 * small.shape[0]
    if spare:
        pieces.append(jnp.zeros((spare, in_ch), F32))
    pieces = jnp.concatenate(pieces, axis=0).astype(BF16)
    for n in range(out.shape[0] - TAPS - 1):
        out[TAPS + 1 + n] = pieces[n * out_ch : (n + 1) * out_ch]


def bank_grad_kernel(samples, small_rows, place, bank, *refs):
    parts, (bank_out, style_grad, latents, held, bank_grad, sems) = refs[:samples], refs[samples:]
    copies = [pltpu.make_async_copy(bank_grad.at[:, tap], bank_out.at[:, tap], sems.at[tap]) for tap in range(TAPS)]
    for part, step in zip(parts, steps_of(samples)):
        held[partner(place[0], step, samples)] = part[...]
    filters, in_ch = bank.shape[0], bank.shape[3]
    last = latents.shape[1] // in_ch
    sel, styles, scales, falls = [], [], [], []
    for b in range(samples):
        rows = jnp.concatenate([held[b, n].astype(F32) for n in range(TAPS + 1, held.shape[1])], axis=0)
        small = rows[:small_rows] + rows[small_rows : 2 * small_rows] + rows[2 * small_rows : 3 * small_rows]
        latents[b : b + 1] = beside([small[n : n + 1] for n in range(last)])
        styles.append(small[last : last + 1])
        sel.append([small[last + 1 : last + 2, k : k + 1] for k in range(filters)])
        falls.append(get_column(held[b, TAPS]))
        scales.append(get_column(held[b, TAPS], 1))
    sums = [jnp.zeros(bank.shape[2:], F32) for _ in range(samples)]
    for tap in range(TAPS):
        totals = [None] * filters
        for b in range(samples):
            kern = mixed(bank, sel[b], tap)
            plain_grad = held[b, tap].astype(F32) * scales[b] - kern * styles[b] * falls[b]
            sums[b] = sums[b] + plain_grad * kern
            kernel_grad = plain_grad * styles[b]
            for k in range(filters):
                term = sel[b][k] * kernel_grad
                totals[k] = term if totals[k] is None else totals[k] + term
        for k in range(filters):
            bank_grad[k, tap] = totals[k]
        copies[tap].start()
    for b in range(samples):
        value = jnp.sum(sums[b], axis=0, keepdims=True)
        style_grad[b : b + 1] = value
    for copy in copies:
        copy.wait()


def pair_sum(parts):
    while len(parts) > 1:
        parts = [x + y for x, y in zip(parts[::2], parts[1::2])]
    return parts[0]


def affine_kernel(samples, latents, *refs):
    parts, (w_grad, b_grad) = refs[:-2], refs[-2:]
    style_grad = pair_sum([part[...] for part in parts])
    high, mid, low = split3(latents[...])
    top, middle, bottom = split3(style_grad)
    w_grad[...] = lax.dot_general(
        jnp.concatenate([high, high, mid, high, mid, low], axis=0).astype(BF16),
        jnp.concatenate([top, middle, top, bottom, middle, top], axis=0).astype(BF16),
        (((0,), (0,)), ((), ())),
        preferred_element_type=F32,
    )
    bias = style_grad[0:1]
    for b in range(1, samples):
        bias = bias + style_grad[b : b + 1]
    b_grad[...] = bias


def call(kernel, name, outs, *operands, scalars=0, fetched=0, kept=0, scratch=(), flops=10**6):
    outs = tuple(jax.ShapeDtypeStruct(*o) for o in outs)
    moved = sum(o.size * o.dtype.itemsize for o in (*outs, *operands))
    return pl.pallas_call(
        kernel,
        out_shape=outs,
        in_specs=sspec(scalars)
        + vspec(len(operands) - scalars - fetched)
        + [pl.BlockSpec(memory_space=pltpu.HBM)] * fetched,
        out_specs=tuple([pl.BlockSpec(memory_space=pltpu.HBM)] * kept + vspec(len(outs) - kept)),
        scratch_shapes=[pltpu.VMEM(*s) if isinstance(s, tuple) else s for s in scratch],
        compiler_params=params(),
        cost_estimate=cost(flops, moved),
        name=name,
    )(*operands)


def partner(at, step, size):
    return at ^ step if size & (size - 1) == 0 else (at - step + size) % size


def steps_of(size):
    return [0] + sorted(range(1, size), key=lambda n: (n < 2, n))


def exchange_pairs(x, axis):
    size = lax.axis_size(axis)
    return [x] + [
        lax.ppermute(x, axis, [(partner(i, step, size), i) for i in range(size)]) for step in steps_of(size)[1:]
    ]


def exchange(x, axis):
    size = lax.axis_size(axis)
    return [x] + [
        lax.ppermute(x, axis, [(i, (i + s) % size) for i in range(size)]) for s in range(1, size)
    ]


def terms_of_sum(x, axis):
    size = lax.axis_size(axis)
    if size & (size - 1):
        return [lax.psum(x, axis)]
    return [x] + [lax.ppermute(x, axis, [(i, i ^ step) for i in range(size)]) for step in range(1, size)]


def from_sides(first, last, axis):
    size, at = lax.axis_size(axis), lax.axis_index(axis)
    if size == 2:
        edge = last if first is None else jnp.where(at == 0, last, first)
        got = lax.ppermute(edge, axis, [(0, 1), (1, 0)])
        nothing = jnp.zeros_like(got)
        return jnp.where(at == 1, got, nothing), jnp.where(at == 0, got, nothing)
    up = [(i, i + 1) for i in range(size - 1)]
    down = [(i + 1, i) for i in range(size - 1)]
    return lax.ppermute(last, axis, up), lax.ppermute(first, axis, down)


def on_device(feature, out_grad, bank, select, latent, affine_w, affine_b):
    rows, samples, size = (lax.axis_size(a) for a in ("rows", "samples", "chan"))
    row_at, sample_at, chan_at = (lax.axis_index(a) for a in ("rows", "samples", "chan"))
    _, ch, height, width = feature.shape
    out_ch, in_ch = bank.shape[2:]
    pixels, all_ch = height * width, ch * size
    sign = 1 - 2 * jnp.remainder(sample_at, 2)
    place = jnp.stack([sample_at, chan_at, row_at, sign]).astype(jnp.int32)
    flops = 2 * TAPS * ch * ch * size * pixels

    def along(x, pairs):
        whole = []
        for b in range(samples):
            for i, j in pairs:
                if b % 2:
                    i, j = size - 1 - i, size - 1 - j
                whole.append((b * size + i, b * size + j))
        return lax.ppermute(x, ("samples", "chan"), whole)

    cotan = out_grad[0].reshape(ch, pixels)
    first, second = [], []

    def step(number, x, y):
        first.append(along(x, [(i, i + 1) for i in range(number - 1, size - 1)]))
        second.append(along(y, [(i + 1, i) for i in range(size - number)]))

    step(1, cotan, cotan)

    small_rows = -(-(latent.shape[1] // in_ch + 2) // 8) * 8
    plain, small = call(
        plain_kernel,
        "plain",
        [((TAPS + 1, out_ch, in_ch), F32), ((small_rows, in_ch), F32)],
        select,
        latent,
        affine_b[None],
        affine_w,
        bank,
        fetched=5,
        scratch=[
            pltpu.SMEM(select.shape, jnp.int32),
            (latent.shape, F32),
            ((1, in_ch), F32),
            (affine_w.shape, F32),
            (bank.shape, F32),
            pltpu.SemaphoreType.DMA((5,)),
        ],
    )
    plains = exchange(plain, "rows")
    feature, cotan = lax.optimization_barrier((feature, cotan))
    feat = feature[0].reshape(ch, pixels)
    feat_before, feat_after = from_sides(feat[:, :width], feat[:, pixels - width :], "rows")
    extended = ((ch, (height + 2) * width), BF16)
    (feat,) = call(
        functools.partial(rows_kernel, height, width), "feat_rows", [extended], feat, feat_before, feat_after
    )
    feat, plain = lax.optimization_barrier((feat, plain))
    feat_end = lax.ppermute(feat, "chan", [(0, 1), (size - 1, size - 2)])
    message = ((ch, TAPS * ch), BF16)
    whole_mod, scale, *mods = call(
        functools.partial(blocks_kernel, rows, size),
        "mod_blocks",
        [((TAPS, out_ch, all_ch), BF16), ((out_ch, 128), F32)] + [message] * (size + 1),
        place,
        *plains,
        scalars=1,
        scratch=[((rows, TAPS, out_ch, in_ch), F32), ((size, *message[0]), BF16)],
    )
    first[0], second[0], plains = lax.optimization_barrier((first[0], second[0], plains))

    step(2, first[0], second[0])
    double = ((2 * ch, TAPS * ch), BF16)
    own_grad, to_behind, to_ahead, wide = call(
        functools.partial(near_grad_kernel, height, width),
        "near_grad",
        [message, double, double, ((3 * ch, (height + 2) * width), BF16)],
        cotan,
        first[0],
        second[0],
        feat,
        mods[size - 1],
        mods[1],
        scratch=[((3 * ch, pixels), BF16), ((3, 3 * ch, 3 * ch), F32)],
        flops=flops * 3 // size,
    )
    from_ahead = along(to_behind, [(i + 1, i) for i in range(size - 1)])
    from_behind = along(to_ahead, [(i, i + 1) for i in range(size - 1)])
    first[1], second[1], feat_end, wide, whole_mod = lax.optimization_barrier(
        (first[1], second[1], feat_end, wide, whole_mod)
    )

    count = size - 3
    grad_others, middle, end_block = call(
        functools.partial(middle_grad_kernel, count, height, width),
        "middle_grad",
        [((2 * count * ch, TAPS * ch), BF16), ((count * ch, pixels), BF16), ((ch, pixels), BF16)],
        *first[1:],
        *second[1:],
        wide,
        *mods[2 : size - 1],
        scratch=[((3, count * ch, 3 * ch), F32)],
        flops=flops // size,
    )
    (grad_end,) = call(
        functools.partial(end_grad_kernel, height, width),
        "end_grad",
        [message],
        end_block,
        feat_end,
        scratch=[((3 * ch, (height + 2) * width), BF16), ((3, ch, 3 * ch), F32)],
        flops=flops // size,
    )
    from_others = along(grad_others, [(i, (i + 2) % size) for i in range(size)])
    from_end = lax.ppermute(grad_end, "chan", [(1, size - 1), (size - 2, 0)])
    end_block, grad_end = lax.optimization_barrier((end_block, grad_end))
    far = lax.ppermute(end_block, "chan", [(1, 0), (size - 2, size - 1)])
    parts = call(
        functools.partial(collect_kernel, rows, size),
        "collect",
        [((TAPS + 1, out_ch, in_ch), BF16)] * rows,
        place,
        scale,
        whole_mod,
        own_grad,
        from_ahead,
        from_behind,
        from_others,
        from_end,
        scalars=1,
        scratch=[((size, *message[0]), F32), ((rows, TAPS, out_ch, in_ch), BF16)],
        flops=COLLECT_FLOPS,
    )
    parts, mods = lax.optimization_barrier((parts, mods))
    end_mod = lax.ppermute(mods[size], "chan", [(0, size - 1), (size - 1, 0)])
    parts = [parts[0]] + [
        lax.ppermute(parts[r], "rows", [(i, (i + r) % rows) for i in range(rows)])
        for r in range(1, rows)
    ]
    slots = TAPS + 1 - (-3 * small_rows // out_ch)
    (own,) = call(row_sum_kernel, "row_sum", [((slots, out_ch, in_ch), BF16)], scale, small, *parts)
    every = exchange_pairs(own, "samples")

    own, end_mod, far = lax.optimization_barrier((own, end_mod, far))
    main, before, after = call(
        functools.partial(input_grad_kernel, rows, size, height, width),
        "input_grad",
        [((ch, pixels), F32), ((ch, width), F32), ((ch, width), F32)],
        place,
        cotan,
        first[0],
        second[0],
        middle,
        far,
        mods[0],
        from_behind,
        from_ahead,
        from_others,
        end_mod,
        scalars=1,
        scratch=[
            ((all_ch, pixels), BF16),
            ((TAPS * ch, all_ch), BF16),
        ],
        flops=INPUT_FLOPS,
    )
    every, main, before, after = lax.optimization_barrier((every, main, before, after))
    from_above, from_below = from_sides(None if rows == 2 else before, after, "rows")
    bank_grad, style_part, latents = call(
        functools.partial(bank_grad_kernel, samples, small_rows),
        "bank_grad",
        [(bank.shape, F32), ((samples, in_ch), F32), ((samples, latent.shape[1]), F32)],
        place,
        bank,
        *every,
        scalars=1,
        scratch=[((samples, slots, out_ch, in_ch), BF16), (bank.shape, F32), pltpu.SemaphoreType.DMA((TAPS,))],
        kept=1,
    )
    style_parts = terms_of_sum(style_part, "chan")
    edge = jnp.concatenate(
        [from_above[:, None], jnp.zeros((ch, height - 2, width), F32), from_below[:, None]], axis=1
    )
    feature_grad = (main.reshape(ch, height, width) + edge).astype(BF16)[None]
    style_parts, feature_grad = lax.optimization_barrier((style_parts, feature_grad))
    affine_w_grad, affine_b_grad = call(
        functools.partial(affine_kernel, samples),
        "affine",
        [(affine_w.shape, F32), ((1, in_ch), F32)],
        latents,
        *style_parts,
    )
    return (feature_grad, bank_grad, affine_w_grad, affine_b_grad[0])


def solution(mesh):
    return jax.shard_map(
        on_device,
        mesh=mesh,
        in_specs=(
            P("samples", "chan", "rows", None),
            P("samples", "chan", "rows", None),
            P(None, None, "chan", "rows"),
            P("samples", None),
            P("samples", None),
            P(None, "rows"),
            P("rows"),
        ),
        out_specs=(
            P("samples", "chan", "rows", None),
            P(None, None, "chan", "rows"),
            P(None, "rows"),
            P("rows"),
        ),
        check_vma=False,
    )
```
